32 devices in a mesh: dp: 8 (over z, y), ctx: 4 (over x, core).
Axes of the slice: x: 2, y: 2, z: 4, core: 2. Of those that a mesh axis runs over, the one named last changes fastest.
Arguments:
- tokens: bfloat16 [16, 2048, 768], P('dp', 'ctx'), may hold values from -6 to 6
- segments: int32 [16, 2048], P('dp'), may hold values from 0 to 3, as said below
- ln1_gain: bfloat16 [768], P(('dp', 'ctx')), may hold values from 0.5 to 1.5
- ln1_bias: bfloat16 [768], P(('dp', 'ctx')), may hold values from -4 to 4
- qkv_weight: bfloat16 [768, 2304], P(('dp', 'ctx')), may hold values from -0.21875 to 0.21875
- q_bias: bfloat16 [768], P(('dp', 'ctx')), may hold values from -4 to 4
- v_bias: bfloat16 [768], P(('dp', 'ctx')), may hold values from -4 to 4
- out_weight: bfloat16 [768, 768], P(('dp', 'ctx')), may hold values from -0.875 to 0.875
- out_bias: bfloat16 [768], P(('dp', 'ctx')), may hold values from -4 to 4
- ln2_gain: bfloat16 [768], P(('dp', 'ctx')), may hold values from 0.5 to 1.5
- ln2_bias: bfloat16 [768], P(('dp', 'ctx')), may hold values from -4 to 4
- up_weight: bfloat16 [768, 3072], P(('dp', 'ctx')), may hold values from -0.21875 to 0.21875
- up_bias: bfloat16 [3072], P(('dp', 'ctx')), may hold values from -4 to 4
- down_weight: bfloat16 [3072, 768], P(('dp', 'ctx')), may hold values from -0.21875 to 0.21875
- down_bias: bfloat16 [768], P(('dp', 'ctx')), may hold values from -4 to 4
- cotangent: bfloat16 [16, 2048, 768], P('dp', 'ctx'), may hold values from -6 to 6
Outputs:
- mixed: bfloat16 [16, 2048, 768], P('dp', 'ctx')
- token_grad: bfloat16 [16, 2048, 768], P('dp', 'ctx')
- grad_ln1_gain: float32 [768], P(('dp', 'ctx'))
- grad_ln1_bias: float32 [768], P(('dp', 'ctx'))
- grad_qkv_weight: float32 [768, 2304], P(('dp', 'ctx'))
- grad_q_bias: float32 [768], P(('dp', 'ctx'))
- grad_v_bias: float32 [768], P(('dp', 'ctx'))
- grad_out_weight: float32 [768, 768], P(('dp', 'ctx'))
- grad_out_bias: float32 [768], P(('dp', 'ctx'))
- grad_ln2_gain: float32 [768], P(('dp', 'ctx'))
- grad_ln2_bias: float32 [768], P(('dp', 'ctx'))
- grad_up_weight: float32 [768, 3072], P(('dp', 'ctx'))
- grad_up_bias: float32 [3072], P(('dp', 'ctx'))
- grad_down_weight: float32 [3072, 768], P(('dp', 'ctx'))
- grad_down_bias: float32 [768], P(('dp', 'ctx'))
The draws below stay inside these ranges and needn't reach their ends.
Inputs may be any that keep to these rules, and one draw needn't show every extreme that they name: `segments`: segment numbers never fall along a sequence.
All inputs are finite; a program needn't handle non-finite values.
Results may differ from the reference program's by a relative error of at most 0.014.
Values may be sent and summed in bfloat16 or wider, within the bound.
No kernel may reach another device: no remote copies, remote signals or barrier semaphores. Data moves between devices by JAX's collectives and lax.ppermute only.
A program may use at most 256 MiB of HBM per device.

```python
import jax
import jax.numpy as jnp
from jax import lax

D = 768
HEADS = 12
HEAD_DIM = 64
FF = 3072
LENGTH = 2048
SEQ_DEV = 2
SEQS = 16


def draw_segments(key, part):
    key = jax.random.fold_in(key, 11)
    cut_key, pick_key = jax.random.split(key)
    cuts = jax.random.randint(cut_key, (SEQS, 3), 1, LENGTH)
    places = jnp.arange(LENGTH)
    counted = jnp.sum((places[None, :, None] >= cuts[:, None, :]).astype(jnp.int32), axis=2)
    chosen = jax.random.randint(pick_key, (SEQS // SEQ_DEV,), 0, SEQ_DEV)
    single = jnp.arange(SEQS) % SEQ_DEV == jnp.repeat(chosen, SEQ_DEV)
    return jnp.where(single[:, None], 0, counted).astype(jnp.int32)


def shard_levels(own_key, dims, shards, low, high):
    factor_of, own = 1.0, jax.random.fold_in(own_key, 6)
    for axis_at, blocks in shards:
        heights = jnp.exp(jax.random.uniform(jax.random.fold_in(own, axis_at), (blocks,), jnp.float32, low / len(shards), high / len(shards)))
        factor_of = factor_of * jnp.repeat(heights, dims[axis_at] // blocks).reshape([-1 if axis == axis_at else 1 for axis in range(len(dims))])
    return factor_of


def normal_values(rng, dims, width, limit, shards=(), dtype=jnp.bfloat16):
    drawn = jax.random.normal(rng, dims, jnp.float32) * width
    if len(shards) > 0:
        drawn = shard_levels(rng, dims, shards, -0.22, 0.18) * drawn
    return jnp.clip(drawn, min=-limit, max=limit).astype(dtype)


def setup_inputs(seed: int = 0) -> dict:
    key_of = jax.random.split(jax.random.key(seed), 17)
    tokens = normal_values(key_of[0], (SEQS, LENGTH, D), 1.0, 6.0, ((0, 8), (1, 4)))
    segments = draw_segments(jax.random.fold_in(key_of[16], 71), 0)
    ln1_gain = jnp.clip(1.0 + 0.1 * jax.random.normal(key_of[2], (D,), jnp.float32), 0.5, 1.5).astype(jnp.bfloat16)
    ln1_bias = normal_values(key_of[3], (D,), 0.3, 4.0, ((0, 32),))
    qkv_weight = normal_values(key_of[4], (D, 3 * D), D ** -0.5, 0.21875, ((0, 32),))
    q_bias = normal_values(key_of[5], (D,), 0.3, 4.0, ((0, 32),))
    v_bias = normal_values(key_of[6], (D,), 0.3, 4.0, ((0, 32),))
    out_weight = normal_values(key_of[7], (D, D), (D // 16) ** -0.5, 0.875, ((0, 32),))
    out_bias = normal_values(key_of[8], (D,), 0.3, 4.0, ((0, 32),))
    ln2_gain = jnp.clip(1.0 + 0.1 * jax.random.normal(key_of[9], (D,), jnp.float32), 0.5, 1.5).astype(jnp.bfloat16)
    ln2_bias = normal_values(key_of[10], (D,), 0.3, 4.0, ((0, 32),))
    up_weight = normal_values(key_of[11], (D, FF), D ** -0.5, 0.21875, ((0, 32),))
    up_bias = normal_values(key_of[12], (FF,), 0.3, 4.0, ((0, 32),))
    down_weight = normal_values(key_of[13], (FF, D), (FF // 4) ** -0.5, 0.21875, ((0, 32),))
    down_bias = normal_values(key_of[14], (D,), 0.3, 4.0, ((0, 32),))
    cotangent = normal_values(key_of[15], (SEQS, LENGTH, D), 1.0, 6.0, ((0, 8), (1, 4)))
    return {"tokens": tokens, "segments": segments, "ln1_gain": ln1_gain, "ln1_bias": ln1_bias, "qkv_weight": qkv_weight, "q_bias": q_bias, "v_bias": v_bias, "out_weight": out_weight, "out_bias": out_bias, "ln2_gain": ln2_gain, "ln2_bias": ln2_bias, "up_weight": up_weight, "up_bias": up_bias, "down_weight": down_weight, "down_bias": down_bias, "cotangent": cotangent}


@jax.custom_vjp
def low(v):
    return lax.optimization_barrier(v.astype(jnp.bfloat16)).astype(jnp.float32)

@jax.custom_vjp
def low_back(v):
    return v

def low_keep(v):
    return (low(v), None)

def low_pass(kept, grad):
    return (grad,)

def back_keep(v):
    return (v, None)

def back_low(kept, grad):
    return (low(grad),)
low.defvjp(low_keep, low_pass)
low_back.defvjp(back_keep, back_low)
EPSILON = 1e-05
PRECISE = lax.Precision.HIGHEST

def layer_norm(source, scale_vec, shift_vec):
    average = lax.optimization_barrier(jnp.mean(source, axis=-1, keepdims=True))
    centred = source - average
    spread = lax.optimization_barrier(jnp.mean(centred * centred, axis=-1, keepdims=True))
    return centred * lax.rsqrt(spread + EPSILON) * scale_vec + shift_vec

def gelu_tanh(source):
    return jax.nn.gelu(source, approximate=True)

def attend_sequence(queries, key_rows, value_rows, segment_ids):
    positions = jnp.arange(LENGTH)
    q_heads = queries.reshape(LENGTH, HEADS, HEAD_DIM)
    k_heads = key_rows.reshape(LENGTH, HEADS, HEAD_DIM)
    v_heads = value_rows.reshape(LENGTH, HEADS, HEAD_DIM)
    scores = low_back(jnp.einsum('qhd,khd->hqk', q_heads, k_heads, precision=PRECISE))
    allowed = (positions[None, :] <= positions[:, None]) & (segment_ids[None, :] == segment_ids[:, None])
    scores = jnp.where(allowed[None], scores, -1e+30)
    probs = low(jax.nn.softmax(scores, axis=-1))
    attended = jnp.einsum('hqk,khd->qhd', probs, v_heads, precision=PRECISE)
    return attended.reshape(LENGTH, D)
attend_block = jax.checkpoint(attend_sequence)

def layer(inputs, params, segment_ids):
    ln1_gain, ln1_bias, qkv_weight, q_bias, v_bias, out_weight, out_bias, ln2_gain, ln2_bias, up_weight, up_bias, down_weight, down_bias = params
    group = inputs.shape[0]
    flat_in = inputs.reshape(group * LENGTH, D)
    normed = low(layer_norm(flat_in, ln1_gain, ln1_bias))
    joint = jnp.dot(normed, qkv_weight, precision=PRECISE)
    queries = low(low_back((joint[:, :D] + q_bias) * 0.125))
    key_rows = low(low_back(joint[:, D:2 * D]))
    value_rows = low(low_back(joint[:, 2 * D:] + v_bias))

    def attend_pieces(blocks):
        return attend_block(blocks[0], blocks[1], blocks[2], blocks[3])
    attended = lax.map(attend_pieces, (queries.reshape(group, LENGTH, D), key_rows.reshape(group, LENGTH, D), value_rows.reshape(group, LENGTH, D), segment_ids))
    attended = low(low_back(attended.reshape(group * LENGTH, D)))
    branch = low_back(jnp.dot(attended, out_weight, precision=PRECISE) + out_bias)
    middle = flat_in + branch
    normed_two = low(layer_norm(middle, ln2_gain, ln2_bias))
    hidden_pre = low_back(jnp.dot(normed_two, up_weight, precision=PRECISE) + up_bias)
    hidden = low(gelu_tanh(hidden_pre))
    ffn_out = low_back(jnp.dot(hidden, down_weight, precision=PRECISE) + down_bias)
    return (middle + ffn_out).reshape(group, LENGTH, D)

def reference(tokens, segments, ln1_gain, ln1_bias, qkv_weight, q_bias, v_bias, out_weight, out_bias, ln2_gain, ln2_bias, up_weight, up_bias, down_weight, down_bias, cotangent):
    params = tuple((tensor.astype(jnp.float32) for tensor in (ln1_gain, ln1_bias, qkv_weight, q_bias, v_bias, out_weight, out_bias, ln2_gain, ln2_bias, up_weight, up_bias, down_weight, down_bias)))
    groups = SEQS // SEQ_DEV
    inputs = tokens.astype(jnp.float32).reshape(groups, SEQ_DEV, LENGTH, D)
    back_in = cotangent.astype(jnp.float32).reshape(groups, SEQ_DEV, LENGTH, D)
    seg_groups = segments.reshape(groups, SEQ_DEV, LENGTH)
    totals = tuple((jnp.zeros_like(tensor) for tensor in params))

    def step(carry, blocks):
        block_in, block_seg, block_back = blocks

        def forward(source, weights):
            return layer(source, weights, block_seg)
        result, pull = jax.vjp(forward, block_in, params)
        grad_in, grad_params = pull(block_back)
        carry = tuple((first + second for first, second in zip(carry, grad_params)))
        return (carry, (result.astype(jnp.bfloat16), grad_in.astype(jnp.bfloat16)))
    totals, (outputs, in_grads) = lax.scan(step, totals, (inputs, seg_groups, back_in))
    return (outputs.reshape(SEQS, LENGTH, D), in_grads.reshape(SEQS, LENGTH, D), totals[0], totals[1], totals[2], totals[3], totals[4], totals[5], totals[6], totals[7], totals[8], totals[9], totals[10], totals[11], totals[12])
```

```python
import functools

import jax
import jax.numpy as jnp
from jax import lax
from jax.experimental import pallas as pl
from jax.experimental.pallas import tpu as pltpu
from jax.sharding import Mesh, PartitionSpec as P

HEAD_DIM = 64
PAIR = 2 * HEAD_DIM
EPSILON = 1e-05
NEG = -1e30
BLK = 512
F32 = jnp.float32
BF16 = jnp.bfloat16

NN = (((1,), (0,)), ((), ()))
NT = (((1,), (1,)), ((), ()))
TN = (((0,), (0,)), ((), ()))


def mm(left, right, dims=NN):
    return lax.dot_general(left, right, dims, preferred_element_type=F32)


def build_scores_operands(qkv_ref, qs_ref, ks_ref, rows, qx, kx):
    lane = lax.broadcasted_iota(jnp.int32, (BLK, PAIR), 1)
    first = lane < HEAD_DIM
    q = qkv_ref[rows, 0:PAIR].astype(F32)
    k = qkv_ref[rows, PAIR : 2 * PAIR].astype(F32)
    qs = qs_ref[rows, :].astype(F32)
    ks = ks_ref[rows, :].astype(F32)
    qx[0, rows, :] = jnp.where(first, q, qs).astype(BF16)
    qx[1, rows, :] = jnp.where(first, qs, q).astype(BF16)
    kx[0, rows, :] = jnp.where(first, k, ks).astype(BF16)
    kx[1, rows, :] = jnp.where(first, ks, k).astype(BF16)
    return first, q, k


def causal_block(scores):
    key_at = lax.broadcasted_iota(jnp.int32, scores.shape, 0)
    query_at = lax.broadcasted_iota(jnp.int32, scores.shape, 1)
    return jnp.where(key_at <= query_at, scores, NEG)


def attention_forward_kernel(qkv_ref, qs_ref, ks_ref, o_ref, lse_ref, qx, kx, vt, acc):
    length = qkv_ref.shape[0]
    blocks = length // BLK

    @pl.loop(0, blocks)
    def _(i):
        rows = pl.ds(pl.multiple_of(i * BLK, BLK), BLK)
        build_scores_operands(qkv_ref, qs_ref, ks_ref, rows, qx, kx)
        v_t = qkv_ref[rows, 2 * PAIR : 3 * PAIR].astype(F32).T
        ones = jnp.ones((16, BLK), BF16)
        for h in range(2):
            vt[h, 0:HEAD_DIM, rows] = v_t[h * HEAD_DIM : (h + 1) * HEAD_DIM].astype(BF16)
            vt[h, HEAD_DIM : HEAD_DIM + 16, rows] = ones

    @pl.loop(0, blocks)
    def _(i):
        rows = pl.ds(pl.multiple_of(i * BLK, BLK), BLK)
        queries = [qx[h, rows, :] for h in range(2)]
        tops = []
        for h in range(2):
            s = causal_block(mm(kx[h, rows, :], queries[h], NT))
            top = jnp.max(s, axis=0, keepdims=True)
            p = jnp.exp(s - top).astype(BF16)
            acc[h] = mm(vt[h, :, rows], p)
            tops.append(top)

        def step(j, carry):
            keys = pl.ds(pl.multiple_of(j * BLK, BLK), BLK)
            out = []
            for h in range(2):
                s = mm(kx[h, keys, :], qx[h, rows, :], NT)
                top = jnp.maximum(carry[h], jnp.max(s, axis=0, keepdims=True))
                p = jnp.exp(s - top).astype(BF16)
                acc[h] = acc[h] * jnp.exp(carry[h] - top) + mm(vt[h, :, keys], p)
                out.append(top)
            return tuple(out)

        tops = lax.fori_loop(0, i, step, tuple(tops))
        parts = []
        for h in range(2):
            total = acc[h, HEAD_DIM : HEAD_DIM + 1, :]
            parts.append(acc[h, 0:HEAD_DIM, :] / total)
            lse_ref[0, h : h + 1, rows] = tops[h] + jnp.log(total)
        o_ref[rows, :] = jnp.concatenate(parts, axis=0).T.astype(BF16)


def attention_backward_kernel(
    qkv_ref, qs_ref, ks_ref, o_ref, do_ref, lse_ref, d_ref, qx, kx, qm, dm, kt, delta, dqt, dk, dv
):
    length = qkv_ref.shape[0]
    blocks = length // BLK

    @pl.loop(0, blocks)
    def _(i):
        rows = pl.ds(pl.multiple_of(i * BLK, BLK), BLK)
        first, q, k = build_scores_operands(qkv_ref, qs_ref, ks_ref, rows, qx, kx)
        do = do_ref[rows, :].astype(F32)
        zero = jnp.zeros_like(q)
        qm[0, rows, :] = jnp.where(first, q, zero).astype(BF16)
        qm[1, rows, :] = jnp.where(first, zero, q).astype(BF16)
        dm[0, rows, :] = jnp.where(first, do, zero).astype(BF16)
        dm[1, rows, :] = jnp.where(first, zero, do).astype(BF16)
        kt[:, rows] = k.T.astype(BF16)
        inner = (do * o_ref[rows, :].astype(F32)).T
        for h in range(2):
            delta[h : h + 1, rows] = jnp.sum(
                inner[h * HEAD_DIM : (h + 1) * HEAD_DIM], axis=0, keepdims=True
            )
        dqt[:, rows] = jnp.zeros((PAIR, BLK), F32)

    def tile(keys, rows, masked):
        values = qkv_ref[keys, 2 * PAIR : 3 * PAIR]
        dv_part, dk_part = None, None
        for h in range(2):
            s = mm(kx[h, keys, :], qx[h, rows, :], NT)
            if masked:
                s = causal_block(s)
            p = jnp.exp(s - lse_ref[0, h : h + 1, rows])
            dp = mm(values, dm[h, rows, :], NT)
            ds = (p * (dp - delta[h : h + 1, rows])).astype(BF16)
            dv_h = mm(p.astype(BF16), dm[h, rows, :])
            dk_h = mm(ds, qm[h, rows, :])
            dv_part = dv_h if h == 0 else dv_part + dv_h
            dk_part = dk_h if h == 0 else dk_part + dk_h
            part = slice(h * HEAD_DIM, (h + 1) * HEAD_DIM)
            dqt[part, rows] += mm(kt[part, keys], ds)
        return dk_part, dv_part

    @pl.loop(0, blocks)
    def _(j):
        keys = pl.ds(pl.multiple_of(j * BLK, BLK), BLK)
        dk[...], dv[...] = tile(keys, keys, True)

        @pl.loop(j + 1, blocks)
        def _(i):
            dk_part, dv_part = tile(keys, pl.ds(pl.multiple_of(i * BLK, BLK), BLK), False)
            dk[...] += dk_part
            dv[...] += dv_part

        d_ref[keys, PAIR : 2 * PAIR] = dk[...].astype(BF16)
        d_ref[keys, 2 * PAIR : 3 * PAIR] = dv[...].astype(BF16)

    @pl.loop(0, blocks)
    def _(i):
        rows = pl.ds(pl.multiple_of(i * BLK, BLK), BLK)
        d_ref[rows, 0:PAIR] = (dqt[:, rows].T.astype(BF16).astype(F32) * 0.125).astype(BF16)


VMEM_LIMIT = 48 * 1024 * 1024


def attention_forward(qkv, query_code, key_code):
    length, width = qkv.shape
    pairs = width // (3 * PAIR)
    tiles = pairs * 2 * length * length
    return pl.pallas_call(
        attention_forward_kernel,
        grid=(pairs,),
        in_specs=[
            pl.BlockSpec((length, 3 * PAIR), lambda p: (0, p)),
            pl.BlockSpec((length, PAIR), lambda p: (0, 0)),
            pl.BlockSpec((length, PAIR), lambda p: (0, 0)),
        ],
        out_specs=[
            pl.BlockSpec((length, PAIR), lambda p: (0, p)),
            pl.BlockSpec((1, 8, length), lambda p: (p, 0, 0)),
        ],
        out_shape=[
            jax.ShapeDtypeStruct((length, pairs * PAIR), BF16),
            jax.ShapeDtypeStruct((pairs, 8, length), F32),
        ],
        scratch_shapes=[
            pltpu.VMEM((2, length, PAIR), BF16),
            pltpu.VMEM((2, length, PAIR), BF16),
            pltpu.VMEM((2, HEAD_DIM + 16, length), BF16),
            pltpu.VMEM((2, HEAD_DIM + 16, BLK), F32),
        ],
        compiler_params=pltpu.CompilerParams(vmem_limit_bytes=VMEM_LIMIT),
        cost_estimate=pl.CostEstimate(
            flops=tiles * 1024, bytes_accessed=length * width * 3, transcendentals=tiles // 2
        ),
    )(qkv, query_code, key_code)


def attention_backward(qkv, query_code, key_code, attended, grad_attended, log_total):
    length, width = qkv.shape
    pairs = width // (3 * PAIR)
    tiles = pairs * 2 * length * length
    return pl.pallas_call(
        attention_backward_kernel,
        grid=(pairs,),
        in_specs=[
            pl.BlockSpec((length, 3 * PAIR), lambda p: (0, p)),
            pl.BlockSpec((length, PAIR), lambda p: (0, 0)),
            pl.BlockSpec((length, PAIR), lambda p: (0, 0)),
            pl.BlockSpec((length, PAIR), lambda p: (0, p)),
            pl.BlockSpec((length, PAIR), lambda p: (0, p)),
            pl.BlockSpec((1, 8, length), lambda p: (p, 0, 0)),
        ],
        out_specs=pl.BlockSpec((length, 3 * PAIR), lambda p: (0, p)),
        out_shape=jax.ShapeDtypeStruct((length, width), BF16),
        scratch_shapes=[
            pltpu.VMEM((2, length, PAIR), BF16),
            pltpu.VMEM((2, length, PAIR), BF16),
            pltpu.VMEM((2, length, PAIR), BF16),
            pltpu.VMEM((2, length, PAIR), BF16),
            pltpu.VMEM((PAIR, length), BF16),
            pltpu.VMEM((8, length), F32),
            pltpu.VMEM((PAIR, length), F32),
            pltpu.VMEM((BLK, PAIR), F32),
            pltpu.VMEM((BLK, PAIR), F32),
        ],
        compiler_params=pltpu.CompilerParams(vmem_limit_bytes=VMEM_LIMIT),
        cost_estimate=pl.CostEstimate(
            flops=tiles * 2560, bytes_accessed=length * width * 6, transcendentals=tiles // 2
        ),
    )(qkv, query_code, key_code, attended, grad_attended, log_total)


def norm_forward(source):
    average = jnp.mean(source, axis=-1, keepdims=True)
    centred = source - average
    spread = jnp.mean(centred * centred, axis=-1, keepdims=True)
    scale = lax.rsqrt(spread + EPSILON)
    return centred * scale, scale


def norm_backward(normal, scale, grad):
    return scale * (
        grad
        - jnp.mean(grad, axis=-1, keepdims=True)
        - normal * jnp.mean(grad * normal, axis=-1, keepdims=True)
    )


GELU_A = 0.7978845608028654
GELU_B = 0.044715


def gelu_parts(source):
    square = source * source
    inner = jnp.tanh(GELU_A * (source + GELU_B * source * square))
    value = 0.5 * source * (1.0 + inner)
    slope = 0.5 * (1.0 + inner) + 0.5 * source * (1.0 - inner * inner) * (
        GELU_A * (1.0 + 3.0 * GELU_B * square)
    )
    return value, slope


def swap(value, axis):
    return lax.ppermute(value, axis, [(0, 1), (1, 0)])


def pick(flag, first, second):
    return jnp.where(flag == 0, first, second), jnp.where(flag == 0, second, first)


def body(
    tokens,
    segments,
    ln1_gain,
    ln1_bias,
    qkv_weight,
    q_bias,
    v_bias,
    out_weight,
    out_bias,
    ln2_gain,
    ln2_bias,
    up_weight,
    up_bias,
    down_weight,
    down_bias,
    cotangent,
):
    side = lax.axis_index("xx")
    core = lax.axis_index("core")
    chips = lax.axis_size("dp") * lax.axis_size("xx")
    seq_count, quarter, width = tokens.shape
    length = segments.shape[1]
    own = qkv_weight.shape[0]
    pair_row = 2 * own
    hidden_own = up_bias.shape[0]
    half = width // 2
    cols = 3 * half
    pairs = half // PAIR
    splits = hidden_own // pair_row
    hidden = splits * width

    def at_index(array, index):
        return lax.dynamic_index_in_dim(array, index, 0, keepdims=False)

    def to_sequence(array):
        kept = at_index(array, side)
        come = swap(at_index(array, 1 - side), "xx")
        low, high = pick(side, kept, come)
        mine = jnp.stack([low, high])
        other = swap(mine, "core")
        even, odd = pick(core, mine, other)
        return jnp.stack([even, odd], axis=1).reshape(length, width)

    def own_rows(array):
        return lax.dynamic_index_in_dim(
            array.reshape(2, 2, quarter, array.shape[-1]), core, 1, keepdims=False
        )

    def other_rows(array):
        return lax.dynamic_index_in_dim(
            array.reshape(2, 2, quarter, array.shape[-1]), 1 - core, 1, keepdims=False
        )

    def from_sequence(mine):
        come = swap(at_index(mine, 1 - side), "xx")
        first, second = pick(side, at_index(mine, side), come)
        return jnp.stack([first, second])

    qkv_cols = qkv_weight.reshape(own, 3, 2, pairs, PAIR).transpose(2, 0, 3, 1, 4).reshape(2, own, cols)
    up_cols = (
        up_weight.reshape(own, chips, 2, splits, pair_row)
        .transpose(2, 0, 3, 1, 4)
        .reshape(2, own, hidden)
    )
    vectors = jnp.stack(
        [ln1_gain, ln1_bias, q_bias, v_bias, out_bias, ln2_gain, ln2_bias, down_bias], axis=1
    )
    vectors = jnp.pad(vectors, ((0, 0), (0, PAIR - vectors.shape[1])))

    def with_partner(two):
        mine, theirs = at_index(two, core), at_index(two, 1 - core)
        first, second = pick(core, mine, swap(theirs, "core"))
        return jnp.concatenate([first, second], axis=0)

    early = with_partner(
        jnp.concatenate([qkv_cols, jnp.broadcast_to(vectors, (2, own, PAIR))], axis=2)
    )
    early = jnp.concatenate(
        [
            early[:, : cols + 8],
            up_bias.reshape(splits, pair_row).T,
            early[:, cols + 8 + splits :],
        ],
        axis=1,
    )
    late = with_partner(
        jnp.concatenate([up_cols, jnp.broadcast_to(out_weight, (2, own, width))], axis=2)
    )
    down_own = down_weight.reshape(splits, pair_row, width)
    late = jnp.concatenate([late] + [down_own[i] for i in range(splits)], axis=1)
    early = lax.all_gather(early, ("dp", "xx"), axis=0, tiled=True)
    late = lax.all_gather(late, ("dp", "xx"), axis=0, tiled=True)
    proj_qkv = early[:, :cols]
    small = early[:, cols:].astype(F32).T
    gain_one, shift_one, query_shift, value_shift, out_shift, gain_two, shift_two, down_shift = (
        small[i] for i in range(8)
    )
    up_shift = small[8 : 8 + splits].reshape(hidden)
    proj_up = late[:, :hidden]
    proj_out = lax.dynamic_slice_in_dim(late[:, hidden : hidden + width], core * half, half, 0)
    proj_down = jnp.concatenate(
        [late[:, hidden + (1 + i) * width : hidden + (2 + i) * width] for i in range(splits)], axis=0
    )

    inputs = to_sequence(tokens).astype(F32)
    grad_out_low = to_sequence(cotangent)
    seg = at_index(segments, side)
    numbers = jnp.arange(PAIR, dtype=jnp.int32) % HEAD_DIM
    same = seg[:, None] == numbers[None, :]
    coded = numbers[None, :] < 4
    query_code = jnp.where(same & coded, 1.0, 0.0).astype(BF16)
    key_code = jnp.where(same | ~coded, 0.0, NEG).astype(BF16)

    normal_one, scale_one = norm_forward(inputs)
    normed_low = (normal_one * gain_one + shift_one).astype(BF16)

    def head_cols(vector):
        return lax.dynamic_slice_in_dim(vector, core * half, half, 0).reshape(pairs, 1, PAIR)

    zeros = jnp.zeros((pairs, 1, PAIR), F32)
    qkv_shift = jnp.concatenate(
        [head_cols(query_shift), zeros, head_cols(value_shift)], axis=1
    ).reshape(1, cols)
    qkv_scale = jnp.tile(jnp.repeat(jnp.array([0.125, 1.0, 1.0], F32), PAIR), pairs)[None]
    qkv = ((mm(normed_low, proj_qkv) + qkv_shift) * qkv_scale).astype(BF16)
    attended, log_total = attention_forward(qkv, query_code, key_code)

    branch = mm(attended, proj_out).astype(BF16)
    middle = inputs + (branch.astype(F32) + swap(branch, "core").astype(F32)) + out_shift
    normal_two, scale_two = norm_forward(middle)
    normed_two_low = (normal_two * gain_two + shift_two).astype(BF16)
    hidden_value, hidden_slope = gelu_parts(mm(normed_two_low, proj_up) + up_shift)
    hidden_low = hidden_value.astype(BF16)
    ffn = mm(hidden_low, proj_down)
    ffn_own = own_rows(ffn) + swap(other_rows(ffn).astype(BF16), "core").astype(F32)
    mixed = from_sequence((own_rows(middle) + ffn_own + down_shift).astype(BF16))

    grad_mixed = grad_out_low.astype(F32)
    grad_hidden = mm(grad_out_low, proj_down, NT)
    grad_pre_low = (hidden_slope * grad_hidden).astype(BF16)
    grad_proj_down = [
        mm(hidden_low[:, i * width : (i + 1) * width], grad_out_low, TN) for i in range(splits)
    ]
    grad_proj_up = mm(normed_two_low, grad_pre_low, TN)
    partial_two = mm(grad_pre_low, proj_up, NT).astype(BF16)
    grad_normed_two = partial_two.astype(F32) + swap(partial_two, "core").astype(F32)
    grad_middle = grad_mixed + norm_backward(normal_two, scale_two, grad_normed_two * gain_two)
    branch_low = grad_middle.astype(BF16)
    grad_proj_out = mm(attended, branch_low, TN)
    grad_attended = mm(branch_low, proj_out, NT).astype(BF16)

    def as_column(vectors):
        table = jnp.stack(vectors, axis=1)
        return jnp.pad(table, ((0, 0), (0, PAIR - table.shape[1])))

    def only_mine(flag, array):
        return jnp.where(flag, array, jnp.zeros_like(array))

    small_two = as_column(
        [
            jnp.sum(branch_low.astype(F32), axis=0),
            jnp.sum(grad_normed_two * normal_two, axis=0),
            jnp.sum(grad_normed_two, axis=0),
            jnp.sum(grad_mixed, axis=0),
        ]
        + [
            jnp.sum(grad_pre_low[:, i * width : (i + 1) * width].astype(F32), axis=0)
            for i in range(splits)
        ]
    )
    grad_out_low_b = grad_proj_out.astype(BF16)
    late_grads = jnp.concatenate(
        [
            grad_proj_up.astype(BF16),
            jnp.concatenate(
                [only_mine(core == 0, grad_out_low_b), only_mine(core == 1, grad_out_low_b)], axis=0
            ),
        ]
        + [part.astype(BF16) for part in grad_proj_down]
        + [small_two.astype(BF16)],
        axis=1,
    )
    late_own = lax.psum_scatter(late_grads, ("dp", "xx"), scatter_dimension=0, tiled=True)

    grad_qkv = attention_backward(qkv, query_code, key_code, attended, grad_attended, log_total)
    grad_proj_qkv = mm(normed_low, grad_qkv, TN)
    partial_one = mm(grad_qkv, proj_qkv, NT).astype(BF16)
    grad_normed = own_rows(partial_one).astype(F32) + swap(other_rows(partial_one), "core").astype(F32)
    normal_own, scale_own = norm_forward(own_rows(inputs))
    token_grad = from_sequence(
        (
            own_rows(grad_middle) + norm_backward(normal_own, scale_own, grad_normed * gain_one)
        ).astype(BF16)
    )
    grad_by_pair = jnp.sum(grad_qkv.astype(F32), axis=0).reshape(pairs, 3, PAIR)

    def padded(vector):
        vector = vector.reshape(half)
        return jnp.concatenate([only_mine(core == 0, vector), only_mine(core == 1, vector)])

    small_one = as_column(
        [
            jnp.sum(grad_normed * normal_own, axis=(0, 1)),
            jnp.sum(grad_normed, axis=(0, 1)),
            padded(grad_by_pair[:, 0]),
            padded(grad_by_pair[:, 2]),
        ]
    )
    early_grads = jnp.concatenate([grad_proj_qkv.astype(BF16), small_one.astype(BF16)], axis=1)
    early_own = lax.psum_scatter(early_grads, ("dp", "xx"), scatter_dimension=0, tiled=True)

    def rows_of(array, index):
        return lax.dynamic_slice_in_dim(array, index * own, own, 0)

    late_mine = rows_of(late_own, core)
    late_come = swap(rows_of(late_own, 1 - core)[:, : hidden + width], "core")
    early_mine = rows_of(early_own, core)
    early_come = swap(rows_of(early_own, 1 - core), "core")

    def by_core(mine, come):
        return jnp.stack(pick(core, mine, come))

    out_grad = (late_mine[:, hidden : hidden + width] + late_come[:, hidden:]).astype(F32)
    up_grad = (
        by_core(late_mine[:, :hidden], late_come[:, :hidden])
        .reshape(2, own, splits, chips, pair_row)
        .transpose(1, 3, 0, 2, 4)
        .reshape(own, 2 * hidden)
        .astype(F32)
    )
    down_grad = jnp.concatenate(
        [late_own[:, hidden + (1 + i) * width : hidden + (2 + i) * width] for i in range(splits)],
        axis=0,
    ).astype(F32)
    tail = hidden + (1 + splits) * width
    up_shift_grad = late_own[:, tail + 4 : tail + 4 + splits].T.reshape(hidden_own).astype(F32)
    qkv_grad = (
        by_core(early_mine[:, :cols], early_come[:, :cols])
        .reshape(2, own, pairs, 3, PAIR)
        .transpose(1, 3, 0, 2, 4)
        .reshape(own, 2 * cols)
        .astype(F32)
    )
    one = early_mine[:, cols : cols + 4].astype(F32) + early_come[:, cols : cols + 4].astype(F32)
    two = late_mine[:, tail : tail + 4].astype(F32)
    return (
        mixed,
        token_grad,
        one[:, 0],
        one[:, 1],
        qkv_grad,
        one[:, 2],
        one[:, 3],
        out_grad,
        two[:, 0],
        two[:, 1],
        two[:, 2],
        up_grad,
        up_shift_grad,
        down_grad,
        two[:, 3],
    )


def solution(mesh):
    parts = (mesh.shape["dp"], mesh.shape["ctx"] // 2, 2)
    split_mesh = Mesh(mesh.devices.reshape(parts), ("dp", "xx", "core"))
    rows = ("dp", "xx", "core")
    acts = P("dp", ("xx", "core"), None)
    vec, mat = P(rows), P(rows, None)
    return jax.shard_map(
        body,
        mesh=split_mesh,
        in_specs=(
            acts, P("dp", None), vec, vec, mat, vec, vec, mat, vec, vec, vec, mat, vec, mat, vec, acts,
        ),
        out_specs=(
            acts, acts, vec, vec, mat, vec, vec, mat, vec, vec, vec, mat, vec, mat, vec,
        ),
        check_vma=False,
    )
```

```python
import functools

import jax
import jax.numpy as jnp
from jax import lax
from jax.experimental import pallas as pl
from jax.experimental.pallas import tpu as pltpu
from jax.sharding import Mesh, PartitionSpec as P

HEAD_DIM = 64
PAIR = 2 * HEAD_DIM
EPSILON = 1e-05
NEG = -1e30
BLK = 512
F32 = jnp.float32
BF16 = jnp.bfloat16

NN = (((1,), (0,)), ((), ()))
NT = (((1,), (1,)), ((), ()))
TN = (((0,), (0,)), ((), ()))


def mm(left, right, dims=NN):
    return lax.dot_general(left, right, dims, preferred_element_type=F32)


def build_scores_operands(qkv_ref, qs_ref, ks_ref, rows, qx, kx):
    lane = lax.broadcasted_iota(jnp.int32, (BLK, PAIR), 1)
    first = lane < HEAD_DIM
    q = qkv_ref[rows, 0:PAIR].astype(F32)
    k = qkv_ref[rows, PAIR : 2 * PAIR].astype(F32)
    qs = qs_ref[rows, :].astype(F32)
    ks = ks_ref[rows, :].astype(F32)
    qx[0, rows, :] = jnp.where(first, q, qs).astype(BF16)
    qx[1, rows, :] = jnp.where(first, qs, q).astype(BF16)
    kx[0, rows, :] = jnp.where(first, k, ks).astype(BF16)
    kx[1, rows, :] = jnp.where(first, ks, k).astype(BF16)
    return first, q, k


def causal_block(scores):
    key_at = lax.broadcasted_iota(jnp.int32, scores.shape, 0)
    query_at = lax.broadcasted_iota(jnp.int32, scores.shape, 1)
    return jnp.where(key_at <= query_at, scores, NEG)


def attention_forward_kernel(qkv_ref, qs_ref, ks_ref, o_ref, lse_ref, qx, kx, vt, acc):
    length = qkv_ref.shape[0]
    blocks = length // BLK

    @pl.loop(0, blocks)
    def _(i):
        rows = pl.ds(pl.multiple_of(i * BLK, BLK), BLK)
        build_scores_operands(qkv_ref, qs_ref, ks_ref, rows, qx, kx)
        v_t = qkv_ref[rows, 2 * PAIR : 3 * PAIR].astype(F32).T
        ones = jnp.ones((16, BLK), BF16)
        for h in range(2):
            vt[h, 0:HEAD_DIM, rows] = v_t[h * HEAD_DIM : (h + 1) * HEAD_DIM].astype(BF16)
            vt[h, HEAD_DIM : HEAD_DIM + 16, rows] = ones

    @pl.loop(0, blocks)
    def _(i):
        rows = pl.ds(pl.multiple_of(i * BLK, BLK), BLK)
        queries = [qx[h, rows, :] for h in range(2)]
        tops = []
        for h in range(2):
            s = causal_block(mm(kx[h, rows, :], queries[h], NT))
            top = jnp.max(s, axis=0, keepdims=True)
            p = jnp.exp(s - top).astype(BF16)
            acc[h] = mm(vt[h, :, rows], p)
            tops.append(top)

        def step(j, carry):
            keys = pl.ds(pl.multiple_of(j * BLK, BLK), BLK)
            out = []
            for h in range(2):
                s = mm(kx[h, keys, :], qx[h, rows, :], NT)
                top = jnp.maximum(carry[h], jnp.max(s, axis=0, keepdims=True))
                p = jnp.exp(s - top).astype(BF16)
                acc[h] = acc[h] * jnp.exp(carry[h] - top) + mm(vt[h, :, keys], p)
                out.append(top)
            return tuple(out)

        tops = lax.fori_loop(0, i, step, tuple(tops))
        parts = []
        for h in range(2):
            total = acc[h, HEAD_DIM : HEAD_DIM + 1, :]
            parts.append(acc[h, 0:HEAD_DIM, :] / total)
            lse_ref[0, h : h + 1, rows] = tops[h] + jnp.log(total)
        o_ref[rows, :] = jnp.concatenate(parts, axis=0).T.astype(BF16)


def attention_backward_kernel(qkv_ref, qs_ref, ks_ref, o_ref, do_ref, lse_ref, *rest):
    d_ref, qx, kx, qm, dm, kt, delta, dqt, dk, dv = rest[-10:]
    length = qkv_ref.shape[0]
    blocks = length // BLK

    @pl.loop(0, blocks)
    def _(i):
        rows = pl.ds(pl.multiple_of(i * BLK, BLK), BLK)
        first, q, k = build_scores_operands(qkv_ref, qs_ref, ks_ref, rows, qx, kx)
        do = do_ref[rows, :].astype(F32)
        zero = jnp.zeros_like(q)
        qm[0, rows, :] = jnp.where(first, q, zero).astype(BF16)
        qm[1, rows, :] = jnp.where(first, zero, q).astype(BF16)
        dm[0, rows, :] = jnp.where(first, do, zero).astype(BF16)
        dm[1, rows, :] = jnp.where(first, zero, do).astype(BF16)
        kt[:, rows] = k.T.astype(BF16)
        inner = (do * o_ref[rows, :].astype(F32)).T
        for h in range(2):
            delta[h : h + 1, rows] = jnp.sum(
                inner[h * HEAD_DIM : (h + 1) * HEAD_DIM], axis=0, keepdims=True
            )
        dqt[:, rows] = jnp.zeros((PAIR, BLK), F32)

    def tile(keys, rows, masked):
        values = qkv_ref[keys, 2 * PAIR : 3 * PAIR]
        dv_part, dk_part = None, None
        for h in range(2):
            s = mm(kx[h, keys, :], qx[h, rows, :], NT)
            if masked:
                s = causal_block(s)
            p = jnp.exp(s - lse_ref[0, h : h + 1, rows])
            dp = mm(values, dm[h, rows, :], NT)
            ds = (p * (dp - delta[h : h + 1, rows])).astype(BF16)
            dv_h = mm(p.astype(BF16), dm[h, rows, :])
            dk_h = mm(ds, qm[h, rows, :])
            dv_part = dv_h if h == 0 else dv_part + dv_h
            dk_part = dk_h if h == 0 else dk_part + dk_h
            part = slice(h * HEAD_DIM, (h + 1) * HEAD_DIM)
            dqt[part, rows] += mm(kt[part, keys], ds)
        return dk_part, dv_part

    @pl.loop(0, blocks)
    def _(j):
        keys = pl.ds(pl.multiple_of(j * BLK, BLK), BLK)
        dk[...], dv[...] = tile(keys, keys, True)

        @pl.loop(j + 1, blocks)
        def _(i):
            dk_part, dv_part = tile(keys, pl.ds(pl.multiple_of(i * BLK, BLK), BLK), False)
            dk[...] += dk_part
            dv[...] += dv_part

        d_ref[keys, PAIR : 2 * PAIR] = dk[...].astype(BF16)
        d_ref[keys, 2 * PAIR : 3 * PAIR] = dv[...].astype(BF16)

    @pl.loop(0, blocks)
    def _(i):
        rows = pl.ds(pl.multiple_of(i * BLK, BLK), BLK)
        d_ref[rows, 0:PAIR] = (dqt[:, rows].T.astype(BF16).astype(F32) * 0.125).astype(BF16)


VMEM_LIMIT = 48 * 1024 * 1024


def attention_forward(qkv, query_code, key_code):
    length, width = qkv.shape
    pairs = width // (3 * PAIR)
    tiles = pairs * 2 * length * length
    return pl.pallas_call(
        attention_forward_kernel,
        grid=(pairs,),
        in_specs=[
            pl.BlockSpec((length, 3 * PAIR), lambda p: (0, p)),
            pl.BlockSpec((length, PAIR), lambda p: (0, 0)),
            pl.BlockSpec((length, PAIR), lambda p: (0, 0)),
        ],
        out_specs=[
            pl.BlockSpec((length, PAIR), lambda p: (0, p)),
            pl.BlockSpec((1, 8, length), lambda p: (p, 0, 0)),
        ],
        out_shape=[
            jax.ShapeDtypeStruct((length, pairs * PAIR), BF16),
            jax.ShapeDtypeStruct((pairs, 8, length), F32),
        ],
        scratch_shapes=[
            pltpu.VMEM((2, length, PAIR), BF16),
            pltpu.VMEM((2, length, PAIR), BF16),
            pltpu.VMEM((2, HEAD_DIM + 16, length), BF16),
            pltpu.VMEM((2, HEAD_DIM + 16, BLK), F32),
        ],
        compiler_params=pltpu.CompilerParams(vmem_limit_bytes=VMEM_LIMIT),
        cost_estimate=pl.CostEstimate(
            flops=tiles * 1024, bytes_accessed=length * width * 3, transcendentals=tiles // 2
        ),
    )(qkv, query_code, key_code)


def attention_backward(pair, qkv, query_code, key_code, attended, grad_attended, log_total, after):
    length = qkv.shape[0]
    tiles = 2 * length * length
    return pl.pallas_call(
        attention_backward_kernel,
        grid=(1,),
        in_specs=[
            pl.BlockSpec((length, 3 * PAIR), lambda p: (0, pair)),
            pl.BlockSpec((length, PAIR), lambda p: (0, 0)),
            pl.BlockSpec((length, PAIR), lambda p: (0, 0)),
            pl.BlockSpec((length, PAIR), lambda p: (0, pair)),
            pl.BlockSpec((length, PAIR), lambda p: (0, pair)),
            pl.BlockSpec((1, 8, length), lambda p: (pair, 0, 0)),
        ]
        + [pl.BlockSpec(memory_space=pl.ANY)] * len(after),
        out_specs=pl.BlockSpec((length, 3 * PAIR), lambda p: (0, 0)),
        out_shape=jax.ShapeDtypeStruct((length, 3 * PAIR), BF16),
        scratch_shapes=[
            pltpu.VMEM((2, length, PAIR), BF16),
            pltpu.VMEM((2, length, PAIR), BF16),
            pltpu.VMEM((2, length, PAIR), BF16),
            pltpu.VMEM((2, length, PAIR), BF16),
            pltpu.VMEM((PAIR, length), BF16),
            pltpu.VMEM((8, length), F32),
            pltpu.VMEM((PAIR, length), F32),
            pltpu.VMEM((BLK, PAIR), F32),
            pltpu.VMEM((BLK, PAIR), F32),
        ],
        compiler_params=pltpu.CompilerParams(vmem_limit_bytes=VMEM_LIMIT),
        cost_estimate=pl.CostEstimate(
            flops=tiles * 2560, bytes_accessed=length * PAIR * 24, transcendentals=tiles // 2
        ),
    )(qkv, query_code, key_code, attended, grad_attended, log_total, *after)


def norm_forward(source):
    average = jnp.mean(source, axis=-1, keepdims=True)
    centred = source - average
    spread = jnp.mean(centred * centred, axis=-1, keepdims=True)
    scale = lax.rsqrt(spread + EPSILON)
    return centred * scale, scale


def norm_backward(normal, scale, grad):
    return scale * (
        grad
        - jnp.mean(grad, axis=-1, keepdims=True)
        - normal * jnp.mean(grad * normal, axis=-1, keepdims=True)
    )


GELU_A = 0.7978845608028654
GELU_B = 0.044715


def gelu_parts(source):
    square = source * source
    inner = jnp.tanh(GELU_A * (source + GELU_B * source * square))
    value = 0.5 * source * (1.0 + inner)
    slope = 0.5 * (1.0 + inner) + 0.5 * source * (1.0 - inner * inner) * (
        GELU_A * (1.0 + 3.0 * GELU_B * square)
    )
    return value, slope


def swap(value, axis):
    return lax.ppermute(value, axis, [(0, 1), (1, 0)])


def pick(flag, first, second):
    return jnp.where(flag == 0, first, second), jnp.where(flag == 0, second, first)


class Links:
    def __init__(self):
        self.size = lax.axis_size("dp")
        at = lax.axis_index("dp")
        self.groups = {}
        shift, name = 0, "y"
        while (1 << shift) < self.size:
            bits = 1 if shift == 0 else min(2, self.size.bit_length() - 1 - shift)
            self.groups[name] = (shift, bits, (at >> shift) & ((1 << bits) - 1))
            shift += bits
            name = "z" + str(shift)
        self.rest = [name for name in reversed(self.groups) if name != "y"]
        self.dims = self.rest + ["y", "x"]
        self.side = lax.axis_index("xx")

    def counts(self, dims):
        return [2 if d == "x" else 1 << self.groups[d][1] for d in dims]

    def send(self, value, d, mask):
        if d == "x":
            return swap(value, "xx")
        move = mask << self.groups[d][0]
        return lax.ppermute(value, "dp", [(i, i ^ move) for i in range(self.size)])

    def place(self, d):
        return self.side if d == "x" else self.groups[d][2]

    def reduce(self, state, d):
        array, dims = state
        axis, at = dims.index(d), self.place(d)
        total = lax.dynamic_index_in_dim(array, at, axis, keepdims=False).astype(F32)
        for mask in range(1, array.shape[axis]):
            block = lax.dynamic_index_in_dim(array, at ^ mask, axis, keepdims=False)
            total = total + self.send(block, d, mask).astype(F32)
        return total.astype(BF16), [other for other in dims if other != d]

    def gather(self, state, d):
        array, dims = state
        parts = [array] + [self.send(array, d, mask) for mask in range(1, self.counts([d])[0])]
        for bit in range(len(parts).bit_length() - 1):
            flag = (self.place(d) >> bit) & 1
            for low in range(len(parts)):
                if not low & (1 << bit):
                    high = low | (1 << bit)
                    parts[low], parts[high] = pick(flag, parts[low], parts[high])
        dims = [other for other in self.dims if other in dims or other == d]
        return jnp.stack(parts, axis=dims.index(d)), dims

    def rows(self, array, lead=()):
        shape = list(lead) + self.counts(self.dims)
        count = 1
        for size in shape:
            count *= size
        names = ["lead"] * len(lead) + self.dims
        return array.reshape(shape + [array.shape[0] // count, array.shape[1]]), names


def body(
    tokens,
    segments,
    ln1_gain,
    ln1_bias,
    qkv_weight,
    q_bias,
    v_bias,
    out_weight,
    out_bias,
    ln2_gain,
    ln2_bias,
    up_weight,
    up_bias,
    down_weight,
    down_bias,
    cotangent,
):
    side = lax.axis_index("xx")
    core = lax.axis_index("core")
    chips = lax.axis_size("dp") * lax.axis_size("xx")
    seq_count, quarter, width = tokens.shape
    length = segments.shape[1]
    own = qkv_weight.shape[0]
    pair_row = 2 * own
    hidden_own = up_bias.shape[0]
    half = width // 2
    cols = 3 * half
    pairs = half // PAIR
    splits = hidden_own // pair_row
    hidden = splits * width

    def at_index(array, index):
        return lax.dynamic_index_in_dim(array, index, 0, keepdims=False)

    def to_sequence(array):
        kept = at_index(array, side)
        come = swap(at_index(array, 1 - side), "xx")
        low, high = pick(side, kept, come)
        mine = jnp.stack([low, high])
        other = swap(mine, "core")
        even, odd = pick(core, mine, other)
        return jnp.stack([even, odd], axis=1).reshape(length, width)

    def own_rows(array):
        return lax.dynamic_index_in_dim(
            array.reshape(2, 2, quarter, array.shape[-1]), core, 1, keepdims=False
        )

    def other_rows(array):
        return lax.dynamic_index_in_dim(
            array.reshape(2, 2, quarter, array.shape[-1]), 1 - core, 1, keepdims=False
        )

    def from_sequence(mine):
        come = swap(at_index(mine, 1 - side), "xx")
        first, second = pick(side, at_index(mine, side), come)
        return jnp.stack([first, second])

    qkv_cols = qkv_weight.reshape(own, 3, 2, pairs, PAIR).transpose(2, 0, 3, 1, 4).reshape(2, own, cols)
    up_cols = (
        up_weight.reshape(own, chips, 2, splits, pair_row)
        .transpose(2, 0, 3, 1, 4)
        .reshape(2, own, hidden)
    )
    vectors = jnp.stack(
        [ln1_gain, ln1_bias, q_bias, v_bias, out_bias, ln2_gain, ln2_bias, down_bias], axis=1
    )
    vectors = jnp.pad(vectors, ((0, 0), (0, PAIR - vectors.shape[1])))

    def with_partner(two):
        mine, theirs = at_index(two, core), at_index(two, 1 - core)
        first, second = pick(core, mine, swap(theirs, "core"))
        return jnp.concatenate([first, second], axis=0)

    early = with_partner(
        jnp.concatenate([qkv_cols, jnp.broadcast_to(vectors, (2, own, PAIR))], axis=2)
    )
    early = jnp.concatenate(
        [
            early[:, : cols + 8],
            up_bias.reshape(splits, pair_row).T,
            early[:, cols + 8 + splits :],
        ],
        axis=1,
    )
    late = with_partner(
        jnp.concatenate([up_cols, jnp.broadcast_to(out_weight, (2, own, width))], axis=2)
    )
    down_own = down_weight.reshape(splits, pair_row, width)
    late = jnp.concatenate([late] + [down_own[i] for i in range(splits)], axis=1)
    links = Links()
    state = (early, [])
    for d in links.rest:
        state = links.gather(state, d)
    middle_col = early.shape[1] // 2
    halves = []
    for order, part in (("yx", slice(0, middle_col)), ("xy", slice(middle_col, None))):
        piece = (state[0][..., part], state[1])
        for d in order:
            piece = links.gather(piece, d)
        halves.append(piece[0].reshape(width, middle_col))
    early = jnp.concatenate(halves, axis=1)
    late = lax.all_gather(late, ("dp", "xx"), axis=0, tiled=True)
    proj_qkv = early[:, :cols]
    small = early[:, cols:].astype(F32).T
    gain_one, shift_one, query_shift, value_shift, out_shift, gain_two, shift_two, down_shift = (
        small[i] for i in range(8)
    )
    up_shift = small[8 : 8 + splits].reshape(hidden)
    proj_up = late[:, :hidden]
    proj_out = lax.dynamic_slice_in_dim(late[:, hidden : hidden + width], core * half, half, 0)
    proj_down = jnp.concatenate(
        [late[:, hidden + (1 + i) * width : hidden + (2 + i) * width] for i in range(splits)], axis=0
    )

    inputs = to_sequence(tokens).astype(F32)
    grad_out_low = to_sequence(cotangent)
    seg = at_index(segments, side)
    numbers = jnp.arange(PAIR, dtype=jnp.int32) % HEAD_DIM
    same = seg[:, None] == numbers[None, :]
    coded = numbers[None, :] < 4
    query_code = jnp.where(same & coded, 1.0, 0.0).astype(BF16)
    key_code = jnp.where(same | ~coded, 0.0, NEG).astype(BF16)

    normal_one, scale_one = norm_forward(inputs)
    normed_low = (normal_one * gain_one + shift_one).astype(BF16)

    def head_cols(vector):
        return lax.dynamic_slice_in_dim(vector, core * half, half, 0).reshape(pairs, 1, PAIR)

    zeros = jnp.zeros((pairs, 1, PAIR), F32)
    qkv_shift = jnp.concatenate(
        [head_cols(query_shift), zeros, head_cols(value_shift)], axis=1
    ).reshape(1, cols)
    qkv_scale = jnp.tile(jnp.repeat(jnp.array([0.125, 1.0, 1.0], F32), PAIR), pairs)[None]
    qkv = ((mm(normed_low, proj_qkv) + qkv_shift) * qkv_scale).astype(BF16)
    attended, log_total = attention_forward(qkv, query_code, key_code)

    branch = mm(attended, proj_out).astype(BF16)
    middle = inputs + (branch.astype(F32) + swap(branch, "core").astype(F32)) + out_shift
    normal_two, scale_two = norm_forward(middle)
    normed_two_low = (normal_two * gain_two + shift_two).astype(BF16)
    hidden_value, hidden_slope = gelu_parts(mm(normed_two_low, proj_up) + up_shift)
    hidden_low = hidden_value.astype(BF16)
    ffn = mm(hidden_low, proj_down)
    ffn_own = own_rows(ffn) + swap(other_rows(ffn).astype(BF16), "core").astype(F32)
    mixed = from_sequence((own_rows(middle) + ffn_own + down_shift).astype(BF16))

    grad_mixed = grad_out_low.astype(F32)
    grad_hidden = mm(grad_out_low, proj_down, NT)
    grad_pre_low = (hidden_slope * grad_hidden).astype(BF16)
    grad_proj_down = [
        mm(hidden_low[:, i * width : (i + 1) * width], grad_out_low, TN) for i in range(splits)
    ]
    grad_proj_up = mm(normed_two_low, grad_pre_low, TN)
    partial_two = mm(grad_pre_low, proj_up, NT).astype(BF16)
    grad_normed_two = partial_two.astype(F32) + swap(partial_two, "core").astype(F32)
    grad_middle = grad_mixed + norm_backward(normal_two, scale_two, grad_normed_two * gain_two)
    branch_low = grad_middle.astype(BF16)
    grad_proj_out = mm(attended, branch_low, TN)
    grad_attended = mm(branch_low, proj_out, NT).astype(BF16)

    def as_column(vectors):
        table = jnp.stack(vectors, axis=1)
        return jnp.pad(table, ((0, 0), (0, PAIR - table.shape[1])))

    def only_mine(flag, array):
        return jnp.where(flag, array, jnp.zeros_like(array))

    small_two = (
        [
            jnp.sum(branch_low.astype(F32), axis=0),
            jnp.sum(grad_normed_two * normal_two, axis=0),
            jnp.sum(grad_normed_two, axis=0),
            jnp.sum(grad_mixed, axis=0),
        ]
        + [
            jnp.sum(grad_pre_low[:, i * width : (i + 1) * width].astype(F32), axis=0)
            for i in range(splits)
        ]
    )
    down_piece = links.rows(
        jnp.concatenate([part.astype(BF16) for part in grad_proj_down], axis=0), (splits,)
    )
    up_piece = links.rows(grad_proj_up.astype(BF16))
    out_piece = (
        grad_proj_out.astype(BF16).reshape(chips // 8, 2, 2, pair_row, width),
        ["rest", "y", "x"],
    )

    def reduce_rest(piece):
        for d in links.rest:
            piece = links.reduce(piece, d)
        return piece

    def pair_backward(pair, after):
        grad = attention_backward(
            pair, qkv, query_code, key_code, attended, grad_attended, log_total, after
        )
        return grad, links.rows(mm(normed_low, grad, TN).astype(BF16))

    down_piece = links.reduce(down_piece, "x")
    grads, pieces = [], []
    for pair in range(pairs):
        if pair == 0:
            after = [down_piece[0], mixed]
        elif pair == 1:
            down_piece = links.reduce(down_piece, "y")
            up_piece = links.reduce(up_piece, "y")
            after = [down_piece[0], up_piece[0]]
        else:
            down_piece = reduce_rest(down_piece)
            up_piece = links.reduce(up_piece, "x")
            out_piece = links.reduce(out_piece, "x")
            after = [down_piece[0], up_piece[0], out_piece[0]]
        grad, piece = pair_backward(pair, after)
        grads.append(grad)
        pieces.append(piece)
    grad_qkv = jnp.concatenate(grads, axis=1)
    up_piece = reduce_rest(up_piece)
    out_part = links.reduce(out_piece, "y")[0]
    empty = jnp.zeros_like(out_part)
    out_part = jnp.concatenate(pick(core, out_part, empty), axis=0)
    out_piece = reduce_rest(
        (out_part.reshape(links.counts(links.rest) + [pair_row, width]), links.rest)
    )
    qkv_own = jnp.concatenate(
        [
            reduce_rest(links.reduce(links.reduce(piece, order[0]), order[1]))[0]
            for piece, order in zip(pieces, ("yx", "xy", "yx"))
        ],
        axis=1,
    )
    partial_one_wide = mm(grad_qkv, proj_qkv, NT)
    partial_one = partial_one_wide.astype(BF16)
    grad_normed = own_rows(partial_one).astype(F32) + swap(other_rows(partial_one), "core").astype(F32)
    normal_own, scale_own = norm_forward(own_rows(inputs))
    token_grad = from_sequence(
        (
            own_rows(grad_middle) + norm_backward(normal_own, scale_own, grad_normed * gain_one)
        ).astype(BF16)
    )
    grad_by_pair = jnp.sum(grad_qkv.astype(F32), axis=0).reshape(pairs, 3, PAIR)

    def padded(vector):
        vector = vector.reshape(half)
        return jnp.concatenate([only_mine(core == 0, vector), only_mine(core == 1, vector)])

    small = as_column(
        [
            jnp.sum(partial_one_wide * normal_one, axis=0),
            jnp.sum(partial_one_wide, axis=0),
            padded(grad_by_pair[:, 0]),
            padded(grad_by_pair[:, 2]),
        ]
        + small_two
    )
    small_own = reduce_rest(links.reduce(links.reduce(links.rows(small.astype(BF16)), "y"), "x"))[0]

    def rows_of(array, index):
        return lax.dynamic_slice_in_dim(array, index * own, own, 0)

    def by_core(mine, come):
        return jnp.stack(pick(core, mine, come))

    def shared(array):
        return rows_of(array, core), swap(rows_of(array, 1 - core), "core")

    late_mine, late_come = shared(jnp.concatenate([up_piece[0], out_piece[0]], axis=1))
    early_mine, early_come = shared(jnp.concatenate([qkv_own, small_own], axis=1))
    out_grad = late_mine[:, hidden:].astype(F32) + late_come[:, hidden:].astype(F32)
    up_grad = (
        by_core(late_mine[:, :hidden], late_come[:, :hidden])
        .reshape(2, own, splits, chips, pair_row)
        .transpose(1, 3, 0, 2, 4)
        .reshape(own, 2 * hidden)
        .astype(F32)
    )
    down_grad = down_piece[0].reshape(hidden_own, width).astype(F32)
    up_shift_grad = small_own[:, 8 : 8 + splits].T.reshape(hidden_own).astype(F32)
    qkv_grad = (
        by_core(early_mine[:, :cols], early_come[:, :cols])
        .reshape(2, own, pairs, 3, PAIR)
        .transpose(1, 3, 0, 2, 4)
        .reshape(own, 2 * cols)
        .astype(F32)
    )
    small_mine = early_mine[:, cols : cols + 8].astype(F32)
    one = small_mine[:, :4] + early_come[:, cols : cols + 4].astype(F32)
    two = small_mine[:, 4:]
    return (
        mixed,
        token_grad,
        one[:, 0],
        one[:, 1],
        qkv_grad,
        one[:, 2],
        one[:, 3],
        out_grad,
        two[:, 0],
        two[:, 1],
        two[:, 2],
        up_grad,
        up_shift_grad,
        down_grad,
        two[:, 3],
    )


def solution(mesh):
    parts = (mesh.shape["dp"], mesh.shape["ctx"] // 2, 2)
    split_mesh = Mesh(mesh.devices.reshape(parts), ("dp", "xx", "core"))
    rows = ("dp", "xx", "core")
    acts = P("dp", ("xx", "core"), None)
    vec, mat = P(rows), P(rows, None)
    return jax.shard_map(
        body,
        mesh=split_mesh,
        in_specs=(
            acts, P("dp", None), vec, vec, mat, vec, vec, mat, vec, vec, vec, mat, vec, mat, vec, acts,
        ),
        out_specs=(
            acts, acts, vec, vec, mat, vec, vec, mat, vec, vec, vec, mat, vec, mat, vec,
        ),
        check_vma=False,
    )
```

```python
import functools

import jax
import jax.numpy as jnp
from jax import lax
from jax.experimental import pallas as pl
from jax.experimental.pallas import tpu as pltpu
from jax.sharding import Mesh, PartitionSpec as P

HEAD_DIM = 64
PAIR = 2 * HEAD_DIM
EPSILON = 1e-05
NEG = -1e30
BLK = 512
F32 = jnp.float32
BF16 = jnp.bfloat16

NN = (((1,), (0,)), ((), ()))
NT = (((1,), (1,)), ((), ()))
TN = (((0,), (0,)), ((), ()))


def mm(left, right, dims=NN):
    return lax.dot_general(left, right, dims, preferred_element_type=F32)


def build_scores_operands(qkv_ref, qs_ref, ks_ref, rows, qx, kx):
    lane = lax.broadcasted_iota(jnp.int32, (BLK, PAIR), 1)
    first = lane < HEAD_DIM
    q = qkv_ref[rows, 0:PAIR].astype(F32)
    k = qkv_ref[rows, PAIR : 2 * PAIR].astype(F32)
    qs = qs_ref[rows, :].astype(F32)
    ks = ks_ref[rows, :].astype(F32)
    qx[0, rows, :] = jnp.where(first, q, qs).astype(BF16)
    qx[1, rows, :] = jnp.where(first, qs, q).astype(BF16)
    kx[0, rows, :] = jnp.where(first, k, ks).astype(BF16)
    kx[1, rows, :] = jnp.where(first, ks, k).astype(BF16)
    return first, q, k


def causal_block(scores):
    key_at = lax.broadcasted_iota(jnp.int32, scores.shape, 0)
    query_at = lax.broadcasted_iota(jnp.int32, scores.shape, 1)
    return jnp.where(key_at <= query_at, scores, NEG)


def attention_forward_kernel(qkv_ref, qs_ref, ks_ref, *rest):
    o_ref, lse_ref, tick_ref, qx, kx, vt, acc = rest[-7:]
    tick_ref[...] = jnp.zeros_like(tick_ref)
    length = qkv_ref.shape[0]
    blocks = length // BLK

    @pl.loop(0, blocks)
    def _(i):
        rows = pl.ds(pl.multiple_of(i * BLK, BLK), BLK)
        build_scores_operands(qkv_ref, qs_ref, ks_ref, rows, qx, kx)
        v_t = qkv_ref[rows, 2 * PAIR : 3 * PAIR].astype(F32).T
        ones = jnp.ones((16, BLK), BF16)
        for h in range(2):
            vt[h, 0:HEAD_DIM, rows] = v_t[h * HEAD_DIM : (h + 1) * HEAD_DIM].astype(BF16)
            vt[h, HEAD_DIM : HEAD_DIM + 16, rows] = ones

    @pl.loop(0, blocks)
    def _(i):
        rows = pl.ds(pl.multiple_of(i * BLK, BLK), BLK)
        queries = [qx[h, rows, :] for h in range(2)]
        tops = []
        for h in range(2):
            s = causal_block(mm(kx[h, rows, :], queries[h], NT))
            top = jnp.max(s, axis=0, keepdims=True)
            p = jnp.exp(s - top).astype(BF16)
            acc[h] = mm(vt[h, :, rows], p)
            tops.append(top)

        def step(j, carry):
            keys = pl.ds(pl.multiple_of(j * BLK, BLK), BLK)
            out = []
            for h in range(2):
                s = mm(kx[h, keys, :], qx[h, rows, :], NT)
                top = jnp.maximum(carry[h], jnp.max(s, axis=0, keepdims=True))
                p = jnp.exp(s - top).astype(BF16)
                acc[h] = acc[h] * jnp.exp(carry[h] - top) + mm(vt[h, :, keys], p)
                out.append(top)
            return tuple(out)

        tops = lax.fori_loop(0, i, step, tuple(tops))
        parts = []
        for h in range(2):
            total = acc[h, HEAD_DIM : HEAD_DIM + 1, :]
            parts.append(acc[h, 0:HEAD_DIM, :] / total)
            lse_ref[0, h : h + 1, rows] = tops[h] + jnp.log(total)
        o_ref[rows, :] = jnp.concatenate(parts, axis=0).T.astype(BF16)


def attention_backward_kernel(qkv_ref, qs_ref, ks_ref, o_ref, do_ref, lse_ref, *rest):
    d_ref, tick_ref, qx, kx, qm, dm, kt, delta, dqt, dk, dv = rest[-11:]
    tick_ref[...] = jnp.zeros_like(tick_ref)
    length = qkv_ref.shape[0]
    blocks = length // BLK

    @pl.loop(0, blocks)
    def _(i):
        rows = pl.ds(pl.multiple_of(i * BLK, BLK), BLK)
        first, q, k = build_scores_operands(qkv_ref, qs_ref, ks_ref, rows, qx, kx)
        do = do_ref[rows, :].astype(F32)
        zero = jnp.zeros_like(q)
        qm[0, rows, :] = jnp.where(first, q, zero).astype(BF16)
        qm[1, rows, :] = jnp.where(first, zero, q).astype(BF16)
        dm[0, rows, :] = jnp.where(first, do, zero).astype(BF16)
        dm[1, rows, :] = jnp.where(first, zero, do).astype(BF16)
        kt[:, rows] = k.T.astype(BF16)
        inner = (do * o_ref[rows, :].astype(F32)).T
        for h in range(2):
            delta[h : h + 1, rows] = jnp.sum(
                inner[h * HEAD_DIM : (h + 1) * HEAD_DIM], axis=0, keepdims=True
            )
        dqt[:, rows] = jnp.zeros((PAIR, BLK), F32)

    def tile(keys, rows, masked):
        values = qkv_ref[keys, 2 * PAIR : 3 * PAIR]
        dv_part, dk_part = None, None
        for h in range(2):
            s = mm(kx[h, keys, :], qx[h, rows, :], NT)
            if masked:
                s = causal_block(s)
            p = jnp.exp(s - lse_ref[0, h : h + 1, rows])
            dp = mm(values, dm[h, rows, :], NT)
            ds = (p * (dp - delta[h : h + 1, rows])).astype(BF16)
            dv_h = mm(p.astype(BF16), dm[h, rows, :])
            dk_h = mm(ds, qm[h, rows, :])
            dv_part = dv_h if h == 0 else dv_part + dv_h
            dk_part = dk_h if h == 0 else dk_part + dk_h
            part = slice(h * HEAD_DIM, (h + 1) * HEAD_DIM)
            dqt[part, rows] += mm(kt[part, keys], ds)
        return dk_part, dv_part

    @pl.loop(0, blocks)
    def _(j):
        keys = pl.ds(pl.multiple_of(j * BLK, BLK), BLK)
        dk[...], dv[...] = tile(keys, keys, True)

        @pl.loop(j + 1, blocks)
        def _(i):
            dk_part, dv_part = tile(keys, pl.ds(pl.multiple_of(i * BLK, BLK), BLK), False)
            dk[...] += dk_part
            dv[...] += dv_part

        d_ref[keys, PAIR : 2 * PAIR] = dk[...].astype(BF16)
        d_ref[keys, 2 * PAIR : 3 * PAIR] = dv[...].astype(BF16)

    @pl.loop(0, blocks)
    def _(i):
        rows = pl.ds(pl.multiple_of(i * BLK, BLK), BLK)
        d_ref[rows, 0:PAIR] = (dqt[:, rows].T.astype(BF16).astype(F32) * 0.125).astype(BF16)


VMEM_LIMIT = 48 * 1024 * 1024


SMALL_COST = pl.CostEstimate(flops=10**8, bytes_accessed=10**6, transcendentals=0)


TICK = jax.ShapeDtypeStruct((8, 128), F32)
TICK_SPEC = pl.BlockSpec((8, 128), lambda i: (0, 0))
ANY_SPEC = pl.BlockSpec(memory_space=pl.ANY)


def gate_kernel(*refs):
    refs[-1][...] = jnp.zeros_like(refs[-1])


def gate(after):
    return pl.pallas_call(
        gate_kernel,
        grid=(1,),
        in_specs=[ANY_SPEC] * len(after),
        out_specs=TICK_SPEC,
        out_shape=TICK,
        cost_estimate=SMALL_COST,
    )(*after)


def qkv_kernel(x_ref, w_ref, vec_ref, col_ref, a_ref, qkv_ref, tick_ref):
    normal, _ = norm_forward(x_ref[...].astype(F32))
    normed = (normal * vec_ref[0:1, :] + vec_ref[1:2, :]).astype(BF16)
    a_ref[...] = normed
    qkv_ref[...] = ((mm(normed, w_ref[...]) + col_ref[0:1, :]) * col_ref[1:2, :]).astype(BF16)
    tick_ref[...] = jnp.zeros_like(tick_ref)


def qkv_projection(inputs, weight, vectors, columns):
    length, width = inputs.shape
    cols = weight.shape[1]
    return pl.pallas_call(
        qkv_kernel,
        grid=(length // ROWS,),
        in_specs=[
            pl.BlockSpec((ROWS, width), lambda i: (i, 0)),
            pl.BlockSpec((width, cols), lambda i: (0, 0)),
            pl.BlockSpec(vectors.shape, lambda i: (0, 0)),
            pl.BlockSpec(columns.shape, lambda i: (0, 0)),
        ],
        out_specs=[
            pl.BlockSpec((ROWS, width), lambda i: (i, 0)),
            pl.BlockSpec((ROWS, cols), lambda i: (i, 0)),
            TICK_SPEC,
        ],
        out_shape=[
            jax.ShapeDtypeStruct((length, width), BF16),
            jax.ShapeDtypeStruct((length, cols), BF16),
            TICK,
        ],
        compiler_params=pltpu.CompilerParams(vmem_limit_bytes=VMEM_LIMIT),
        cost_estimate=SMALL_COST,
    )(inputs, weight, vectors, columns)


ROWS = 256


def norm_one_input_kernel(core_ref, mine_ref, come_ref, x_ref, mid_ref, vec_ref, out_ref, tick_ref):
    grad = (mine_ref[...].astype(F32) + come_ref[...].astype(F32)) * vec_ref[0:1, :]
    normal, scale = norm_forward(x_ref[...].astype(F32))
    out_ref[...] = (mid_ref[...] + norm_backward(normal, scale, grad)).astype(BF16)
    tick_ref[...] = jnp.zeros_like(tick_ref)


def norm_one_input(core, partial, come, inputs, grad_middle, vectors):
    length, width = inputs.shape
    count = come.shape[0] // ROWS
    per = count // 2

    def own_block(i, core_ref):
        return ((i // per) * 2 + core_ref[0]) * per + i % per, 0

    own = pl.BlockSpec((ROWS, width), own_block)
    plain = pl.BlockSpec((ROWS, width), lambda i, core_ref: (i, 0))
    return pl.pallas_call(
        norm_one_input_kernel,
        grid_spec=pltpu.PrefetchScalarGridSpec(
            num_scalar_prefetch=1,
            grid=(count,),
            in_specs=[own, plain, own, own, pl.BlockSpec(vectors.shape, lambda i, core_ref: (0, 0))],
            out_specs=[plain, pl.BlockSpec((8, 128), lambda i, core_ref: (0, 0))],
        ),
        out_shape=[jax.ShapeDtypeStruct((count * ROWS, width), BF16), TICK],
        compiler_params=pltpu.CompilerParams(vmem_limit_bytes=VMEM_LIMIT),
        cost_estimate=SMALL_COST,
    )(core.reshape(1).astype(jnp.int32), partial, come, inputs, grad_middle, vectors)


def attention_forward(pair, qkv, query_code, key_code, after):
    length = qkv.shape[0]
    return pl.pallas_call(
        attention_forward_kernel,
        grid=(1,),
        in_specs=[
            pl.BlockSpec((length, 3 * PAIR), lambda p: (0, pair)),
            pl.BlockSpec((length, PAIR), lambda p: (0, 0)),
            pl.BlockSpec((length, PAIR), lambda p: (0, 0)),
        ]
        + [pl.BlockSpec(memory_space=pl.ANY)] * len(after),
        out_specs=[
            pl.BlockSpec((length, PAIR), lambda p: (0, 0)),
            pl.BlockSpec((1, 8, length), lambda p: (0, 0, 0)),
            TICK_SPEC,
        ],
        out_shape=[
            jax.ShapeDtypeStruct((length, PAIR), BF16),
            jax.ShapeDtypeStruct((1, 8, length), F32),
            TICK,
        ],
        scratch_shapes=[
            pltpu.VMEM((2, length, PAIR), BF16),
            pltpu.VMEM((2, length, PAIR), BF16),
            pltpu.VMEM((2, HEAD_DIM + 16, length), BF16),
            pltpu.VMEM((2, HEAD_DIM + 16, BLK), F32),
        ],
        compiler_params=pltpu.CompilerParams(vmem_limit_bytes=VMEM_LIMIT),
        cost_estimate=SMALL_COST,
    )(qkv, query_code, key_code, *after)


def norm_one_grad_kernel(d0_ref, d1_ref, d2_ref, w_ref, x_ref, *rest):
    out_ref, sums_ref, bias_ref, tick_ref = rest[-4:]

    @pl.when(pl.program_id(0) == 0)
    def _():
        sums_ref[...] = jnp.zeros_like(sums_ref)
        bias_ref[...] = jnp.zeros_like(bias_ref)
        tick_ref[...] = jnp.zeros_like(tick_ref)

    total = None
    for i, ref in enumerate((d0_ref, d1_ref, d2_ref)):
        cols = slice(i * 3 * PAIR, (i + 1) * 3 * PAIR)
        grad = ref[...]
        part = mm(grad, w_ref[:, cols], NT)
        total = part if i == 0 else total + part
        bias_ref[0:1, cols] += jnp.sum(grad.astype(F32), axis=0, keepdims=True)
    normal, _ = norm_forward(x_ref[...].astype(F32))
    sums_ref[0:1, :] += jnp.sum(total * normal, axis=0, keepdims=True)
    sums_ref[1:2, :] += jnp.sum(total, axis=0, keepdims=True)
    out_ref[...] = total.astype(BF16)


def norm_one_grad(grads, weight, inputs, after):
    length, width = inputs.shape
    cols = weight.shape[1]
    block = pl.BlockSpec((ROWS, 3 * PAIR), lambda i: (i, 0))
    return pl.pallas_call(
        norm_one_grad_kernel,
        grid=(length // ROWS,),
        in_specs=[block] * 3
        + [
            pl.BlockSpec((width, cols), lambda i: (0, 0)),
            pl.BlockSpec((ROWS, width), lambda i: (i, 0)),
        ]
        + [pl.BlockSpec(memory_space=pl.ANY)] * len(after),
        out_specs=[
            pl.BlockSpec((ROWS, width), lambda i: (i, 0)),
            pl.BlockSpec((8, width), lambda i: (0, 0)),
            pl.BlockSpec((8, cols), lambda i: (0, 0)),
            TICK_SPEC,
        ],
        out_shape=[
            jax.ShapeDtypeStruct((length, width), BF16),
            jax.ShapeDtypeStruct((8, width), F32),
            jax.ShapeDtypeStruct((8, cols), F32),
            TICK,
        ],
        compiler_params=pltpu.CompilerParams(vmem_limit_bytes=VMEM_LIMIT),
        cost_estimate=SMALL_COST,
    )(*grads, weight, inputs, *after)


def attention_backward(pair, qkv, query_code, key_code, attended, grad_attended, log_total, after):
    length = qkv.shape[0]
    return pl.pallas_call(
        attention_backward_kernel,
        grid=(1,),
        in_specs=[
            pl.BlockSpec((length, 3 * PAIR), lambda p: (0, pair)),
            pl.BlockSpec((length, PAIR), lambda p: (0, 0)),
            pl.BlockSpec((length, PAIR), lambda p: (0, 0)),
            pl.BlockSpec((length, PAIR), lambda p: (0, 0)),
            pl.BlockSpec((length, PAIR), lambda p: (0, pair)),
            pl.BlockSpec((1, 8, length), lambda p: (0, 0, 0)),
        ]
        + [pl.BlockSpec(memory_space=pl.ANY)] * len(after),
        out_specs=[pl.BlockSpec((length, 3 * PAIR), lambda p: (0, 0)), TICK_SPEC],
        out_shape=[jax.ShapeDtypeStruct((length, 3 * PAIR), BF16), TICK],
        scratch_shapes=[
            pltpu.VMEM((2, length, PAIR), BF16),
            pltpu.VMEM((2, length, PAIR), BF16),
            pltpu.VMEM((2, length, PAIR), BF16),
            pltpu.VMEM((2, length, PAIR), BF16),
            pltpu.VMEM((PAIR, length), BF16),
            pltpu.VMEM((8, length), F32),
            pltpu.VMEM((PAIR, length), F32),
            pltpu.VMEM((BLK, PAIR), F32),
            pltpu.VMEM((BLK, PAIR), F32),
        ],
        compiler_params=pltpu.CompilerParams(vmem_limit_bytes=VMEM_LIMIT),
        cost_estimate=SMALL_COST,
    )(qkv, query_code, key_code, attended, grad_attended, log_total, *after)


def norm_forward(source):
    average = jnp.mean(source, axis=-1, keepdims=True)
    centred = source - average
    spread = jnp.mean(centred * centred, axis=-1, keepdims=True)
    scale = lax.rsqrt(spread + EPSILON)
    return centred * scale, scale


def norm_backward(normal, scale, grad):
    return scale * (
        grad
        - jnp.mean(grad, axis=-1, keepdims=True)
        - normal * jnp.mean(grad * normal, axis=-1, keepdims=True)
    )


GELU_A = 0.7978845608028654
GELU_B = 0.044715


def gelu_parts(source):
    square = source * source
    inner = jnp.tanh(GELU_A * (source + GELU_B * source * square))
    value = 0.5 * source * (1.0 + inner)
    slope = 0.5 * (1.0 + inner) + 0.5 * source * (1.0 - inner * inner) * (
        GELU_A * (1.0 + 3.0 * GELU_B * square)
    )
    return value, slope


def swap(value, axis):
    return lax.ppermute(value, axis, [(0, 1), (1, 0)])


def pick(flag, first, second):
    return jnp.where(flag == 0, first, second), jnp.where(flag == 0, second, first)


class Links:
    def __init__(self):
        self.size = lax.axis_size("dp")
        at = lax.axis_index("dp")
        self.groups = {}
        shift, name = 0, "y"
        while (1 << shift) < self.size:
            bits = 1 if shift == 0 else min(2, self.size.bit_length() - 1 - shift)
            self.groups[name] = (shift, bits, (at >> shift) & ((1 << bits) - 1))
            shift += bits
            name = "z" + str(shift)
        self.rest = [name for name in reversed(self.groups) if name != "y"]
        self.dims = self.rest + ["y", "x"]
        self.side = lax.axis_index("xx")

    def counts(self, dims):
        return [2 if d == "x" else 1 << self.groups[d][1] for d in dims]

    def send(self, value, d, mask):
        if d == "x":
            return swap(value, "xx")
        move = mask << self.groups[d][0]
        return lax.ppermute(value, "dp", [(i, i ^ move) for i in range(self.size)])

    def place(self, d):
        return self.side if d == "x" else self.groups[d][2]

    def reduce(self, state, d, tick=None):
        array, dims = state
        axis, at = dims.index(d), self.place(d)
        total = lax.dynamic_index_in_dim(array, at, axis, keepdims=False).astype(F32)
        for mask in range(1, array.shape[axis]):
            block = lax.dynamic_index_in_dim(array, at ^ mask, axis, keepdims=False)
            total = total + self.send(block, d, mask).astype(F32)
        if tick is not None:
            total = total + tick[0, 0]
        return total.astype(BF16), [other for other in dims if other != d]

    def gather(self, state, d, tick=None):
        array, dims = state
        parts = [array] + [self.send(array, d, mask) for mask in range(1, self.counts([d])[0])]
        for bit in range(len(parts).bit_length() - 1):
            flag = (self.place(d) >> bit) & 1
            for low in range(len(parts)):
                if not low & (1 << bit):
                    high = low | (1 << bit)
                    parts[low], parts[high] = pick(flag, parts[low], parts[high])
        dims = [other for other in self.dims if other in dims or other == d]
        joined = jnp.stack(parts, axis=dims.index(d))
        if tick is not None:
            joined = joined + tick[0, 0].astype(joined.dtype)
        return joined, dims

    def rows(self, array, lead=()):
        shape = list(lead) + self.counts(self.dims)
        count = 1
        for size in shape:
            count *= size
        names = ["lead"] * len(lead) + self.dims
        return array.reshape(shape + [array.shape[0] // count, array.shape[1]]), names


def body(
    tokens,
    segments,
    ln1_gain,
    ln1_bias,
    qkv_weight,
    q_bias,
    v_bias,
    out_weight,
    out_bias,
    ln2_gain,
    ln2_bias,
    up_weight,
    up_bias,
    down_weight,
    down_bias,
    cotangent,
):
    side = lax.axis_index("xx")
    core = lax.axis_index("core")
    chips = lax.axis_size("dp") * lax.axis_size("xx")
    seq_count, quarter, width = tokens.shape
    length = segments.shape[1]
    own = qkv_weight.shape[0]
    pair_row = 2 * own
    hidden_own = up_bias.shape[0]
    half = width // 2
    cols = 3 * half
    pairs = half // PAIR
    splits = hidden_own // pair_row
    hidden = splits * width

    def at_index(array, index):
        return lax.dynamic_index_in_dim(array, index, 0, keepdims=False)

    def to_sequence(array, tick=None):
        kept = at_index(array, side)
        sent = at_index(array, 1 - side)
        if tick is not None:
            sent = sent + tick[0, 0].astype(sent.dtype)
        come = swap(sent, "xx")
        low, high = pick(side, kept, come)
        mine = jnp.stack([low, high])
        other = swap(mine, "core")
        even, odd = pick(core, mine, other)
        return jnp.stack([even, odd], axis=1).reshape(length, width), come

    def own_rows(array):
        return lax.dynamic_index_in_dim(
            array.reshape(2, 2, quarter, array.shape[-1]), core, 1, keepdims=False
        )

    def other_rows(array):
        return lax.dynamic_index_in_dim(
            array.reshape(2, 2, quarter, array.shape[-1]), 1 - core, 1, keepdims=False
        )

    def from_sequence(mine):
        come = swap(at_index(mine, 1 - side), "xx")
        first, second = pick(side, at_index(mine, side), come)
        return jnp.stack([first, second]), come

    qkv_cols = qkv_weight.reshape(own, 3, 2, pairs, PAIR).transpose(2, 0, 3, 1, 4).reshape(2, own, cols)
    up_cols = (
        up_weight.reshape(own, chips, 2, splits, pair_row)
        .transpose(2, 0, 3, 1, 4)
        .reshape(2, own, hidden)
    )
    vectors = jnp.stack(
        [ln1_gain, ln1_bias, q_bias, v_bias, out_bias, ln2_gain, ln2_bias, down_bias], axis=1
    )
    vectors = jnp.pad(vectors, ((0, 0), (0, PAIR - vectors.shape[1])))

    def with_partner(two):
        mine, theirs = at_index(two, core), at_index(two, 1 - core)
        first, second = pick(core, mine, swap(theirs, "core"))
        return jnp.concatenate([first, second], axis=0)

    early = with_partner(
        jnp.concatenate([qkv_cols, jnp.broadcast_to(vectors, (2, own, PAIR))], axis=2)
    )
    early = jnp.concatenate(
        [
            early[:, : cols + 8],
            up_bias.reshape(splits, pair_row).T,
            early[:, cols + 8 + splits :],
        ],
        axis=1,
    )
    links = Links()

    def gather_rest(array, tick=None):
        state = (array, [])
        for d in links.rest:
            state = links.gather(state, d, tick if d == links.rest[-1] else None)
        return state

    def halves_of(state):
        middle = state[0].shape[-1] // 2
        return [(state[0][..., :middle], state[1]), (state[0][..., middle:], state[1])]

    def joined(halves):
        return [half_state[0].reshape(width, -1) for half_state in halves]

    inputs_low, come = to_sequence(tokens)
    grad_out_low, _ = to_sequence(cotangent, gate([come]))
    early_halves = [
        links.gather(links.gather(piece, order[0]), order[1])
        for piece, order in zip(halves_of(gather_rest(early)), ("yx", "xy"))
    ]
    early = jnp.concatenate(joined(early_halves), axis=1)
    late = with_partner(
        jnp.concatenate([up_cols, jnp.broadcast_to(out_weight, (2, own, width))], axis=2)
    )
    down_own = down_weight.reshape(splits, pair_row, width)
    late = jnp.concatenate([late] + [down_own[i] for i in range(splits)], axis=1)
    proj_qkv = early[:, :cols]
    small = early[:, cols:].astype(F32).T
    gain_one, shift_one, query_shift, value_shift, out_shift, gain_two, shift_two, down_shift = (
        small[i] for i in range(8)
    )
    up_shift = small[8 : 8 + splits].reshape(hidden)

    inputs = inputs_low.astype(F32)
    seg = at_index(segments, side)
    numbers = jnp.arange(PAIR, dtype=jnp.int32) % HEAD_DIM
    same = seg[:, None] == numbers[None, :]
    coded = numbers[None, :] < 4
    query_code = jnp.where(same & coded, 1.0, 0.0).astype(BF16)
    key_code = jnp.where(same | ~coded, 0.0, NEG).astype(BF16)

    def head_cols(vector):
        return lax.dynamic_slice_in_dim(vector, core * half, half, 0).reshape(pairs, 1, PAIR)

    zeros = jnp.zeros((pairs, 1, PAIR), F32)
    qkv_shift = jnp.concatenate(
        [head_cols(query_shift), zeros, head_cols(value_shift)], axis=1
    ).reshape(1, cols)
    qkv_scale = jnp.tile(jnp.repeat(jnp.array([0.125, 1.0, 1.0], F32), PAIR), pairs)[None]
    normed_low, qkv, tick = qkv_projection(
        inputs_low,
        proj_qkv,
        jnp.pad(jnp.stack([gain_one, shift_one]), ((0, 6), (0, 0))),
        jnp.pad(jnp.concatenate([qkv_shift, qkv_scale]), ((0, 6), (0, 0))),
    )
    attended_pairs, log_totals = [], []
    late_halves = halves_of(gather_rest(late, tick))
    for pair in range(pairs):
        if pair == 0:
            after = [piece[0] for piece in late_halves]
        else:
            after = [attended_pairs[-1]]
        if pair == 1:
            late_halves = [links.gather(piece, d, tick) for piece, d in zip(late_halves, "xy")]
            after += [piece[0] for piece in late_halves]
        one_pair = attention_forward(pair, qkv, query_code, key_code, after)
        attended_pairs.append(one_pair[0])
        log_totals.append(one_pair[1])
        tick = one_pair[2]
    attended = jnp.concatenate(attended_pairs, axis=1)
    late_halves = joined([links.gather(piece, d, tick) for piece, d in zip(late_halves, "yx")])
    late = jnp.concatenate(late_halves, axis=1)
    proj_up = late[:, :hidden]
    proj_out = lax.dynamic_slice_in_dim(late[:, hidden : hidden + width], core * half, half, 0)
    proj_down = jnp.concatenate(
        [late[:, hidden + (1 + i) * width : hidden + (2 + i) * width] for i in range(splits)], axis=0
    )

    branch = mm(attended, proj_out).astype(BF16)
    middle = inputs + (branch.astype(F32) + swap(branch, "core").astype(F32)) + out_shift
    normal_two, scale_two = norm_forward(middle)
    normed_two_low = (normal_two * gain_two + shift_two).astype(BF16)
    hidden_value, hidden_slope = gelu_parts(mm(normed_two_low, proj_up) + up_shift)
    hidden_low = hidden_value.astype(BF16)
    ffn = mm(hidden_low, proj_down)
    ffn_own = own_rows(ffn) + swap(other_rows(ffn).astype(BF16), "core").astype(F32)
    mixed, _ = from_sequence((own_rows(middle) + ffn_own + down_shift).astype(BF16))

    grad_mixed = grad_out_low.astype(F32)
    grad_hidden = mm(grad_out_low, proj_down, NT)
    grad_pre_low = (hidden_slope * grad_hidden).astype(BF16)
    grad_proj_down = [
        mm(hidden_low[:, i * width : (i + 1) * width], grad_out_low, TN) for i in range(splits)
    ]
    grad_proj_up = mm(normed_two_low, grad_pre_low, TN)
    partial_two = mm(grad_pre_low, proj_up, NT).astype(BF16)
    grad_normed_two = partial_two.astype(F32) + swap(partial_two, "core").astype(F32)
    grad_middle = grad_mixed + norm_backward(normal_two, scale_two, grad_normed_two * gain_two)
    branch_low = grad_middle.astype(BF16)
    grad_proj_out = mm(attended, branch_low, TN)
    grad_attended = mm(branch_low, proj_out, NT).astype(BF16)

    def as_column(vectors):
        table = jnp.stack(vectors, axis=1)
        return jnp.pad(table, ((0, 0), (0, PAIR - table.shape[1])))

    def only_mine(flag, array):
        return jnp.where(flag, array, jnp.zeros_like(array))

    small_two = (
        [
            jnp.sum(branch_low.astype(F32), axis=0),
            jnp.sum(grad_normed_two * normal_two, axis=0),
            jnp.sum(grad_normed_two, axis=0),
            jnp.sum(grad_mixed, axis=0),
        ]
        + [
            jnp.sum(grad_pre_low[:, i * width : (i + 1) * width].astype(F32), axis=0)
            for i in range(splits)
        ]
    )
    down_piece = links.rows(
        jnp.concatenate([part.astype(BF16) for part in grad_proj_down], axis=0), (splits,)
    )
    up_piece = links.rows(grad_proj_up.astype(BF16))
    out_low = grad_proj_out.astype(BF16)
    grad_out_rows = jnp.concatenate(
        [only_mine(core == 0, out_low), only_mine(core == 1, out_low)], axis=0
    )

    def reduce_rest(piece, tick=None):
        for d in links.rest:
            piece = links.reduce(piece, d, tick if d == links.rest[0] else None)
        return piece

    grads, weight_grads, tick = [], [grad_out_rows], None
    after = [mixed]
    for pair in range(pairs):
        grad, tick = attention_backward(
            pair,
            qkv,
            query_code,
            key_code,
            attended_pairs[pair],
            grad_attended,
            log_totals[pair],
            after + grads[-1:],
        )
        grads.append(grad)
        if pair == 0:
            down_piece = links.reduce(down_piece, "x", tick)
            up_piece = links.reduce(up_piece, "y", tick)
            after = [down_piece[0], up_piece[0]]
        elif pair == 1:
            down_piece = links.reduce(down_piece, "y", tick)
            up_piece = links.reduce(up_piece, "x", tick)
            after = [down_piece[0], up_piece[0]]
        if pair < pairs - 1:
            weight_grads.append(mm(normed_low, grad, TN).astype(BF16))
    first_piece = links.rows(jnp.concatenate(weight_grads, axis=1))
    partial_one, norm_sums, bias_sums, tick = norm_one_grad(grads, proj_qkv, inputs_low, [])
    first_piece = links.reduce(first_piece, "x", tick)
    come = swap(other_rows(partial_one), "core").reshape(2 * quarter, width)
    norm_vectors = jnp.pad(jnp.stack([gain_one, shift_one]), ((0, 6), (0, 0)))
    token_own, tick = norm_one_input(
        core, partial_one, come, inputs_low, grad_middle, norm_vectors
    )
    down_piece = reduce_rest(down_piece, tick)
    up_piece = reduce_rest(up_piece, tick)
    token_grad, come = from_sequence(token_own.reshape(2, quarter, width))
    grad_by_pair = bias_sums[0].reshape(pairs, 3, PAIR)

    def padded(vector):
        vector = vector.reshape(half)
        return jnp.concatenate([only_mine(core == 0, vector), only_mine(core == 1, vector)])

    small = as_column(
        [
            norm_sums[0],
            norm_sums[1],
            padded(grad_by_pair[:, 0]),
            padded(grad_by_pair[:, 2]),
        ]
        + small_two
    )
    last_piece = links.rows(
        jnp.concatenate([mm(normed_low, grads[-1], TN).astype(BF16), small.astype(BF16)], axis=1)
    )
    last_piece = links.reduce(links.reduce(last_piece, "y", tick), "x")
    last_own = reduce_rest(last_piece, gate([come]))[0]
    first_own = reduce_rest(links.reduce(first_piece, "y", tick))[0]

    def rows_of(array, index):
        return lax.dynamic_slice_in_dim(array, index * own, own, 0)

    def by_core(mine, come):
        return jnp.stack(pick(core, mine, come))

    def shared(array):
        return rows_of(array, core), swap(rows_of(array, 1 - core), "core")

    late_mine, late_come = shared(up_piece[0])
    early_mine, early_come = shared(jnp.concatenate([first_own, last_own], axis=1))
    out_grad = early_mine[:, :width].astype(F32) + early_come[:, :width].astype(F32)
    up_grad = (
        by_core(late_mine, late_come)
        .reshape(2, own, splits, chips, pair_row)
        .transpose(1, 3, 0, 2, 4)
        .reshape(own, 2 * hidden)
        .astype(F32)
    )
    down_grad = down_piece[0].reshape(hidden_own, width).astype(F32)
    qkv_grad = (
        by_core(early_mine[:, width : width + cols], early_come[:, width : width + cols])
        .reshape(2, own, pairs, 3, PAIR)
        .transpose(1, 3, 0, 2, 4)
        .reshape(own, 2 * cols)
        .astype(F32)
    )
    tail = width + cols
    small_mine = early_mine[:, tail : tail + 8].astype(F32)
    one = small_mine[:, :4] + early_come[:, tail : tail + 4].astype(F32)
    up_shift_grad = (
        last_own[:, cols // pairs + 8 : cols // pairs + 8 + splits].T.reshape(hidden_own).astype(F32)
    )
    two = small_mine[:, 4:]
    return (
        mixed,
        token_grad,
        one[:, 0],
        one[:, 1],
        qkv_grad,
        one[:, 2],
        one[:, 3],
        out_grad,
        two[:, 0],
        two[:, 1],
        two[:, 2],
        up_grad,
        up_shift_grad,
        down_grad,
        two[:, 3],
    )


def solution(mesh):
    parts = (mesh.shape["dp"], mesh.shape["ctx"] // 2, 2)
    split_mesh = Mesh(mesh.devices.reshape(parts), ("dp", "xx", "core"))
    rows = ("dp", "xx", "core")
    acts = P("dp", ("xx", "core"), None)
    vec, mat = P(rows), P(rows, None)
    return jax.shard_map(
        body,
        mesh=split_mesh,
        in_specs=(
            acts, P("dp", None), vec, vec, mat, vec, vec, mat, vec, vec, vec, mat, vec, mat, vec, acts,
        ),
        out_specs=(
            acts, acts, vec, vec, mat, vec, vec, mat, vec, vec, vec, mat, vec, mat, vec,
        ),
        check_vma=False,
    )
```

```python
import functools

import jax
import jax.numpy as jnp
from jax import lax
from jax.experimental import pallas as pl
from jax.experimental.pallas import tpu as pltpu
from jax.sharding import Mesh, PartitionSpec as P

HEAD_DIM = 64
PAIR = 2 * HEAD_DIM
EPSILON = 1e-05
NEG = -1e30
BLK = 512
F32 = jnp.float32
BF16 = jnp.bfloat16

NN = (((1,), (0,)), ((), ()))
NT = (((1,), (1,)), ((), ()))
TN = (((0,), (0,)), ((), ()))


def mm(left, right, dims=NN):
    return lax.dot_general(left, right, dims, preferred_element_type=F32)


def build_scores_operands(qkv_ref, qs_ref, ks_ref, rows, qx, kx):
    lane = lax.broadcasted_iota(jnp.int32, (BLK, PAIR), 1)
    first = lane < HEAD_DIM
    q = qkv_ref[rows, 0:PAIR].astype(F32)
    k = qkv_ref[rows, PAIR : 2 * PAIR].astype(F32)
    qs = qs_ref[rows, :].astype(F32)
    ks = ks_ref[rows, :].astype(F32)
    qx[0, rows, :] = jnp.where(first, q, qs).astype(BF16)
    qx[1, rows, :] = jnp.where(first, qs, q).astype(BF16)
    kx[0, rows, :] = jnp.where(first, k, ks).astype(BF16)
    kx[1, rows, :] = jnp.where(first, ks, k).astype(BF16)
    return first, q, k


def causal_block(scores):
    key_at = lax.broadcasted_iota(jnp.int32, scores.shape, 0)
    query_at = lax.broadcasted_iota(jnp.int32, scores.shape, 1)
    return jnp.where(key_at <= query_at, scores, NEG)


def attention_forward_kernel(qkv_ref, qs_ref, ks_ref, *rest):
    o_ref, lse_ref, tick_ref, qx, kx, vt, acc = rest[-7:]
    tick_ref[...] = jnp.zeros_like(tick_ref)
    length = qkv_ref.shape[0]
    blocks = length // BLK

    @pl.loop(0, blocks)
    def _(i):
        rows = pl.ds(pl.multiple_of(i * BLK, BLK), BLK)
        build_scores_operands(qkv_ref, qs_ref, ks_ref, rows, qx, kx)
        v_t = qkv_ref[rows, 2 * PAIR : 3 * PAIR].astype(F32).T
        ones = jnp.ones((16, BLK), BF16)
        for h in range(2):
            vt[h, 0:HEAD_DIM, rows] = v_t[h * HEAD_DIM : (h + 1) * HEAD_DIM].astype(BF16)
            vt[h, HEAD_DIM : HEAD_DIM + 16, rows] = ones

    @pl.loop(0, blocks)
    def _(i):
        rows = pl.ds(pl.multiple_of(i * BLK, BLK), BLK)
        queries = [qx[h, rows, :] for h in range(2)]
        tops = []
        for h in range(2):
            s = causal_block(mm(kx[h, rows, :], queries[h], NT))
            top = jnp.max(s, axis=0, keepdims=True)
            p = jnp.exp(s - top).astype(BF16)
            acc[h] = mm(vt[h, :, rows], p)
            tops.append(top)

        def step(j, carry):
            keys = pl.ds(pl.multiple_of(j * BLK, BLK), BLK)
            out = []
            for h in range(2):
                s = mm(kx[h, keys, :], qx[h, rows, :], NT)
                top = jnp.maximum(carry[h], jnp.max(s, axis=0, keepdims=True))
                p = jnp.exp(s - top).astype(BF16)
                acc[h] = acc[h] * jnp.exp(carry[h] - top) + mm(vt[h, :, keys], p)
                out.append(top)
            return tuple(out)

        tops = lax.fori_loop(0, i, step, tuple(tops))
        parts = []
        for h in range(2):
            total = acc[h, HEAD_DIM : HEAD_DIM + 1, :]
            parts.append(acc[h, 0:HEAD_DIM, :] / total)
            lse_ref[0, h : h + 1, rows] = tops[h] + jnp.log(total)
        o_ref[rows, :] = jnp.concatenate(parts, axis=0).T.astype(BF16)


def attention_backward_kernel(qkv_ref, qs_ref, ks_ref, o_ref, do_ref, lse_ref, at_ref, *rest):
    d_ref, dw_ref, tick_ref, qx, kx, qm, dm, kt, delta, dqt, dk, dv = rest[-12:]
    tick_ref[...] = jnp.zeros_like(tick_ref)
    length = qkv_ref.shape[0]
    blocks = length // BLK

    @pl.loop(0, blocks)
    def _(i):
        rows = pl.ds(pl.multiple_of(i * BLK, BLK), BLK)
        first, q, k = build_scores_operands(qkv_ref, qs_ref, ks_ref, rows, qx, kx)
        do = do_ref[rows, :].astype(F32)
        zero = jnp.zeros_like(q)
        qm[0, rows, :] = jnp.where(first, q, zero).astype(BF16)
        qm[1, rows, :] = jnp.where(first, zero, q).astype(BF16)
        dm[0, rows, :] = jnp.where(first, do, zero).astype(BF16)
        dm[1, rows, :] = jnp.where(first, zero, do).astype(BF16)
        kt[:, rows] = k.T.astype(BF16)
        inner = (do * o_ref[rows, :].astype(F32)).T
        for h in range(2):
            delta[h : h + 1, rows] = jnp.sum(
                inner[h * HEAD_DIM : (h + 1) * HEAD_DIM], axis=0, keepdims=True
            )
        dqt[:, rows] = jnp.zeros((PAIR, BLK), F32)

    def tile(keys, rows, masked):
        values = qkv_ref[keys, 2 * PAIR : 3 * PAIR]
        dv_part, dk_part = None, None
        for h in range(2):
            s = mm(kx[h, keys, :], qx[h, rows, :], NT)
            if masked:
                s = causal_block(s)
            p = jnp.exp(s - lse_ref[0, h : h + 1, rows])
            dp = mm(values, dm[h, rows, :], NT)
            ds = (p * (dp - delta[h : h + 1, rows])).astype(BF16)
            dv_h = mm(p.astype(BF16), dm[h, rows, :])
            dk_h = mm(ds, qm[h, rows, :])
            dv_part = dv_h if h == 0 else dv_part + dv_h
            dk_part = dk_h if h == 0 else dk_part + dk_h
            part = slice(h * HEAD_DIM, (h + 1) * HEAD_DIM)
            dqt[part, rows] += mm(kt[part, keys], ds)
        return dk_part, dv_part

    @pl.loop(0, blocks)
    def _(j):
        keys = pl.ds(pl.multiple_of(j * BLK, BLK), BLK)
        dk[...], dv[...] = tile(keys, keys, True)

        @pl.loop(j + 1, blocks)
        def _(i):
            dk_part, dv_part = tile(keys, pl.ds(pl.multiple_of(i * BLK, BLK), BLK), False)
            dk[...] += dk_part
            dv[...] += dv_part

        d_ref[keys, PAIR : 2 * PAIR] = dk[...].astype(BF16)
        d_ref[keys, 2 * PAIR : 3 * PAIR] = dv[...].astype(BF16)

    @pl.loop(0, blocks)
    def _(i):
        rows = pl.ds(pl.multiple_of(i * BLK, BLK), BLK)
        d_ref[rows, 0:PAIR] = (dqt[:, rows].T.astype(BF16).astype(F32) * 0.125).astype(BF16)

    @pl.loop(0, dw_ref.shape[0] // ROWS)
    def _(i):
        rows = pl.ds(pl.multiple_of(i * ROWS, ROWS), ROWS)
        dw_ref[rows, :] = mm(at_ref[rows, :], d_ref[...]).astype(BF16)


VMEM_LIMIT = 48 * 1024 * 1024


SMALL_COST = pl.CostEstimate(flops=10**8, bytes_accessed=10**6, transcendentals=0)


TICK = jax.ShapeDtypeStruct((8, 128), F32)
TICK_SPEC = pl.BlockSpec((8, 128), lambda i: (0, 0))
ANY_SPEC = pl.BlockSpec(memory_space=pl.ANY)


def gate_kernel(*refs):
    refs[-1][...] = jnp.zeros_like(refs[-1])


def gate(after):
    return pl.pallas_call(
        gate_kernel,
        grid=(1,),
        in_specs=[ANY_SPEC] * len(after),
        out_specs=TICK_SPEC,
        out_shape=TICK,
        cost_estimate=SMALL_COST,
    )(*after)


def qkv_kernel(x_ref, wa_ref, wb_ref, vec_ref, col_ref, *rest_refs):
    a_ref, qkv_ref, tick_ref = rest_refs[-3:]
    split = wa_ref.shape[1]
    rest = qkv_ref.shape[1] - split
    for part in range(2):
        rows = slice(part * ROWS, (part + 1) * ROWS)
        normal, _ = norm_forward(x_ref[rows, :].astype(F32))
        normed = (normal * vec_ref[0:1, :] + vec_ref[1:2, :]).astype(BF16)
        a_ref[:, rows] = normed.astype(F32).T.astype(BF16)
        for w, cols in ((wa_ref[...], slice(0, split)), (wb_ref[:, :rest], slice(split, None))):
            shift, scale = col_ref[0:1, cols], col_ref[1:2, cols]
            qkv_ref[rows, cols] = ((mm(normed, w) + shift) * scale).astype(BF16)
    tick_ref[...] = jnp.zeros_like(tick_ref)


def qkv_projection(inputs, weight_a, weight_b, vectors, columns, after):
    length, width = inputs.shape
    cols = columns.shape[1]
    return pl.pallas_call(
        qkv_kernel,
        grid=(length // (2 * ROWS),),
        in_specs=[
            pl.BlockSpec((2 * ROWS, width), lambda i: (i, 0)),
            pl.BlockSpec(weight_a.shape, lambda i: (0, 0)),
            pl.BlockSpec(weight_b.shape, lambda i: (0, 0)),
            pl.BlockSpec(vectors.shape, lambda i: (0, 0)),
            pl.BlockSpec(columns.shape, lambda i: (0, 0)),
        ]
        + [ANY_SPEC] * len(after),
        out_specs=[
            pl.BlockSpec((width, 2 * ROWS), lambda i: (0, i)),
            pl.BlockSpec((2 * ROWS, cols), lambda i: (i, 0)),
            TICK_SPEC,
        ],
        out_shape=[
            jax.ShapeDtypeStruct((width, length), BF16),
            jax.ShapeDtypeStruct((length, cols), BF16),
            TICK,
        ],
        compiler_params=pltpu.CompilerParams(vmem_limit_bytes=VMEM_LIMIT),
        cost_estimate=SMALL_COST,
    )(inputs, weight_a, weight_b, vectors, columns, *after)


def feed_forward_kernel(
    x_ref, b0_ref, b1_ref, dy_ref, up_ref, down_ref, vec_ref, shift_ref,
    a_ref, g_ref, du_ref, ffn_ref, dh_ref, sums_ref,
):
    @pl.when(pl.program_id(0) == 0)
    def _():
        sums_ref[...] = jnp.zeros_like(sums_ref)

    middle = x_ref[...].astype(F32) + (b0_ref[...].astype(F32) + b1_ref[...].astype(F32)) + vec_ref[0:1, :]
    normal, _ = norm_forward(middle)
    normed = (normal * vec_ref[1:2, :] + vec_ref[2:3, :]).astype(BF16)
    a_ref[...] = normed
    dy = dy_ref[...]
    ffn, dh = None, None
    for at in range(0, up_ref.shape[1], HIDDEN):
        cols = slice(at, at + HIDDEN)
        up, down = up_ref[:, cols], down_ref[cols, :]
        value, slope = gelu_parts(mm(normed, up) + shift_ref[0:1, cols])
        du = slope * mm(dy, down, NT)
        value, du = value.astype(BF16), du.astype(BF16)
        g_ref[:, cols] = value
        du_ref[:, cols] = du
        sums_ref[0:1, cols] += jnp.sum(du.astype(F32), axis=0, keepdims=True)
        ffn_part, dh_part = mm(value, down), mm(du, up, NT)
        ffn = ffn_part if at == 0 else ffn + ffn_part
        dh = dh_part if at == 0 else dh + dh_part
    ffn_ref[...] = ffn.astype(BF16)
    dh_ref[...] = dh.astype(BF16)


HIDDEN = 512


def feed_forward(inputs, branch, branch_come, grad_out, up, down, vectors, up_shift):
    length, width = inputs.shape
    hidden = up.shape[1]
    narrow = pl.BlockSpec((ROWS, width), lambda i: (i, 0))
    wide = pl.BlockSpec((ROWS, hidden), lambda i: (i, 0))

    def whole(array):
        return pl.BlockSpec(array.shape, lambda i: (0, 0))

    return pl.pallas_call(
        feed_forward_kernel,
        grid=(length // ROWS,),
        in_specs=[narrow] * 4 + [whole(up), whole(down), whole(vectors), whole(up_shift)],
        out_specs=[narrow, wide, wide, narrow, narrow, pl.BlockSpec((8, hidden), lambda i: (0, 0))],
        out_shape=[
            jax.ShapeDtypeStruct((length, width), BF16),
            jax.ShapeDtypeStruct((length, hidden), BF16),
            jax.ShapeDtypeStruct((length, hidden), BF16),
            jax.ShapeDtypeStruct((length, width), BF16),
            jax.ShapeDtypeStruct((length, width), BF16),
            jax.ShapeDtypeStruct((8, hidden), F32),
        ],
        compiler_params=pltpu.CompilerParams(vmem_limit_bytes=VMEM_LIMIT),
        cost_estimate=SMALL_COST,
    )(inputs, branch, branch_come, grad_out, up, down, vectors, up_shift)


def norm_two_kernel(
    x_ref, b0_ref, b1_ref, dy_ref, p0_ref, p1_ref, w_ref, vec_ref, *rest
):
    mid_ref, low_ref, do_ref, sums_ref, tick_ref = rest[-5:]

    @pl.when(pl.program_id(0) == 0)
    def _():
        sums_ref[...] = jnp.zeros_like(sums_ref)
        tick_ref[...] = jnp.zeros_like(tick_ref)

    middle = x_ref[...].astype(F32) + (b0_ref[...].astype(F32) + b1_ref[...].astype(F32)) + vec_ref[0:1, :]
    normal, scale = norm_forward(middle)
    grad = p0_ref[...].astype(F32) + p1_ref[...].astype(F32)
    dy = dy_ref[...].astype(F32)
    mid = dy + norm_backward(normal, scale, grad * vec_ref[1:2, :])
    low = mid.astype(BF16)
    mid_ref[...] = mid
    low_ref[...] = low
    do_ref[...] = mm(low, w_ref[...], NT).astype(BF16)
    for i, value in enumerate((low.astype(F32), grad * normal, grad, dy)):
        sums_ref[i : i + 1, :] += jnp.sum(value, axis=0, keepdims=True)


def norm_two(inputs, branch, branch_come, grad_out, partial, partial_come, weight, vectors, after):
    length, width = inputs.shape
    cols = weight.shape[0]
    narrow = pl.BlockSpec((ROWS, width), lambda i: (i, 0))

    def whole(array):
        return pl.BlockSpec(array.shape, lambda i: (0, 0))

    return pl.pallas_call(
        norm_two_kernel,
        grid=(length // ROWS,),
        in_specs=[narrow] * 6 + [whole(weight), whole(vectors)] + [ANY_SPEC] * len(after),
        out_specs=[
            narrow,
            narrow,
            pl.BlockSpec((ROWS, cols), lambda i: (i, 0)),
            pl.BlockSpec((8, width), lambda i: (0, 0)),
            TICK_SPEC,
        ],
        out_shape=[
            jax.ShapeDtypeStruct((length, width), F32),
            jax.ShapeDtypeStruct((length, width), BF16),
            jax.ShapeDtypeStruct((length, cols), BF16),
            jax.ShapeDtypeStruct((8, width), F32),
            TICK,
        ],
        compiler_params=pltpu.CompilerParams(vmem_limit_bytes=VMEM_LIMIT),
        cost_estimate=SMALL_COST,
    )(inputs, branch, branch_come, grad_out, partial, partial_come, weight, vectors, *after)


ROWS = 256


def attention_forward(pair, qkv, query_code, key_code, after):
    length = qkv.shape[0]
    return pl.pallas_call(
        attention_forward_kernel,
        grid=(1,),
        in_specs=[
            pl.BlockSpec((length, 3 * PAIR), lambda p: (0, pair)),
            pl.BlockSpec((length, PAIR), lambda p: (0, 0)),
            pl.BlockSpec((length, PAIR), lambda p: (0, 0)),
        ]
        + [pl.BlockSpec(memory_space=pl.ANY)] * len(after),
        out_specs=[
            pl.BlockSpec((length, PAIR), lambda p: (0, 0)),
            pl.BlockSpec((1, 8, length), lambda p: (0, 0, 0)),
            TICK_SPEC,
        ],
        out_shape=[
            jax.ShapeDtypeStruct((length, PAIR), BF16),
            jax.ShapeDtypeStruct((1, 8, length), F32),
            TICK,
        ],
        scratch_shapes=[
            pltpu.VMEM((2, length, PAIR), BF16),
            pltpu.VMEM((2, length, PAIR), BF16),
            pltpu.VMEM((2, HEAD_DIM + 16, length), BF16),
            pltpu.VMEM((2, HEAD_DIM + 16, BLK), F32),
        ],
        compiler_params=pltpu.CompilerParams(vmem_limit_bytes=VMEM_LIMIT),
        cost_estimate=SMALL_COST,
    )(qkv, query_code, key_code, *after)


def norm_one_kernel(own, core_ref, d0_ref, d1_ref, d2_ref, wa_ref, wb_ref, x_ref, *rest):
    if own:
        come_ref, mid_ref, vec_ref, out_ref, sums_ref, bias_ref, tick_ref, w = rest
    else:
        out_ref, sums_ref, bias_ref, tick_ref, w = rest
    split = wa_ref.shape[1]

    @pl.when(pl.program_id(0) == 0)
    def _():
        sums_ref[...] = jnp.zeros_like(sums_ref)
        bias_ref[...] = jnp.zeros_like(bias_ref)
        w[:, :split] = wa_ref[...]
        w[:, split:] = wb_ref[:, : w.shape[1] - split]
        tick_ref[...] = jnp.zeros_like(tick_ref)

    total = None
    for i, ref in enumerate((d0_ref, d1_ref, d2_ref)):
        cols = slice(i * 3 * PAIR, (i + 1) * 3 * PAIR)
        grad = ref[...]
        part = mm(grad, w[:, cols], NT)
        total = part if i == 0 else total + part
        bias_ref[0:1, cols] += jnp.sum(grad.astype(F32), axis=0, keepdims=True)
    normal, scale = norm_forward(x_ref[...].astype(F32))
    sums_ref[0:1, :] += jnp.sum(total * normal, axis=0, keepdims=True)
    sums_ref[1:2, :] += jnp.sum(total, axis=0, keepdims=True)
    if own:
        grad = (total + come_ref[...].astype(F32)) * vec_ref[0:1, :]
        out_ref[...] = (mid_ref[...] + norm_backward(normal, scale, grad)).astype(BF16)
    else:
        out_ref[...] = total.astype(BF16)


def norm_one(own, core, grads, weight_a, weight_b, cols, inputs, extra, after):
    length, width = inputs.shape
    count = length // (2 * ROWS)
    per = count // 2

    def block(i, core_ref):
        which = core_ref[0] if own else 1 - core_ref[0]
        return ((i // per) * 2 + which) * per + i % per, 0

    def at_zero(i, core_ref):
        return 0, 0

    plain = pl.BlockSpec((ROWS, width), lambda i, core_ref: (i, 0))
    rows = pl.BlockSpec((ROWS, width), block)
    in_specs = [pl.BlockSpec((ROWS, 3 * PAIR), block)] * 3 + [
        pl.BlockSpec(weight_a.shape, at_zero),
        pl.BlockSpec(weight_b.shape, at_zero),
        rows,
    ]
    out_specs = [
        plain,
        pl.BlockSpec((8, width), at_zero),
        pl.BlockSpec((8, cols), at_zero),
        pl.BlockSpec((8, 128), at_zero),
    ]
    out_shape = [
        jax.ShapeDtypeStruct((count * ROWS, width), BF16),
        jax.ShapeDtypeStruct((8, width), F32),
        jax.ShapeDtypeStruct((8, cols), F32),
        TICK,
    ]
    if own:
        in_specs += [plain, rows, pl.BlockSpec(extra[2].shape, at_zero)]

    def kernel(*refs):
        inner = refs[: 1 + len(in_specs)] + refs[1 + len(in_specs) + len(after) :]
        norm_one_kernel(own, *inner)

    return pl.pallas_call(
        kernel,
        grid_spec=pltpu.PrefetchScalarGridSpec(
            num_scalar_prefetch=1,
            grid=(count,),
            in_specs=in_specs + [ANY_SPEC] * len(after),
            out_specs=out_specs,
            scratch_shapes=[pltpu.VMEM((width, cols), BF16)],
        ),
        out_shape=out_shape,
        compiler_params=pltpu.CompilerParams(vmem_limit_bytes=VMEM_LIMIT),
        cost_estimate=SMALL_COST,
    )(core.reshape(1).astype(jnp.int32), *grads, weight_a, weight_b, inputs, *extra, *after)


def attention_backward(
    pair, qkv, query_code, key_code, attended, grad_attended, log_total, normed_t, after
):
    length = qkv.shape[0]
    return pl.pallas_call(
        attention_backward_kernel,
        grid=(1,),
        in_specs=[
            pl.BlockSpec((length, 3 * PAIR), lambda p: (0, pair)),
            pl.BlockSpec((length, PAIR), lambda p: (0, 0)),
            pl.BlockSpec((length, PAIR), lambda p: (0, 0)),
            pl.BlockSpec((length, PAIR), lambda p: (0, 0)),
            pl.BlockSpec((length, PAIR), lambda p: (0, pair)),
            pl.BlockSpec((1, 8, length), lambda p: (0, 0, 0)),
            pl.BlockSpec(normed_t.shape, lambda p: (0, 0)),
        ]
        + [pl.BlockSpec(memory_space=pl.ANY)] * len(after),
        out_specs=[
            pl.BlockSpec((length, 3 * PAIR), lambda p: (0, 0)),
            pl.BlockSpec((normed_t.shape[0], 3 * PAIR), lambda p: (0, 0)),
            TICK_SPEC,
        ],
        out_shape=[
            jax.ShapeDtypeStruct((length, 3 * PAIR), BF16),
            jax.ShapeDtypeStruct((normed_t.shape[0], 3 * PAIR), BF16),
            TICK,
        ],
        scratch_shapes=[
            pltpu.VMEM((2, length, PAIR), BF16),
            pltpu.VMEM((2, length, PAIR), BF16),
            pltpu.VMEM((2, length, PAIR), BF16),
            pltpu.VMEM((2, length, PAIR), BF16),
            pltpu.VMEM((PAIR, length), BF16),
            pltpu.VMEM((8, length), F32),
            pltpu.VMEM((PAIR, length), F32),
            pltpu.VMEM((BLK, PAIR), F32),
            pltpu.VMEM((BLK, PAIR), F32),
        ],
        compiler_params=pltpu.CompilerParams(vmem_limit_bytes=VMEM_LIMIT),
        cost_estimate=SMALL_COST,
    )(qkv, query_code, key_code, attended, grad_attended, log_total, normed_t, *after)


def norm_forward(source):
    average = jnp.mean(source, axis=-1, keepdims=True)
    centred = source - average
    spread = jnp.mean(centred * centred, axis=-1, keepdims=True)
    scale = lax.rsqrt(spread + EPSILON)
    return centred * scale, scale


def norm_backward(normal, scale, grad):
    return scale * (
        grad
        - jnp.mean(grad, axis=-1, keepdims=True)
        - normal * jnp.mean(grad * normal, axis=-1, keepdims=True)
    )


GELU_A = 0.7978845608028654
GELU_B = 0.044715


def gelu_parts(source):
    square = source * source
    inner = jnp.tanh(GELU_A * (source + GELU_B * source * square))
    value = 0.5 * source * (1.0 + inner)
    slope = 0.5 * (1.0 + inner) + 0.5 * source * (1.0 - inner * inner) * (
        GELU_A * (1.0 + 3.0 * GELU_B * square)
    )
    return value, slope


def swap(value, axis):
    return lax.ppermute(value, axis, [(0, 1), (1, 0)])


def pick(flag, first, second):
    return jnp.where(flag == 0, first, second), jnp.where(flag == 0, second, first)


class Links:
    def __init__(self):
        self.size = lax.axis_size("dp")
        at = lax.axis_index("dp")
        self.groups = {}
        shift, name = 0, "y"
        while (1 << shift) < self.size:
            bits = 1 if shift == 0 else min(2, self.size.bit_length() - 1 - shift)
            self.groups[name] = (shift, bits, (at >> shift) & ((1 << bits) - 1))
            shift += bits
            name = "z" + str(shift)
        self.rest = [name for name in reversed(self.groups) if name != "y"]
        self.dims = self.rest + ["y", "x"]
        self.side = lax.axis_index("xx")

    def counts(self, dims):
        return [2 if d == "x" else 1 << self.groups[d][1] for d in dims]

    def send(self, value, d, mask):
        if d == "x":
            return swap(value, "xx")
        move = mask << self.groups[d][0]
        return lax.ppermute(value, "dp", [(i, i ^ move) for i in range(self.size)])

    def place(self, d):
        return self.side if d == "x" else self.groups[d][2]

    def begin_reduce(self, state, d):
        array, dims = state
        axis, at = dims.index(d), self.place(d)
        kept = lax.dynamic_index_in_dim(array, at, axis, keepdims=False)
        come = [
            self.send(lax.dynamic_index_in_dim(array, at ^ mask, axis, keepdims=False), d, mask)
            for mask in range(1, array.shape[axis])
        ]
        return kept, come, [other for other in dims if other != d]

    def end_reduce(self, begun, tick=None):
        kept, come, dims = begun
        total = kept.astype(F32)
        for block in come:
            total = total + block.astype(F32)
        if tick is not None:
            total = total + tick[0, 0]
        return total.astype(BF16), dims

    def reduce(self, state, d, tick=None):
        return self.end_reduce(self.begin_reduce(state, d), tick)

    def begin_gather(self, state, d):
        array, dims = state
        come = [self.send(array, d, mask) for mask in range(1, self.counts([d])[0])]
        return array, come, dims, d

    def end_gather(self, begun, tick=None):
        array, come, dims, d = begun
        parts = [array] + come
        for bit in range(len(parts).bit_length() - 1):
            flag = (self.place(d) >> bit) & 1
            for low in range(len(parts)):
                if not low & (1 << bit):
                    high = low | (1 << bit)
                    parts[low], parts[high] = pick(flag, parts[low], parts[high])
        dims = [other for other in self.dims if other in dims or other == d]
        joined = jnp.stack(parts, axis=dims.index(d))
        if tick is not None:
            joined = joined + tick[0, 0].astype(joined.dtype)
        return joined, dims

    def gather(self, state, d, tick=None):
        return self.end_gather(self.begin_gather(state, d), tick)

    def settle(self, tick, *stages):
        return gate([tick] + [block for stage in stages for block in stage[1]])

    def rows(self, array, lead=()):
        shape = list(lead) + self.counts(self.dims)
        count = 1
        for size in shape:
            count *= size
        names = ["lead"] * len(lead) + self.dims
        return array.reshape(shape + [array.shape[0] // count, array.shape[1]]), names


def body(
    tokens,
    segments,
    ln1_gain,
    ln1_bias,
    qkv_weight,
    q_bias,
    v_bias,
    out_weight,
    out_bias,
    ln2_gain,
    ln2_bias,
    up_weight,
    up_bias,
    down_weight,
    down_bias,
    cotangent,
):
    side = lax.axis_index("xx")
    core = lax.axis_index("core")
    chips = lax.axis_size("dp") * lax.axis_size("xx")
    seq_count, quarter, width = tokens.shape
    length = segments.shape[1]
    own = qkv_weight.shape[0]
    pair_row = 2 * own
    hidden_own = up_bias.shape[0]
    half = width // 2
    cols = 3 * half
    pairs = half // PAIR
    splits = hidden_own // pair_row
    hidden = splits * width

    def at_index(array, index):
        return lax.dynamic_index_in_dim(array, index, 0, keepdims=False)

    def to_sequence(array, tick=None):
        kept = at_index(array, side)
        sent = at_index(array, 1 - side)
        if tick is not None:
            sent = sent + tick[0, 0].astype(sent.dtype)
        come = swap(sent, "xx")
        low, high = pick(side, kept, come)
        mine = jnp.stack([low, high])
        other = swap(mine, "core")
        even, odd = pick(core, mine, other)
        return jnp.stack([even, odd], axis=1).reshape(length, width), come, other

    def own_rows(array):
        return lax.dynamic_index_in_dim(
            array.reshape(2, 2, quarter, array.shape[-1]), core, 1, keepdims=False
        )

    def other_rows(array):
        return lax.dynamic_index_in_dim(
            array.reshape(2, 2, quarter, array.shape[-1]), 1 - core, 1, keepdims=False
        )

    def from_sequence(mine):
        come = swap(at_index(mine, 1 - side), "xx")
        return merged(at_index(mine, side), come), come

    def merged(kept, come, tick=None):
        if tick is not None:
            kept = kept + tick[0, 0].astype(kept.dtype)
        first, second = pick(side, kept, come)
        return jnp.stack([first, second])

    qkv_cols = qkv_weight.reshape(own, 3, 2, pairs, PAIR).transpose(2, 0, 3, 1, 4).reshape(2, own, cols)
    up_cols = (
        up_weight.reshape(own, chips, 2, splits, pair_row)
        .transpose(2, 0, 3, 1, 4)
        .reshape(2, own, hidden)
    )
    vectors = jnp.stack(
        [ln1_gain, ln1_bias, q_bias, v_bias, out_bias, ln2_gain, ln2_bias, down_bias], axis=1
    )
    vectors = jnp.pad(vectors, ((0, 0), (0, PAIR - vectors.shape[1])))

    def with_partner(two):
        mine, theirs = at_index(two, core), at_index(two, 1 - core)
        first, second = pick(core, mine, swap(theirs, "core"))
        return jnp.concatenate([first, second], axis=0)

    early = with_partner(
        jnp.concatenate([qkv_cols, jnp.broadcast_to(vectors, (2, own, PAIR))], axis=2)
    )
    early = jnp.concatenate(
        [
            early[:, : cols + 8],
            up_bias.reshape(splits, pair_row).T,
            early[:, cols + 8 + splits :],
        ],
        axis=1,
    )
    links = Links()

    def gather_rest(array, tick=None):
        state = (array, [])
        for d in links.rest:
            state = links.gather(state, d, tick if d == links.rest[-1] else None)
        return state

    def halves_of(state):
        middle = state[0].shape[-1] // 2
        return [(state[0][..., :middle], state[1]), (state[0][..., middle:], state[1])]

    def joined(halves):
        return [half_state[0].reshape(width, -1) for half_state in halves]

    inputs_low, come, other = to_sequence(tokens)
    grad_out_low, _, _ = to_sequence(cotangent, gate([come]))
    begun = [
        links.begin_gather(piece, d) for piece, d in zip(halves_of(gather_rest(early)), "yx")
    ]
    late_tick = gate([block for piece in begun for block in piece[1]] + [other])
    early_halves = [links.end_gather(piece, late_tick) for piece in begun]
    early_a, early_b = joined(
        [links.gather(piece, d) for piece, d in zip(early_halves, "xy")]
    )
    split = early_a.shape[1]
    late = with_partner(
        jnp.concatenate([up_cols, jnp.broadcast_to(out_weight, (2, own, width))], axis=2)
    )
    down_own = down_weight.reshape(splits, pair_row, width)
    late = jnp.concatenate([late] + [down_own[i] for i in range(splits)], axis=1)
    late = late + late_tick[0, 0].astype(BF16)
    late_one, late_two = halves_of((late, []))
    late_one = gather_rest(late_one[0])
    small = early_b[:, cols - split :].astype(F32).T
    gain_one, shift_one, query_shift, value_shift, out_shift, gain_two, shift_two, down_shift = (
        small[i] for i in range(8)
    )
    up_shift = small[8 : 8 + splits].reshape(hidden)

    inputs = inputs_low.astype(F32)
    seg = at_index(segments, side)
    numbers = jnp.arange(PAIR, dtype=jnp.int32) % HEAD_DIM
    same = seg[:, None] == numbers[None, :]
    coded = numbers[None, :] < 4
    query_code = jnp.where(same & coded, 1.0, 0.0).astype(BF16)
    key_code = jnp.where(same | ~coded, 0.0, NEG).astype(BF16)

    def head_cols(vector):
        return lax.dynamic_slice_in_dim(vector, core * half, half, 0).reshape(pairs, 1, PAIR)

    zeros = jnp.zeros((pairs, 1, PAIR), F32)
    qkv_shift = jnp.concatenate(
        [head_cols(query_shift), zeros, head_cols(value_shift)], axis=1
    ).reshape(1, cols)
    qkv_scale = jnp.tile(jnp.repeat(jnp.array([0.125, 1.0, 1.0], F32), PAIR), pairs)[None]
    normed_t, qkv, tick = qkv_projection(
        inputs_low,
        early_a,
        early_b,
        jnp.pad(jnp.stack([gain_one, shift_one]), ((0, 6), (0, 0))),
        jnp.pad(jnp.concatenate([qkv_shift, qkv_scale]), ((0, 6), (0, 0))),
        [late_one[0]],
    )
    attended_pairs, log_totals = [], []
    for d in links.rest[:-1]:
        late_two = links.gather(late_two, d)
    begun = links.begin_gather(late_two, links.rest[-1])
    stage_one = links.begin_gather(late_one, "x")
    late_two = links.end_gather(begun, links.settle(tick, begun))
    stage_two = links.begin_gather(late_two, "y")
    after = [late_two[0]]
    for pair in range(pairs):
        one_pair = attention_forward(pair, qkv, query_code, key_code, after)
        attended_pairs.append(one_pair[0])
        log_totals.append(one_pair[1])
        tick = one_pair[2]
        after = [one_pair[0]]
        if pair == 0:
            tick = links.settle(tick, stage_one, stage_two)
            late_one, late_two = links.end_gather(stage_one, tick), links.end_gather(stage_two, tick)
            after += [late_one[0], late_two[0]]
            stage_one = links.begin_gather(late_one, "y")
            stage_two = links.begin_gather(late_two, "x")
    attended = jnp.concatenate(attended_pairs, axis=1)
    tick = links.settle(tick, stage_one, stage_two)
    late_halves = joined([links.end_gather(stage, tick) for stage in (stage_one, stage_two)])
    late = jnp.concatenate(late_halves, axis=1)
    proj_up = late[:, :hidden]
    proj_out = lax.dynamic_slice_in_dim(late[:, hidden : hidden + width], core * half, half, 0)
    proj_down = jnp.concatenate(
        [late[:, hidden + (1 + i) * width : hidden + (2 + i) * width] for i in range(splits)], axis=0
    )

    branch = mm(attended, proj_out).astype(BF16)
    branch_come = swap(branch, "core")
    mid_vectors = jnp.pad(jnp.stack([out_shift, gain_two, shift_two]), ((0, 5), (0, 0)))
    normed_two_low, hidden_low, grad_pre_low, ffn, partial_two, up_sums = feed_forward(
        inputs_low,
        branch,
        branch_come,
        grad_out_low,
        proj_up,
        proj_down,
        mid_vectors,
        jnp.pad(up_shift[None], ((0, 7), (0, 0))),
    )
    partial_come = swap(partial_two, "core")
    middle_own = own_rows(inputs_low).astype(F32) + (
        own_rows(branch).astype(F32) + own_rows(branch_come).astype(F32)
    )

    grad_proj_down = [
        mm(hidden_low[:, i * width : (i + 1) * width], grad_out_low, TN).astype(BF16)
        for i in range(splits)
    ]
    grad_proj_up = mm(normed_two_low, grad_pre_low, TN).astype(BF16)
    grad_middle, branch_low, grad_attended, mid_sums, tick = norm_two(
        inputs_low,
        branch,
        branch_come,
        grad_out_low,
        partial_two,
        partial_come,
        proj_out,
        mid_vectors,
        [*grad_proj_down, grad_proj_up],
    )
    grad_proj_out = mm(attended, branch_low, TN)

    def as_column(vectors):
        table = jnp.stack(vectors, axis=1)
        return jnp.pad(table, ((0, 0), (0, PAIR - table.shape[1])))

    def only_mine(flag, array):
        return jnp.where(flag, array, jnp.zeros_like(array))

    small_two = [mid_sums[i] for i in range(4)] + [
        up_sums[0, i * width : (i + 1) * width] for i in range(splits)
    ]
    down_piece = links.rows(
        jnp.concatenate(grad_proj_down, axis=0) + tick[0, 0].astype(BF16), (splits,)
    )
    up_piece = links.rows(grad_proj_up + tick[0, 0].astype(BF16))
    ffn_come = swap(other_rows(ffn) + tick[0, 0].astype(BF16), "core")
    out_low = grad_proj_out.astype(BF16)
    grad_out_rows = jnp.concatenate(
        [only_mine(core == 0, out_low), only_mine(core == 1, out_low)], axis=0
    )

    def reduce_rest(piece, start=0):
        for d in links.rest[start:]:
            piece = links.reduce(piece, d)
        return piece

    grads, weight_grads, after = [], [], [down_piece[0], up_piece[0]]
    for pair in range(pairs):
        grad, weight_grad, tick = attention_backward(
            pair,
            qkv,
            query_code,
            key_code,
            attended_pairs[pair],
            grad_attended,
            log_totals[pair],
            normed_t,
            after + grads[-1:],
        )
        grads.append(grad)
        weight_grads.append(weight_grad)
        if pair == 0:
            begun = [links.begin_reduce(down_piece, "x"), links.begin_reduce(up_piece, "y")]
            tick = links.settle(tick, *begun, (None, [ffn_come]))
            down_piece, up_piece = [links.end_reduce(piece, tick) for piece in begun]
            first_piece = links.rows(
                jnp.concatenate([grad_out_rows, weight_grad], axis=1) + tick[0, 0].astype(BF16)
            )
            after = [down_piece[0], up_piece[0], first_piece[0]]
        elif pair == 1:
            begun = [
                links.begin_reduce(down_piece, links.rest[0]),
                links.begin_reduce(up_piece, "x"),
                links.begin_reduce(first_piece, "y"),
            ]
            tick = links.settle(tick, *begun)
            ffn_own = own_rows(ffn).astype(F32) + ffn_come.astype(F32)
            mixed_own = (middle_own + out_shift + ffn_own + down_shift + tick[0, 0]).astype(BF16)
            mixed_come = swap(at_index(mixed_own, 1 - side), "xx")
            down_piece, up_piece, first_piece = [links.end_reduce(piece, tick) for piece in begun]
            down_piece = reduce_rest(down_piece, 1)
            after = [down_piece[0], up_piece[0], first_piece[0]]
        else:
            begun = [
                links.begin_reduce(down_piece, "y"),
                links.begin_reduce(up_piece, links.rest[0]),
            ]
            tick = links.settle(tick, *begun, (None, [mixed_come]))
            mixed = merged(at_index(mixed_own, side), mixed_come, tick)
            down_piece, up_piece = [links.end_reduce(piece, tick) for piece in begun]
            up_piece = reduce_rest(up_piece, 1)
            after = [down_piece[0], up_piece[0]]
    first_piece = (first_piece[0] + tick[0, 0].astype(BF16), first_piece[1])
    begun = [
        links.begin_reduce(first_piece, "x"),
        links.begin_reduce(links.rows(weight_grads[1] + tick[0, 0].astype(BF16)), "y"),
    ]
    norm_vectors = jnp.pad(jnp.stack([gain_one, shift_one]), ((0, 6), (0, 0)))
    partial_one, norm_sums, bias_sums, _ = norm_one(
        False, core, grads, early_a, early_b, cols, inputs_low, [], after
    )
    come = swap(partial_one, "core")
    token_own, norm_sums_own, bias_sums_own, tick = norm_one(
        True,
        core,
        grads,
        early_a,
        early_b,
        cols,
        inputs_low,
        [come, grad_middle, norm_vectors],
        [],
    )
    norm_sums = norm_sums + norm_sums_own
    bias_sums = bias_sums + bias_sums_own
    token_grad, come = from_sequence(token_own.reshape(2, quarter, width))
    grad_by_pair = bias_sums[0].reshape(pairs, 3, PAIR)

    def padded(vector):
        vector = vector.reshape(half)
        return jnp.concatenate([only_mine(core == 0, vector), only_mine(core == 1, vector)])

    small = as_column(
        [
            norm_sums[0],
            norm_sums[1],
            padded(grad_by_pair[:, 0]),
            padded(grad_by_pair[:, 2]),
        ]
        + small_two
    )
    tick = links.settle(tick, *begun)
    first_piece, middle_piece = [links.end_reduce(piece, tick) for piece in begun]
    begun = links.begin_reduce(first_piece, links.rest[0])
    first_own = reduce_rest(links.end_reduce(begun), 1)[0]
    last_piece = links.reduce(
        links.rows(jnp.concatenate([weight_grads[2], small.astype(BF16)], axis=1)), "y"
    )
    last_piece = (jnp.concatenate([middle_piece[0], last_piece[0]], axis=-1), last_piece[1])
    begun = links.begin_reduce(links.reduce(last_piece, "x"), links.rest[0])
    tick = links.settle(tick, begun, (None, [come]))
    last_own = reduce_rest(links.end_reduce(begun, tick), 1)[0]

    def rows_of(array, index):
        return lax.dynamic_slice_in_dim(array, index * own, own, 0)

    def by_core(mine, come):
        return jnp.stack(pick(core, mine, come))

    def shared(array):
        return rows_of(array, core), swap(rows_of(array, 1 - core), "core")

    late_mine, late_come = shared(up_piece[0])
    early_mine, early_come = shared(jnp.concatenate([first_own, last_own], axis=1))
    out_grad = early_mine[:, :width].astype(F32) + early_come[:, :width].astype(F32)
    up_grad = (
        by_core(late_mine, late_come)
        .reshape(2, own, splits, chips, pair_row)
        .transpose(1, 3, 0, 2, 4)
        .reshape(own, 2 * hidden)
        .astype(F32)
    )
    down_grad = down_piece[0].reshape(hidden_own, width).astype(F32)
    qkv_grad = (
        by_core(early_mine[:, width : width + cols], early_come[:, width : width + cols])
        .reshape(2, own, pairs, 3, PAIR)
        .transpose(1, 3, 0, 2, 4)
        .reshape(own, 2 * cols)
        .astype(F32)
    )
    tail, first = width + cols + 8, first_own.shape[1]
    small_mine = early_mine[:, tail - 8 : tail].astype(F32)
    one = small_mine[:, :4] + early_come[:, tail - 8 : tail - 4].astype(F32)
    up_shift_grad = (
        last_own[:, tail - first : tail - first + splits].T.reshape(hidden_own).astype(F32)
    )
    two = small_mine[:, 4:]
    return (
        mixed,
        token_grad,
        one[:, 0],
        one[:, 1],
        qkv_grad,
        one[:, 2],
        one[:, 3],
        out_grad,
        two[:, 0],
        two[:, 1],
        two[:, 2],
        up_grad,
        up_shift_grad,
        down_grad,
        two[:, 3],
    )


def solution(mesh):
    parts = (mesh.shape["dp"], mesh.shape["ctx"] // 2, 2)
    split_mesh = Mesh(mesh.devices.reshape(parts), ("dp", "xx", "core"))
    rows = ("dp", "xx", "core")
    acts = P("dp", ("xx", "core"), None)
    vec, mat = P(rows), P(rows, None)
    return jax.shard_map(
        body,
        mesh=split_mesh,
        in_specs=(
            acts, P("dp", None), vec, vec, mat, vec, vec, mat, vec, vec, vec, mat, vec, mat, vec, acts,
        ),
        out_specs=(
            acts, acts, vec, vec, mat, vec, vec, mat, vec, vec, vec, mat, vec, mat, vec,
        ),
        check_vma=False,
    )
```

```python
import functools

import jax
import jax.numpy as jnp
from jax import lax
from jax.experimental import pallas as pl
from jax.experimental.pallas import tpu as pltpu
from jax.sharding import Mesh, PartitionSpec as P

HEAD_DIM = 64
PAIR = 2 * HEAD_DIM
EPSILON = 1e-05
NEG = -1e30
BLK = 512
F32 = jnp.float32
BF16 = jnp.bfloat16

NN = (((1,), (0,)), ((), ()))
NT = (((1,), (1,)), ((), ()))
TN = (((0,), (0,)), ((), ()))


def mm(left, right, dims=NN):
    return lax.dot_general(left, right, dims, preferred_element_type=F32)


def build_scores_operands(qkv_ref, qs_ref, ks_ref, rows, qx, kx):
    lane = lax.broadcasted_iota(jnp.int32, (BLK, PAIR), 1)
    first = lane < HEAD_DIM
    q = qkv_ref[rows, 0:PAIR].astype(F32)
    k = qkv_ref[rows, PAIR : 2 * PAIR].astype(F32)
    qs = qs_ref[rows, :].astype(F32)
    ks = ks_ref[rows, :].astype(F32)
    qx[0, rows, :] = jnp.where(first, q, qs).astype(BF16)
    qx[1, rows, :] = jnp.where(first, qs, q).astype(BF16)
    kx[0, rows, :] = jnp.where(first, k, ks).astype(BF16)
    kx[1, rows, :] = jnp.where(first, ks, k).astype(BF16)
    return first, q, k


def causal_block(scores):
    key_at = lax.broadcasted_iota(jnp.int32, scores.shape, 0)
    query_at = lax.broadcasted_iota(jnp.int32, scores.shape, 1)
    return jnp.where(key_at <= query_at, scores, NEG)


def attention_forward_kernel(qkv_ref, qs_ref, ks_ref, *rest):
    o_ref, lse_ref, tick_ref, qx, kx, vt, acc = rest[-7:]
    tick_ref[...] = jnp.zeros_like(tick_ref)
    length = qkv_ref.shape[0]
    blocks = length // BLK

    @pl.loop(0, blocks)
    def _(i):
        rows = pl.ds(pl.multiple_of(i * BLK, BLK), BLK)
        build_scores_operands(qkv_ref, qs_ref, ks_ref, rows, qx, kx)
        v_t = qkv_ref[rows, 2 * PAIR : 3 * PAIR].astype(F32).T
        ones = jnp.ones((16, BLK), BF16)
        for h in range(2):
            vt[h, 0:HEAD_DIM, rows] = v_t[h * HEAD_DIM : (h + 1) * HEAD_DIM].astype(BF16)
            vt[h, HEAD_DIM : HEAD_DIM + 16, rows] = ones

    @pl.loop(0, blocks)
    def _(i):
        rows = pl.ds(pl.multiple_of(i * BLK, BLK), BLK)
        queries = [qx[h, rows, :] for h in range(2)]
        tops = []
        for h in range(2):
            s = causal_block(mm(kx[h, rows, :], queries[h], NT))
            top = jnp.max(s, axis=0, keepdims=True)
            p = jnp.exp(s - top).astype(BF16)
            acc[h] = mm(vt[h, :, rows], p)
            tops.append(top)

        def step(j, carry):
            keys = pl.ds(pl.multiple_of(j * BLK, BLK), BLK)
            out = []
            for h in range(2):
                s = mm(kx[h, keys, :], qx[h, rows, :], NT)
                top = jnp.maximum(carry[h], jnp.max(s, axis=0, keepdims=True))
                p = jnp.exp(s - top).astype(BF16)
                acc[h] = acc[h] * jnp.exp(carry[h] - top) + mm(vt[h, :, keys], p)
                out.append(top)
            return tuple(out)

        tops = lax.fori_loop(0, i, step, tuple(tops))
        parts = []
        for h in range(2):
            total = acc[h, HEAD_DIM : HEAD_DIM + 1, :]
            parts.append(acc[h, 0:HEAD_DIM, :] / total)
            lse_ref[0, h : h + 1, rows] = tops[h] + jnp.log(total)
        o_ref[rows, :] = jnp.concatenate(parts, axis=0).T.astype(BF16)


def attention_backward_kernel(qkv_ref, qs_ref, ks_ref, o_ref, do_ref, lse_ref, at_ref, *rest):
    d_ref, dw_ref, tick_ref, qx, kx, qm, dm, kt, delta, dqt, dk, dv = rest[-12:]
    tick_ref[...] = jnp.zeros_like(tick_ref)
    length = qkv_ref.shape[0]
    blocks = length // BLK

    @pl.loop(0, blocks)
    def _(i):
        rows = pl.ds(pl.multiple_of(i * BLK, BLK), BLK)
        first, q, k = build_scores_operands(qkv_ref, qs_ref, ks_ref, rows, qx, kx)
        do = do_ref[rows, :].astype(F32)
        zero = jnp.zeros_like(q)
        qm[0, rows, :] = jnp.where(first, q, zero).astype(BF16)
        qm[1, rows, :] = jnp.where(first, zero, q).astype(BF16)
        dm[0, rows, :] = jnp.where(first, do, zero).astype(BF16)
        dm[1, rows, :] = jnp.where(first, zero, do).astype(BF16)
        kt[:, rows] = k.T.astype(BF16)
        inner = (do * o_ref[rows, :].astype(F32)).T
        for h in range(2):
            delta[h : h + 1, rows] = jnp.sum(
                inner[h * HEAD_DIM : (h + 1) * HEAD_DIM], axis=0, keepdims=True
            )
        dqt[:, rows] = jnp.zeros((PAIR, BLK), F32)

    def tile(keys, rows, masked):
        values = qkv_ref[keys, 2 * PAIR : 3 * PAIR]
        dv_part, dk_part = None, None
        for h in range(2):
            s = mm(kx[h, keys, :], qx[h, rows, :], NT)
            if masked:
                s = causal_block(s)
            p = jnp.exp(s - lse_ref[0, h : h + 1, rows])
            dp = mm(values, dm[h, rows, :], NT)
            ds = (p * (dp - delta[h : h + 1, rows])).astype(BF16)
            dv_h = mm(p.astype(BF16), dm[h, rows, :])
            dk_h = mm(ds, qm[h, rows, :])
            dv_part = dv_h if h == 0 else dv_part + dv_h
            dk_part = dk_h if h == 0 else dk_part + dk_h
            part = slice(h * HEAD_DIM, (h + 1) * HEAD_DIM)
            dqt[part, rows] += mm(kt[part, keys], ds)
        return dk_part, dv_part

    @pl.loop(0, blocks)
    def _(j):
        keys = pl.ds(pl.multiple_of(j * BLK, BLK), BLK)
        dk[...], dv[...] = tile(keys, keys, True)

        @pl.loop(j + 1, blocks)
        def _(i):
            dk_part, dv_part = tile(keys, pl.ds(pl.multiple_of(i * BLK, BLK), BLK), False)
            dk[...] += dk_part
            dv[...] += dv_part

        d_ref[keys, PAIR : 2 * PAIR] = dk[...].astype(BF16)
        d_ref[keys, 2 * PAIR : 3 * PAIR] = dv[...].astype(BF16)

    @pl.loop(0, blocks)
    def _(i):
        rows = pl.ds(pl.multiple_of(i * BLK, BLK), BLK)
        d_ref[rows, 0:PAIR] = (dqt[:, rows].T.astype(BF16).astype(F32) * 0.125).astype(BF16)

    @pl.loop(0, dw_ref.shape[0] // ROWS)
    def _(i):
        rows = pl.ds(pl.multiple_of(i * ROWS, ROWS), ROWS)
        dw_ref[rows, :] = mm(at_ref[rows, :], d_ref[...]).astype(BF16)


VMEM_LIMIT = 48 * 1024 * 1024


SMALL_COST = pl.CostEstimate(flops=10**8, bytes_accessed=10**6, transcendentals=0)


TICK = jax.ShapeDtypeStruct((8, 128), F32)
TICK_SPEC = pl.BlockSpec((8, 128), lambda i: (0, 0))
ANY_SPEC = pl.BlockSpec(memory_space=pl.ANY)


def pack_kernel(count, refs):
    refs[-1][...] = jnp.concatenate([ref[...] for ref in refs[:count]], axis=-1)


def pack(parts, after):
    rows = parts[0].shape[0]
    width = sum(part.shape[1] for part in parts)
    return pl.pallas_call(
        lambda *refs: pack_kernel(len(parts), refs),
        grid=(1,),
        in_specs=[pl.BlockSpec(part.shape, lambda i: (0, 0)) for part in parts]
        + [ANY_SPEC] * len(after),
        out_specs=pl.BlockSpec((rows, width), lambda i: (0, 0)),
        out_shape=jax.ShapeDtypeStruct((rows, width), BF16),
        compiler_params=pltpu.CompilerParams(vmem_limit_bytes=VMEM_LIMIT),
        cost_estimate=SMALL_COST,
    )(*parts, *after)


def widen(source, width, after):
    rows, cols = source.shape
    count = cols // width - 2

    def kernel(source_ref, *refs):
        up_ref, down_ref = refs[-2:]
        up_ref[...] = source_ref[:, : 2 * width].astype(F32)
        for i in range(count):
            down_ref[i] = source_ref[:, (2 + i) * width : (3 + i) * width].astype(F32)

    return pl.pallas_call(
        kernel,
        grid=(1,),
        in_specs=[pl.BlockSpec((rows, cols), lambda i: (0, 0))] + [ANY_SPEC] * len(after),
        out_specs=[
            pl.BlockSpec((rows, 2 * width), lambda i: (0, 0)),
            pl.BlockSpec((count, rows, width), lambda i: (0, 0, 0)),
        ],
        out_shape=[
            jax.ShapeDtypeStruct((rows, 2 * width), F32),
            jax.ShapeDtypeStruct((count, rows, width), F32),
        ],
        compiler_params=pltpu.CompilerParams(vmem_limit_bytes=VMEM_LIMIT),
        cost_estimate=SMALL_COST,
    )(source, *after)


def gate_kernel(*refs):
    refs[-1][...] = jnp.zeros_like(refs[-1])


def gate(after):
    return pl.pallas_call(
        gate_kernel,
        grid=(1,),
        in_specs=[ANY_SPEC] * len(after),
        out_specs=TICK_SPEC,
        out_shape=TICK,
        cost_estimate=SMALL_COST,
    )(*after)


def fold_kernel(counts, refs):
    parts, comes, outs = counts
    first = refs[1 : 1 + parts * outs]
    second = refs[1 + parts * outs : 1 + (parts + comes) * outs]
    for m in range(outs):
        value = jnp.concatenate([ref[0] for ref in first[m * parts : (m + 1) * parts]], axis=-1)
        if comes:
            value = value.astype(F32)
            for ref in second[m * comes : (m + 1) * comes]:
                value = value + ref[0].astype(F32)
            value = value.astype(BF16)
        refs[len(refs) - outs + m][0] = value


def fold(parts, comes, sizes, axis, at, after):
    blocks, rows = parts[0].shape[:2]
    width = sum(part.shape[2] for part in parts)
    outs = sizes[axis] if axis is not None else 1
    inner = 1
    if axis is not None:
        for size in sizes[axis + 1 :]:
            inner *= size

    def spec(array, m):
        def index(j, at_ref):
            if axis is None:
                return j, 0, 0
            return (j // inner) * (outs * inner) + (at_ref[0] ^ m) * inner + j % inner, 0, 0

        return pl.BlockSpec((1, rows, array.shape[2]), index)

    def kernel(*refs):
        ins = 1 + (len(parts) + len(comes)) * outs
        fold_kernel((len(parts), len(comes), outs), refs[:ins] + refs[ins + len(after) :])

    out = pl.BlockSpec((1, rows, width), lambda j, at_ref: (j, 0, 0))
    return pl.pallas_call(
        kernel,
        grid_spec=pltpu.PrefetchScalarGridSpec(
            num_scalar_prefetch=1,
            grid=(blocks // outs,),
            in_specs=[spec(part, m) for m in range(outs) for part in parts]
            + [spec(come, m) for m in range(outs) for come in comes]
            + [ANY_SPEC] * len(after),
            out_specs=[out] * outs,
        ),
        out_shape=[jax.ShapeDtypeStruct((blocks // outs, rows, width), BF16)] * outs,
        compiler_params=pltpu.CompilerParams(vmem_limit_bytes=VMEM_LIMIT),
        cost_estimate=SMALL_COST,
    )(at.reshape(1).astype(jnp.int32), *(list(parts) * outs), *(list(comes) * outs), *after)


def qkv_kernel(x_ref, wa_ref, wb_ref, vec_ref, col_ref, *rest_refs):
    a_ref, qkv_ref, tick_ref = rest_refs[-3:]
    split = wa_ref.shape[1]
    rest = qkv_ref.shape[1] - split
    for part in range(2):
        rows = slice(part * ROWS, (part + 1) * ROWS)
        normal, _ = norm_forward(x_ref[rows, :].astype(F32))
        normed = (normal * vec_ref[0:1, :] + vec_ref[1:2, :]).astype(BF16)
        a_ref[:, rows] = normed.astype(F32).T.astype(BF16)
        for w, cols in ((wa_ref[...], slice(0, split)), (wb_ref[:, :rest], slice(split, None))):
            shift, scale = col_ref[0:1, cols], col_ref[1:2, cols]
            qkv_ref[rows, cols] = ((mm(normed, w) + shift) * scale).astype(BF16)
    tick_ref[...] = jnp.zeros_like(tick_ref)


def qkv_projection(inputs, weight_a, weight_b, vectors, columns, after):
    length, width = inputs.shape
    cols = columns.shape[1]
    return pl.pallas_call(
        qkv_kernel,
        grid=(length // (2 * ROWS),),
        in_specs=[
            pl.BlockSpec((2 * ROWS, width), lambda i: (i, 0)),
            pl.BlockSpec(weight_a.shape, lambda i: (0, 0)),
            pl.BlockSpec(weight_b.shape, lambda i: (0, 0)),
            pl.BlockSpec(vectors.shape, lambda i: (0, 0)),
            pl.BlockSpec(columns.shape, lambda i: (0, 0)),
        ]
        + [ANY_SPEC] * len(after),
        out_specs=[
            pl.BlockSpec((width, 2 * ROWS), lambda i: (0, i)),
            pl.BlockSpec((2 * ROWS, cols), lambda i: (i, 0)),
            TICK_SPEC,
        ],
        out_shape=[
            jax.ShapeDtypeStruct((width, length), BF16),
            jax.ShapeDtypeStruct((length, cols), BF16),
            TICK,
        ],
        compiler_params=pltpu.CompilerParams(vmem_limit_bytes=VMEM_LIMIT),
        cost_estimate=SMALL_COST,
    )(inputs, weight_a, weight_b, vectors, columns, *after)


def feed_forward_kernel(
    x_ref, b0_ref, b1_ref, dy_ref, up_ref, down_ref, vec_ref, shift_ref,
    a_ref, g_ref, du_ref, ffn_ref, dh_ref, sums_ref,
):
    @pl.when(pl.program_id(0) == 0)
    def _():
        sums_ref[...] = jnp.zeros_like(sums_ref)

    middle = x_ref[...].astype(F32) + (b0_ref[...].astype(F32) + b1_ref[...].astype(F32)) + vec_ref[0:1, :]
    normal, _ = norm_forward(middle)
    normed = (normal * vec_ref[1:2, :] + vec_ref[2:3, :]).astype(BF16)
    a_ref[...] = normed
    dy = dy_ref[...]
    ffn, dh = None, None
    for at in range(0, up_ref.shape[1], HIDDEN):
        cols = slice(at, at + HIDDEN)
        up, down = up_ref[:, cols], down_ref[cols, :]
        value, slope = gelu_parts(mm(normed, up) + shift_ref[0:1, cols])
        du = slope * mm(dy, down, NT)
        value, du = value.astype(BF16), du.astype(BF16)
        g_ref[:, cols] = value
        du_ref[:, cols] = du
        sums_ref[0:1, cols] += jnp.sum(du.astype(F32), axis=0, keepdims=True)
        ffn_part, dh_part = mm(value, down), mm(du, up, NT)
        ffn = ffn_part if at == 0 else ffn + ffn_part
        dh = dh_part if at == 0 else dh + dh_part
    ffn_ref[...] = ffn.astype(BF16)
    dh_ref[...] = dh.astype(BF16)


HIDDEN = 512


def feed_forward(inputs, branch, branch_come, grad_out, up, down, vectors, up_shift):
    length, width = inputs.shape
    hidden = up.shape[1]
    narrow = pl.BlockSpec((ROWS, width), lambda i: (i, 0))
    wide = pl.BlockSpec((ROWS, hidden), lambda i: (i, 0))

    def whole(array):
        return pl.BlockSpec(array.shape, lambda i: (0, 0))

    return pl.pallas_call(
        feed_forward_kernel,
        grid=(length // ROWS,),
        in_specs=[narrow] * 4 + [whole(up), whole(down), whole(vectors), whole(up_shift)],
        out_specs=[narrow, wide, wide, narrow, narrow, pl.BlockSpec((8, hidden), lambda i: (0, 0))],
        out_shape=[
            jax.ShapeDtypeStruct((length, width), BF16),
            jax.ShapeDtypeStruct((length, hidden), BF16),
            jax.ShapeDtypeStruct((length, hidden), BF16),
            jax.ShapeDtypeStruct((length, width), BF16),
            jax.ShapeDtypeStruct((length, width), BF16),
            jax.ShapeDtypeStruct((8, hidden), F32),
        ],
        compiler_params=pltpu.CompilerParams(vmem_limit_bytes=VMEM_LIMIT),
        cost_estimate=SMALL_COST,
    )(inputs, branch, branch_come, grad_out, up, down, vectors, up_shift)


def norm_two_kernel(
    x_ref, b0_ref, b1_ref, dy_ref, p0_ref, p1_ref, w_ref, vec_ref, *rest
):
    mid_ref, low_ref, do_ref, sums_ref, tick_ref = rest[-5:]

    @pl.when(pl.program_id(0) == 0)
    def _():
        sums_ref[...] = jnp.zeros_like(sums_ref)
        tick_ref[...] = jnp.zeros_like(tick_ref)

    middle = x_ref[...].astype(F32) + (b0_ref[...].astype(F32) + b1_ref[...].astype(F32)) + vec_ref[0:1, :]
    normal, scale = norm_forward(middle)
    grad = p0_ref[...].astype(F32) + p1_ref[...].astype(F32)
    dy = dy_ref[...].astype(F32)
    mid = dy + norm_backward(normal, scale, grad * vec_ref[1:2, :])
    low = mid.astype(BF16)
    mid_ref[...] = mid
    low_ref[...] = low
    do_ref[...] = mm(low, w_ref[...], NT).astype(BF16)
    for i, value in enumerate((low.astype(F32), grad * normal, grad, dy)):
        sums_ref[i : i + 1, :] += jnp.sum(value, axis=0, keepdims=True)


def norm_two(inputs, branch, branch_come, grad_out, partial, partial_come, weight, vectors, after):
    length, width = inputs.shape
    cols = weight.shape[0]
    narrow = pl.BlockSpec((ROWS, width), lambda i: (i, 0))

    def whole(array):
        return pl.BlockSpec(array.shape, lambda i: (0, 0))

    return pl.pallas_call(
        norm_two_kernel,
        grid=(length // ROWS,),
        in_specs=[narrow] * 6 + [whole(weight), whole(vectors)] + [ANY_SPEC] * len(after),
        out_specs=[
            narrow,
            narrow,
            pl.BlockSpec((ROWS, cols), lambda i: (i, 0)),
            pl.BlockSpec((8, width), lambda i: (0, 0)),
            TICK_SPEC,
        ],
        out_shape=[
            jax.ShapeDtypeStruct((length, width), F32),
            jax.ShapeDtypeStruct((length, width), BF16),
            jax.ShapeDtypeStruct((length, cols), BF16),
            jax.ShapeDtypeStruct((8, width), F32),
            TICK,
        ],
        compiler_params=pltpu.CompilerParams(vmem_limit_bytes=VMEM_LIMIT),
        cost_estimate=SMALL_COST,
    )(inputs, branch, branch_come, grad_out, partial, partial_come, weight, vectors, *after)


ROWS = 256


def attention_forward(qkv, query_code, key_code):
    length, width = qkv.shape
    pairs = width // (3 * PAIR)
    return pl.pallas_call(
        attention_forward_kernel,
        grid=(pairs,),
        in_specs=[
            pl.BlockSpec((length, 3 * PAIR), lambda p: (0, p)),
            pl.BlockSpec((length, PAIR), lambda p: (0, 0)),
            pl.BlockSpec((length, PAIR), lambda p: (0, 0)),
        ],
        out_specs=[
            pl.BlockSpec((length, PAIR), lambda p: (0, p)),
            pl.BlockSpec((1, 8, length), lambda p: (p, 0, 0)),
            TICK_SPEC,
        ],
        out_shape=[
            jax.ShapeDtypeStruct((length, pairs * PAIR), BF16),
            jax.ShapeDtypeStruct((pairs, 8, length), F32),
            TICK,
        ],
        scratch_shapes=[
            pltpu.VMEM((2, length, PAIR), BF16),
            pltpu.VMEM((2, length, PAIR), BF16),
            pltpu.VMEM((2, HEAD_DIM + 16, length), BF16),
            pltpu.VMEM((2, HEAD_DIM + 16, BLK), F32),
        ],
        compiler_params=pltpu.CompilerParams(vmem_limit_bytes=VMEM_LIMIT),
        cost_estimate=SMALL_COST,
    )(qkv, query_code, key_code)


def norm_one_kernel(own, core_ref, d0_ref, d1_ref, wa_ref, wb_ref, x_ref, *rest):
    if own:
        come_ref, mid_ref, vec_ref, out_ref, sums_ref, bias_ref, tick_ref, w = rest
    else:
        out_ref, sums_ref, bias_ref, tick_ref, w = rest
    split = wa_ref.shape[1]

    @pl.when(pl.program_id(0) == 0)
    def _():
        sums_ref[...] = jnp.zeros_like(sums_ref)
        bias_ref[...] = jnp.zeros_like(bias_ref)
        w[:, :split] = wa_ref[...]
        w[:, split:] = wb_ref[:, : w.shape[1] - split]
        tick_ref[...] = jnp.zeros_like(tick_ref)

    total = None
    for i, ref in enumerate((d0_ref, d1_ref)):
        cols = slice(0, ref.shape[1]) if i == 0 else slice(d0_ref.shape[1], None)
        grad = ref[...]
        part = mm(grad, w[:, cols], NT)
        total = part if i == 0 else total + part
        bias_ref[0:1, cols] += jnp.sum(grad.astype(F32), axis=0, keepdims=True)
    normal, scale = norm_forward(x_ref[...].astype(F32))
    sums_ref[0:1, :] += jnp.sum(total * normal, axis=0, keepdims=True)
    sums_ref[1:2, :] += jnp.sum(total, axis=0, keepdims=True)
    if own:
        grad = (total + come_ref[...].astype(F32)) * vec_ref[0:1, :]
        out_ref[...] = (mid_ref[...] + norm_backward(normal, scale, grad)).astype(BF16)
    else:
        out_ref[...] = total.astype(BF16)


def norm_one(own, core, grads, weight_a, weight_b, cols, inputs, extra, after):
    length, width = inputs.shape
    count = length // (2 * ROWS)
    per = count // 2

    def block(i, core_ref):
        which = core_ref[0] if own else 1 - core_ref[0]
        return ((i // per) * 2 + which) * per + i % per, 0

    def at_zero(i, core_ref):
        return 0, 0

    plain = pl.BlockSpec((ROWS, width), lambda i, core_ref: (i, 0))
    rows = pl.BlockSpec((ROWS, width), block)
    in_specs = [pl.BlockSpec((ROWS, grad.shape[1]), block) for grad in grads] + [
        pl.BlockSpec(weight_a.shape, at_zero),
        pl.BlockSpec(weight_b.shape, at_zero),
        rows,
    ]
    out_specs = [
        plain,
        pl.BlockSpec((8, width), at_zero),
        pl.BlockSpec((8, cols), at_zero),
        pl.BlockSpec((8, 128), at_zero),
    ]
    out_shape = [
        jax.ShapeDtypeStruct((count * ROWS, width), BF16),
        jax.ShapeDtypeStruct((8, width), F32),
        jax.ShapeDtypeStruct((8, cols), F32),
        TICK,
    ]
    if own:
        in_specs += [plain, rows, pl.BlockSpec(extra[2].shape, at_zero)]

    def kernel(*refs):
        inner = refs[: 1 + len(in_specs)] + refs[1 + len(in_specs) + len(after) :]
        norm_one_kernel(own, *inner)

    return pl.pallas_call(
        kernel,
        grid_spec=pltpu.PrefetchScalarGridSpec(
            num_scalar_prefetch=1,
            grid=(count,),
            in_specs=in_specs + [ANY_SPEC] * len(after),
            out_specs=out_specs,
            scratch_shapes=[pltpu.VMEM((width, cols), BF16)],
        ),
        out_shape=out_shape,
        compiler_params=pltpu.CompilerParams(vmem_limit_bytes=VMEM_LIMIT),
        cost_estimate=SMALL_COST,
    )(core.reshape(1).astype(jnp.int32), *grads, weight_a, weight_b, inputs, *extra, *after)


def attention_backward(
    first, count, qkv, query_code, key_code, attended, grad_attended, log_total, normed_t, after
):
    length = qkv.shape[0]
    width = normed_t.shape[0]
    return pl.pallas_call(
        attention_backward_kernel,
        grid=(count,),
        in_specs=[
            pl.BlockSpec((length, 3 * PAIR), lambda p: (0, first + p)),
            pl.BlockSpec((length, PAIR), lambda p: (0, 0)),
            pl.BlockSpec((length, PAIR), lambda p: (0, 0)),
            pl.BlockSpec((length, PAIR), lambda p: (0, first + p)),
            pl.BlockSpec((length, PAIR), lambda p: (0, first + p)),
            pl.BlockSpec((1, 8, length), lambda p: (first + p, 0, 0)),
            pl.BlockSpec(normed_t.shape, lambda p: (0, 0)),
        ]
        + [ANY_SPEC] * len(after),
        out_specs=[
            pl.BlockSpec((length, 3 * PAIR), lambda p: (0, p)),
            pl.BlockSpec((width, 3 * PAIR), lambda p: (0, p)),
            TICK_SPEC,
        ],
        out_shape=[
            jax.ShapeDtypeStruct((length, count * 3 * PAIR), BF16),
            jax.ShapeDtypeStruct((width, count * 3 * PAIR), BF16),
            TICK,
        ],
        scratch_shapes=[
            pltpu.VMEM((2, length, PAIR), BF16),
            pltpu.VMEM((2, length, PAIR), BF16),
            pltpu.VMEM((2, length, PAIR), BF16),
            pltpu.VMEM((2, length, PAIR), BF16),
            pltpu.VMEM((PAIR, length), BF16),
            pltpu.VMEM((8, length), F32),
            pltpu.VMEM((PAIR, length), F32),
            pltpu.VMEM((BLK, PAIR), F32),
            pltpu.VMEM((BLK, PAIR), F32),
        ],
        compiler_params=pltpu.CompilerParams(vmem_limit_bytes=VMEM_LIMIT),
        cost_estimate=SMALL_COST,
    )(qkv, query_code, key_code, attended, grad_attended, log_total, normed_t, *after)


def norm_forward(source):
    average = jnp.mean(source, axis=-1, keepdims=True)
    centred = source - average
    spread = jnp.mean(centred * centred, axis=-1, keepdims=True)
    scale = lax.rsqrt(spread + EPSILON)
    return centred * scale, scale


def norm_backward(normal, scale, grad):
    return scale * (
        grad
        - jnp.mean(grad, axis=-1, keepdims=True)
        - normal * jnp.mean(grad * normal, axis=-1, keepdims=True)
    )


GELU_A = 0.7978845608028654
GELU_B = 0.044715


def gelu_parts(source):
    square = source * source
    inner = jnp.tanh(GELU_A * (source + GELU_B * source * square))
    value = 0.5 * source * (1.0 + inner)
    slope = 0.5 * (1.0 + inner) + 0.5 * source * (1.0 - inner * inner) * (
        GELU_A * (1.0 + 3.0 * GELU_B * square)
    )
    return value, slope


def swap(value, axis):
    return lax.ppermute(value, axis, [(0, 1), (1, 0)])


def pick(flag, first, second):
    return jnp.where(flag == 0, first, second), jnp.where(flag == 0, second, first)


class Links:
    def __init__(self):
        self.size = lax.axis_size("dp")
        at = lax.axis_index("dp")
        self.groups = {}
        shift, name = 0, "y"
        while (1 << shift) < self.size:
            bits = 1 if shift == 0 else min(2, self.size.bit_length() - 1 - shift)
            self.groups[name] = (shift, bits, (at >> shift) & ((1 << bits) - 1))
            shift += bits
            name = "z" + str(shift)
        self.rest = [name for name in reversed(self.groups) if name != "y"]
        self.dims = self.rest + ["y", "x"]
        self.side = lax.axis_index("xx")

    def counts(self, dims):
        return [2 if d == "x" else 1 << self.groups[d][1] for d in dims]

    def send(self, value, d, mask):
        if d == "x":
            return swap(value, "xx")
        move = mask << self.groups[d][0]
        return lax.ppermute(value, "dp", [(i, i ^ move) for i in range(self.size)])

    def place(self, d):
        return self.side if d == "x" else self.groups[d][2]

    def scatter(self, parts, comes, dims, d, after=()):
        axis = dims.index(d)
        shares = fold(parts, comes, self.counts(dims), axis, self.place(d), list(after))
        come = [self.send(share, d, mask) for mask, share in enumerate(shares) if mask > 0]
        return [shares[0]], come, [other for other in dims if other != d]

    def scatter_rest(self, state):
        for d in self.rest:
            state = self.scatter(*state, d)
        return self.total(state)

    def total(self, state):
        parts, comes, dims = state
        total = parts[0].astype(F32)
        for come in comes:
            total = total + come.astype(F32)
        return total[0]

    def begin_gather(self, state, d):
        array, dims = state
        come = [self.send(array, d, mask) for mask in range(1, self.counts([d])[0])]
        return array, come, dims, d

    def end_gather(self, begun, tick=None):
        array, come, dims, d = begun
        parts = [array] + come
        for bit in range(len(parts).bit_length() - 1):
            flag = (self.place(d) >> bit) & 1
            for low in range(len(parts)):
                if not low & (1 << bit):
                    high = low | (1 << bit)
                    parts[low], parts[high] = pick(flag, parts[low], parts[high])
        dims = [other for other in self.dims if other in dims or other == d]
        joined = jnp.stack(parts, axis=dims.index(d))
        if tick is not None:
            joined = joined + tick[0, 0].astype(joined.dtype)
        return joined, dims

    def gather(self, state, d, tick=None):
        return self.end_gather(self.begin_gather(state, d), tick)

def body(
    tokens,
    segments,
    ln1_gain,
    ln1_bias,
    qkv_weight,
    q_bias,
    v_bias,
    out_weight,
    out_bias,
    ln2_gain,
    ln2_bias,
    up_weight,
    up_bias,
    down_weight,
    down_bias,
    cotangent,
):
    side = lax.axis_index("xx")
    core = lax.axis_index("core")
    chips = lax.axis_size("dp") * lax.axis_size("xx")
    seq_count, quarter, width = tokens.shape
    length = segments.shape[1]
    own = qkv_weight.shape[0]
    pair_row = 2 * own
    hidden_own = up_bias.shape[0]
    half = width // 2
    cols = 3 * half
    pairs = half // PAIR
    splits = hidden_own // pair_row
    hidden = splits * width

    def at_index(array, index):
        return lax.dynamic_index_in_dim(array, index, 0, keepdims=False)

    def to_sequence(array, tick=None):
        kept = at_index(array, side)
        sent = at_index(array, 1 - side)
        if tick is not None:
            sent = sent + tick[0, 0].astype(sent.dtype)
        come = swap(sent, "xx")
        low, high = pick(side, kept, come)
        mine = jnp.stack([low, high])
        other = swap(mine, "core")
        even, odd = pick(core, mine, other)
        return jnp.stack([even, odd], axis=1).reshape(length, width), come, other

    def own_rows(array):
        return lax.dynamic_index_in_dim(
            array.reshape(2, 2, quarter, array.shape[-1]), core, 1, keepdims=False
        )

    def other_rows(array):
        return lax.dynamic_index_in_dim(
            array.reshape(2, 2, quarter, array.shape[-1]), 1 - core, 1, keepdims=False
        )

    def from_sequence(mine):
        come = swap(at_index(mine, 1 - side), "xx")
        return merged(at_index(mine, side), come), come

    def merged(kept, come, tick=None):
        if tick is not None:
            kept = kept + tick[0, 0].astype(kept.dtype)
        first, second = pick(side, kept, come)
        return jnp.stack([first, second])

    qkv_cols = qkv_weight.reshape(own, 3, 2, pairs, PAIR).transpose(2, 0, 3, 1, 4).reshape(2, own, cols)
    up_cols = (
        up_weight.reshape(own, chips, 2, splits, pair_row)
        .transpose(2, 0, 3, 1, 4)
        .reshape(2, own, hidden)
    )
    vectors = jnp.stack(
        [ln1_gain, ln1_bias, q_bias, v_bias, out_bias, ln2_gain, ln2_bias, down_bias], axis=1
    )
    vectors = jnp.pad(vectors, ((0, 0), (0, PAIR - vectors.shape[1])))

    def with_partner(two):
        mine, theirs = at_index(two, core), at_index(two, 1 - core)
        first, second = pick(core, mine, swap(theirs, "core"))
        return jnp.concatenate([first, second], axis=0)

    early = with_partner(
        jnp.concatenate([qkv_cols, jnp.broadcast_to(vectors, (2, own, PAIR))], axis=2)
    )
    early = jnp.concatenate(
        [
            early[:, : cols + 8],
            up_bias.reshape(splits, pair_row).T,
            early[:, cols + 8 + splits :],
        ],
        axis=1,
    )
    links = Links()

    def gather_rest(array, tick=None):
        state = (array, [])
        for d in links.rest:
            state = links.gather(state, d, tick if d == links.rest[-1] else None)
        return state

    def halves_of(state):
        middle = state[0].shape[-1] // 2
        return [(state[0][..., :middle], state[1]), (state[0][..., middle:], state[1])]

    def joined(halves):
        return [half_state[0].reshape(width, -1) for half_state in halves]

    inputs_low, come, other = to_sequence(tokens)
    grad_out_low, _, _ = to_sequence(cotangent, gate([come]))
    begun = [
        links.begin_gather(piece, d) for piece, d in zip(halves_of(gather_rest(early)), "yx")
    ]
    early_halves = [links.end_gather(piece) for piece in begun]
    early_a, early_b = joined(
        [links.gather(piece, d) for piece, d in zip(early_halves, "xy")]
    )
    split = early_a.shape[1]
    late = with_partner(
        jnp.concatenate([up_cols, jnp.broadcast_to(out_weight, (2, own, width))], axis=2)
    )
    down_own = down_weight.reshape(splits, pair_row, width)
    late = lax.all_gather(
        pack([late, *(down_own[i] for i in range(splits))], [begun[0][1][0], begun[1][1][0], other]),
        ("dp", "xx"),
        axis=0,
        tiled=True,
    )
    small = early_b[:, cols - split :].astype(F32).T
    gain_one, shift_one, query_shift, value_shift, out_shift, gain_two, shift_two, down_shift = (
        small[i] for i in range(8)
    )
    up_shift = small[8 : 8 + splits].reshape(hidden)

    inputs = inputs_low.astype(F32)
    seg = at_index(segments, side)
    numbers = jnp.arange(PAIR, dtype=jnp.int32) % HEAD_DIM
    same = seg[:, None] == numbers[None, :]
    coded = numbers[None, :] < 4
    query_code = jnp.where(same & coded, 1.0, 0.0).astype(BF16)
    key_code = jnp.where(same | ~coded, 0.0, NEG).astype(BF16)

    def head_cols(vector):
        return lax.dynamic_slice_in_dim(vector, core * half, half, 0).reshape(pairs, 1, PAIR)

    zeros = jnp.zeros((pairs, 1, PAIR), F32)
    qkv_shift = jnp.concatenate(
        [head_cols(query_shift), zeros, head_cols(value_shift)], axis=1
    ).reshape(1, cols)
    qkv_scale = jnp.tile(jnp.repeat(jnp.array([0.125, 1.0, 1.0], F32), PAIR), pairs)[None]
    normed_t, qkv, tick = qkv_projection(
        inputs_low,
        early_a,
        early_b,
        jnp.pad(jnp.stack([gain_one, shift_one]), ((0, 6), (0, 0))),
        jnp.pad(jnp.concatenate([qkv_shift, qkv_scale]), ((0, 6), (0, 0))),
        [],
    )
    attended, log_total, _ = attention_forward(qkv, query_code, key_code)
    proj_up = late[:, :hidden]
    proj_out = lax.dynamic_slice_in_dim(late[:, hidden : hidden + width], core * half, half, 0)
    proj_down = jnp.concatenate(
        [late[:, hidden + (1 + i) * width : hidden + (2 + i) * width] for i in range(splits)], axis=0
    )

    branch = mm(attended, proj_out).astype(BF16)
    branch_come = swap(branch, "core")
    mid_vectors = jnp.pad(jnp.stack([out_shift, gain_two, shift_two]), ((0, 5), (0, 0)))
    normed_two_low, hidden_low, grad_pre_low, ffn, partial_two, up_sums = feed_forward(
        inputs_low,
        branch,
        branch_come,
        grad_out_low,
        proj_up,
        proj_down,
        mid_vectors,
        jnp.pad(up_shift[None], ((0, 7), (0, 0))),
    )
    partial_come = swap(partial_two, "core")
    ffn_own = own_rows(ffn).astype(F32) + swap(other_rows(ffn), "core").astype(F32)
    middle_own = own_rows(inputs_low).astype(F32) + (
        own_rows(branch).astype(F32) + own_rows(branch_come).astype(F32)
    )

    mixed, _ = from_sequence((middle_own + out_shift + ffn_own + down_shift).astype(BF16))

    grad_proj_down = [
        mm(hidden_low[:, i * width : (i + 1) * width], grad_out_low, TN).astype(BF16)
        for i in range(splits)
    ]
    grad_proj_up = mm(normed_two_low, grad_pre_low, TN).astype(BF16)
    late_grads = jnp.concatenate([grad_proj_up, *grad_proj_down], axis=1)
    late_own = lax.psum_scatter(late_grads, ("dp", "xx"), scatter_dimension=0, tiled=True)
    grad_middle, branch_low, grad_attended, mid_sums, tick = norm_two(
        inputs_low,
        branch,
        branch_come,
        grad_out_low,
        partial_two,
        partial_come,
        proj_out,
        mid_vectors,
        [late_grads],
    )
    grad_proj_out = mm(attended, branch_low, TN)

    def as_column(vectors):
        table = jnp.stack(vectors, axis=1)
        return jnp.pad(table, ((0, 0), (0, PAIR - table.shape[1])))

    def only_mine(flag, array):
        return jnp.where(flag, array, jnp.zeros_like(array))

    small_two = [mid_sums[i] for i in range(4)] + [
        up_sums[0, i * width : (i + 1) * width] for i in range(splits)
    ]
    out_low = grad_proj_out.astype(BF16)
    grad_out_rows = jnp.concatenate(
        [only_mine(core == 0, out_low), only_mine(core == 1, out_low)], axis=0
    )

    def blocks(array):
        return array.reshape(chips, pair_row, array.shape[1])

    def pairs_backward(first, count, after):
        return attention_backward(
            first, count, qkv, query_code, key_code, attended, grad_attended, log_total, normed_t, after
        )

    grad_a, weight_grad_a, tick = pairs_backward(0, pairs - 1, [])
    first_piece = links.scatter(
        [blocks(grad_out_rows), blocks(weight_grad_a)], [], links.dims, "y", [tick]
    )
    grad_b, weight_grad_b, tick = pairs_backward(pairs - 1, 1, [first_piece[0][0], tick, mixed])
    grads = [grad_a, grad_b]
    first_piece = links.scatter(*first_piece, "x", [tick])
    norm_vectors = jnp.pad(jnp.stack([gain_one, shift_one]), ((0, 6), (0, 0)))
    partial_one, norm_sums, bias_sums, _ = norm_one(
        False, core, grads, early_a, early_b, cols, inputs_low, [], [first_piece[0][0]]
    )
    come = swap(partial_one, "core")
    token_own, norm_sums_own, bias_sums_own, tick = norm_one(
        True,
        core,
        grads,
        early_a,
        early_b,
        cols,
        inputs_low,
        [come, grad_middle, norm_vectors],
        [],
    )
    norm_sums = norm_sums + norm_sums_own
    bias_sums = bias_sums + bias_sums_own
    token_grad, come = from_sequence(token_own.reshape(2, quarter, width))
    grad_by_pair = bias_sums[0].reshape(pairs, 3, PAIR)

    def padded(vector):
        vector = vector.reshape(half)
        return jnp.concatenate([only_mine(core == 0, vector), only_mine(core == 1, vector)])

    small = as_column(
        [
            norm_sums[0],
            norm_sums[1],
            padded(grad_by_pair[:, 0]),
            padded(grad_by_pair[:, 2]),
        ]
        + small_two
    )
    last_piece = links.scatter(
        [blocks(weight_grad_b), blocks(small.astype(BF16))], [], links.dims, "y", [tick]
    )
    first_own = links.scatter_rest(first_piece)
    last_piece = links.scatter(*last_piece, "x", [come])
    last_own = links.scatter_rest(last_piece)

    def rows_of(array, index):
        return lax.dynamic_slice_in_dim(array, index * own, own, 0)

    def by_core(mine, come):
        return jnp.stack(pick(core, mine, come))

    def shared(array):
        return rows_of(array, core), swap(rows_of(array, 1 - core), "core")

    up_own, down_grad = widen(late_own, width, [last_own])
    late_mine, late_come = shared(up_own)
    early_mine, early_come = shared(jnp.concatenate([first_own, last_own], axis=1).astype(BF16))
    out_grad = early_mine[:, :width].astype(F32) + early_come[:, :width].astype(F32)
    up_grad = (
        by_core(late_mine, late_come)
        .reshape(2, own, splits, chips, pair_row)
        .transpose(1, 3, 0, 2, 4)
        .reshape(own, 2 * hidden)
        .astype(F32)
    )
    down_grad = down_grad.reshape(hidden_own, width)
    qkv_grad = (
        by_core(early_mine[:, width : width + cols], early_come[:, width : width + cols])
        .reshape(2, own, pairs, 3, PAIR)
        .transpose(1, 3, 0, 2, 4)
        .reshape(own, 2 * cols)
        .astype(F32)
    )
    tail, first = width + cols + 8, first_own.shape[1]
    small_mine = early_mine[:, tail - 8 : tail].astype(F32)
    one = small_mine[:, :4] + early_come[:, tail - 8 : tail - 4].astype(F32)
    up_shift_grad = (
        last_own[:, tail - first : tail - first + splits].T.reshape(hidden_own).astype(F32)
    )
    two = small_mine[:, 4:]
    return (
        mixed,
        token_grad,
        one[:, 0],
        one[:, 1],
        qkv_grad,
        one[:, 2],
        one[:, 3],
        out_grad,
        two[:, 0],
        two[:, 1],
        two[:, 2],
        up_grad,
        up_shift_grad,
        down_grad,
        two[:, 3],
    )


def solution(mesh):
    parts = (mesh.shape["dp"], mesh.shape["ctx"] // 2, 2)
    split_mesh = Mesh(mesh.devices.reshape(parts), ("dp", "xx", "core"))
    rows = ("dp", "xx", "core")
    acts = P("dp", ("xx", "core"), None)
    vec, mat = P(rows), P(rows, None)
    return jax.shard_map(
        body,
        mesh=split_mesh,
        in_specs=(
            acts, P("dp", None), vec, vec, mat, vec, vec, mat, vec, vec, vec, mat, vec, mat, vec, acts,
        ),
        out_specs=(
            acts, acts, vec, vec, mat, vec, vec, mat, vec, vec, vec, mat, vec, mat, vec,
        ),
        check_vma=False,
    )
```

```python
import functools

import jax
import jax.numpy as jnp
from jax import lax
from jax.experimental import pallas as pl
from jax.experimental.pallas import tpu as pltpu
from jax.sharding import Mesh, PartitionSpec as P

HEAD_DIM = 64
PAIR = 2 * HEAD_DIM
EPSILON = 1e-05
NEG = -1e30
BLK = 512
F32 = jnp.float32
BF16 = jnp.bfloat16

NN = (((1,), (0,)), ((), ()))
NT = (((1,), (1,)), ((), ()))
TN = (((0,), (0,)), ((), ()))


def mm(left, right, dims=NN):
    return lax.dot_general(left, right, dims, preferred_element_type=F32)


def build_scores_operands(qkv_ref, qs_ref, ks_ref, rows, qx, kx):
    lane = lax.broadcasted_iota(jnp.int32, (BLK, PAIR), 1)
    first = lane < HEAD_DIM
    q = qkv_ref[rows, 0:PAIR].astype(F32)
    k = qkv_ref[rows, PAIR : 2 * PAIR].astype(F32)
    qs = qs_ref[rows, :].astype(F32)
    ks = ks_ref[rows, :].astype(F32)
    qx[0, rows, :] = jnp.where(first, q, qs).astype(BF16)
    qx[1, rows, :] = jnp.where(first, qs, q).astype(BF16)
    kx[0, rows, :] = jnp.where(first, k, ks).astype(BF16)
    kx[1, rows, :] = jnp.where(first, ks, k).astype(BF16)
    return first, q, k


def causal_block(scores):
    key_at = lax.broadcasted_iota(jnp.int32, scores.shape, 0)
    query_at = lax.broadcasted_iota(jnp.int32, scores.shape, 1)
    return jnp.where(key_at <= query_at, scores, NEG)


def attention_forward_kernel(qkv_ref, qs_ref, ks_ref, *rest):
    o_ref, lse_ref, tick_ref, qx, kx, vt, acc = rest[-7:]
    tick_ref[...] = jnp.zeros_like(tick_ref)
    length = qkv_ref.shape[0]
    blocks = length // BLK

    @pl.loop(0, blocks)
    def _(i):
        rows = pl.ds(pl.multiple_of(i * BLK, BLK), BLK)
        build_scores_operands(qkv_ref, qs_ref, ks_ref, rows, qx, kx)
        v_t = qkv_ref[rows, 2 * PAIR : 3 * PAIR].astype(F32).T
        ones = jnp.ones((16, BLK), BF16)
        for h in range(2):
            vt[h, 0:HEAD_DIM, rows] = v_t[h * HEAD_DIM : (h + 1) * HEAD_DIM].astype(BF16)
            vt[h, HEAD_DIM : HEAD_DIM + 16, rows] = ones

    @pl.loop(0, blocks)
    def _(i):
        rows = pl.ds(pl.multiple_of(i * BLK, BLK), BLK)
        queries = [qx[h, rows, :] for h in range(2)]
        tops = []
        for h in range(2):
            s = causal_block(mm(kx[h, rows, :], queries[h], NT))
            top = jnp.max(s, axis=0, keepdims=True)
            p = jnp.exp(s - top).astype(BF16)
            acc[h] = mm(vt[h, :, rows], p)
            tops.append(top)

        def step(j, carry):
            keys = pl.ds(pl.multiple_of(j * BLK, BLK), BLK)
            out = []
            for h in range(2):
                s = mm(kx[h, keys, :], qx[h, rows, :], NT)
                top = jnp.maximum(carry[h], jnp.max(s, axis=0, keepdims=True))
                p = jnp.exp(s - top).astype(BF16)
                acc[h] = acc[h] * jnp.exp(carry[h] - top) + mm(vt[h, :, keys], p)
                out.append(top)
            return tuple(out)

        tops = lax.fori_loop(0, i, step, tuple(tops))
        parts = []
        for h in range(2):
            total = acc[h, HEAD_DIM : HEAD_DIM + 1, :]
            parts.append(acc[h, 0:HEAD_DIM, :] / total)
            lse_ref[0, h : h + 1, rows] = tops[h] + jnp.log(total)
        o_ref[rows, :] = jnp.concatenate(parts, axis=0).T.astype(BF16)


def attention_backward_kernel(qkv_ref, qs_ref, ks_ref, o_ref, do_ref, lse_ref, at_ref, *rest):
    d_ref, dw_ref, tick_ref, qx, kx, qm, dm, kt, delta, dqt, dk, dv = rest[-12:]
    tick_ref[...] = jnp.zeros_like(tick_ref)
    length = qkv_ref.shape[0]
    blocks = length // BLK

    @pl.loop(0, blocks)
    def _(i):
        rows = pl.ds(pl.multiple_of(i * BLK, BLK), BLK)
        first, q, k = build_scores_operands(qkv_ref, qs_ref, ks_ref, rows, qx, kx)
        do = do_ref[rows, :].astype(F32)
        zero = jnp.zeros_like(q)
        qm[0, rows, :] = jnp.where(first, q, zero).astype(BF16)
        qm[1, rows, :] = jnp.where(first, zero, q).astype(BF16)
        dm[0, rows, :] = jnp.where(first, do, zero).astype(BF16)
        dm[1, rows, :] = jnp.where(first, zero, do).astype(BF16)
        kt[:, rows] = k.T.astype(BF16)
        inner = (do * o_ref[rows, :].astype(F32)).T
        for h in range(2):
            delta[h : h + 1, rows] = jnp.sum(
                inner[h * HEAD_DIM : (h + 1) * HEAD_DIM], axis=0, keepdims=True
            )
        dqt[:, rows] = jnp.zeros((PAIR, BLK), F32)

    def tile(keys, rows, masked):
        values = qkv_ref[keys, 2 * PAIR : 3 * PAIR]
        dv_part, dk_part = None, None
        for h in range(2):
            s = mm(kx[h, keys, :], qx[h, rows, :], NT)
            if masked:
                s = causal_block(s)
            p = jnp.exp(s - lse_ref[0, h : h + 1, rows])
            dp = mm(values, dm[h, rows, :], NT)
            ds = (p * (dp - delta[h : h + 1, rows])).astype(BF16)
            dv_h = mm(p.astype(BF16), dm[h, rows, :])
            dk_h = mm(ds, qm[h, rows, :])
            dv_part = dv_h if h == 0 else dv_part + dv_h
            dk_part = dk_h if h == 0 else dk_part + dk_h
            part = slice(h * HEAD_DIM, (h + 1) * HEAD_DIM)
            dqt[part, rows] += mm(kt[part, keys], ds)
        return dk_part, dv_part

    @pl.loop(0, blocks)
    def _(j):
        keys = pl.ds(pl.multiple_of(j * BLK, BLK), BLK)
        dk[...], dv[...] = tile(keys, keys, True)

        @pl.loop(j + 1, blocks)
        def _(i):
            dk_part, dv_part = tile(keys, pl.ds(pl.multiple_of(i * BLK, BLK), BLK), False)
            dk[...] += dk_part
            dv[...] += dv_part

        d_ref[keys, PAIR : 2 * PAIR] = dk[...].astype(BF16)
        d_ref[keys, 2 * PAIR : 3 * PAIR] = dv[...].astype(BF16)

    @pl.loop(0, blocks)
    def _(i):
        rows = pl.ds(pl.multiple_of(i * BLK, BLK), BLK)
        d_ref[rows, 0:PAIR] = (dqt[:, rows].T.astype(BF16).astype(F32) * 0.125).astype(BF16)

    @pl.loop(0, dw_ref.shape[0] // ROWS)
    def _(i):
        rows = pl.ds(pl.multiple_of(i * ROWS, ROWS), ROWS)
        dw_ref[rows, :] = mm(at_ref[rows, :], d_ref[...]).astype(BF16)


VMEM_LIMIT = 48 * 1024 * 1024


SMALL_COST = pl.CostEstimate(flops=1000, bytes_accessed=1000, transcendentals=0)


TICK = jax.ShapeDtypeStruct((8, 128), F32)
TICK_SPEC = pl.BlockSpec((8, 128), lambda i: (0, 0))
ANY_SPEC = pl.BlockSpec(memory_space=pl.ANY)


def pack_kernel(count, refs):
    refs[-1][...] = jnp.concatenate([ref[...] for ref in refs[:count]], axis=-1)


def pack(parts, after):
    rows = parts[0].shape[0]
    width = sum(part.shape[1] for part in parts)
    return pl.pallas_call(
        lambda *refs: pack_kernel(len(parts), refs),
        grid=(1,),
        in_specs=[pl.BlockSpec(part.shape, lambda i: (0, 0)) for part in parts]
        + [ANY_SPEC] * len(after),
        out_specs=pl.BlockSpec((rows, width), lambda i: (0, 0)),
        out_shape=jax.ShapeDtypeStruct((rows, width), BF16),
        compiler_params=pltpu.CompilerParams(vmem_limit_bytes=VMEM_LIMIT),
        cost_estimate=SMALL_COST,
    )(*parts, *after)


def widen(source, width, after):
    rows, cols = source.shape
    count = cols // width - 2

    def kernel(source_ref, *refs):
        up_ref, down_ref = refs[-2:]
        up_ref[...] = source_ref[:, : 2 * width].astype(F32)
        for i in range(count):
            down_ref[i] = source_ref[:, (2 + i) * width : (3 + i) * width].astype(F32)

    return pl.pallas_call(
        kernel,
        grid=(1,),
        in_specs=[pl.BlockSpec((rows, cols), lambda i: (0, 0))] + [ANY_SPEC] * len(after),
        out_specs=[
            pl.BlockSpec((rows, 2 * width), lambda i: (0, 0)),
            pl.BlockSpec((count, rows, width), lambda i: (0, 0, 0)),
        ],
        out_shape=[
            jax.ShapeDtypeStruct((rows, 2 * width), F32),
            jax.ShapeDtypeStruct((count, rows, width), F32),
        ],
        compiler_params=pltpu.CompilerParams(vmem_limit_bytes=VMEM_LIMIT),
        cost_estimate=SMALL_COST,
    )(source, *after)


def merge(kept, come, side, after):
    def kernel(side_ref, kept_ref, come_ref, *rest):
        mine = pl.program_id(0) == side_ref[0]

        @pl.when(mine)
        def _():
            rest[-1][0] = kept_ref[...]

        @pl.when(jnp.logical_not(mine))
        def _():
            rest[-1][0] = come_ref[...]

    whole = pl.BlockSpec(kept.shape, lambda i, side_ref: (0, 0))
    return pl.pallas_call(
        kernel,
        grid_spec=pltpu.PrefetchScalarGridSpec(
            num_scalar_prefetch=1,
            grid=(2,),
            in_specs=[whole, whole] + [ANY_SPEC] * len(after),
            out_specs=pl.BlockSpec((1, *kept.shape), lambda i, side_ref: (i, 0, 0)),
        ),
        out_shape=jax.ShapeDtypeStruct((2, *kept.shape), kept.dtype),
        compiler_params=pltpu.CompilerParams(vmem_limit_bytes=VMEM_LIMIT),
        cost_estimate=SMALL_COST,
    )(side.reshape(1).astype(jnp.int32), kept, come, *after)


def gate_kernel(*refs):
    refs[-1][...] = jnp.zeros_like(refs[-1])


def gate(after):
    return pl.pallas_call(
        gate_kernel,
        grid=(1,),
        in_specs=[ANY_SPEC] * len(after),
        out_specs=TICK_SPEC,
        out_shape=TICK,
        cost_estimate=SMALL_COST,
    )(*after)


def fold_kernel(parts, comes, outs, refs):
    for m in range(outs):
        value = None
        for term in range(1 + comes):
            at = 1 + (term * outs + m) * parts
            side = jnp.concatenate([ref[0] for ref in refs[at : at + parts]], axis=-1)
            if comes:
                side = side.astype(F32)
            value = side if term == 0 else value + side
        refs[len(refs) - outs + m][0] = value.astype(BF16)


def fold(parts, comes, sizes, axis, at, after):
    blocks, rows = parts[0].shape[:2]
    width = sum(part.shape[2] for part in parts)
    outs = sizes[axis] if axis is not None else 1
    inner = 1
    if axis is not None:
        for size in sizes[axis + 1 :]:
            inner *= size

    def spec(array, m):
        def index(j, at_ref):
            if axis is None:
                return j, 0, 0
            return (j // inner) * (outs * inner) + (at_ref[0] ^ m) * inner + j % inner, 0, 0

        return pl.BlockSpec((1, rows, array.shape[2]), index)

    def kernel(*refs):
        ins = 1 + (1 + len(comes)) * len(parts) * outs
        fold_kernel(len(parts), len(comes), outs, refs[:ins] + refs[ins + len(after) :])

    out = pl.BlockSpec((1, rows, width), lambda j, at_ref: (j, 0, 0))
    return pl.pallas_call(
        kernel,
        grid_spec=pltpu.PrefetchScalarGridSpec(
            num_scalar_prefetch=1,
            grid=(blocks // outs,),
            in_specs=[spec(part, m) for m in range(outs) for part in parts]
            + [spec(part, m) for come in comes for m in range(outs) for part in come]
            + [ANY_SPEC] * len(after),
            out_specs=[out] * outs,
        ),
        out_shape=[jax.ShapeDtypeStruct((blocks // outs, rows, width), BF16)] * outs,
        compiler_params=pltpu.CompilerParams(vmem_limit_bytes=VMEM_LIMIT),
        cost_estimate=SMALL_COST,
    )(at.reshape(1).astype(jnp.int32), *(list(parts) * outs), *[part for come in comes for part in list(come) * outs], *after)


def qkv_kernel(x_ref, wa_ref, wb_ref, vec_ref, col_ref, *rest_refs):
    a_ref, qkv_ref, tick_ref = rest_refs[-3:]
    split = wa_ref.shape[1]
    rest = qkv_ref.shape[1] - split
    for part in range(2):
        rows = slice(part * ROWS, (part + 1) * ROWS)
        normal, _ = norm_forward(x_ref[rows, :].astype(F32))
        normed = (normal * vec_ref[0:1, :] + vec_ref[1:2, :]).astype(BF16)
        a_ref[:, rows] = normed.astype(F32).T.astype(BF16)
        for w, cols in ((wa_ref[...], slice(0, split)), (wb_ref[:, :rest], slice(split, None))):
            shift, scale = col_ref[0:1, cols], col_ref[1:2, cols]
            qkv_ref[rows, cols] = ((mm(normed, w) + shift) * scale).astype(BF16)
    tick_ref[...] = jnp.zeros_like(tick_ref)


def qkv_projection(inputs, weight_a, weight_b, vectors, columns, after):
    length, width = inputs.shape
    cols = columns.shape[1]
    return pl.pallas_call(
        qkv_kernel,
        grid=(length // (2 * ROWS),),
        in_specs=[
            pl.BlockSpec((2 * ROWS, width), lambda i: (i, 0)),
            pl.BlockSpec(weight_a.shape, lambda i: (0, 0)),
            pl.BlockSpec(weight_b.shape, lambda i: (0, 0)),
            pl.BlockSpec(vectors.shape, lambda i: (0, 0)),
            pl.BlockSpec(columns.shape, lambda i: (0, 0)),
        ]
        + [ANY_SPEC] * len(after),
        out_specs=[
            pl.BlockSpec((width, 2 * ROWS), lambda i: (0, i)),
            pl.BlockSpec((2 * ROWS, cols), lambda i: (i, 0)),
            TICK_SPEC,
        ],
        out_shape=[
            jax.ShapeDtypeStruct((width, length), BF16),
            jax.ShapeDtypeStruct((length, cols), BF16),
            TICK,
        ],
        compiler_params=pltpu.CompilerParams(vmem_limit_bytes=VMEM_LIMIT),
        cost_estimate=SMALL_COST,
    )(inputs, weight_a, weight_b, vectors, columns, *after)


def out_projection(core, attended, late, block, after):
    length, cols = attended.shape
    width = late.shape[0]
    rows = length // 4

    def kernel(core_ref, a_ref, w_ref, *rest):
        rest[-1][...] = mm(a_ref[...], w_ref[...]).astype(BF16)

    return pl.pallas_call(
        kernel,
        grid_spec=pltpu.PrefetchScalarGridSpec(
            num_scalar_prefetch=1,
            grid=(4,),
            in_specs=[
                pl.BlockSpec((rows, cols), lambda i, core_ref: (i, 0)),
                pl.BlockSpec((cols, width), lambda i, core_ref: (core_ref[0], block)),
            ]
            + [ANY_SPEC] * len(after),
            out_specs=pl.BlockSpec((rows, width), lambda i, core_ref: (i, 0)),
        ),
        out_shape=jax.ShapeDtypeStruct((length, width), BF16),
        compiler_params=pltpu.CompilerParams(vmem_limit_bytes=VMEM_LIMIT),
        cost_estimate=SMALL_COST,
    )(core, attended, late, *after)


def middle_of(x_ref, b0_ref, b1_ref, vec_ref):
    both = b0_ref[...].astype(F32) + b1_ref[...].astype(F32)
    return x_ref[...].astype(F32) + both + vec_ref[0:1, :]


def feed_forward_kernel(splits, core_ref, x_ref, b0_ref, b1_ref, dy_ref, up_ref, *rest):
    down_refs, (vec_ref, shift_ref) = rest[:splits], rest[splits : splits + 2]
    a_ref, g_ref, du_ref, own_ref, other_ref, dh_ref, sums_ref = rest[splits + 2 :]
    at = pl.program_id(0)

    @pl.when(at == 0)
    def _():
        sums_ref[...] = jnp.zeros_like(sums_ref)

    middle = middle_of(x_ref, b0_ref, b1_ref, vec_ref)
    normal, _ = norm_forward(middle)
    normed = (normal * vec_ref[1:2, :] + vec_ref[2:3, :]).astype(BF16)
    a_ref[...] = normed
    dy = dy_ref[...]
    ffn, dh = None, None
    width = dy.shape[1]
    for i, down_ref in enumerate(down_refs):
        cols = slice(i * width, (i + 1) * width)
        up, down = up_ref[:, cols], down_ref[...]
        value, slope = gelu_parts(mm(normed, up) + shift_ref[0:1, cols])
        du = slope * mm(dy, down, NT)
        value, du = value.astype(BF16), du.astype(BF16)
        g_ref[:, cols] = value
        du_ref[:, cols] = du
        sums_ref[0:1, cols] += jnp.sum(du.astype(F32), axis=0, keepdims=True)
        ffn_part, dh_part = mm(value, down), mm(du, up, NT)
        ffn = ffn_part if i == 0 else ffn + ffn_part
        dh = dh_part if i == 0 else dh + dh_part
    dh_ref[...] = dh.astype(BF16)
    mine = at % 2 == core_ref[0]

    @pl.when(mine)
    def _():
        own_ref[...] = middle_of(x_ref, b0_ref, b1_ref, vec_ref) + ffn + vec_ref[3:4, :]

    @pl.when(jnp.logical_not(mine))
    def _():
        other_ref[...] = ffn.astype(BF16)


def feed_forward(core, inputs, branch, branch_come, grad_out, late, splits, vectors, up_shift):
    length, width = inputs.shape
    rows = length // 4
    hidden = splits * width
    narrow = pl.BlockSpec((rows, width), lambda i, core_ref: (i, 0))
    wide = pl.BlockSpec((rows, hidden), lambda i, core_ref: (i, 0))
    shared = pl.BlockSpec((rows, width), lambda i, core_ref: (i // 2, 0))

    def whole(array):
        return pl.BlockSpec(array.shape, lambda i, core_ref: (0, 0))

    def down(i):
        return pl.BlockSpec((width, width), lambda _, core_ref: (0, splits + 1 + i))

    return pl.pallas_call(
        functools.partial(feed_forward_kernel, splits),
        grid_spec=pltpu.PrefetchScalarGridSpec(
            num_scalar_prefetch=1,
            grid=(4,),
            in_specs=[narrow] * 4
            + [pl.BlockSpec((width, hidden), lambda i, core_ref: (0, 0))]
            + [down(i) for i in range(splits)]
            + [whole(vectors), whole(up_shift)],
            out_specs=[
                narrow, wide, wide, shared, shared, narrow,
                pl.BlockSpec((8, hidden), lambda i, core_ref: (0, 0)),
            ],
        ),
        out_shape=[
            jax.ShapeDtypeStruct((length, width), BF16),
            jax.ShapeDtypeStruct((length, hidden), BF16),
            jax.ShapeDtypeStruct((length, hidden), BF16),
            jax.ShapeDtypeStruct((length // 2, width), F32),
            jax.ShapeDtypeStruct((length // 2, width), BF16),
            jax.ShapeDtypeStruct((length, width), BF16),
            jax.ShapeDtypeStruct((8, hidden), F32),
        ],
        compiler_params=pltpu.CompilerParams(vmem_limit_bytes=VMEM_LIMIT),
        cost_estimate=SMALL_COST,
    )(core, inputs, branch, branch_come, grad_out, late, *([late] * splits), vectors, up_shift)


def norm_two_kernel(core_ref, x_ref, b0_ref, b1_ref, dy_ref, p0_ref, p1_ref, w_ref, vec_ref, *rest):
    mid_ref, low_ref, do_ref, sums_ref = rest[-4:]

    @pl.when(pl.program_id(0) == 0)
    def _():
        sums_ref[...] = jnp.zeros_like(sums_ref)

    normal, scale = norm_forward(middle_of(x_ref, b0_ref, b1_ref, vec_ref))
    grad = p0_ref[...].astype(F32) + p1_ref[...].astype(F32)
    dy = dy_ref[...].astype(F32)
    mid = dy + norm_backward(normal, scale, grad * vec_ref[1:2, :])
    low = mid.astype(BF16)
    low_ref[...] = low
    do_ref[...] = mm(low, w_ref[...], NT).astype(BF16)
    for i, value in enumerate((low.astype(F32), grad * normal, grad, dy)):
        sums_ref[i : i + 1, :] += jnp.sum(value, axis=0, keepdims=True)

    @pl.when(pl.program_id(0) % 2 == core_ref[0])
    def _():
        mid_ref[...] = mid


def norm_two(core, inputs, branch, branch_come, grad_out, partial, partial_come, late, block, vectors, after):
    length, width = inputs.shape
    rows = length // 4
    cols = width // 2
    narrow = pl.BlockSpec((rows, width), lambda i, core_ref: (i, 0))
    return pl.pallas_call(
        norm_two_kernel,
        grid_spec=pltpu.PrefetchScalarGridSpec(
            num_scalar_prefetch=1,
            grid=(4,),
            in_specs=[narrow] * 6
            + [
                pl.BlockSpec((cols, width), lambda i, core_ref: (core_ref[0], block)),
                pl.BlockSpec(vectors.shape, lambda i, core_ref: (0, 0)),
            ]
            + [ANY_SPEC] * len(after),
            out_specs=[
                pl.BlockSpec((rows, width), lambda i, core_ref: (i // 2, 0)),
                narrow,
                pl.BlockSpec((rows, cols), lambda i, core_ref: (i, 0)),
                pl.BlockSpec((8, width), lambda i, core_ref: (0, 0)),
            ],
        ),
        out_shape=[
            jax.ShapeDtypeStruct((length // 2, width), F32),
            jax.ShapeDtypeStruct((length, width), BF16),
            jax.ShapeDtypeStruct((length, cols), BF16),
            jax.ShapeDtypeStruct((8, width), F32),
        ],
        compiler_params=pltpu.CompilerParams(vmem_limit_bytes=VMEM_LIMIT),
        cost_estimate=SMALL_COST,
    )(core, inputs, branch, branch_come, grad_out, partial, partial_come, late, vectors, *after)


ROWS = 256


def attention_forward(qkv, query_code, key_code):
    length, width = qkv.shape
    pairs = width // (3 * PAIR)
    return pl.pallas_call(
        attention_forward_kernel,
        grid=(pairs,),
        in_specs=[
            pl.BlockSpec((length, 3 * PAIR), lambda p: (0, p)),
            pl.BlockSpec((length, PAIR), lambda p: (0, 0)),
            pl.BlockSpec((length, PAIR), lambda p: (0, 0)),
        ],
        out_specs=[
            pl.BlockSpec((length, PAIR), lambda p: (0, p)),
            pl.BlockSpec((1, 8, length), lambda p: (p, 0, 0)),
            TICK_SPEC,
        ],
        out_shape=[
            jax.ShapeDtypeStruct((length, pairs * PAIR), BF16),
            jax.ShapeDtypeStruct((pairs, 8, length), F32),
            TICK,
        ],
        scratch_shapes=[
            pltpu.VMEM((2, length, PAIR), BF16),
            pltpu.VMEM((2, length, PAIR), BF16),
            pltpu.VMEM((2, HEAD_DIM + 16, length), BF16),
            pltpu.VMEM((2, HEAD_DIM + 16, BLK), F32),
        ],
        compiler_params=pltpu.CompilerParams(vmem_limit_bytes=VMEM_LIMIT),
        cost_estimate=SMALL_COST,
    )(qkv, query_code, key_code)


def norm_one_kernel(own, core_ref, d0_ref, d1_ref, wa_ref, wb_ref, x_ref, *rest):
    if own:
        come_ref, mid_ref, vec_ref, out_ref, sums_ref, bias_ref, tick_ref, w = rest
    else:
        out_ref, sums_ref, bias_ref, tick_ref, w = rest
    split = wa_ref.shape[1]

    @pl.when(pl.program_id(0) == 0)
    def _():
        sums_ref[...] = jnp.zeros_like(sums_ref)
        bias_ref[...] = jnp.zeros_like(bias_ref)
        w[:, :split] = wa_ref[...]
        w[:, split:] = wb_ref[:, : w.shape[1] - split]
        tick_ref[...] = jnp.zeros_like(tick_ref)

    total = None
    for i, ref in enumerate((d0_ref, d1_ref)):
        cols = slice(0, ref.shape[1]) if i == 0 else slice(d0_ref.shape[1], None)
        grad = ref[...]
        part = mm(grad, w[:, cols], NT)
        total = part if i == 0 else total + part
        bias_ref[0:1, cols] += jnp.sum(grad.astype(F32), axis=0, keepdims=True)
    normal, scale = norm_forward(x_ref[...].astype(F32))
    sums_ref[0:1, :] += jnp.sum(total * normal, axis=0, keepdims=True)
    sums_ref[1:2, :] += jnp.sum(total, axis=0, keepdims=True)
    if own:
        grad = (total + come_ref[...].astype(F32)) * vec_ref[0:1, :]
        out_ref[...] = (mid_ref[...] + norm_backward(normal, scale, grad)).astype(BF16)
    else:
        out_ref[...] = total.astype(BF16)


def norm_one(own, core, grads, weight_a, weight_b, cols, inputs, extra, after):
    length, width = inputs.shape
    count = length // (2 * ROWS)
    per = count // 2

    def block(i, core_ref):
        which = core_ref[0] if own else 1 - core_ref[0]
        return ((i // per) * 2 + which) * per + i % per, 0

    def at_zero(i, core_ref):
        return 0, 0

    plain = pl.BlockSpec((ROWS, width), lambda i, core_ref: (i, 0))
    rows = pl.BlockSpec((ROWS, width), block)
    in_specs = [pl.BlockSpec((ROWS, grad.shape[1]), block) for grad in grads] + [
        pl.BlockSpec(weight_a.shape, at_zero),
        pl.BlockSpec(weight_b.shape, at_zero),
        rows,
    ]
    out_specs = [
        plain,
        pl.BlockSpec((8, width), at_zero),
        pl.BlockSpec((8, cols), at_zero),
        pl.BlockSpec((8, 128), at_zero),
    ]
    out_shape = [
        jax.ShapeDtypeStruct((count * ROWS, width), BF16),
        jax.ShapeDtypeStruct((8, width), F32),
        jax.ShapeDtypeStruct((8, cols), F32),
        TICK,
    ]
    if own:
        in_specs += [plain, plain, pl.BlockSpec(extra[2].shape, at_zero)]

    def kernel(*refs):
        inner = refs[: 1 + len(in_specs)] + refs[1 + len(in_specs) + len(after) :]
        norm_one_kernel(own, *inner)

    return pl.pallas_call(
        kernel,
        grid_spec=pltpu.PrefetchScalarGridSpec(
            num_scalar_prefetch=1,
            grid=(count,),
            in_specs=in_specs + [ANY_SPEC] * len(after),
            out_specs=out_specs,
            scratch_shapes=[pltpu.VMEM((width, cols), BF16)],
        ),
        out_shape=out_shape,
        compiler_params=pltpu.CompilerParams(vmem_limit_bytes=VMEM_LIMIT),
        cost_estimate=SMALL_COST,
    )(core, *grads, weight_a, weight_b, inputs, *extra, *after)


def attention_backward(
    first, count, qkv, query_code, key_code, attended, grad_attended, log_total, normed_t, after
):
    length = qkv.shape[0]
    width = normed_t.shape[0]
    return pl.pallas_call(
        attention_backward_kernel,
        grid=(count,),
        in_specs=[
            pl.BlockSpec((length, 3 * PAIR), lambda p: (0, first + p)),
            pl.BlockSpec((length, PAIR), lambda p: (0, 0)),
            pl.BlockSpec((length, PAIR), lambda p: (0, 0)),
            pl.BlockSpec((length, PAIR), lambda p: (0, first + p)),
            pl.BlockSpec((length, PAIR), lambda p: (0, first + p)),
            pl.BlockSpec((1, 8, length), lambda p: (first + p, 0, 0)),
            pl.BlockSpec(normed_t.shape, lambda p: (0, 0)),
        ]
        + [ANY_SPEC] * len(after),
        out_specs=[
            pl.BlockSpec((length, 3 * PAIR), lambda p: (0, p)),
            pl.BlockSpec((width, 3 * PAIR), lambda p: (0, p)),
            TICK_SPEC,
        ],
        out_shape=[
            jax.ShapeDtypeStruct((length, count * 3 * PAIR), BF16),
            jax.ShapeDtypeStruct((width, count * 3 * PAIR), BF16),
            TICK,
        ],
        scratch_shapes=[
            pltpu.VMEM((2, length, PAIR), BF16),
            pltpu.VMEM((2, length, PAIR), BF16),
            pltpu.VMEM((2, length, PAIR), BF16),
            pltpu.VMEM((2, length, PAIR), BF16),
            pltpu.VMEM((PAIR, length), BF16),
            pltpu.VMEM((8, length), F32),
            pltpu.VMEM((PAIR, length), F32),
            pltpu.VMEM((BLK, PAIR), F32),
            pltpu.VMEM((BLK, PAIR), F32),
        ],
        compiler_params=pltpu.CompilerParams(vmem_limit_bytes=VMEM_LIMIT),
        cost_estimate=SMALL_COST,
    )(qkv, query_code, key_code, attended, grad_attended, log_total, normed_t, *after)


def norm_forward(source):
    average = jnp.mean(source, axis=-1, keepdims=True)
    centred = source - average
    spread = jnp.mean(centred * centred, axis=-1, keepdims=True)
    scale = lax.rsqrt(spread + EPSILON)
    return centred * scale, scale


def norm_backward(normal, scale, grad):
    return scale * (
        grad
        - jnp.mean(grad, axis=-1, keepdims=True)
        - normal * jnp.mean(grad * normal, axis=-1, keepdims=True)
    )


GELU_A = 0.7978845608028654
GELU_B = 0.044715


def gelu_parts(source):
    square = source * source
    inner = jnp.tanh(GELU_A * (source + GELU_B * source * square))
    value = 0.5 * source * (1.0 + inner)
    slope = 0.5 * (1.0 + inner) + 0.5 * source * (1.0 - inner * inner) * (
        GELU_A * (1.0 + 3.0 * GELU_B * square)
    )
    return value, slope


def swap(value, axis):
    return lax.ppermute(value, axis, [(0, 1), (1, 0)])


def pick(flag, first, second):
    return jnp.where(flag == 0, first, second), jnp.where(flag == 0, second, first)


class Links:
    def __init__(self):
        self.size = lax.axis_size("dp")
        at = lax.axis_index("dp")
        self.groups = {}
        shift, name = 0, "y"
        while (1 << shift) < self.size:
            bits = 1 if shift == 0 else min(2, self.size.bit_length() - 1 - shift)
            self.groups[name] = (shift, bits, (at >> shift) & ((1 << bits) - 1))
            shift += bits
            name = "z" + str(shift)
        self.rest = [name for name in reversed(self.groups) if name != "y"]
        self.dims = self.rest + ["y", "x"]
        self.side = lax.axis_index("xx")

    def counts(self, dims):
        return [2 if d == "x" else 1 << self.groups[d][1] for d in dims]

    def send(self, value, d, mask):
        if d == "x":
            return swap(value, "xx")
        move = mask << self.groups[d][0]
        return lax.ppermute(value, "dp", [(i, i ^ move) for i in range(self.size)])

    def place(self, d):
        return self.side if d == "x" else self.groups[d][2]

    def scatter(self, parts, comes, dims, d, after=()):
        axis = dims.index(d)
        shares = fold(parts, comes, self.counts(dims), axis, self.place(d), list(after))
        come = [[self.send(share, d, mask)] for mask, share in enumerate(shares) if mask > 0]
        return [shares[0]], come, [other for other in dims if other != d]

    def scatter_rest(self, state, after):
        for d in self.rest:
            state = self.scatter(*state, d, after)
        return self.total(state)

    def total(self, state):
        parts, comes, dims = state
        total = parts[0].astype(F32)
        for (come,) in comes:
            total = total + come.astype(F32)
        return total[0]

    def begin_gather(self, state, d):
        array, dims = state
        come = [self.send(array, d, mask) for mask in range(1, self.counts([d])[0])]
        return array, come, dims, d

    def end_gather(self, begun, tick=None):
        array, come, dims, d = begun
        parts = [array] + come
        for bit in range(len(parts).bit_length() - 1):
            flag = (self.place(d) >> bit) & 1
            for low in range(len(parts)):
                if not low & (1 << bit):
                    high = low | (1 << bit)
                    parts[low], parts[high] = pick(flag, parts[low], parts[high])
        dims = [other for other in self.dims if other in dims or other == d]
        joined = jnp.stack(parts, axis=dims.index(d))
        if tick is not None:
            joined = joined + tick[0, 0].astype(joined.dtype)
        return joined, dims

    def gather(self, state, d, tick=None):
        return self.end_gather(self.begin_gather(state, d), tick)

def body(
    tokens,
    segments,
    ln1_gain,
    ln1_bias,
    qkv_weight,
    q_bias,
    v_bias,
    out_weight,
    out_bias,
    ln2_gain,
    ln2_bias,
    up_weight,
    up_bias,
    down_weight,
    down_bias,
    cotangent,
):
    side = lax.axis_index("xx")
    core = lax.axis_index("core")
    chips = lax.axis_size("dp") * lax.axis_size("xx")
    seq_count, quarter, width = tokens.shape
    length = segments.shape[1]
    own = qkv_weight.shape[0]
    pair_row = 2 * own
    hidden_own = up_bias.shape[0]
    half = width // 2
    cols = 3 * half
    pairs = half // PAIR
    splits = hidden_own // pair_row
    hidden = splits * width

    def at_index(array, index):
        return lax.dynamic_index_in_dim(array, index, 0, keepdims=False)

    def to_sequence(array, tick=None):
        kept = at_index(array, side)
        sent = at_index(array, 1 - side)
        if tick is not None:
            sent = sent + tick[0, 0].astype(sent.dtype)
        come = swap(sent, "xx")
        low, high = pick(side, kept, come)
        mine = jnp.stack([low, high])
        other = swap(mine, "core")
        even, odd = pick(core, mine, other)
        return jnp.stack([even, odd], axis=1).reshape(length, width), come, other

    def own_rows(array):
        return lax.dynamic_index_in_dim(
            array.reshape(2, 2, quarter, array.shape[-1]), core, 1, keepdims=False
        )

    def other_rows(array):
        return lax.dynamic_index_in_dim(
            array.reshape(2, 2, quarter, array.shape[-1]), 1 - core, 1, keepdims=False
        )

    def from_sequence(mine):
        come = swap(at_index(mine, 1 - side), "xx")
        return merged(at_index(mine, side), come), come

    def merged(kept, come, tick=None):
        if tick is not None:
            kept = kept + tick[0, 0].astype(kept.dtype)
        first, second = pick(side, kept, come)
        return jnp.stack([first, second])

    qkv_cols = qkv_weight.reshape(own, 3, 2, pairs, PAIR).transpose(2, 0, 3, 1, 4).reshape(2, own, cols)
    up_cols = (
        up_weight.reshape(own, chips, 2, splits, pair_row)
        .transpose(2, 0, 3, 1, 4)
        .reshape(2, own, hidden)
    )
    vectors = jnp.stack(
        [ln1_gain, ln1_bias, q_bias, v_bias, out_bias, ln2_gain, ln2_bias, down_bias], axis=1
    )
    vectors = jnp.pad(vectors, ((0, 0), (0, PAIR - vectors.shape[1])))

    def with_partner(two):
        mine, theirs = at_index(two, core), at_index(two, 1 - core)
        first, second = pick(core, mine, swap(theirs, "core"))
        return jnp.concatenate([first, second], axis=0)

    early = with_partner(
        jnp.concatenate([qkv_cols, jnp.broadcast_to(vectors, (2, own, PAIR))], axis=2)
    )
    early = jnp.concatenate(
        [
            early[:, : cols + 8],
            up_bias.reshape(splits, pair_row).T,
            early[:, cols + 8 + splits :],
        ],
        axis=1,
    )
    links = Links()

    def gather_rest(array, tick=None):
        state = (array, [])
        for d in links.rest:
            state = links.gather(state, d, tick if d == links.rest[-1] else None)
        return state

    def halves_of(state):
        middle = state[0].shape[-1] // 2
        return [(state[0][..., :middle], state[1]), (state[0][..., middle:], state[1])]

    def joined(halves):
        return [half_state[0].reshape(width, -1) for half_state in halves]

    inputs_low, come, other = to_sequence(tokens)
    grad_out_low, _, _ = to_sequence(cotangent, gate([come]))
    state = (early, [])
    for d in links.rest[:-1]:
        state = links.gather(state, d)
    first_stage = links.begin_gather(state, links.rest[-1])
    begun = [
        links.begin_gather(piece, d)
        for piece, d in zip(halves_of(links.end_gather(first_stage)), "yx")
    ]
    early_halves = [links.end_gather(piece) for piece in begun]
    early_a, early_b = joined(
        [links.gather(piece, d) for piece, d in zip(early_halves, "xy")]
    )
    split = early_a.shape[1]
    late = with_partner(
        jnp.concatenate([up_cols, jnp.broadcast_to(out_weight, (2, own, width))], axis=2)
    )
    down_own = down_weight.reshape(splits, pair_row, width)
    late = lax.all_gather(
        pack([late, *(down_own[i] for i in range(splits))], [first_stage[1][-1]]),
        ("dp", "xx"),
        axis=0,
        tiled=True,
    )
    small = early_b[:, cols - split :].astype(F32).T
    gain_one, shift_one, query_shift, value_shift, out_shift, gain_two, shift_two, down_shift = (
        small[i] for i in range(8)
    )
    up_shift = small[8 : 8 + splits].reshape(hidden)

    inputs = inputs_low.astype(F32)
    seg = at_index(segments, side)
    numbers = jnp.arange(PAIR, dtype=jnp.int32) % HEAD_DIM
    same = seg[:, None] == numbers[None, :]
    coded = numbers[None, :] < 4
    query_code = jnp.where(same & coded, 1.0, 0.0).astype(BF16)
    key_code = jnp.where(same | ~coded, 0.0, NEG).astype(BF16)

    def head_cols(vector):
        return lax.dynamic_slice_in_dim(vector, core * half, half, 0).reshape(pairs, 1, PAIR)

    zeros = jnp.zeros((pairs, 1, PAIR), F32)
    qkv_shift = jnp.concatenate(
        [head_cols(query_shift), zeros, head_cols(value_shift)], axis=1
    ).reshape(1, cols)
    qkv_scale = jnp.tile(jnp.repeat(jnp.array([0.125, 1.0, 1.0], F32), PAIR), pairs)[None]
    normed_t, qkv, tick = qkv_projection(
        inputs_low,
        early_a,
        early_b,
        jnp.pad(jnp.stack([gain_one, shift_one]), ((0, 6), (0, 0))),
        jnp.pad(jnp.concatenate([qkv_shift, qkv_scale]), ((0, 6), (0, 0))),
        [],
    )
    attended, log_total, _ = attention_forward(qkv, query_code, key_code)
    core_at = core.reshape(1).astype(jnp.int32)
    branch = out_projection(core_at, attended, late, splits, [grad_out_low])
    branch_come = swap(branch, "core")
    mid_vectors = jnp.pad(
        jnp.stack([out_shift, gain_two, shift_two, down_shift]), ((0, 4), (0, 0))
    )
    normed_two_low, hidden_low, grad_pre_low, mixed_part, ffn_other, partial_two, up_sums = feed_forward(
        core_at,
        inputs_low,
        branch,
        branch_come,
        grad_out_low,
        late,
        splits,
        mid_vectors,
        jnp.pad(up_shift[None], ((0, 7), (0, 0))),
    )
    partial_come = swap(partial_two, "core")
    mixed_own = (mixed_part + swap(ffn_other, "core").astype(F32)).astype(BF16)
    mixed_own = mixed_own.reshape(2, quarter, width)
    mixed_come = swap(at_index(mixed_own, 1 - side), "xx")

    grad_proj_down = [
        mm(hidden_low[:, i * width : (i + 1) * width], grad_out_low, TN).astype(BF16)
        for i in range(splits)
    ]
    grad_proj_up = mm(normed_two_low, grad_pre_low, TN).astype(BF16)
    late_grads = jnp.concatenate([grad_proj_up, *grad_proj_down], axis=1)
    late_own = lax.psum_scatter(late_grads, ("dp", "xx"), scatter_dimension=0, tiled=True)
    grad_middle, branch_low, grad_attended, mid_sums = norm_two(
        core_at,
        inputs_low,
        branch,
        branch_come,
        grad_out_low,
        partial_two,
        partial_come,
        late,
        splits,
        mid_vectors,
        [late_grads],
    )
    grad_proj_out = mm(attended, branch_low, TN)

    def as_column(vectors):
        table = jnp.stack(vectors, axis=1)
        return jnp.pad(table, ((0, 0), (0, PAIR - table.shape[1])))

    def only_mine(flag, array):
        return jnp.where(flag, array, jnp.zeros_like(array))

    small_two = [mid_sums[i] for i in range(4)] + [
        up_sums[0, i * width : (i + 1) * width] for i in range(splits)
    ]
    out_low = grad_proj_out.astype(BF16)
    grad_out_rows = jnp.concatenate(
        [only_mine(core == 0, out_low), only_mine(core == 1, out_low)], axis=0
    )

    def blocks(array):
        return array.reshape(chips, pair_row, array.shape[1])

    def pairs_backward(first, count, after):
        return attention_backward(
            first, count, qkv, query_code, key_code, attended, grad_attended, log_total, normed_t, after
        )

    out_piece = links.scatter([blocks(grad_out_rows)], [], links.dims, "y")
    grad_a, weight_grad_a, tick = pairs_backward(0, pairs - 1, [out_piece[0][0]])
    out_piece = links.scatter(*out_piece, "x", [tick])
    first_piece = links.scatter([blocks(weight_grad_a)], [], links.dims, "y", [tick])
    mixed = merge(at_index(mixed_own, side), mixed_come, side, [tick])
    grad_b, weight_grad_b, tick = pairs_backward(
        pairs - 1, 1, [out_piece[0][0], first_piece[0][0], tick, mixed]
    )
    grads = [grad_a, grad_b]
    first_piece = links.scatter(*first_piece, "x", [tick])
    norm_vectors = jnp.pad(jnp.stack([gain_one, shift_one]), ((0, 6), (0, 0)))
    partial_one, norm_sums, bias_sums, tick = norm_one(
        False, core_at, grads, early_a, early_b, cols, inputs_low, [], [first_piece[0][0]]
    )
    come = swap(partial_one, "core")
    token_own, norm_sums_own, bias_sums_own, tick = norm_one(
        True,
        core_at,
        grads,
        early_a,
        early_b,
        cols,
        inputs_low,
        [come, grad_middle, norm_vectors],
        [],
    )
    norm_sums = norm_sums + norm_sums_own
    bias_sums = bias_sums + bias_sums_own
    token_grad, come = from_sequence(token_own.reshape(2, quarter, width))
    grad_by_pair = bias_sums[0].reshape(pairs, 3, PAIR)

    def padded(vector):
        vector = vector.reshape(half)
        return jnp.concatenate([only_mine(core == 0, vector), only_mine(core == 1, vector)])

    small = as_column(
        [
            norm_sums[0],
            norm_sums[1],
            padded(grad_by_pair[:, 0]),
            padded(grad_by_pair[:, 2]),
        ]
        + small_two
    )
    last_piece = links.scatter(
        [blocks(weight_grad_b), blocks(small.astype(BF16))], [], links.dims, "y", [tick]
    )
    first_piece = (
        out_piece[0] + first_piece[0],
        [out_piece[1][0] + first_piece[1][0]],
        first_piece[2],
    )
    first_own = links.scatter_rest(first_piece, [tick])
    last_piece = links.scatter(*last_piece, "x")
    last_ready = last_piece[0][0]
    last_own = links.scatter_rest(last_piece, [come])

    def rows_of(array, index):
        return lax.dynamic_slice_in_dim(array, index * own, own, 0)

    def by_core(mine, come):
        return jnp.stack(pick(core, mine, come))

    def shared(array):
        return rows_of(array, core), swap(rows_of(array, 1 - core), "core")

    up_own, down_grad = widen(late_own, width, [last_ready])
    late_mine, late_come = shared(up_own)
    early_mine, early_come = shared(jnp.concatenate([first_own, last_own], axis=1).astype(BF16))
    out_grad = early_mine[:, :width].astype(F32) + early_come[:, :width].astype(F32)
    up_grad = (
        by_core(late_mine, late_come)
        .reshape(2, own, splits, chips, pair_row)
        .transpose(1, 3, 0, 2, 4)
        .reshape(own, 2 * hidden)
        .astype(F32)
    )
    down_grad = down_grad.reshape(hidden_own, width)
    qkv_grad = (
        by_core(early_mine[:, width : width + cols], early_come[:, width : width + cols])
        .reshape(2, own, pairs, 3, PAIR)
        .transpose(1, 3, 0, 2, 4)
        .reshape(own, 2 * cols)
        .astype(F32)
    )
    tail, first = width + cols + 8, first_own.shape[1]
    small_mine = early_mine[:, tail - 8 : tail].astype(F32)
    one = small_mine[:, :4] + early_come[:, tail - 8 : tail - 4].astype(F32)
    up_shift_grad = (
        last_own[:, tail - first : tail - first + splits].T.reshape(hidden_own).astype(F32)
    )
    two = small_mine[:, 4:]
    return (
        mixed,
        token_grad,
        one[:, 0],
        one[:, 1],
        qkv_grad,
        one[:, 2],
        one[:, 3],
        out_grad,
        two[:, 0],
        two[:, 1],
        two[:, 2],
        up_grad,
        up_shift_grad,
        down_grad,
        two[:, 3],
    )


def solution(mesh):
    parts = (mesh.shape["dp"], mesh.shape["ctx"] // 2, 2)
    split_mesh = Mesh(mesh.devices.reshape(parts), ("dp", "xx", "core"))
    rows = ("dp", "xx", "core")
    acts = P("dp", ("xx", "core"), None)
    vec, mat = P(rows), P(rows, None)
    return jax.shard_map(
        body,
        mesh=split_mesh,
        in_specs=(
            acts, P("dp", None), vec, vec, mat, vec, vec, mat, vec, vec, vec, mat, vec, mat, vec, acts,
        ),
        out_specs=(
            acts, acts, vec, vec, mat, vec, vec, mat, vec, vec, vec, mat, vec, mat, vec,
        ),
        check_vma=False,
    )
```

```python
import functools

import jax
import jax.numpy as jnp
from jax import lax
from jax.experimental import pallas as pl
from jax.experimental.pallas import tpu as pltpu
from jax.sharding import Mesh, PartitionSpec as P

HEAD_DIM = 64
PAIR = 2 * HEAD_DIM
EPSILON = 1e-05
NEG = -1e30
BLK = 512
F32 = jnp.float32
BF16 = jnp.bfloat16

NN = (((1,), (0,)), ((), ()))
NT = (((1,), (1,)), ((), ()))
TN = (((0,), (0,)), ((), ()))


def mm(left, right, dims=NN):
    return lax.dot_general(left, right, dims, preferred_element_type=F32)


def build_scores_operands(qkv_ref, qs_ref, ks_ref, rows, qx, kx):
    lane = lax.broadcasted_iota(jnp.int32, (BLK, PAIR), 1)
    first = lane < HEAD_DIM
    q = qkv_ref[rows, 0:PAIR].astype(F32)
    k = qkv_ref[rows, PAIR : 2 * PAIR].astype(F32)
    qs = qs_ref[rows, :].astype(F32)
    ks = ks_ref[rows, :].astype(F32)
    qx[0, rows, :] = jnp.where(first, q, qs).astype(BF16)
    qx[1, rows, :] = jnp.where(first, qs, q).astype(BF16)
    kx[0, rows, :] = jnp.where(first, k, ks).astype(BF16)
    kx[1, rows, :] = jnp.where(first, ks, k).astype(BF16)
    return first, q, k


def causal_block(scores):
    key_at = lax.broadcasted_iota(jnp.int32, scores.shape, 0)
    query_at = lax.broadcasted_iota(jnp.int32, scores.shape, 1)
    return jnp.where(key_at <= query_at, scores, NEG)


def attention_forward_kernel(qkv_ref, qs_ref, ks_ref, *rest):
    o_ref, lse_ref, tick_ref, qx, kx, vt, acc = rest[-7:]
    tick_ref[...] = jnp.zeros_like(tick_ref)
    length = qkv_ref.shape[0]
    blocks = length // BLK

    @pl.loop(0, blocks)
    def _(i):
        rows = pl.ds(pl.multiple_of(i * BLK, BLK), BLK)
        build_scores_operands(qkv_ref, qs_ref, ks_ref, rows, qx, kx)
        v_t = qkv_ref[rows, 2 * PAIR : 3 * PAIR].astype(F32).T
        ones = jnp.ones((16, BLK), BF16)
        for h in range(2):
            vt[h, 0:HEAD_DIM, rows] = v_t[h * HEAD_DIM : (h + 1) * HEAD_DIM].astype(BF16)
            vt[h, HEAD_DIM : HEAD_DIM + 16, rows] = ones

    @pl.loop(0, blocks)
    def _(i):
        rows = pl.ds(pl.multiple_of(i * BLK, BLK), BLK)
        queries = [qx[h, rows, :] for h in range(2)]
        tops = []
        for h in range(2):
            s = causal_block(mm(kx[h, rows, :], queries[h], NT))
            top = jnp.max(s, axis=0, keepdims=True)
            p = jnp.exp(s - top).astype(BF16)
            acc[h] = mm(vt[h, :, rows], p)
            tops.append(top)

        def step(j, carry):
            keys = pl.ds(pl.multiple_of(j * BLK, BLK), BLK)
            out = []
            for h in range(2):
                s = mm(kx[h, keys, :], qx[h, rows, :], NT)
                top = jnp.maximum(carry[h], jnp.max(s, axis=0, keepdims=True))
                p = jnp.exp(s - top).astype(BF16)
                acc[h] = acc[h] * jnp.exp(carry[h] - top) + mm(vt[h, :, keys], p)
                out.append(top)
            return tuple(out)

        tops = lax.fori_loop(0, i, step, tuple(tops))
        parts = []
        for h in range(2):
            total = acc[h, HEAD_DIM : HEAD_DIM + 1, :]
            parts.append(acc[h, 0:HEAD_DIM, :] / total)
            lse_ref[0, h : h + 1, rows] = tops[h] + jnp.log(total)
        o_ref[rows, :] = jnp.concatenate(parts, axis=0).T.astype(BF16)


def attention_backward_kernel(qkv_ref, qs_ref, ks_ref, o_ref, do_ref, lse_ref, at_ref, *rest):
    d_ref, dw_ref, tick_ref, qx, kx, qm, dm, kt, delta, dqt, dk, dv = rest[-12:]
    tick_ref[...] = jnp.zeros_like(tick_ref)
    length = qkv_ref.shape[0]
    blocks = length // BLK

    @pl.loop(0, blocks)
    def _(i):
        rows = pl.ds(pl.multiple_of(i * BLK, BLK), BLK)
        first, q, k = build_scores_operands(qkv_ref, qs_ref, ks_ref, rows, qx, kx)
        do = do_ref[rows, :].astype(F32)
        zero = jnp.zeros_like(q)
        qm[0, rows, :] = jnp.where(first, q, zero).astype(BF16)
        qm[1, rows, :] = jnp.where(first, zero, q).astype(BF16)
        dm[0, rows, :] = jnp.where(first, do, zero).astype(BF16)
        dm[1, rows, :] = jnp.where(first, zero, do).astype(BF16)
        kt[:, rows] = k.T.astype(BF16)
        inner = (do * o_ref[rows, :].astype(F32)).T
        for h in range(2):
            delta[h : h + 1, rows] = jnp.sum(
                inner[h * HEAD_DIM : (h + 1) * HEAD_DIM], axis=0, keepdims=True
            )
        dqt[:, rows] = jnp.zeros((PAIR, BLK), F32)

    def tile(keys, rows, masked):
        values = qkv_ref[keys, 2 * PAIR : 3 * PAIR]
        dv_part, dk_part = None, None
        for h in range(2):
            s = mm(kx[h, keys, :], qx[h, rows, :], NT)
            if masked:
                s = causal_block(s)
            p = jnp.exp(s - lse_ref[0, h : h + 1, rows])
            dp = mm(values, dm[h, rows, :], NT)
            ds = (p * (dp - delta[h : h + 1, rows])).astype(BF16)
            dv_h = mm(p.astype(BF16), dm[h, rows, :])
            dk_h = mm(ds, qm[h, rows, :])
            dv_part = dv_h if h == 0 else dv_part + dv_h
            dk_part = dk_h if h == 0 else dk_part + dk_h
            part = slice(h * HEAD_DIM, (h + 1) * HEAD_DIM)
            dqt[part, rows] += mm(kt[part, keys], ds)
        return dk_part, dv_part

    @pl.loop(0, blocks)
    def _(j):
        keys = pl.ds(pl.multiple_of(j * BLK, BLK), BLK)
        dk[...], dv[...] = tile(keys, keys, True)

        @pl.loop(j + 1, blocks)
        def _(i):
            dk_part, dv_part = tile(keys, pl.ds(pl.multiple_of(i * BLK, BLK), BLK), False)
            dk[...] += dk_part
            dv[...] += dv_part

        d_ref[keys, PAIR : 2 * PAIR] = dk[...].astype(BF16)
        d_ref[keys, 2 * PAIR : 3 * PAIR] = dv[...].astype(BF16)

    @pl.loop(0, blocks)
    def _(i):
        rows = pl.ds(pl.multiple_of(i * BLK, BLK), BLK)
        d_ref[rows, 0:PAIR] = (dqt[:, rows].T.astype(BF16).astype(F32) * 0.125).astype(BF16)

    @pl.loop(0, dw_ref.shape[0] // ROWS)
    def _(i):
        rows = pl.ds(pl.multiple_of(i * ROWS, ROWS), ROWS)
        dw_ref[rows, :] = mm(at_ref[rows, :], d_ref[...]).astype(BF16)


VMEM_LIMIT = 48 * 1024 * 1024


SMALL_COST = pl.CostEstimate(flops=1000, bytes_accessed=1000, transcendentals=0)


TICK = jax.ShapeDtypeStruct((8, 128), F32)
TICK_SPEC = pl.BlockSpec((8, 128), lambda i: (0, 0))
ANY_SPEC = pl.BlockSpec(memory_space=pl.ANY)


def pack_kernel(count, refs):
    refs[-1][...] = jnp.concatenate([ref[...] for ref in refs[:count]], axis=-1)


def pack(parts, after):
    rows = parts[0].shape[0]
    width = sum(part.shape[1] for part in parts)
    return pl.pallas_call(
        lambda *refs: pack_kernel(len(parts), refs),
        grid=(1,),
        in_specs=[pl.BlockSpec(part.shape, lambda i: (0, 0)) for part in parts]
        + [ANY_SPEC] * len(after),
        out_specs=pl.BlockSpec((rows, width), lambda i: (0, 0)),
        out_shape=jax.ShapeDtypeStruct((rows, width), BF16),
        compiler_params=pltpu.CompilerParams(vmem_limit_bytes=VMEM_LIMIT),
        cost_estimate=SMALL_COST,
    )(*parts, *after)


def widen(source, width, after):
    rows, cols = source.shape
    count = cols // width - 2

    def kernel(source_ref, *refs):
        up_ref, down_ref = refs[-2:]
        up_ref[...] = source_ref[:, : 2 * width].astype(F32)
        for i in range(count):
            down_ref[i] = source_ref[:, (2 + i) * width : (3 + i) * width].astype(F32)

    return pl.pallas_call(
        kernel,
        grid=(1,),
        in_specs=[pl.BlockSpec((rows, cols), lambda i: (0, 0))] + [ANY_SPEC] * len(after),
        out_specs=[
            pl.BlockSpec((rows, 2 * width), lambda i: (0, 0)),
            pl.BlockSpec((count, rows, width), lambda i: (0, 0, 0)),
        ],
        out_shape=[
            jax.ShapeDtypeStruct((rows, 2 * width), F32),
            jax.ShapeDtypeStruct((count, rows, width), F32),
        ],
        compiler_params=pltpu.CompilerParams(vmem_limit_bytes=VMEM_LIMIT),
        cost_estimate=SMALL_COST,
    )(source, *after)


def merge(kept, come, side, after):
    def kernel(side_ref, kept_ref, come_ref, *rest):
        mine = pl.program_id(0) == side_ref[0]

        @pl.when(mine)
        def _():
            rest[-1][0] = kept_ref[...]

        @pl.when(jnp.logical_not(mine))
        def _():
            rest[-1][0] = come_ref[...]

    whole = pl.BlockSpec(kept.shape, lambda i, side_ref: (0, 0))
    return pl.pallas_call(
        kernel,
        grid_spec=pltpu.PrefetchScalarGridSpec(
            num_scalar_prefetch=1,
            grid=(2,),
            in_specs=[whole, whole] + [ANY_SPEC] * len(after),
            out_specs=pl.BlockSpec((1, *kept.shape), lambda i, side_ref: (i, 0, 0)),
        ),
        out_shape=jax.ShapeDtypeStruct((2, *kept.shape), kept.dtype),
        compiler_params=pltpu.CompilerParams(vmem_limit_bytes=VMEM_LIMIT),
        cost_estimate=SMALL_COST,
    )(side.reshape(1).astype(jnp.int32), kept, come, *after)


def gate_kernel(*refs):
    refs[-1][...] = jnp.zeros_like(refs[-1])


def gate(after):
    return pl.pallas_call(
        gate_kernel,
        grid=(1,),
        in_specs=[ANY_SPEC] * len(after),
        out_specs=TICK_SPEC,
        out_shape=TICK,
        cost_estimate=SMALL_COST,
    )(*after)


def fold(pieces, sizes, axis, at, after):
    blocks, rows = pieces[0][0].shape[:2]
    width = sum(piece[0].shape[2] for piece in pieces)
    outs = sizes[axis] if axis is not None else 1
    inner = 1
    if axis is not None:
        for size in sizes[axis + 1 :]:
            inner *= size
    flat = [array for piece in pieces for array in piece]

    def spec(array, m):
        def index(j, at_ref):
            if axis is None:
                return j, 0, 0
            return (j // inner) * (outs * inner) + (at_ref[0] ^ m) * inner + j % inner, 0, 0

        return pl.BlockSpec((1, rows, array.shape[2]), index)

    def kernel(at_ref, *refs):
        for m in range(outs):
            left = list(refs[m * len(flat) : (m + 1) * len(flat)])
            sides = []
            for piece in pieces:
                value = left.pop(0)[0]
                for _ in piece[1:]:
                    value = value.astype(F32) + left.pop(0)[0].astype(F32)
                sides.append(value.astype(BF16))
            refs[len(refs) - outs + m][0] = jnp.concatenate(sides, axis=-1)

    out = pl.BlockSpec((1, rows, width), lambda j, at_ref: (j, 0, 0))
    return pl.pallas_call(
        kernel,
        grid_spec=pltpu.PrefetchScalarGridSpec(
            num_scalar_prefetch=1,
            grid=(blocks // outs,),
            in_specs=[spec(array, m) for m in range(outs) for array in flat]
            + [ANY_SPEC] * len(after),
            out_specs=[out] * outs,
        ),
        out_shape=[jax.ShapeDtypeStruct((blocks // outs, rows, width), BF16)] * outs,
        compiler_params=pltpu.CompilerParams(vmem_limit_bytes=VMEM_LIMIT),
        cost_estimate=SMALL_COST,
    )(at.reshape(1).astype(jnp.int32), *(flat * outs), *after)


def qkv_kernel(x_ref, wa_ref, wb_ref, vec_ref, col_ref, *rest_refs):
    a_ref, qkv_ref, tick_ref = rest_refs[-3:]
    split = wa_ref.shape[1]
    rest = qkv_ref.shape[1] - split
    for part in range(2):
        rows = slice(part * ROWS, (part + 1) * ROWS)
        normal, _ = norm_forward(x_ref[rows, :].astype(F32))
        normed = (normal * vec_ref[0:1, :] + vec_ref[1:2, :]).astype(BF16)
        a_ref[:, rows] = normed.astype(F32).T.astype(BF16)
        for w, cols in ((wa_ref[...], slice(0, split)), (wb_ref[:, :rest], slice(split, None))):
            shift, scale = col_ref[0:1, cols], col_ref[1:2, cols]
            qkv_ref[rows, cols] = ((mm(normed, w) + shift) * scale).astype(BF16)
    tick_ref[...] = jnp.zeros_like(tick_ref)


def qkv_projection(inputs, weight_a, weight_b, vectors, columns, after):
    length, width = inputs.shape
    cols = columns.shape[1]
    return pl.pallas_call(
        qkv_kernel,
        grid=(length // (2 * ROWS),),
        in_specs=[
            pl.BlockSpec((2 * ROWS, width), lambda i: (i, 0)),
            pl.BlockSpec(weight_a.shape, lambda i: (0, 0)),
            pl.BlockSpec(weight_b.shape, lambda i: (0, 0)),
            pl.BlockSpec(vectors.shape, lambda i: (0, 0)),
            pl.BlockSpec(columns.shape, lambda i: (0, 0)),
        ]
        + [ANY_SPEC] * len(after),
        out_specs=[
            pl.BlockSpec((width, 2 * ROWS), lambda i: (0, i)),
            pl.BlockSpec((2 * ROWS, cols), lambda i: (i, 0)),
            TICK_SPEC,
        ],
        out_shape=[
            jax.ShapeDtypeStruct((width, length), BF16),
            jax.ShapeDtypeStruct((length, cols), BF16),
            TICK,
        ],
        compiler_params=pltpu.CompilerParams(vmem_limit_bytes=VMEM_LIMIT),
        cost_estimate=SMALL_COST,
    )(inputs, weight_a, weight_b, vectors, columns, *after)


def out_projection(core, attended, late, block, after):
    length, cols = attended.shape
    width = late.shape[0]
    rows = length // 4

    def kernel(core_ref, a_ref, w_ref, *rest):
        rest[-1][...] = mm(a_ref[...], w_ref[...]).astype(BF16)

    return pl.pallas_call(
        kernel,
        grid_spec=pltpu.PrefetchScalarGridSpec(
            num_scalar_prefetch=1,
            grid=(4,),
            in_specs=[
                pl.BlockSpec((rows, cols), lambda i, core_ref: (i, 0)),
                pl.BlockSpec((cols, width), lambda i, core_ref: (core_ref[0], block)),
            ]
            + [ANY_SPEC] * len(after),
            out_specs=pl.BlockSpec((rows, width), lambda i, core_ref: (i, 0)),
        ),
        out_shape=jax.ShapeDtypeStruct((length, width), BF16),
        compiler_params=pltpu.CompilerParams(vmem_limit_bytes=VMEM_LIMIT),
        cost_estimate=SMALL_COST,
    )(core, attended, late, *after)


def middle_of(x_ref, b0_ref, b1_ref, vec_ref):
    both = b0_ref[...].astype(F32) + b1_ref[...].astype(F32)
    return x_ref[...].astype(F32) + both + vec_ref[0:1, :]


def feed_forward_kernel(splits, core_ref, x_ref, b0_ref, b1_ref, dy_ref, up_ref, *rest):
    down_refs, (vec_ref, shift_ref) = rest[:splits], rest[splits : splits + 2]
    a_ref, g_ref, du_ref, own_ref, other_ref, dh_ref, sums_ref = rest[splits + 2 :]
    at = pl.program_id(0)

    @pl.when(at == 0)
    def _():
        sums_ref[...] = jnp.zeros_like(sums_ref)

    middle = middle_of(x_ref, b0_ref, b1_ref, vec_ref)
    normal, _ = norm_forward(middle)
    normed = (normal * vec_ref[1:2, :] + vec_ref[2:3, :]).astype(BF16)
    a_ref[...] = normed
    dy = dy_ref[...]
    ffn, dh = None, None
    width = dy.shape[1]
    for i, down_ref in enumerate(down_refs):
        cols = slice(i * width, (i + 1) * width)
        up, down = up_ref[:, cols], down_ref[...]
        value, slope = gelu_parts(mm(normed, up) + shift_ref[0:1, cols])
        du = slope * mm(dy, down, NT)
        value, du = value.astype(BF16), du.astype(BF16)
        g_ref[:, cols] = value
        du_ref[:, cols] = du
        sums_ref[0:1, cols] += jnp.sum(du.astype(F32), axis=0, keepdims=True)
        ffn_part, dh_part = mm(value, down), mm(du, up, NT)
        ffn = ffn_part if i == 0 else ffn + ffn_part
        dh = dh_part if i == 0 else dh + dh_part
    dh_ref[...] = dh.astype(BF16)
    mine = at % 2 == core_ref[0]

    @pl.when(mine)
    def _():
        own_ref[...] = middle_of(x_ref, b0_ref, b1_ref, vec_ref) + ffn + vec_ref[3:4, :]

    @pl.when(jnp.logical_not(mine))
    def _():
        other_ref[...] = ffn.astype(BF16)


def feed_forward(core, inputs, branch, branch_come, grad_out, late, splits, vectors, up_shift):
    length, width = inputs.shape
    rows = length // 4
    hidden = splits * width
    narrow = pl.BlockSpec((rows, width), lambda i, core_ref: (i, 0))
    wide = pl.BlockSpec((rows, hidden), lambda i, core_ref: (i, 0))
    shared = pl.BlockSpec((rows, width), lambda i, core_ref: (i // 2, 0))

    def whole(array):
        return pl.BlockSpec(array.shape, lambda i, core_ref: (0, 0))

    def down(i):
        return pl.BlockSpec((width, width), lambda _, core_ref: (0, splits + 1 + i))

    return pl.pallas_call(
        functools.partial(feed_forward_kernel, splits),
        grid_spec=pltpu.PrefetchScalarGridSpec(
            num_scalar_prefetch=1,
            grid=(4,),
            in_specs=[narrow] * 4
            + [pl.BlockSpec((width, hidden), lambda i, core_ref: (0, 0))]
            + [down(i) for i in range(splits)]
            + [whole(vectors), whole(up_shift)],
            out_specs=[
                narrow, wide, wide, shared, shared, narrow,
                pl.BlockSpec((8, hidden), lambda i, core_ref: (0, 0)),
            ],
        ),
        out_shape=[
            jax.ShapeDtypeStruct((length, width), BF16),
            jax.ShapeDtypeStruct((length, hidden), BF16),
            jax.ShapeDtypeStruct((length, hidden), BF16),
            jax.ShapeDtypeStruct((length // 2, width), F32),
            jax.ShapeDtypeStruct((length // 2, width), BF16),
            jax.ShapeDtypeStruct((length, width), BF16),
            jax.ShapeDtypeStruct((8, hidden), F32),
        ],
        compiler_params=pltpu.CompilerParams(vmem_limit_bytes=VMEM_LIMIT),
        cost_estimate=SMALL_COST,
    )(core, inputs, branch, branch_come, grad_out, late, *([late] * splits), vectors, up_shift)


def norm_two_kernel(core_ref, x_ref, b0_ref, b1_ref, dy_ref, p0_ref, p1_ref, w_ref, vec_ref, *rest):
    mid_ref, low_ref, do_ref, sums_ref = rest[-4:]

    @pl.when(pl.program_id(0) == 0)
    def _():
        sums_ref[...] = jnp.zeros_like(sums_ref)

    normal, scale = norm_forward(middle_of(x_ref, b0_ref, b1_ref, vec_ref))
    grad = p0_ref[...].astype(F32) + p1_ref[...].astype(F32)
    dy = dy_ref[...].astype(F32)
    mid = dy + norm_backward(normal, scale, grad * vec_ref[1:2, :])
    low = mid.astype(BF16)
    low_ref[...] = low
    do_ref[...] = mm(low, w_ref[...], NT).astype(BF16)
    for i, value in enumerate((low.astype(F32), grad * normal, grad, dy)):
        sums_ref[i : i + 1, :] += jnp.sum(value, axis=0, keepdims=True)

    @pl.when(pl.program_id(0) % 2 == core_ref[0])
    def _():
        mid_ref[...] = mid


def norm_two(core, inputs, branch, branch_come, grad_out, partial, partial_come, late, block, vectors, after):
    length, width = inputs.shape
    rows = length // 4
    cols = width // 2
    narrow = pl.BlockSpec((rows, width), lambda i, core_ref: (i, 0))
    return pl.pallas_call(
        norm_two_kernel,
        grid_spec=pltpu.PrefetchScalarGridSpec(
            num_scalar_prefetch=1,
            grid=(4,),
            in_specs=[narrow] * 6
            + [
                pl.BlockSpec((cols, width), lambda i, core_ref: (core_ref[0], block)),
                pl.BlockSpec(vectors.shape, lambda i, core_ref: (0, 0)),
            ]
            + [ANY_SPEC] * len(after),
            out_specs=[
                pl.BlockSpec((rows, width), lambda i, core_ref: (i // 2, 0)),
                narrow,
                pl.BlockSpec((rows, cols), lambda i, core_ref: (i, 0)),
                pl.BlockSpec((8, width), lambda i, core_ref: (0, 0)),
            ],
        ),
        out_shape=[
            jax.ShapeDtypeStruct((length // 2, width), F32),
            jax.ShapeDtypeStruct((length, width), BF16),
            jax.ShapeDtypeStruct((length, cols), BF16),
            jax.ShapeDtypeStruct((8, width), F32),
        ],
        compiler_params=pltpu.CompilerParams(vmem_limit_bytes=VMEM_LIMIT),
        cost_estimate=SMALL_COST,
    )(core, inputs, branch, branch_come, grad_out, partial, partial_come, late, vectors, *after)


ROWS = 256


def attention_forward(qkv, query_code, key_code):
    length, width = qkv.shape
    pairs = width // (3 * PAIR)
    return pl.pallas_call(
        attention_forward_kernel,
        grid=(pairs,),
        in_specs=[
            pl.BlockSpec((length, 3 * PAIR), lambda p: (0, p)),
            pl.BlockSpec((length, PAIR), lambda p: (0, 0)),
            pl.BlockSpec((length, PAIR), lambda p: (0, 0)),
        ],
        out_specs=[
            pl.BlockSpec((length, PAIR), lambda p: (0, p)),
            pl.BlockSpec((1, 8, length), lambda p: (p, 0, 0)),
            TICK_SPEC,
        ],
        out_shape=[
            jax.ShapeDtypeStruct((length, pairs * PAIR), BF16),
            jax.ShapeDtypeStruct((pairs, 8, length), F32),
            TICK,
        ],
        scratch_shapes=[
            pltpu.VMEM((2, length, PAIR), BF16),
            pltpu.VMEM((2, length, PAIR), BF16),
            pltpu.VMEM((2, HEAD_DIM + 16, length), BF16),
            pltpu.VMEM((2, HEAD_DIM + 16, BLK), F32),
        ],
        compiler_params=pltpu.CompilerParams(vmem_limit_bytes=VMEM_LIMIT),
        cost_estimate=SMALL_COST,
    )(qkv, query_code, key_code)


def norm_one_kernel(own, core_ref, d0_ref, d1_ref, wa_ref, wb_ref, x_ref, *rest):
    if own:
        come_ref, mid_ref, vec_ref, out_ref, sums_ref, bias_ref, tick_ref, w = rest
    else:
        out_ref, sums_ref, bias_ref, tick_ref, w = rest
    split = wa_ref.shape[1]

    @pl.when(pl.program_id(0) == 0)
    def _():
        sums_ref[...] = jnp.zeros_like(sums_ref)
        bias_ref[...] = jnp.zeros_like(bias_ref)
        w[:, :split] = wa_ref[...]
        w[:, split:] = wb_ref[:, : w.shape[1] - split]
        tick_ref[...] = jnp.zeros_like(tick_ref)

    total = None
    for i, ref in enumerate((d0_ref, d1_ref)):
        cols = slice(0, ref.shape[1]) if i == 0 else slice(d0_ref.shape[1], None)
        grad = ref[...]
        part = mm(grad, w[:, cols], NT)
        total = part if i == 0 else total + part
        bias_ref[0:1, cols] += jnp.sum(grad.astype(F32), axis=0, keepdims=True)
    normal, scale = norm_forward(x_ref[...].astype(F32))
    sums_ref[0:1, :] += jnp.sum(total * normal, axis=0, keepdims=True)
    sums_ref[1:2, :] += jnp.sum(total, axis=0, keepdims=True)
    if own:
        grad = (total + come_ref[...].astype(F32)) * vec_ref[0:1, :]
        out_ref[...] = (mid_ref[...] + norm_backward(normal, scale, grad)).astype(BF16)
    else:
        out_ref[...] = total.astype(BF16)


def norm_one(own, core, grads, weight_a, weight_b, cols, inputs, extra, after):
    length, width = inputs.shape
    count = length // (2 * ROWS)
    per = count // 2

    def block(i, core_ref):
        which = core_ref[0] if own else 1 - core_ref[0]
        return ((i // per) * 2 + which) * per + i % per, 0

    def at_zero(i, core_ref):
        return 0, 0

    plain = pl.BlockSpec((ROWS, width), lambda i, core_ref: (i, 0))
    rows = pl.BlockSpec((ROWS, width), block)
    in_specs = [pl.BlockSpec((ROWS, grad.shape[1]), block) for grad in grads] + [
        pl.BlockSpec(weight_a.shape, at_zero),
        pl.BlockSpec(weight_b.shape, at_zero),
        rows,
    ]
    out_specs = [
        plain,
        pl.BlockSpec((8, width), at_zero),
        pl.BlockSpec((8, cols), at_zero),
        pl.BlockSpec((8, 128), at_zero),
    ]
    out_shape = [
        jax.ShapeDtypeStruct((count * ROWS, width), BF16),
        jax.ShapeDtypeStruct((8, width), F32),
        jax.ShapeDtypeStruct((8, cols), F32),
        TICK,
    ]
    if own:
        in_specs += [plain, plain, pl.BlockSpec(extra[2].shape, at_zero)]

    def kernel(*refs):
        inner = refs[: 1 + len(in_specs)] + refs[1 + len(in_specs) + len(after) :]
        norm_one_kernel(own, *inner)

    return pl.pallas_call(
        kernel,
        grid_spec=pltpu.PrefetchScalarGridSpec(
            num_scalar_prefetch=1,
            grid=(count,),
            in_specs=in_specs + [ANY_SPEC] * len(after),
            out_specs=out_specs,
            scratch_shapes=[pltpu.VMEM((width, cols), BF16)],
        ),
        out_shape=out_shape,
        compiler_params=pltpu.CompilerParams(vmem_limit_bytes=VMEM_LIMIT),
        cost_estimate=SMALL_COST,
    )(core, *grads, weight_a, weight_b, inputs, *extra, *after)


def attention_backward(
    first, count, qkv, query_code, key_code, attended, grad_attended, log_total, normed_t, after
):
    length = qkv.shape[0]
    width = normed_t.shape[0]
    return pl.pallas_call(
        attention_backward_kernel,
        grid=(count,),
        in_specs=[
            pl.BlockSpec((length, 3 * PAIR), lambda p: (0, first + p)),
            pl.BlockSpec((length, PAIR), lambda p: (0, 0)),
            pl.BlockSpec((length, PAIR), lambda p: (0, 0)),
            pl.BlockSpec((length, PAIR), lambda p: (0, first + p)),
            pl.BlockSpec((length, PAIR), lambda p: (0, first + p)),
            pl.BlockSpec((1, 8, length), lambda p: (first + p, 0, 0)),
            pl.BlockSpec(normed_t.shape, lambda p: (0, 0)),
        ]
        + [ANY_SPEC] * len(after),
        out_specs=[
            pl.BlockSpec((length, 3 * PAIR), lambda p: (0, p)),
            pl.BlockSpec((width, 3 * PAIR), lambda p: (0, p)),
            TICK_SPEC,
        ],
        out_shape=[
            jax.ShapeDtypeStruct((length, count * 3 * PAIR), BF16),
            jax.ShapeDtypeStruct((width, count * 3 * PAIR), BF16),
            TICK,
        ],
        scratch_shapes=[
            pltpu.VMEM((2, length, PAIR), BF16),
            pltpu.VMEM((2, length, PAIR), BF16),
            pltpu.VMEM((2, length, PAIR), BF16),
            pltpu.VMEM((2, length, PAIR), BF16),
            pltpu.VMEM((PAIR, length), BF16),
            pltpu.VMEM((8, length), F32),
            pltpu.VMEM((PAIR, length), F32),
            pltpu.VMEM((BLK, PAIR), F32),
            pltpu.VMEM((BLK, PAIR), F32),
        ],
        compiler_params=pltpu.CompilerParams(vmem_limit_bytes=VMEM_LIMIT),
        cost_estimate=SMALL_COST,
    )(qkv, query_code, key_code, attended, grad_attended, log_total, normed_t, *after)


def norm_forward(source):
    average = jnp.mean(source, axis=-1, keepdims=True)
    centred = source - average
    spread = jnp.mean(centred * centred, axis=-1, keepdims=True)
    scale = lax.rsqrt(spread + EPSILON)
    return centred * scale, scale


def norm_backward(normal, scale, grad):
    return scale * (
        grad
        - jnp.mean(grad, axis=-1, keepdims=True)
        - normal * jnp.mean(grad * normal, axis=-1, keepdims=True)
    )


GELU_A = 0.7978845608028654
GELU_B = 0.044715


def gelu_parts(source):
    square = source * source
    inner = jnp.tanh(GELU_A * (source + GELU_B * source * square))
    value = 0.5 * source * (1.0 + inner)
    slope = 0.5 * (1.0 + inner) + 0.5 * source * (1.0 - inner * inner) * (
        GELU_A * (1.0 + 3.0 * GELU_B * square)
    )
    return value, slope


def swap(value, axis):
    return lax.ppermute(value, axis, [(0, 1), (1, 0)])


def pick(flag, first, second):
    return jnp.where(flag == 0, first, second), jnp.where(flag == 0, second, first)


class Links:
    def __init__(self):
        self.size = lax.axis_size("dp")
        at = lax.axis_index("dp")
        self.groups = {}
        shift, name = 0, "y"
        while (1 << shift) < self.size:
            bits = 1 if shift == 0 else min(2, self.size.bit_length() - 1 - shift)
            self.groups[name] = (shift, bits, (at >> shift) & ((1 << bits) - 1))
            shift += bits
            name = "z" + str(shift)
        self.rest = [name for name in reversed(self.groups) if name != "y"]
        self.dims = self.rest + ["y", "x"]
        self.side = lax.axis_index("xx")

    def counts(self, dims):
        return [{"x": 2, "yx": 4}.get(d) or 1 << self.groups[d][1] for d in dims]

    def send(self, value, d, mask):
        if d == "x":
            return swap(value, "xx")
        if d == "yx":
            return lax.ppermute(
                value, ("dp", "xx"), [(i, i ^ mask) for i in range(2 * self.size)]
            )
        move = mask << self.groups[d][0]
        return lax.ppermute(value, "dp", [(i, i ^ move) for i in range(self.size)])

    def place(self, d):
        if d == "yx":
            return self.groups["y"][2] * 2 + self.side
        return self.side if d == "x" else self.groups[d][2]

    def scatter(self, pieces, dims, d, after=()):
        axis = dims.index(d)
        shares = fold(pieces, self.counts(dims), axis, self.place(d), list(after))
        come = [self.send(share, d, mask) for mask, share in enumerate(shares) if mask > 0]
        return [[shares[0], *come]], [other for other in dims if other != d]

    def scatter_rest(self, state):
        for d in self.rest:
            state = self.scatter(*state, d)
        total = 0.0
        for array in state[0][0]:
            total = total + array.astype(F32)
        return total[0]

    def begin_gather(self, state, d):
        array, dims = state
        come = [self.send(array, d, mask) for mask in range(1, self.counts([d])[0])]
        return array, come, dims, d

    def end_gather(self, begun, tick=None):
        array, come, dims, d = begun
        parts = [array] + come
        for bit in range(len(parts).bit_length() - 1):
            flag = (self.place(d) >> bit) & 1
            for low in range(len(parts)):
                if not low & (1 << bit):
                    high = low | (1 << bit)
                    parts[low], parts[high] = pick(flag, parts[low], parts[high])
        dims = [other for other in self.dims if other in dims or other == d]
        joined = jnp.stack(parts, axis=dims.index(d))
        if tick is not None:
            joined = joined + tick[0, 0].astype(joined.dtype)
        return joined, dims

    def gather(self, state, d, tick=None):
        return self.end_gather(self.begin_gather(state, d), tick)

def body(
    tokens,
    segments,
    ln1_gain,
    ln1_bias,
    qkv_weight,
    q_bias,
    v_bias,
    out_weight,
    out_bias,
    ln2_gain,
    ln2_bias,
    up_weight,
    up_bias,
    down_weight,
    down_bias,
    cotangent,
):
    side = lax.axis_index("xx")
    core = lax.axis_index("core")
    chips = lax.axis_size("dp") * lax.axis_size("xx")
    seq_count, quarter, width = tokens.shape
    length = segments.shape[1]
    own = qkv_weight.shape[0]
    pair_row = 2 * own
    hidden_own = up_bias.shape[0]
    half = width // 2
    cols = 3 * half
    pairs = half // PAIR
    splits = hidden_own // pair_row
    hidden = splits * width

    def at_index(array, index):
        return lax.dynamic_index_in_dim(array, index, 0, keepdims=False)

    def to_sequence(array, tick=None, core_tick=None):
        kept = at_index(array, side)
        sent = at_index(array, 1 - side)
        if tick is not None:
            sent = sent + tick[0, 0].astype(sent.dtype)
        come = swap(sent, "xx")
        low, high = pick(side, kept, come)
        mine = jnp.stack([low, high])
        if core_tick is not None:
            mine = mine + core_tick[0, 0].astype(mine.dtype)
        other = swap(mine, "core")
        even, odd = pick(core, mine, other)
        return jnp.stack([even, odd], axis=1).reshape(length, width), come, other

    def own_rows(array):
        return lax.dynamic_index_in_dim(
            array.reshape(2, 2, quarter, array.shape[-1]), core, 1, keepdims=False
        )

    def other_rows(array):
        return lax.dynamic_index_in_dim(
            array.reshape(2, 2, quarter, array.shape[-1]), 1 - core, 1, keepdims=False
        )

    def from_sequence(mine):
        come = swap(at_index(mine, 1 - side), "xx")
        return merged(at_index(mine, side), come), come

    def merged(kept, come, tick=None):
        if tick is not None:
            kept = kept + tick[0, 0].astype(kept.dtype)
        first, second = pick(side, kept, come)
        return jnp.stack([first, second])

    qkv_cols = qkv_weight.reshape(own, 3, 2, pairs, PAIR).transpose(2, 0, 3, 1, 4).reshape(2, own, cols)
    up_cols = (
        up_weight.reshape(own, chips, 2, splits, pair_row)
        .transpose(2, 0, 3, 1, 4)
        .reshape(2, own, hidden)
    )
    vectors = jnp.stack(
        [ln1_gain, ln1_bias, q_bias, v_bias, out_bias, ln2_gain, ln2_bias, down_bias], axis=1
    )
    vectors = jnp.pad(vectors, ((0, 0), (0, PAIR - vectors.shape[1])))

    def with_partner(two):
        mine, theirs = at_index(two, core), at_index(two, 1 - core)
        first, second = pick(core, mine, swap(theirs, "core"))
        return jnp.concatenate([first, second], axis=0)

    early = with_partner(
        jnp.concatenate([qkv_cols, jnp.broadcast_to(vectors, (2, own, PAIR))], axis=2)
    )
    early = jnp.concatenate(
        [
            early[:, : cols + 8],
            up_bias.reshape(splits, pair_row).T,
            early[:, cols + 8 + splits :],
        ],
        axis=1,
    )
    links = Links()

    def gather_rest(array, tick=None):
        state = (array, [])
        for d in links.rest:
            state = links.gather(state, d, tick if d == links.rest[-1] else None)
        return state

    def halves_of(state):
        middle = state[0].shape[-1] // 2
        return [(state[0][..., :middle], state[1]), (state[0][..., middle:], state[1])]

    def joined(halves):
        return [half_state[0].reshape(width, -1) for half_state in halves]

    inputs_low, come, other = to_sequence(tokens)
    state = (early, [])
    for d in links.rest[:-1]:
        state = links.gather(state, d)
    first_stage = links.begin_gather(state, links.rest[-1])
    begun = [
        links.begin_gather(piece, d)
        for piece, d in zip(halves_of(links.end_gather(first_stage)), "yx")
    ]
    early_halves = [links.end_gather(piece) for piece in begun]
    early_a, early_b = joined(
        [links.gather(piece, d) for piece, d in zip(early_halves, "xy")]
    )
    split = early_a.shape[1]
    late = with_partner(
        jnp.concatenate([up_cols, jnp.broadcast_to(out_weight, (2, own, width))], axis=2)
    )
    down_own = down_weight.reshape(splits, pair_row, width)
    late = pack(
        [late, *(down_own[i] for i in range(splits))], [block for block in first_stage[1]] + [come]
    )
    late_come = swap(late, "xx")
    late = jnp.concatenate(pick(side, late, late_come), axis=0)
    late = lax.all_gather(late, "dp", axis=0, tiled=True)
    small = early_b[:, cols - split :].astype(F32).T
    gain_one, shift_one, query_shift, value_shift, out_shift, gain_two, shift_two, down_shift = (
        small[i] for i in range(8)
    )
    up_shift = small[8 : 8 + splits].reshape(hidden)

    inputs = inputs_low.astype(F32)
    seg = at_index(segments, side)
    numbers = jnp.arange(PAIR, dtype=jnp.int32) % HEAD_DIM
    same = seg[:, None] == numbers[None, :]
    coded = numbers[None, :] < 4
    query_code = jnp.where(same & coded, 1.0, 0.0).astype(BF16)
    key_code = jnp.where(same | ~coded, 0.0, NEG).astype(BF16)

    def head_cols(vector):
        return lax.dynamic_slice_in_dim(vector, core * half, half, 0).reshape(pairs, 1, PAIR)

    zeros = jnp.zeros((pairs, 1, PAIR), F32)
    qkv_shift = jnp.concatenate(
        [head_cols(query_shift), zeros, head_cols(value_shift)], axis=1
    ).reshape(1, cols)
    qkv_scale = jnp.tile(jnp.repeat(jnp.array([0.125, 1.0, 1.0], F32), PAIR), pairs)[None]
    normed_t, qkv, tick = qkv_projection(
        inputs_low,
        early_a,
        early_b,
        jnp.pad(jnp.stack([gain_one, shift_one]), ((0, 6), (0, 0))),
        jnp.pad(jnp.concatenate([qkv_shift, qkv_scale]), ((0, 6), (0, 0))),
        [],
    )
    grad_out_low, _, _ = to_sequence(cotangent, gate([late_come]), tick)
    attended, log_total, _ = attention_forward(qkv, query_code, key_code)
    core_at = core.reshape(1).astype(jnp.int32)
    branch = out_projection(core_at, attended, late, splits, [grad_out_low])
    branch_come = swap(branch, "core")
    mid_vectors = jnp.pad(
        jnp.stack([out_shift, gain_two, shift_two, down_shift]), ((0, 4), (0, 0))
    )
    normed_two_low, hidden_low, grad_pre_low, mixed_part, ffn_other, partial_two, up_sums = feed_forward(
        core_at,
        inputs_low,
        branch,
        branch_come,
        grad_out_low,
        late,
        splits,
        mid_vectors,
        jnp.pad(up_shift[None], ((0, 7), (0, 0))),
    )
    partial_come = swap(partial_two, "core")
    mixed_own = (mixed_part + swap(ffn_other, "core").astype(F32)).astype(BF16)
    mixed_own = mixed_own.reshape(2, quarter, width)
    mixed_come = swap(at_index(mixed_own, 1 - side), "xx")

    def blocks(array):
        return array.reshape(chips, pair_row, array.shape[1])

    grad_proj_down = [
        mm(hidden_low[:, i * width : (i + 1) * width], grad_out_low, TN).astype(BF16)
        for i in range(splits)
    ]
    grad_proj_up = mm(normed_two_low, grad_pre_low, TN).astype(BF16)
    late_piece = links.scatter(
        [[blocks(grad_proj_up)], *([blocks(part)] for part in grad_proj_down)], links.dims, "x"
    )
    grad_middle, branch_low, grad_attended, mid_sums = norm_two(
        core_at,
        inputs_low,
        branch,
        branch_come,
        grad_out_low,
        partial_two,
        partial_come,
        late,
        splits,
        mid_vectors,
        [late_piece[0][0][0]],
    )
    grad_proj_out = mm(attended, branch_low, TN)

    def as_column(vectors):
        table = jnp.stack(vectors, axis=1)
        return jnp.pad(table, ((0, 0), (0, PAIR - table.shape[1])))

    def only_mine(flag, array):
        return jnp.where(flag, array, jnp.zeros_like(array))

    small_two = [mid_sums[i] for i in range(4)] + [
        up_sums[0, i * width : (i + 1) * width] for i in range(splits)
    ]
    out_low = grad_proj_out.astype(BF16)
    grad_out_rows = jnp.concatenate(
        [only_mine(core == 0, out_low), only_mine(core == 1, out_low)], axis=0
    )

    def pairs_backward(first, count, after):
        return attention_backward(
            first, count, qkv, query_code, key_code, attended, grad_attended, log_total, normed_t, after
        )

    out_piece = links.scatter([[blocks(grad_out_rows)]], links.dims, "y")
    (late_sum,) = fold(late_piece[0], [chips // 2], None, side, [mid_sums])
    late_own = lax.psum_scatter(
        late_sum.reshape(width // 2, -1),
        "dp",
        scatter_dimension=0,
        tiled=True,
    )
    grad_a, weight_grad_a, tick = pairs_backward(0, pairs - 1, [out_piece[0][0][0], late_sum])
    first_piece = links.scatter([[blocks(weight_grad_a)]], links.dims, "y", [tick])
    mixed = merge(at_index(mixed_own, side), mixed_come, side, [tick])
    grad_b, weight_grad_b, tick = pairs_backward(
        pairs - 1, 1, [first_piece[0][0][0], tick, mixed]
    )
    grads = [grad_a, grad_b]
    first_piece = links.scatter(out_piece[0] + first_piece[0], first_piece[1], "x", [tick])
    last_piece = links.scatter([[blocks(weight_grad_b)]], links.rest + ["yx"], "yx", [tick])
    norm_vectors = jnp.pad(jnp.stack([gain_one, shift_one]), ((0, 6), (0, 0)))
    partial_one, norm_sums, bias_sums, tick = norm_one(
        False, core_at, grads, early_a, early_b, cols, inputs_low, [], [first_piece[0][0][0], last_piece[0][0][0]]
    )
    come = swap(partial_one, "core")
    token_own, norm_sums_own, bias_sums_own, tick = norm_one(
        True,
        core_at,
        grads,
        early_a,
        early_b,
        cols,
        inputs_low,
        [come, grad_middle, norm_vectors],
        [late_own],
    )
    norm_sums = norm_sums + norm_sums_own
    bias_sums = bias_sums + bias_sums_own
    token_grad, come = from_sequence(token_own.reshape(2, quarter, width))
    grad_by_pair = bias_sums[0].reshape(pairs, 3, PAIR)

    def padded(vector):
        vector = vector.reshape(half)
        return jnp.concatenate([only_mine(core == 0, vector), only_mine(core == 1, vector)])

    small = as_column(
        [
            norm_sums[0],
            norm_sums[1],
            padded(grad_by_pair[:, 0]),
            padded(grad_by_pair[:, 2]),
        ]
        + small_two
    )
    small_piece = links.scatter([[blocks(small.astype(BF16))]], links.rest + ["yx"], "yx", [tick])
    first_own = links.scatter_rest(
        (first_piece[0] + last_piece[0] + small_piece[0], first_piece[1])
    )

    def rows_of(array, index):
        return lax.dynamic_slice_in_dim(array, index * own, own, 0)

    def by_core(mine, come):
        return jnp.stack(pick(core, mine, come))

    def shared(array):
        return rows_of(array, core), swap(rows_of(array, 1 - core), "core")

    up_own, down_grad = widen(late_own, width, [])
    late_mine, late_come = shared(up_own)
    early_mine, early_come = shared(first_own)
    out_grad = early_mine[:, :width].astype(F32) + early_come[:, :width].astype(F32)
    up_grad = (
        by_core(late_mine, late_come)
        .reshape(2, own, splits, chips, pair_row)
        .transpose(1, 3, 0, 2, 4)
        .reshape(own, 2 * hidden)
        .astype(F32)
    )
    down_grad = down_grad.reshape(hidden_own, width)
    qkv_grad = (
        by_core(early_mine[:, width : width + cols], early_come[:, width : width + cols])
        .reshape(2, own, pairs, 3, PAIR)
        .transpose(1, 3, 0, 2, 4)
        .reshape(own, 2 * cols)
        .astype(F32)
    )
    tail = width + cols + 8
    small_mine = early_mine[:, tail - 8 : tail].astype(F32)
    one = small_mine[:, :4] + early_come[:, tail - 8 : tail - 4].astype(F32)
    up_shift_grad = (
        first_own[:, tail : tail + splits].T.reshape(hidden_own).astype(F32)
    )
    two = small_mine[:, 4:]
    return (
        mixed,
        token_grad,
        one[:, 0],
        one[:, 1],
        qkv_grad,
        one[:, 2],
        one[:, 3],
        out_grad,
        two[:, 0],
        two[:, 1],
        two[:, 2],
        up_grad,
        up_shift_grad,
        down_grad,
        two[:, 3],
    )


def solution(mesh):
    parts = (mesh.shape["dp"], mesh.shape["ctx"] // 2, 2)
    split_mesh = Mesh(mesh.devices.reshape(parts), ("dp", "xx", "core"))
    rows = ("dp", "xx", "core")
    acts = P("dp", ("xx", "core"), None)
    vec, mat = P(rows), P(rows, None)
    return jax.shard_map(
        body,
        mesh=split_mesh,
        in_specs=(
            acts, P("dp", None), vec, vec, mat, vec, vec, mat, vec, vec, vec, mat, vec, mat, vec, acts,
        ),
        out_specs=(
            acts, acts, vec, vec, mat, vec, vec, mat, vec, vec, vec, mat, vec, mat, vec,
        ),
        check_vma=False,
    )
```

```python
import functools

import jax
import jax.numpy as jnp
from jax import lax
from jax.experimental import pallas as pl
from jax.experimental.pallas import tpu as pltpu
from jax.sharding import Mesh, PartitionSpec as P

HEAD_DIM = 64
PAIR = 2 * HEAD_DIM
EPSILON = 1e-05
NEG = -1e30
BLK = 512
F32 = jnp.float32
BF16 = jnp.bfloat16

NN = (((1,), (0,)), ((), ()))
NT = (((1,), (1,)), ((), ()))
TN = (((0,), (0,)), ((), ()))


def mm(left, right, dims=NN):
    return lax.dot_general(left, right, dims, preferred_element_type=F32)


def build_scores_operands(qkv_ref, qs_ref, ks_ref, rows, qx, kx):
    lane = lax.broadcasted_iota(jnp.int32, (BLK, PAIR), 1)
    first = lane < HEAD_DIM
    q = qkv_ref[rows, 0:PAIR].astype(F32)
    k = qkv_ref[rows, PAIR : 2 * PAIR].astype(F32)
    qs = qs_ref[rows, :].astype(F32)
    ks = ks_ref[rows, :].astype(F32)
    qx[0, rows, :] = jnp.where(first, q, qs).astype(BF16)
    qx[1, rows, :] = jnp.where(first, qs, q).astype(BF16)
    kx[0, rows, :] = jnp.where(first, k, ks).astype(BF16)
    kx[1, rows, :] = jnp.where(first, ks, k).astype(BF16)
    return first, q, k


HALF = BLK // 2


def halves(i):
    start = pl.multiple_of(i * BLK, BLK)
    return pl.ds(start, HALF), pl.ds(pl.multiple_of(start + HALF, HALF), HALF)


def causal_block(scores):
    key_at = lax.broadcasted_iota(jnp.int32, scores.shape, 0)
    query_at = lax.broadcasted_iota(jnp.int32, scores.shape, 1)
    return jnp.where(key_at <= query_at, scores, NEG)


def attention_forward_kernel(qkv_ref, qs_ref, ks_ref, *rest):
    o_ref, lse_ref, tick_ref, qx, kx, vt, acc = rest[-7:]
    tick_ref[...] = jnp.zeros_like(tick_ref)
    length = qkv_ref.shape[0]
    blocks = length // BLK

    @pl.loop(0, blocks)
    def _(i):
        rows = pl.ds(pl.multiple_of(i * BLK, BLK), BLK)
        build_scores_operands(qkv_ref, qs_ref, ks_ref, rows, qx, kx)
        v_t = qkv_ref[rows, 2 * PAIR : 3 * PAIR].astype(F32).T
        ones = jnp.ones((16, BLK), BF16)
        for h in range(2):
            vt[h, 0:HEAD_DIM, rows] = v_t[h * HEAD_DIM : (h + 1) * HEAD_DIM].astype(BF16)
            vt[h, HEAD_DIM : HEAD_DIM + 16, rows] = ones

    @pl.loop(0, blocks)
    def _(i):
        rows = pl.ds(pl.multiple_of(i * BLK, BLK), BLK)
        low, high = halves(i)
        tops = []
        for h in range(2):
            s = causal_block(mm(kx[h, low, :], qx[h, low, :], NT))
            top_low = jnp.max(s, axis=0, keepdims=True)
            acc[h, :, 0:HALF] = mm(vt[h, :, low], jnp.exp(s - top_low).astype(BF16))
            full = mm(kx[h, low, :], qx[h, high, :], NT)
            s = causal_block(mm(kx[h, high, :], qx[h, high, :], NT))
            top = jnp.maximum(
                jnp.max(full, axis=0, keepdims=True), jnp.max(s, axis=0, keepdims=True)
            )
            acc[h, :, HALF:BLK] = mm(vt[h, :, low], jnp.exp(full - top).astype(BF16)) + mm(
                vt[h, :, high], jnp.exp(s - top).astype(BF16)
            )
            tops.append(jnp.concatenate([top_low, top], axis=1))

        def step(j, carry):
            keys = pl.ds(pl.multiple_of(j * BLK, BLK), BLK)
            out = []
            for h in range(2):
                s = mm(kx[h, keys, :], qx[h, rows, :], NT)
                top = jnp.maximum(carry[h], jnp.max(s, axis=0, keepdims=True))
                p = jnp.exp(s - top).astype(BF16)
                acc[h] = acc[h] * jnp.exp(carry[h] - top) + mm(vt[h, :, keys], p)
                out.append(top)
            return tuple(out)

        tops = lax.fori_loop(0, i, step, tuple(tops))
        parts = []
        for h in range(2):
            total = acc[h, HEAD_DIM : HEAD_DIM + 1, :]
            parts.append(acc[h, 0:HEAD_DIM, :] / total)
            lse_ref[0, h : h + 1, rows] = tops[h] + jnp.log(total)
        o_ref[rows, :] = jnp.concatenate(parts, axis=0).T.astype(BF16)


def attention_backward_kernel(qkv_ref, qs_ref, ks_ref, o_ref, do_ref, lse_ref, at_ref, *rest):
    d_ref, dw_ref, tick_ref, qx, kx, qm, dm, kt, delta, dqt, dk, dv = rest[-12:]
    tick_ref[...] = jnp.zeros_like(tick_ref)
    length = qkv_ref.shape[0]
    blocks = length // BLK

    @pl.loop(0, blocks)
    def _(i):
        rows = pl.ds(pl.multiple_of(i * BLK, BLK), BLK)
        first, q, k = build_scores_operands(qkv_ref, qs_ref, ks_ref, rows, qx, kx)
        do = do_ref[rows, :].astype(F32)
        zero = jnp.zeros_like(q)
        qm[0, rows, :] = jnp.where(first, q, zero).astype(BF16)
        qm[1, rows, :] = jnp.where(first, zero, q).astype(BF16)
        dm[0, rows, :] = jnp.where(first, do, zero).astype(BF16)
        dm[1, rows, :] = jnp.where(first, zero, do).astype(BF16)
        kt[:, rows] = k.T.astype(BF16)
        inner = (do * o_ref[rows, :].astype(F32)).T
        for h in range(2):
            delta[h : h + 1, rows] = jnp.sum(
                inner[h * HEAD_DIM : (h + 1) * HEAD_DIM], axis=0, keepdims=True
            )
        dqt[:, rows] = jnp.zeros((PAIR, BLK), F32)

    def tile(keys, rows, masked):
        values = qkv_ref[keys, 2 * PAIR : 3 * PAIR]
        dv_part, dk_part = None, None
        for h in range(2):
            s = mm(kx[h, keys, :], qx[h, rows, :], NT)
            if masked:
                s = causal_block(s)
            p = jnp.exp(s - lse_ref[0, h : h + 1, rows])
            dp = mm(values, dm[h, rows, :], NT)
            ds = (p * (dp - delta[h : h + 1, rows])).astype(BF16)
            dv_h = mm(p.astype(BF16), dm[h, rows, :])
            dk_h = mm(ds, qm[h, rows, :])
            dv_part = dv_h if h == 0 else dv_part + dv_h
            dk_part = dk_h if h == 0 else dk_part + dk_h
            part = slice(h * HEAD_DIM, (h + 1) * HEAD_DIM)
            dqt[part, rows] += mm(kt[part, keys], ds)
        return dk_part, dv_part

    @pl.loop(0, blocks)
    def _(j):
        keys = pl.ds(pl.multiple_of(j * BLK, BLK), BLK)
        low, high = halves(j)
        dk_low, dv_low = tile(low, low, True)
        dk_next, dv_next = tile(low, high, False)
        dk[0:HALF], dv[0:HALF] = dk_low + dk_next, dv_low + dv_next
        dk[HALF:BLK], dv[HALF:BLK] = tile(high, high, True)

        @pl.loop(j + 1, blocks)
        def _(i):
            dk_part, dv_part = tile(keys, pl.ds(pl.multiple_of(i * BLK, BLK), BLK), False)
            dk[...] += dk_part
            dv[...] += dv_part

        d_ref[keys, PAIR : 2 * PAIR] = dk[...].astype(BF16)
        d_ref[keys, 2 * PAIR : 3 * PAIR] = dv[...].astype(BF16)

    @pl.loop(0, blocks)
    def _(i):
        rows = pl.ds(pl.multiple_of(i * BLK, BLK), BLK)
        d_ref[rows, 0:PAIR] = (dqt[:, rows].T.astype(BF16).astype(F32) * 0.125).astype(BF16)

    @pl.loop(0, dw_ref.shape[0] // ROWS)
    def _(i):
        rows = pl.ds(pl.multiple_of(i * ROWS, ROWS), ROWS)
        dw_ref[rows, :] = mm(at_ref[rows, :], d_ref[...]).astype(BF16)


VMEM_LIMIT = 48 * 1024 * 1024


SMALL_COST = pl.CostEstimate(flops=1000, bytes_accessed=1000, transcendentals=0)


TICK = jax.ShapeDtypeStruct((8, 128), F32)
TICK_SPEC = pl.BlockSpec((8, 128), lambda i: (0, 0))
ANY_SPEC = pl.BlockSpec(memory_space=pl.ANY)


def pack_kernel(count, refs):
    refs[-1][...] = jnp.concatenate([ref[...] for ref in refs[:count]], axis=-1)


def pack(parts, after):
    rows = parts[0].shape[0]
    width = sum(part.shape[1] for part in parts)
    return pl.pallas_call(
        lambda *refs: pack_kernel(len(parts), refs),
        grid=(1,),
        in_specs=[pl.BlockSpec(part.shape, lambda i: (0, 0)) for part in parts]
        + [ANY_SPEC] * len(after),
        out_specs=pl.BlockSpec((rows, width), lambda i: (0, 0)),
        out_shape=jax.ShapeDtypeStruct((rows, width), BF16),
        compiler_params=pltpu.CompilerParams(vmem_limit_bytes=VMEM_LIMIT),
        cost_estimate=SMALL_COST,
    )(*parts, *after)


def widen(first, second, width):
    rows, cols = first.shape
    count = cols // width - 2

    def kernel(first_ref, second_ref, up_ref, down_ref):
        total = first_ref[...].astype(F32) + second_ref[...].astype(F32)
        up_ref[...] = total[:, : 2 * width]
        for i in range(count):
            down_ref[i] = total[:, (2 + i) * width : (3 + i) * width]

    return pl.pallas_call(
        kernel,
        grid=(1,),
        in_specs=[pl.BlockSpec((rows, cols), lambda i: (0, 0))] * 2,
        out_specs=[
            pl.BlockSpec((rows, 2 * width), lambda i: (0, 0)),
            pl.BlockSpec((count, rows, width), lambda i: (0, 0, 0)),
        ],
        out_shape=[
            jax.ShapeDtypeStruct((rows, 2 * width), F32),
            jax.ShapeDtypeStruct((count, rows, width), F32),
        ],
        compiler_params=pltpu.CompilerParams(vmem_limit_bytes=VMEM_LIMIT),
        cost_estimate=SMALL_COST,
    )(first, second)


def merge(kept, come, side, after):
    def kernel(side_ref, kept_ref, come_ref, *rest):
        mine = pl.program_id(0) == side_ref[0]

        @pl.when(mine)
        def _():
            rest[-1][0] = kept_ref[...]

        @pl.when(jnp.logical_not(mine))
        def _():
            rest[-1][0] = come_ref[...]

    whole = pl.BlockSpec(kept.shape, lambda i, side_ref: (0, 0))
    return pl.pallas_call(
        kernel,
        grid_spec=pltpu.PrefetchScalarGridSpec(
            num_scalar_prefetch=1,
            grid=(2,),
            in_specs=[whole, whole] + [ANY_SPEC] * len(after),
            out_specs=pl.BlockSpec((1, *kept.shape), lambda i, side_ref: (i, 0, 0)),
        ),
        out_shape=jax.ShapeDtypeStruct((2, *kept.shape), kept.dtype),
        compiler_params=pltpu.CompilerParams(vmem_limit_bytes=VMEM_LIMIT),
        cost_estimate=SMALL_COST,
    )(side.reshape(1).astype(jnp.int32), kept, come, *after)


def gate_kernel(*refs):
    refs[-1][...] = jnp.zeros_like(refs[-1])


def gate(after):
    return pl.pallas_call(
        gate_kernel,
        grid=(1,),
        in_specs=[ANY_SPEC] * len(after),
        out_specs=TICK_SPEC,
        out_shape=TICK,
        cost_estimate=SMALL_COST,
    )(*after)


def fold(pieces, sizes, axis, at, after):
    blocks, rows = pieces[0][0].shape[:2]
    width = sum(piece[0].shape[2] for piece in pieces)
    outs = sizes[axis] if axis is not None else 1
    inner = 1
    if axis is not None:
        for size in sizes[axis + 1 :]:
            inner *= size
    flat = [array for piece in pieces for array in piece]

    def spec(array, m):
        def index(j, at_ref):
            if axis is None:
                return j, 0, 0
            return (j // inner) * (outs * inner) + (at_ref[0] ^ m) * inner + j % inner, 0, 0

        return pl.BlockSpec((1, rows, array.shape[2]), index)

    def kernel(at_ref, *refs):
        for m in range(outs):
            left = list(refs[m * len(flat) : (m + 1) * len(flat)])
            sides = []
            for piece in pieces:
                value = left.pop(0)[0]
                for _ in piece[1:]:
                    value = value.astype(F32) + left.pop(0)[0].astype(F32)
                sides.append(value.astype(BF16))
            refs[len(refs) - outs + m][0] = jnp.concatenate(sides, axis=-1)

    out = pl.BlockSpec((1, rows, width), lambda j, at_ref: (j, 0, 0))
    return pl.pallas_call(
        kernel,
        grid_spec=pltpu.PrefetchScalarGridSpec(
            num_scalar_prefetch=1,
            grid=(blocks // outs,),
            in_specs=[spec(array, m) for m in range(outs) for array in flat]
            + [ANY_SPEC] * len(after),
            out_specs=[out] * outs,
        ),
        out_shape=[jax.ShapeDtypeStruct((blocks // outs, rows, width), BF16)] * outs,
        compiler_params=pltpu.CompilerParams(vmem_limit_bytes=VMEM_LIMIT),
        cost_estimate=SMALL_COST,
    )(at.reshape(1).astype(jnp.int32), *(flat * outs), *after)


def qkv_kernel(x_ref, wa_ref, wb_ref, vec_ref, col_ref, *rest_refs):
    a_ref, qkv_ref, tick_ref = rest_refs[-3:]
    split = wa_ref.shape[1]
    rest = qkv_ref.shape[1] - split
    for part in range(2):
        rows = slice(part * ROWS, (part + 1) * ROWS)
        normal, _ = norm_forward(x_ref[rows, :].astype(F32))
        normed = (normal * vec_ref[0:1, :] + vec_ref[1:2, :]).astype(BF16)
        a_ref[:, rows] = normed.astype(F32).T.astype(BF16)
        for w, cols in ((wa_ref[...], slice(0, split)), (wb_ref[:, :rest], slice(split, None))):
            shift, scale = col_ref[0:1, cols], col_ref[1:2, cols]
            qkv_ref[rows, cols] = ((mm(normed, w) + shift) * scale).astype(BF16)
    tick_ref[...] = jnp.zeros_like(tick_ref)


def qkv_projection(inputs, weight_a, weight_b, vectors, columns, after):
    length, width = inputs.shape
    cols = columns.shape[1]
    return pl.pallas_call(
        qkv_kernel,
        grid=(length // (2 * ROWS),),
        in_specs=[
            pl.BlockSpec((2 * ROWS, width), lambda i: (i, 0)),
            pl.BlockSpec(weight_a.shape, lambda i: (0, 0)),
            pl.BlockSpec(weight_b.shape, lambda i: (0, 0)),
            pl.BlockSpec(vectors.shape, lambda i: (0, 0)),
            pl.BlockSpec(columns.shape, lambda i: (0, 0)),
        ]
        + [ANY_SPEC] * len(after),
        out_specs=[
            pl.BlockSpec((width, 2 * ROWS), lambda i: (0, i)),
            pl.BlockSpec((2 * ROWS, cols), lambda i: (i, 0)),
            TICK_SPEC,
        ],
        out_shape=[
            jax.ShapeDtypeStruct((width, length), BF16),
            jax.ShapeDtypeStruct((length, cols), BF16),
            TICK,
        ],
        compiler_params=pltpu.CompilerParams(vmem_limit_bytes=VMEM_LIMIT),
        cost_estimate=SMALL_COST,
    )(inputs, weight_a, weight_b, vectors, columns, *after)


def out_projection(core, attended, late, block, after):
    length, cols = attended.shape
    width = late.shape[0]
    rows = length // 4

    def kernel(core_ref, a_ref, w_ref, *rest):
        rest[-1][...] = mm(a_ref[...], w_ref[...]).astype(BF16)

    return pl.pallas_call(
        kernel,
        grid_spec=pltpu.PrefetchScalarGridSpec(
            num_scalar_prefetch=1,
            grid=(4,),
            in_specs=[
                pl.BlockSpec((rows, cols), lambda i, core_ref: (i, 0)),
                pl.BlockSpec((cols, width), lambda i, core_ref: (core_ref[0], block)),
            ]
            + [ANY_SPEC] * len(after),
            out_specs=pl.BlockSpec((rows, width), lambda i, core_ref: (i, 0)),
        ),
        out_shape=jax.ShapeDtypeStruct((length, width), BF16),
        compiler_params=pltpu.CompilerParams(vmem_limit_bytes=VMEM_LIMIT),
        cost_estimate=SMALL_COST,
    )(core, attended, late, *after)


def middle_of(x_ref, b0_ref, b1_ref, vec_ref):
    both = b0_ref[...].astype(F32) + b1_ref[...].astype(F32)
    return x_ref[...].astype(F32) + both + vec_ref[0:1, :]


def feed_forward_kernel(splits, core_ref, x_ref, b0_ref, b1_ref, dy_ref, up_ref, *rest):
    down_refs, (vec_ref, shift_ref) = rest[:splits], rest[splits : splits + 2]
    a_ref, g_ref, du_ref, own_ref, other_ref, dh_ref, sums_ref = rest[splits + 2 :]
    at = pl.program_id(0)

    @pl.when(at == 0)
    def _():
        sums_ref[...] = jnp.zeros_like(sums_ref)

    middle = middle_of(x_ref, b0_ref, b1_ref, vec_ref)
    normal, _ = norm_forward(middle)
    normed = (normal * vec_ref[1:2, :] + vec_ref[2:3, :]).astype(BF16)
    a_ref[...] = normed
    dy = dy_ref[...]
    ffn, dh = None, None
    width = dy.shape[1]
    for i, down_ref in enumerate(down_refs):
        cols = slice(i * width, (i + 1) * width)
        up, down = up_ref[:, cols], down_ref[...]
        value, slope = gelu_parts(mm(normed, up) + shift_ref[0:1, cols])
        du = slope * mm(dy, down, NT)
        value, du = value.astype(BF16), du.astype(BF16)
        g_ref[:, cols] = value
        du_ref[:, cols] = du
        sums_ref[0:1, cols] += jnp.sum(du.astype(F32), axis=0, keepdims=True)
        ffn_part, dh_part = mm(value, down), mm(du, up, NT)
        ffn = ffn_part if i == 0 else ffn + ffn_part
        dh = dh_part if i == 0 else dh + dh_part
    dh_ref[...] = dh.astype(BF16)
    mine = at % 2 == core_ref[0]

    @pl.when(mine)
    def _():
        own_ref[...] = middle_of(x_ref, b0_ref, b1_ref, vec_ref) + ffn + vec_ref[3:4, :]

    @pl.when(jnp.logical_not(mine))
    def _():
        other_ref[...] = ffn.astype(BF16)


def feed_forward(core, inputs, branch, branch_come, grad_out, late, splits, vectors, up_shift):
    length, width = inputs.shape
    rows = length // 4
    hidden = splits * width
    narrow = pl.BlockSpec((rows, width), lambda i, core_ref: (i, 0))
    wide = pl.BlockSpec((rows, hidden), lambda i, core_ref: (i, 0))
    shared = pl.BlockSpec((rows, width), lambda i, core_ref: (i // 2, 0))

    def whole(array):
        return pl.BlockSpec(array.shape, lambda i, core_ref: (0, 0))

    def down(i):
        return pl.BlockSpec((width, width), lambda _, core_ref: (0, splits + 1 + i))

    return pl.pallas_call(
        functools.partial(feed_forward_kernel, splits),
        grid_spec=pltpu.PrefetchScalarGridSpec(
            num_scalar_prefetch=1,
            grid=(4,),
            in_specs=[narrow] * 4
            + [pl.BlockSpec((width, hidden), lambda i, core_ref: (0, 0))]
            + [down(i) for i in range(splits)]
            + [whole(vectors), whole(up_shift)],
            out_specs=[
                narrow, wide, wide, shared, shared, narrow,
                pl.BlockSpec((8, hidden), lambda i, core_ref: (0, 0)),
            ],
        ),
        out_shape=[
            jax.ShapeDtypeStruct((length, width), BF16),
            jax.ShapeDtypeStruct((length, hidden), BF16),
            jax.ShapeDtypeStruct((length, hidden), BF16),
            jax.ShapeDtypeStruct((length // 2, width), F32),
            jax.ShapeDtypeStruct((length // 2, width), BF16),
            jax.ShapeDtypeStruct((length, width), BF16),
            jax.ShapeDtypeStruct((8, hidden), F32),
        ],
        compiler_params=pltpu.CompilerParams(vmem_limit_bytes=VMEM_LIMIT),
        cost_estimate=SMALL_COST,
    )(core, inputs, branch, branch_come, grad_out, late, *([late] * splits), vectors, up_shift)


def norm_two_kernel(core_ref, x_ref, b0_ref, b1_ref, dy_ref, p0_ref, p1_ref, w_ref, vec_ref, *rest):
    mid_ref, low_ref, do_ref, sums_ref = rest[-4:]

    @pl.when(pl.program_id(0) == 0)
    def _():
        sums_ref[...] = jnp.zeros_like(sums_ref)

    normal, scale = norm_forward(middle_of(x_ref, b0_ref, b1_ref, vec_ref))
    grad = p0_ref[...].astype(F32) + p1_ref[...].astype(F32)
    dy = dy_ref[...].astype(F32)
    mid = dy + norm_backward(normal, scale, grad * vec_ref[1:2, :])
    low = mid.astype(BF16)
    low_ref[...] = low
    do_ref[...] = mm(low, w_ref[...], NT).astype(BF16)
    for i, value in enumerate((low.astype(F32), grad * normal, grad, dy)):
        sums_ref[i : i + 1, :] += jnp.sum(value, axis=0, keepdims=True)

    @pl.when(pl.program_id(0) % 2 == core_ref[0])
    def _():
        mid_ref[...] = mid


def norm_two(core, inputs, branch, branch_come, grad_out, partial, partial_come, late, block, vectors, after):
    length, width = inputs.shape
    rows = length // 4
    cols = width // 2
    narrow = pl.BlockSpec((rows, width), lambda i, core_ref: (i, 0))
    return pl.pallas_call(
        norm_two_kernel,
        grid_spec=pltpu.PrefetchScalarGridSpec(
            num_scalar_prefetch=1,
            grid=(4,),
            in_specs=[narrow] * 6
            + [
                pl.BlockSpec((cols, width), lambda i, core_ref: (core_ref[0], block)),
                pl.BlockSpec(vectors.shape, lambda i, core_ref: (0, 0)),
            ]
            + [ANY_SPEC] * len(after),
            out_specs=[
                pl.BlockSpec((rows, width), lambda i, core_ref: (i // 2, 0)),
                narrow,
                pl.BlockSpec((rows, cols), lambda i, core_ref: (i, 0)),
                pl.BlockSpec((8, width), lambda i, core_ref: (0, 0)),
            ],
        ),
        out_shape=[
            jax.ShapeDtypeStruct((length // 2, width), F32),
            jax.ShapeDtypeStruct((length, width), BF16),
            jax.ShapeDtypeStruct((length, cols), BF16),
            jax.ShapeDtypeStruct((8, width), F32),
        ],
        compiler_params=pltpu.CompilerParams(vmem_limit_bytes=VMEM_LIMIT),
        cost_estimate=SMALL_COST,
    )(core, inputs, branch, branch_come, grad_out, partial, partial_come, late, vectors, *after)


ROWS = 256


def attention_forward(qkv, query_code, key_code, after):
    length, width = qkv.shape
    pairs = width // (3 * PAIR)
    return pl.pallas_call(
        attention_forward_kernel,
        grid=(pairs,),
        in_specs=[
            pl.BlockSpec((length, 3 * PAIR), lambda p: (0, p)),
            pl.BlockSpec((length, PAIR), lambda p: (0, 0)),
            pl.BlockSpec((length, PAIR), lambda p: (0, 0)),
        ]
        + [ANY_SPEC] * len(after),
        out_specs=[
            pl.BlockSpec((length, PAIR), lambda p: (0, p)),
            pl.BlockSpec((1, 8, length), lambda p: (p, 0, 0)),
            TICK_SPEC,
        ],
        out_shape=[
            jax.ShapeDtypeStruct((length, pairs * PAIR), BF16),
            jax.ShapeDtypeStruct((pairs, 8, length), F32),
            TICK,
        ],
        scratch_shapes=[
            pltpu.VMEM((2, length, PAIR), BF16),
            pltpu.VMEM((2, length, PAIR), BF16),
            pltpu.VMEM((2, HEAD_DIM + 16, length), BF16),
            pltpu.VMEM((2, HEAD_DIM + 16, BLK), F32),
        ],
        compiler_params=pltpu.CompilerParams(vmem_limit_bytes=VMEM_LIMIT),
        cost_estimate=SMALL_COST,
    )(qkv, query_code, key_code, *after)


def norm_one_kernel(own, core_ref, d0_ref, d1_ref, wa_ref, wb_ref, x_ref, *rest):
    if own:
        come_ref, mid_ref, vec_ref, out_ref, sums_ref, bias_ref, tick_ref, w = rest
    else:
        out_ref, sums_ref, bias_ref, tick_ref, w = rest
    split = wa_ref.shape[1]

    @pl.when(pl.program_id(0) == 0)
    def _():
        sums_ref[...] = jnp.zeros_like(sums_ref)
        bias_ref[...] = jnp.zeros_like(bias_ref)
        w[:, :split] = wa_ref[...]
        w[:, split:] = wb_ref[:, : w.shape[1] - split]
        tick_ref[...] = jnp.zeros_like(tick_ref)

    total = None
    for i, ref in enumerate((d0_ref, d1_ref)):
        cols = slice(0, ref.shape[1]) if i == 0 else slice(d0_ref.shape[1], None)
        grad = ref[...]
        part = mm(grad, w[:, cols], NT)
        total = part if i == 0 else total + part
        bias_ref[0:1, cols] += jnp.sum(grad.astype(F32), axis=0, keepdims=True)
    normal, scale = norm_forward(x_ref[...].astype(F32))
    sums_ref[0:1, :] += jnp.sum(total * normal, axis=0, keepdims=True)
    sums_ref[1:2, :] += jnp.sum(total, axis=0, keepdims=True)
    if own:
        grad = (total + come_ref[...].astype(F32)) * vec_ref[0:1, :]
        out_ref[...] = (mid_ref[...] + norm_backward(normal, scale, grad)).astype(BF16)
    else:
        out_ref[...] = total.astype(BF16)


def norm_one(own, core, grads, weight_a, weight_b, cols, inputs, extra, after):
    length, width = inputs.shape
    count = length // (2 * ROWS)
    per = count // 2

    def block(i, core_ref):
        which = core_ref[0] if own else 1 - core_ref[0]
        return ((i // per) * 2 + which) * per + i % per, 0

    def at_zero(i, core_ref):
        return 0, 0

    plain = pl.BlockSpec((ROWS, width), lambda i, core_ref: (i, 0))
    rows = pl.BlockSpec((ROWS, width), block)
    in_specs = [pl.BlockSpec((ROWS, grad.shape[1]), block) for grad in grads] + [
        pl.BlockSpec(weight_a.shape, at_zero),
        pl.BlockSpec(weight_b.shape, at_zero),
        rows,
    ]
    out_specs = [
        plain,
        pl.BlockSpec((8, width), at_zero),
        pl.BlockSpec((8, cols), at_zero),
        pl.BlockSpec((8, 128), at_zero),
    ]
    out_shape = [
        jax.ShapeDtypeStruct((count * ROWS, width), BF16),
        jax.ShapeDtypeStruct((8, width), F32),
        jax.ShapeDtypeStruct((8, cols), F32),
        TICK,
    ]
    if own:
        in_specs += [plain, plain, pl.BlockSpec(extra[2].shape, at_zero)]

    def kernel(*refs):
        inner = refs[: 1 + len(in_specs)] + refs[1 + len(in_specs) + len(after) :]
        norm_one_kernel(own, *inner)

    return pl.pallas_call(
        kernel,
        grid_spec=pltpu.PrefetchScalarGridSpec(
            num_scalar_prefetch=1,
            grid=(count,),
            in_specs=in_specs + [ANY_SPEC] * len(after),
            out_specs=out_specs,
            scratch_shapes=[pltpu.VMEM((width, cols), BF16)],
        ),
        out_shape=out_shape,
        compiler_params=pltpu.CompilerParams(vmem_limit_bytes=VMEM_LIMIT),
        cost_estimate=SMALL_COST,
    )(core, *grads, weight_a, weight_b, inputs, *extra, *after)


def attention_backward(
    first, count, qkv, query_code, key_code, attended, grad_attended, log_total, normed_t, after
):
    length = qkv.shape[0]
    width = normed_t.shape[0]
    return pl.pallas_call(
        attention_backward_kernel,
        grid=(count,),
        in_specs=[
            pl.BlockSpec((length, 3 * PAIR), lambda p: (0, first + p)),
            pl.BlockSpec((length, PAIR), lambda p: (0, 0)),
            pl.BlockSpec((length, PAIR), lambda p: (0, 0)),
            pl.BlockSpec((length, PAIR), lambda p: (0, first + p)),
            pl.BlockSpec((length, PAIR), lambda p: (0, first + p)),
            pl.BlockSpec((1, 8, length), lambda p: (first + p, 0, 0)),
            pl.BlockSpec(normed_t.shape, lambda p: (0, 0)),
        ]
        + [ANY_SPEC] * len(after),
        out_specs=[
            pl.BlockSpec((length, 3 * PAIR), lambda p: (0, p)),
            pl.BlockSpec((width, 3 * PAIR), lambda p: (0, p)),
            TICK_SPEC,
        ],
        out_shape=[
            jax.ShapeDtypeStruct((length, count * 3 * PAIR), BF16),
            jax.ShapeDtypeStruct((width, count * 3 * PAIR), BF16),
            TICK,
        ],
        scratch_shapes=[
            pltpu.VMEM((2, length, PAIR), BF16),
            pltpu.VMEM((2, length, PAIR), BF16),
            pltpu.VMEM((2, length, PAIR), BF16),
            pltpu.VMEM((2, length, PAIR), BF16),
            pltpu.VMEM((PAIR, length), BF16),
            pltpu.VMEM((8, length), F32),
            pltpu.VMEM((PAIR, length), F32),
            pltpu.VMEM((BLK, PAIR), F32),
            pltpu.VMEM((BLK, PAIR), F32),
        ],
        compiler_params=pltpu.CompilerParams(vmem_limit_bytes=VMEM_LIMIT),
        cost_estimate=SMALL_COST,
    )(qkv, query_code, key_code, attended, grad_attended, log_total, normed_t, *after)


def norm_forward(source):
    average = jnp.mean(source, axis=-1, keepdims=True)
    centred = source - average
    spread = jnp.mean(centred * centred, axis=-1, keepdims=True)
    scale = lax.rsqrt(spread + EPSILON)
    return centred * scale, scale


def norm_backward(normal, scale, grad):
    return scale * (
        grad
        - jnp.mean(grad, axis=-1, keepdims=True)
        - normal * jnp.mean(grad * normal, axis=-1, keepdims=True)
    )


GELU_A = 0.7978845608028654
GELU_B = 0.044715


def gelu_parts(source):
    square = source * source
    inner = jnp.tanh(GELU_A * (source + GELU_B * source * square))
    value = 0.5 * source * (1.0 + inner)
    slope = 0.5 * (1.0 + inner) + 0.5 * source * (1.0 - inner * inner) * (
        GELU_A * (1.0 + 3.0 * GELU_B * square)
    )
    return value, slope


def swap(value, axis):
    return lax.ppermute(value, axis, [(0, 1), (1, 0)])


def pick(flag, first, second):
    return jnp.where(flag == 0, first, second), jnp.where(flag == 0, second, first)


class Links:
    def __init__(self):
        self.size = lax.axis_size("dp")
        at = lax.axis_index("dp")
        self.groups = {}
        shift, name = 0, "y"
        while (1 << shift) < self.size:
            bits = 1 if shift == 0 else min(2, self.size.bit_length() - 1 - shift)
            self.groups[name] = (shift, bits, (at >> shift) & ((1 << bits) - 1))
            shift += bits
            name = "z" + str(shift)
        self.rest = [name for name in reversed(self.groups) if name != "y"]
        self.dims = self.rest + ["y", "x"]
        self.side = lax.axis_index("xx")

    def counts(self, dims):
        return [{"x": 2, "yx": 4}.get(d) or 1 << self.groups[d][1] for d in dims]

    def send(self, value, d, mask):
        if d == "x":
            return swap(value, "xx")
        if d == "yx":
            return lax.ppermute(
                value, ("dp", "xx"), [(i, i ^ mask) for i in range(2 * self.size)]
            )
        move = mask << self.groups[d][0]
        return lax.ppermute(value, "dp", [(i, i ^ move) for i in range(self.size)])

    def place(self, d):
        if d == "yx":
            return self.groups["y"][2] * 2 + self.side
        return self.side if d == "x" else self.groups[d][2]

    def scatter(self, pieces, dims, d, after=()):
        axis = dims.index(d)
        shares = fold(pieces, self.counts(dims), axis, self.place(d), list(after))
        come = [self.send(share, d, mask) for mask, share in enumerate(shares) if mask > 0]
        return [[shares[0], *come]], [other for other in dims if other != d]

    def scatter_rest(self, state, start=0):
        for d in self.rest[start:]:
            state = self.scatter(*state, d)
        total = 0.0
        for array in state[0][0]:
            total = total + array.astype(F32)
        return total[0]

    def begin_gather(self, state, d):
        array, dims = state
        come = [self.send(array, d, mask) for mask in range(1, self.counts([d])[0])]
        return array, come, dims, d

    def end_gather(self, begun, tick=None):
        array, come, dims, d = begun
        parts = [array] + come
        for bit in range(len(parts).bit_length() - 1):
            flag = (self.place(d) >> bit) & 1
            for low in range(len(parts)):
                if not low & (1 << bit):
                    high = low | (1 << bit)
                    parts[low], parts[high] = pick(flag, parts[low], parts[high])
        dims = [other for other in self.dims if other in dims or other == d]
        joined = jnp.stack(parts, axis=dims.index(d))
        if tick is not None:
            joined = joined + tick[0, 0].astype(joined.dtype)
        return joined, dims

    def gather(self, state, d, tick=None):
        return self.end_gather(self.begin_gather(state, d), tick)

def body(
    tokens,
    segments,
    ln1_gain,
    ln1_bias,
    qkv_weight,
    q_bias,
    v_bias,
    out_weight,
    out_bias,
    ln2_gain,
    ln2_bias,
    up_weight,
    up_bias,
    down_weight,
    down_bias,
    cotangent,
):
    side = lax.axis_index("xx")
    core = lax.axis_index("core")
    chips = lax.axis_size("dp") * lax.axis_size("xx")
    seq_count, quarter, width = tokens.shape
    length = segments.shape[1]
    own = qkv_weight.shape[0]
    pair_row = 2 * own
    hidden_own = up_bias.shape[0]
    half = width // 2
    cols = 3 * half
    pairs = half // PAIR
    splits = hidden_own // pair_row
    hidden = splits * width

    def at_index(array, index):
        return lax.dynamic_index_in_dim(array, index, 0, keepdims=False)

    def to_sequence(array, tick=None):
        kept = at_index(array, side)
        sent = at_index(array, 1 - side)
        if tick is not None:
            sent = sent + tick[0, 0].astype(sent.dtype)
        come = swap(sent, "xx")
        low, high = pick(side, kept, come)
        mine = jnp.stack([low, high])
        other = swap(mine, "core")
        even, odd = pick(core, mine, other)
        return jnp.stack([even, odd], axis=1).reshape(length, width), come, other

    def own_rows(array):
        return lax.dynamic_index_in_dim(
            array.reshape(2, 2, quarter, array.shape[-1]), core, 1, keepdims=False
        )

    def other_rows(array):
        return lax.dynamic_index_in_dim(
            array.reshape(2, 2, quarter, array.shape[-1]), 1 - core, 1, keepdims=False
        )

    def from_sequence(mine):
        come = swap(at_index(mine, 1 - side), "xx")
        return merged(at_index(mine, side), come), come

    def merged(kept, come, tick=None):
        if tick is not None:
            kept = kept + tick[0, 0].astype(kept.dtype)
        first, second = pick(side, kept, come)
        return jnp.stack([first, second])

    qkv_cols = qkv_weight.reshape(own, 3, 2, pairs, PAIR).transpose(2, 0, 3, 1, 4).reshape(2, own, cols)
    up_cols = (
        up_weight.reshape(own, chips, 2, splits, pair_row)
        .transpose(2, 0, 3, 1, 4)
        .reshape(2, own, hidden)
    )
    vectors = jnp.stack(
        [ln1_gain, ln1_bias, q_bias, v_bias, out_bias, ln2_gain, ln2_bias, down_bias], axis=1
    )
    vectors = jnp.pad(vectors, ((0, 0), (0, PAIR - vectors.shape[1])))

    def with_partner(two):
        mine, theirs = at_index(two, core), at_index(two, 1 - core)
        first, second = pick(core, mine, swap(theirs, "core"))
        return jnp.concatenate([first, second], axis=0)

    early = with_partner(
        jnp.concatenate([qkv_cols, jnp.broadcast_to(vectors, (2, own, PAIR))], axis=2)
    )
    early = jnp.concatenate(
        [
            early[:, : cols + 8],
            up_bias.reshape(splits, pair_row).T,
            early[:, cols + 8 + splits :],
        ],
        axis=1,
    )
    links = Links()

    def gather_rest(array, tick=None):
        state = (array, [])
        for d in links.rest:
            state = links.gather(state, d, tick if d == links.rest[-1] else None)
        return state

    def halves_of(state):
        middle = state[0].shape[-1] // 2
        return [(state[0][..., :middle], state[1]), (state[0][..., middle:], state[1])]

    def joined(halves):
        return [half_state[0].reshape(width, -1) for half_state in halves]

    inputs_low, come, other = to_sequence(tokens)
    grad_out_low, grad_come, _ = to_sequence(cotangent, gate([come]))
    state = (early, [])
    for d in links.rest[:-1]:
        state = links.gather(state, d)
    first_stage = links.begin_gather(state, links.rest[-1])
    begun = [
        links.begin_gather(piece, d)
        for piece, d in zip(halves_of(links.end_gather(first_stage)), "yx")
    ]
    early_halves = [links.end_gather(piece) for piece in begun]
    early_a, early_b = joined(
        [links.gather(piece, d) for piece, d in zip(early_halves, "xy")]
    )
    split = early_a.shape[1]
    late = with_partner(
        jnp.concatenate([up_cols, jnp.broadcast_to(out_weight, (2, own, width))], axis=2)
    )
    down_own = down_weight.reshape(splits, pair_row, width)
    late = pack(
        [late, *(down_own[i] for i in range(splits))], [block for block in first_stage[1]] + [come]
    )
    late = lax.all_gather(late, ("dp", "xx"), axis=0, tiled=True)
    small = early_b[:, cols - split :].astype(F32).T
    gain_one, shift_one, query_shift, value_shift, out_shift, gain_two, shift_two, down_shift = (
        small[i] for i in range(8)
    )
    up_shift = small[8 : 8 + splits].reshape(hidden)

    inputs = inputs_low.astype(F32)
    seg = at_index(segments, side)
    numbers = jnp.arange(PAIR, dtype=jnp.int32) % HEAD_DIM
    same = seg[:, None] == numbers[None, :]
    coded = numbers[None, :] < 4
    query_code = jnp.where(same & coded, 1.0, 0.0).astype(BF16)
    key_code = jnp.where(same | ~coded, 0.0, NEG).astype(BF16)

    def head_cols(vector):
        return lax.dynamic_slice_in_dim(vector, core * half, half, 0).reshape(pairs, 1, PAIR)

    zeros = jnp.zeros((pairs, 1, PAIR), F32)
    qkv_shift = jnp.concatenate(
        [head_cols(query_shift), zeros, head_cols(value_shift)], axis=1
    ).reshape(1, cols)
    qkv_scale = jnp.tile(jnp.repeat(jnp.array([0.125, 1.0, 1.0], F32), PAIR), pairs)[None]
    normed_t, qkv, tick = qkv_projection(
        inputs_low,
        early_a,
        early_b,
        jnp.pad(jnp.stack([gain_one, shift_one]), ((0, 6), (0, 0))),
        jnp.pad(jnp.concatenate([qkv_shift, qkv_scale]), ((0, 6), (0, 0))),
        [],
    )
    attended, log_total, _ = attention_forward(qkv, query_code, key_code, [grad_come])
    core_at = core.reshape(1).astype(jnp.int32)
    branch = out_projection(core_at, attended, late, splits, [])
    branch_come = swap(branch, "core")
    mid_vectors = jnp.pad(
        jnp.stack([out_shift, gain_two, shift_two, down_shift]), ((0, 4), (0, 0))
    )
    normed_two_low, hidden_low, grad_pre_low, mixed_part, ffn_other, partial_two, up_sums = feed_forward(
        core_at,
        inputs_low,
        branch,
        branch_come,
        grad_out_low,
        late,
        splits,
        mid_vectors,
        jnp.pad(up_shift[None], ((0, 7), (0, 0))),
    )
    partial_come = swap(partial_two, "core")
    mixed_own = (mixed_part + swap(ffn_other, "core").astype(F32)).astype(BF16)
    mixed_own = mixed_own.reshape(2, quarter, width)
    mixed_come = swap(at_index(mixed_own, 1 - side), "xx")

    def blocks(array):
        return array.reshape(chips, pair_row, array.shape[1])

    grad_proj_down = [
        mm(hidden_low[:, i * width : (i + 1) * width], grad_out_low, TN).astype(BF16)
        for i in range(splits)
    ]
    grad_proj_up = mm(normed_two_low, grad_pre_low, TN).astype(BF16)
    (late_grads,) = fold(
        [[blocks(grad_proj_up)], *([blocks(part)] for part in grad_proj_down)], [chips], None, side, []
    )
    late_own = lax.psum_scatter(
        late_grads.reshape(width, -1), "dp", scatter_dimension=0, tiled=True
    )
    grad_middle, branch_low, grad_attended, mid_sums = norm_two(
        core_at,
        inputs_low,
        branch,
        branch_come,
        grad_out_low,
        partial_two,
        partial_come,
        late,
        splits,
        mid_vectors,
        [late_grads],
    )
    grad_proj_out = mm(attended, branch_low, TN)

    def as_column(vectors):
        table = jnp.stack(vectors, axis=1)
        return jnp.pad(table, ((0, 0), (0, PAIR - table.shape[1])))

    def only_mine(flag, array):
        return jnp.where(flag, array, jnp.zeros_like(array))

    small_two = [mid_sums[i] for i in range(4)] + [
        up_sums[0, i * width : (i + 1) * width] for i in range(splits)
    ]
    out_low = grad_proj_out.astype(BF16)
    grad_out_rows = jnp.concatenate(
        [only_mine(core == 0, out_low), only_mine(core == 1, out_low)], axis=0
    )

    def pairs_backward(first, count, after):
        return attention_backward(
            first, count, qkv, query_code, key_code, attended, grad_attended, log_total, normed_t, after
        )

    out_piece = links.scatter([[blocks(grad_out_rows)]], links.dims, "y")
    grad_a, weight_grad_a, tick = pairs_backward(0, pairs - 1, [out_piece[0][0][0]])
    first_piece = links.scatter([[blocks(weight_grad_a)]], links.dims, "y", [tick])
    mixed = merge(at_index(mixed_own, side), mixed_come, side, [tick])
    grad_b, weight_grad_b, tick = pairs_backward(
        pairs - 1, 1, [first_piece[0][0][0], tick, mixed]
    )
    grads = [grad_a, grad_b]
    late_piece = links.scatter([[late_own.reshape(2, pair_row, -1)]], ["x"], "x", [tick])
    first_piece = links.scatter(out_piece[0] + first_piece[0], first_piece[1], "x", [tick])
    last_piece = links.scatter([[blocks(weight_grad_b)]], links.dims, "y", [tick])
    norm_vectors = jnp.pad(jnp.stack([gain_one, shift_one]), ((0, 6), (0, 0)))
    partial_one, norm_sums, bias_sums, tick = norm_one(
        False, core_at, grads, early_a, early_b, cols, inputs_low, [], [first_piece[0][0][0], last_piece[0][0][0]]
    )
    come = swap(partial_one, "core")
    token_own, norm_sums_own, bias_sums_own, tick = norm_one(
        True,
        core_at,
        grads,
        early_a,
        early_b,
        cols,
        inputs_low,
        [come, grad_middle, norm_vectors],
        [late_piece[0][0][0]],
    )
    norm_sums = norm_sums + norm_sums_own
    bias_sums = bias_sums + bias_sums_own
    token_grad, come = from_sequence(token_own.reshape(2, quarter, width))
    grad_by_pair = bias_sums[0].reshape(pairs, 3, PAIR)

    def padded(vector):
        vector = vector.reshape(half)
        return jnp.concatenate([only_mine(core == 0, vector), only_mine(core == 1, vector)])

    small = as_column(
        [
            norm_sums[0],
            norm_sums[1],
            padded(grad_by_pair[:, 0]),
            padded(grad_by_pair[:, 2]),
        ]
        + small_two
    )
    first_piece = links.scatter(*first_piece, links.rest[0], [tick])
    first_own = links.scatter_rest(first_piece, 1)
    small_piece = links.scatter(
        [[blocks(small.astype(BF16))]], links.dims, "y", [first_piece[0][0][0]]
    )
    last_piece = links.scatter(last_piece[0] + small_piece[0], last_piece[1], "x")
    last_piece = links.scatter(*last_piece, links.rest[0], [come, *first_piece[0][0][1:]])
    last_own = links.scatter_rest(last_piece, 1)

    def rows_of(array, index):
        return lax.dynamic_slice_in_dim(array, index * own, own, 0)

    def by_core(mine, come):
        return jnp.stack(pick(core, mine, come))

    def shared(array):
        return rows_of(array, core), swap(rows_of(array, 1 - core), "core")

    up_own, down_grad = widen(*(array[0] for array in late_piece[0][0]), width)
    late_mine, late_come = shared(up_own)
    first_mine, first_come = shared(first_own)
    last_mine, last_come = shared(last_own)
    out_grad = first_mine[:, :width] + first_come[:, :width]
    up_grad = (
        by_core(late_mine, late_come)
        .reshape(2, own, splits, chips, pair_row)
        .transpose(1, 3, 0, 2, 4)
        .reshape(own, 2 * hidden)
        .astype(F32)
    )
    down_grad = down_grad.reshape(hidden_own, width)
    most = cols - cols // pairs

    def natural(mine, come):
        return by_core(mine, come).reshape(2, own, -1, 3, PAIR).transpose(1, 3, 0, 2, 4)

    qkv_grad = jnp.concatenate(
        [
            natural(first_mine[:, width:], first_come[:, width:]),
            natural(last_mine[:, : cols - most], last_come[:, : cols - most]),
        ],
        axis=3,
    ).reshape(own, 2 * cols)
    small_mine = last_mine[:, cols - most : cols - most + 8]
    one = small_mine[:, :4] + last_come[:, cols - most : cols - most + 4]
    tail = cols - most + 8
    up_shift_grad = last_own[:, tail : tail + splits].T.reshape(hidden_own)
    two = small_mine[:, 4:]
    return (
        mixed,
        token_grad,
        one[:, 0],
        one[:, 1],
        qkv_grad,
        one[:, 2],
        one[:, 3],
        out_grad,
        two[:, 0],
        two[:, 1],
        two[:, 2],
        up_grad,
        up_shift_grad,
        down_grad,
        two[:, 3],
    )


def solution(mesh):
    parts = (mesh.shape["dp"], mesh.shape["ctx"] // 2, 2)
    split_mesh = Mesh(mesh.devices.reshape(parts), ("dp", "xx", "core"))
    rows = ("dp", "xx", "core")
    acts = P("dp", ("xx", "core"), None)
    vec, mat = P(rows), P(rows, None)
    return jax.shard_map(
        body,
        mesh=split_mesh,
        in_specs=(
            acts, P("dp", None), vec, vec, mat, vec, vec, mat, vec, vec, vec, mat, vec, mat, vec, acts,
        ),
        out_specs=(
            acts, acts, vec, vec, mat, vec, vec, mat, vec, vec, vec, mat, vec, mat, vec,
        ),
        check_vma=False,
    )
```

```python
import functools

import jax
import jax.numpy as jnp
from jax import lax
from jax.experimental import pallas as pl
from jax.experimental.pallas import tpu as pltpu
from jax.sharding import Mesh, PartitionSpec as P

HEAD_DIM = 64
PAIR = 2 * HEAD_DIM
EPSILON = 1e-05
NEG = -1e30
BLK = 512
F32 = jnp.float32
BF16 = jnp.bfloat16

NN = (((1,), (0,)), ((), ()))
NT = (((1,), (1,)), ((), ()))
TN = (((0,), (0,)), ((), ()))


def mm(left, right, dims=NN):
    return lax.dot_general(left, right, dims, preferred_element_type=F32)


def build_scores_operands(qkv_ref, qs_ref, ks_ref, rows, qx, kx):
    lane = lax.broadcasted_iota(jnp.int32, (BLK, PAIR), 1)
    first = lane < HEAD_DIM
    q = qkv_ref[rows, 0:PAIR].astype(F32)
    k = qkv_ref[rows, PAIR : 2 * PAIR].astype(F32)
    qs = qs_ref[rows, :].astype(F32)
    ks = ks_ref[rows, :].astype(F32)
    qx[0, rows, :] = jnp.where(first, q, qs).astype(BF16)
    qx[1, rows, :] = jnp.where(first, qs, q).astype(BF16)
    kx[0, rows, :] = jnp.where(first, k, ks).astype(BF16)
    kx[1, rows, :] = jnp.where(first, ks, k).astype(BF16)
    return first, q, k


def causal_block(scores):
    key_at = lax.broadcasted_iota(jnp.int32, scores.shape, 0)
    query_at = lax.broadcasted_iota(jnp.int32, scores.shape, 1)
    return jnp.where(key_at <= query_at, scores, NEG)


def attention_forward_kernel(qkv_ref, qs_ref, ks_ref, *rest):
    o_ref, lse_ref, tick_ref, qx, kx, vt, acc = rest[-7:]
    tick_ref[...] = jnp.zeros_like(tick_ref)
    length = qkv_ref.shape[0]
    blocks = length // BLK

    @pl.loop(0, blocks)
    def _(i):
        rows = pl.ds(pl.multiple_of(i * BLK, BLK), BLK)
        build_scores_operands(qkv_ref, qs_ref, ks_ref, rows, qx, kx)
        v_t = qkv_ref[rows, 2 * PAIR : 3 * PAIR].astype(F32).T
        ones = jnp.ones((16, BLK), BF16)
        for h in range(2):
            vt[h, 0:HEAD_DIM, rows] = v_t[h * HEAD_DIM : (h + 1) * HEAD_DIM].astype(BF16)
            vt[h, HEAD_DIM : HEAD_DIM + 16, rows] = ones

    @pl.loop(0, blocks)
    def _(i):
        rows = pl.ds(pl.multiple_of(i * BLK, BLK), BLK)
        tops = []
        for h in range(2):
            s = causal_block(mm(kx[h, rows, :], qx[h, rows, :], NT))
            top = jnp.max(s, axis=0, keepdims=True)
            p = jnp.exp(s - top).astype(BF16)
            acc[h] = mm(vt[h, :, rows], p)
            tops.append(top)

        def step(j, carry):
            keys = pl.ds(pl.multiple_of(j * BLK, BLK), BLK)
            out = []
            for h in range(2):
                s = mm(kx[h, keys, :], qx[h, rows, :], NT)
                top = jnp.maximum(carry[h], jnp.max(s, axis=0, keepdims=True))
                p = jnp.exp(s - top).astype(BF16)
                acc[h] = acc[h] * jnp.exp(carry[h] - top) + mm(vt[h, :, keys], p)
                out.append(top)
            return tuple(out)

        tops = lax.fori_loop(0, i, step, tuple(tops))
        parts = []
        for h in range(2):
            total = acc[h, HEAD_DIM : HEAD_DIM + 1, :]
            parts.append(acc[h, 0:HEAD_DIM, :] / total)
            lse_ref[0, h : h + 1, rows] = tops[h] + jnp.log(total)
        o_ref[rows, :] = jnp.concatenate(parts, axis=0).T.astype(BF16)


def attention_backward_kernel(qkv_ref, qs_ref, ks_ref, o_ref, do_ref, lse_ref, at_ref, *rest):
    d_ref, dw_ref, tick_ref, qx, kx, qm, dm, kt, delta, dqt, dk, dv = rest[-12:]
    tick_ref[...] = jnp.zeros_like(tick_ref)
    length = qkv_ref.shape[0]
    blocks = length // BLK

    @pl.loop(0, blocks)
    def _(i):
        rows = pl.ds(pl.multiple_of(i * BLK, BLK), BLK)
        first, q, k = build_scores_operands(qkv_ref, qs_ref, ks_ref, rows, qx, kx)
        do = do_ref[rows, :].astype(F32)
        zero = jnp.zeros_like(q)
        qm[0, rows, :] = jnp.where(first, q, zero).astype(BF16)
        qm[1, rows, :] = jnp.where(first, zero, q).astype(BF16)
        dm[0, rows, :] = jnp.where(first, do, zero).astype(BF16)
        dm[1, rows, :] = jnp.where(first, zero, do).astype(BF16)
        kt[:, rows] = k.T.astype(BF16)
        inner = (do * o_ref[rows, :].astype(F32)).T
        for h in range(2):
            delta[h : h + 1, rows] = jnp.sum(
                inner[h * HEAD_DIM : (h + 1) * HEAD_DIM], axis=0, keepdims=True
            )
        dqt[:, rows] = jnp.zeros((PAIR, BLK), F32)

    def tile(keys, rows, masked):
        values = qkv_ref[keys, 2 * PAIR : 3 * PAIR]
        dv_part, dk_part = None, None
        for h in range(2):
            s = mm(kx[h, keys, :], qx[h, rows, :], NT)
            if masked:
                s = causal_block(s)
            p = jnp.exp(s - lse_ref[0, h : h + 1, rows])
            dp = mm(values, dm[h, rows, :], NT)
            ds = (p * (dp - delta[h : h + 1, rows])).astype(BF16)
            dv_h = mm(p.astype(BF16), dm[h, rows, :])
            dk_h = mm(ds, qm[h, rows, :])
            dv_part = dv_h if h == 0 else dv_part + dv_h
            dk_part = dk_h if h == 0 else dk_part + dk_h
            part = slice(h * HEAD_DIM, (h + 1) * HEAD_DIM)
            dqt[part, rows] += mm(kt[part, keys], ds)
        return dk_part, dv_part

    @pl.loop(0, blocks)
    def _(j):
        keys = pl.ds(pl.multiple_of(j * BLK, BLK), BLK)
        dk[...], dv[...] = tile(keys, keys, True)

        @pl.loop(j + 1, blocks)
        def _(i):
            dk_part, dv_part = tile(keys, pl.ds(pl.multiple_of(i * BLK, BLK), BLK), False)
            dk[...] += dk_part
            dv[...] += dv_part

        d_ref[keys, PAIR : 2 * PAIR] = dk[...].astype(BF16)
        d_ref[keys, 2 * PAIR : 3 * PAIR] = dv[...].astype(BF16)

    @pl.loop(0, blocks)
    def _(i):
        rows = pl.ds(pl.multiple_of(i * BLK, BLK), BLK)
        d_ref[rows, 0:PAIR] = (dqt[:, rows].T.astype(BF16).astype(F32) * 0.125).astype(BF16)

    @pl.loop(0, dw_ref.shape[0] // ROWS)
    def _(i):
        rows = pl.ds(pl.multiple_of(i * ROWS, ROWS), ROWS)
        dw_ref[rows, :] = mm(at_ref[rows, :], d_ref[...]).astype(BF16)


VMEM_LIMIT = 48 * 1024 * 1024


SMALL_COST = pl.CostEstimate(flops=1000, bytes_accessed=1000, transcendentals=0)


TICK = jax.ShapeDtypeStruct((8, 128), F32)
TICK_SPEC = pl.BlockSpec((8, 128), lambda i: (0, 0))
ANY_SPEC = pl.BlockSpec(memory_space=pl.ANY)


def pack_kernel(count, refs):
    refs[-1][...] = jnp.concatenate([ref[...] for ref in refs[:count]], axis=-1)


def pack(parts, after):
    rows = parts[0].shape[0]
    width = sum(part.shape[1] for part in parts)
    return pl.pallas_call(
        lambda *refs: pack_kernel(len(parts), refs),
        grid=(1,),
        in_specs=[pl.BlockSpec(part.shape, lambda i: (0, 0)) for part in parts]
        + [ANY_SPEC] * len(after),
        out_specs=pl.BlockSpec((rows, width), lambda i: (0, 0)),
        out_shape=jax.ShapeDtypeStruct((rows, width), BF16),
        compiler_params=pltpu.CompilerParams(vmem_limit_bytes=VMEM_LIMIT),
        cost_estimate=SMALL_COST,
    )(*parts, *after)


def widen(first, second, width, after):
    rows, cols = first.shape
    count = cols // width - 2

    def kernel(first_ref, second_ref, *refs):
        up_ref, down_ref = refs[-2:]
        total = first_ref[...].astype(F32) + second_ref[...].astype(F32)
        up_ref[...] = total[:, : 2 * width]
        for i in range(count):
            down_ref[i] = total[:, (2 + i) * width : (3 + i) * width]

    return pl.pallas_call(
        kernel,
        grid=(1,),
        in_specs=[pl.BlockSpec((rows, cols), lambda i: (0, 0))] * 2 + [ANY_SPEC] * len(after),
        out_specs=[
            pl.BlockSpec((rows, 2 * width), lambda i: (0, 0)),
            pl.BlockSpec((count, rows, width), lambda i: (0, 0, 0)),
        ],
        out_shape=[
            jax.ShapeDtypeStruct((rows, 2 * width), F32),
            jax.ShapeDtypeStruct((count, rows, width), F32),
        ],
        compiler_params=pltpu.CompilerParams(vmem_limit_bytes=VMEM_LIMIT),
        cost_estimate=SMALL_COST,
    )(first, second, *after)


def merge(kept, come, side, after):
    def kernel(side_ref, kept_ref, come_ref, *rest):
        mine = pl.program_id(0) == side_ref[0]

        @pl.when(mine)
        def _():
            rest[-1][0] = kept_ref[...]

        @pl.when(jnp.logical_not(mine))
        def _():
            rest[-1][0] = come_ref[...]

    whole = pl.BlockSpec(kept.shape, lambda i, side_ref: (0, 0))
    return pl.pallas_call(
        kernel,
        grid_spec=pltpu.PrefetchScalarGridSpec(
            num_scalar_prefetch=1,
            grid=(2,),
            in_specs=[whole, whole] + [ANY_SPEC] * len(after),
            out_specs=pl.BlockSpec((1, *kept.shape), lambda i, side_ref: (i, 0, 0)),
        ),
        out_shape=jax.ShapeDtypeStruct((2, *kept.shape), kept.dtype),
        compiler_params=pltpu.CompilerParams(vmem_limit_bytes=VMEM_LIMIT),
        cost_estimate=SMALL_COST,
    )(side.reshape(1).astype(jnp.int32), kept, come, *after)


def gate_kernel(*refs):
    refs[-1][...] = jnp.zeros_like(refs[-1])


def gate(after):
    return pl.pallas_call(
        gate_kernel,
        grid=(1,),
        in_specs=[ANY_SPEC] * len(after),
        out_specs=TICK_SPEC,
        out_shape=TICK,
        cost_estimate=SMALL_COST,
    )(*after)


def fold(pieces, sizes, axis, at, after):
    blocks, rows = pieces[0][0].shape[:2]
    width = sum(piece[0].shape[2] for piece in pieces)
    outs = sizes[axis] if axis is not None else 1
    inner = 1
    if axis is not None:
        for size in sizes[axis + 1 :]:
            inner *= size
    flat = [array for piece in pieces for array in piece]

    def spec(array, m):
        def index(j, at_ref):
            if axis is None:
                return j, 0, 0
            return (j // inner) * (outs * inner) + (at_ref[0] ^ m) * inner + j % inner, 0, 0

        return pl.BlockSpec((1, rows, array.shape[2]), index)

    def kernel(at_ref, *refs):
        for m in range(outs):
            left = list(refs[m * len(flat) : (m + 1) * len(flat)])
            sides = []
            for piece in pieces:
                value = left.pop(0)[0]
                for _ in piece[1:]:
                    value = value.astype(F32) + left.pop(0)[0].astype(F32)
                sides.append(value.astype(BF16))
            refs[len(refs) - outs + m][0] = jnp.concatenate(sides, axis=-1)

    out = pl.BlockSpec((1, rows, width), lambda j, at_ref: (j, 0, 0))
    return pl.pallas_call(
        kernel,
        grid_spec=pltpu.PrefetchScalarGridSpec(
            num_scalar_prefetch=1,
            grid=(blocks // outs,),
            in_specs=[spec(array, m) for m in range(outs) for array in flat]
            + [ANY_SPEC] * len(after),
            out_specs=[out] * outs,
        ),
        out_shape=[jax.ShapeDtypeStruct((blocks // outs, rows, width), BF16)] * outs,
        compiler_params=pltpu.CompilerParams(vmem_limit_bytes=VMEM_LIMIT),
        cost_estimate=SMALL_COST,
    )(at.reshape(1).astype(jnp.int32), *(flat * outs), *after)


def qkv_kernel(x_ref, wa_ref, wb_ref, vec_ref, col_ref, *rest_refs):
    a_ref, qkv_ref, tick_ref = rest_refs[-3:]
    split = wa_ref.shape[1]
    rest = qkv_ref.shape[1] - split
    for part in range(2):
        rows = slice(part * ROWS, (part + 1) * ROWS)
        normal, _ = norm_forward(x_ref[rows, :].astype(F32))
        normed = (normal * vec_ref[0:1, :] + vec_ref[1:2, :]).astype(BF16)
        a_ref[:, rows] = normed.astype(F32).T.astype(BF16)
        for w, cols in ((wa_ref[...], slice(0, split)), (wb_ref[:, :rest], slice(split, None))):
            shift, scale = col_ref[0:1, cols], col_ref[1:2, cols]
            qkv_ref[rows, cols] = ((mm(normed, w) + shift) * scale).astype(BF16)
    tick_ref[...] = jnp.zeros_like(tick_ref)


def qkv_projection(inputs, weight_a, weight_b, vectors, columns, after):
    length, width = inputs.shape
    cols = columns.shape[1]
    return pl.pallas_call(
        qkv_kernel,
        grid=(length // (2 * ROWS),),
        in_specs=[
            pl.BlockSpec((2 * ROWS, width), lambda i: (i, 0)),
            pl.BlockSpec(weight_a.shape, lambda i: (0, 0)),
            pl.BlockSpec(weight_b.shape, lambda i: (0, 0)),
            pl.BlockSpec(vectors.shape, lambda i: (0, 0)),
            pl.BlockSpec(columns.shape, lambda i: (0, 0)),
        ]
        + [ANY_SPEC] * len(after),
        out_specs=[
            pl.BlockSpec((width, 2 * ROWS), lambda i: (0, i)),
            pl.BlockSpec((2 * ROWS, cols), lambda i: (i, 0)),
            TICK_SPEC,
        ],
        out_shape=[
            jax.ShapeDtypeStruct((width, length), BF16),
            jax.ShapeDtypeStruct((length, cols), BF16),
            TICK,
        ],
        compiler_params=pltpu.CompilerParams(vmem_limit_bytes=VMEM_LIMIT),
        cost_estimate=SMALL_COST,
    )(inputs, weight_a, weight_b, vectors, columns, *after)


def out_projection(core, attended, late, block, after):
    length, cols = attended.shape
    width = late.shape[0]
    rows = length // 4

    def kernel(core_ref, a_ref, w_ref, *rest):
        rest[-1][...] = mm(a_ref[...], w_ref[...]).astype(BF16)

    return pl.pallas_call(
        kernel,
        grid_spec=pltpu.PrefetchScalarGridSpec(
            num_scalar_prefetch=1,
            grid=(4,),
            in_specs=[
                pl.BlockSpec((rows, cols), lambda i, core_ref: (i, 0)),
                pl.BlockSpec((cols, width), lambda i, core_ref: (core_ref[0], block)),
            ]
            + [ANY_SPEC] * len(after),
            out_specs=pl.BlockSpec((rows, width), lambda i, core_ref: (i, 0)),
        ),
        out_shape=jax.ShapeDtypeStruct((length, width), BF16),
        compiler_params=pltpu.CompilerParams(vmem_limit_bytes=VMEM_LIMIT),
        cost_estimate=SMALL_COST,
    )(core, attended, late, *after)


def middle_of(x_ref, b0_ref, b1_ref, vec_ref):
    both = b0_ref[...].astype(F32) + b1_ref[...].astype(F32)
    return x_ref[...].astype(F32) + both + vec_ref[0:1, :]


def feed_forward_kernel(splits, core_ref, x_ref, b0_ref, b1_ref, dy_ref, up_ref, *rest):
    down_refs, (vec_ref, shift_ref) = rest[:splits], rest[splits : splits + 2]
    a_ref, g_ref, du_ref, own_ref, other_ref, dh_ref, sums_ref = rest[splits + 2 :]
    at = pl.program_id(0)

    @pl.when(at == 0)
    def _():
        sums_ref[...] = jnp.zeros_like(sums_ref)

    middle = middle_of(x_ref, b0_ref, b1_ref, vec_ref)
    normal, _ = norm_forward(middle)
    normed = (normal * vec_ref[1:2, :] + vec_ref[2:3, :]).astype(BF16)
    a_ref[...] = normed
    dy = dy_ref[...]
    ffn, dh = None, None
    width = dy.shape[1]
    for i, down_ref in enumerate(down_refs):
        cols = slice(i * width, (i + 1) * width)
        up, down = up_ref[:, cols], down_ref[...]
        value, slope = gelu_parts(mm(normed, up) + shift_ref[0:1, cols])
        du = slope * mm(dy, down, NT)
        value, du = value.astype(BF16), du.astype(BF16)
        g_ref[:, cols] = value
        du_ref[:, cols] = du
        sums_ref[0:1, cols] += jnp.sum(du.astype(F32), axis=0, keepdims=True)
        ffn_part, dh_part = mm(value, down), mm(du, up, NT)
        ffn = ffn_part if i == 0 else ffn + ffn_part
        dh = dh_part if i == 0 else dh + dh_part
    dh_ref[...] = dh.astype(BF16)
    mine = at % 2 == core_ref[0]

    @pl.when(mine)
    def _():
        own_ref[...] = middle_of(x_ref, b0_ref, b1_ref, vec_ref) + ffn + vec_ref[3:4, :]

    @pl.when(jnp.logical_not(mine))
    def _():
        other_ref[...] = ffn.astype(BF16)


def feed_forward(core, inputs, branch, branch_come, grad_out, late, splits, vectors, up_shift):
    length, width = inputs.shape
    rows = length // 4
    hidden = splits * width
    narrow = pl.BlockSpec((rows, width), lambda i, core_ref: (i, 0))
    wide = pl.BlockSpec((rows, hidden), lambda i, core_ref: (i, 0))
    shared = pl.BlockSpec((rows, width), lambda i, core_ref: (i // 2, 0))

    def whole(array):
        return pl.BlockSpec(array.shape, lambda i, core_ref: (0, 0))

    def down(i):
        return pl.BlockSpec((width, width), lambda _, core_ref: (0, splits + 1 + i))

    return pl.pallas_call(
        functools.partial(feed_forward_kernel, splits),
        grid_spec=pltpu.PrefetchScalarGridSpec(
            num_scalar_prefetch=1,
            grid=(4,),
            in_specs=[narrow] * 4
            + [pl.BlockSpec((width, hidden), lambda i, core_ref: (0, 0))]
            + [down(i) for i in range(splits)]
            + [whole(vectors), whole(up_shift)],
            out_specs=[
                narrow, wide, wide, shared, shared, narrow,
                pl.BlockSpec((8, hidden), lambda i, core_ref: (0, 0)),
            ],
        ),
        out_shape=[
            jax.ShapeDtypeStruct((length, width), BF16),
            jax.ShapeDtypeStruct((length, hidden), BF16),
            jax.ShapeDtypeStruct((length, hidden), BF16),
            jax.ShapeDtypeStruct((length // 2, width), F32),
            jax.ShapeDtypeStruct((length // 2, width), BF16),
            jax.ShapeDtypeStruct((length, width), BF16),
            jax.ShapeDtypeStruct((8, hidden), F32),
        ],
        compiler_params=pltpu.CompilerParams(vmem_limit_bytes=VMEM_LIMIT),
        cost_estimate=SMALL_COST,
    )(core, inputs, branch, branch_come, grad_out, late, *([late] * splits), vectors, up_shift)


def norm_two_kernel(core_ref, x_ref, b0_ref, b1_ref, dy_ref, p0_ref, p1_ref, w_ref, vec_ref, *rest):
    mid_ref, low_ref, do_ref, sums_ref = rest[-4:]

    @pl.when(pl.program_id(0) == 0)
    def _():
        sums_ref[...] = jnp.zeros_like(sums_ref)

    normal, scale = norm_forward(middle_of(x_ref, b0_ref, b1_ref, vec_ref))
    grad = p0_ref[...].astype(F32) + p1_ref[...].astype(F32)
    dy = dy_ref[...].astype(F32)
    mid = dy + norm_backward(normal, scale, grad * vec_ref[1:2, :])
    low = mid.astype(BF16)
    low_ref[...] = low
    do_ref[...] = mm(low, w_ref[...], NT).astype(BF16)
    for i, value in enumerate((low.astype(F32), grad * normal, grad, dy)):
        sums_ref[i : i + 1, :] += jnp.sum(value, axis=0, keepdims=True)

    @pl.when(pl.program_id(0) % 2 == core_ref[0])
    def _():
        mid_ref[...] = mid


def norm_two(core, inputs, branch, branch_come, grad_out, partial, partial_come, late, block, vectors, after):
    length, width = inputs.shape
    rows = length // 4
    cols = width // 2
    narrow = pl.BlockSpec((rows, width), lambda i, core_ref: (i, 0))
    return pl.pallas_call(
        norm_two_kernel,
        grid_spec=pltpu.PrefetchScalarGridSpec(
            num_scalar_prefetch=1,
            grid=(4,),
            in_specs=[narrow] * 6
            + [
                pl.BlockSpec((cols, width), lambda i, core_ref: (core_ref[0], block)),
                pl.BlockSpec(vectors.shape, lambda i, core_ref: (0, 0)),
            ]
            + [ANY_SPEC] * len(after),
            out_specs=[
                pl.BlockSpec((rows, width), lambda i, core_ref: (i // 2, 0)),
                narrow,
                pl.BlockSpec((rows, cols), lambda i, core_ref: (i, 0)),
                pl.BlockSpec((8, width), lambda i, core_ref: (0, 0)),
            ],
        ),
        out_shape=[
            jax.ShapeDtypeStruct((length // 2, width), F32),
            jax.ShapeDtypeStruct((length, width), BF16),
            jax.ShapeDtypeStruct((length, cols), BF16),
            jax.ShapeDtypeStruct((8, width), F32),
        ],
        compiler_params=pltpu.CompilerParams(vmem_limit_bytes=VMEM_LIMIT),
        cost_estimate=SMALL_COST,
    )(core, inputs, branch, branch_come, grad_out, partial, partial_come, late, vectors, *after)


ROWS = 256


def attention_forward(qkv, query_code, key_code, after):
    length, width = qkv.shape
    pairs = width // (3 * PAIR)
    return pl.pallas_call(
        attention_forward_kernel,
        grid=(pairs,),
        in_specs=[
            pl.BlockSpec((length, 3 * PAIR), lambda p: (0, p)),
            pl.BlockSpec((length, PAIR), lambda p: (0, 0)),
            pl.BlockSpec((length, PAIR), lambda p: (0, 0)),
        ]
        + [ANY_SPEC] * len(after),
        out_specs=[
            pl.BlockSpec((length, PAIR), lambda p: (0, p)),
            pl.BlockSpec((1, 8, length), lambda p: (p, 0, 0)),
            TICK_SPEC,
        ],
        out_shape=[
            jax.ShapeDtypeStruct((length, pairs * PAIR), BF16),
            jax.ShapeDtypeStruct((pairs, 8, length), F32),
            TICK,
        ],
        scratch_shapes=[
            pltpu.VMEM((2, length, PAIR), BF16),
            pltpu.VMEM((2, length, PAIR), BF16),
            pltpu.VMEM((2, HEAD_DIM + 16, length), BF16),
            pltpu.VMEM((2, HEAD_DIM + 16, BLK), F32),
        ],
        compiler_params=pltpu.CompilerParams(vmem_limit_bytes=VMEM_LIMIT),
        cost_estimate=SMALL_COST,
    )(qkv, query_code, key_code, *after)


def norm_one_kernel(own, core_ref, d0_ref, d1_ref, wa_ref, wb_ref, x_ref, *rest):
    if own:
        come_ref, mid_ref, vec_ref, out_ref, sums_ref, bias_ref, tick_ref, w = rest
    else:
        out_ref, sums_ref, bias_ref, tick_ref, w = rest
    split = wa_ref.shape[1]

    @pl.when(pl.program_id(0) == 0)
    def _():
        sums_ref[...] = jnp.zeros_like(sums_ref)
        bias_ref[...] = jnp.zeros_like(bias_ref)
        w[:, :split] = wa_ref[...]
        w[:, split:] = wb_ref[:, : w.shape[1] - split]
        tick_ref[...] = jnp.zeros_like(tick_ref)

    total = None
    for i, ref in enumerate((d0_ref, d1_ref)):
        cols = slice(0, ref.shape[1]) if i == 0 else slice(d0_ref.shape[1], None)
        grad = ref[...]
        part = mm(grad, w[:, cols], NT)
        total = part if i == 0 else total + part
        bias_ref[0:1, cols] += jnp.sum(grad.astype(F32), axis=0, keepdims=True)
    normal, scale = norm_forward(x_ref[...].astype(F32))
    sums_ref[0:1, :] += jnp.sum(total * normal, axis=0, keepdims=True)
    sums_ref[1:2, :] += jnp.sum(total, axis=0, keepdims=True)
    if own:
        grad = (total + come_ref[...].astype(F32)) * vec_ref[0:1, :]
        out_ref[...] = (mid_ref[...] + norm_backward(normal, scale, grad)).astype(BF16)
    else:
        out_ref[...] = total.astype(BF16)


def norm_one(own, core, grads, weight_a, weight_b, cols, inputs, extra, after):
    length, width = inputs.shape
    count = length // (2 * ROWS)
    per = count // 2

    def block(i, core_ref):
        which = core_ref[0] if own else 1 - core_ref[0]
        return ((i // per) * 2 + which) * per + i % per, 0

    def at_zero(i, core_ref):
        return 0, 0

    plain = pl.BlockSpec((ROWS, width), lambda i, core_ref: (i, 0))
    rows = pl.BlockSpec((ROWS, width), block)
    in_specs = [pl.BlockSpec((ROWS, grad.shape[1]), block) for grad in grads] + [
        pl.BlockSpec(weight_a.shape, at_zero),
        pl.BlockSpec(weight_b.shape, at_zero),
        rows,
    ]
    out_specs = [
        plain,
        pl.BlockSpec((8, width), at_zero),
        pl.BlockSpec((8, cols), at_zero),
        pl.BlockSpec((8, 128), at_zero),
    ]
    out_shape = [
        jax.ShapeDtypeStruct((count * ROWS, width), BF16),
        jax.ShapeDtypeStruct((8, width), F32),
        jax.ShapeDtypeStruct((8, cols), F32),
        TICK,
    ]
    if own:
        in_specs += [plain, plain, pl.BlockSpec(extra[2].shape, at_zero)]

    def kernel(*refs):
        inner = refs[: 1 + len(in_specs)] + refs[1 + len(in_specs) + len(after) :]
        norm_one_kernel(own, *inner)

    return pl.pallas_call(
        kernel,
        grid_spec=pltpu.PrefetchScalarGridSpec(
            num_scalar_prefetch=1,
            grid=(count,),
            in_specs=in_specs + [ANY_SPEC] * len(after),
            out_specs=out_specs,
            scratch_shapes=[pltpu.VMEM((width, cols), BF16)],
        ),
        out_shape=out_shape,
        compiler_params=pltpu.CompilerParams(vmem_limit_bytes=VMEM_LIMIT),
        cost_estimate=SMALL_COST,
    )(core, *grads, weight_a, weight_b, inputs, *extra, *after)


def attention_backward(
    first, count, qkv, query_code, key_code, attended, grad_attended, log_total, normed_t, after
):
    length = qkv.shape[0]
    width = normed_t.shape[0]
    return pl.pallas_call(
        attention_backward_kernel,
        grid=(count,),
        in_specs=[
            pl.BlockSpec((length, 3 * PAIR), lambda p: (0, first + p)),
            pl.BlockSpec((length, PAIR), lambda p: (0, 0)),
            pl.BlockSpec((length, PAIR), lambda p: (0, 0)),
            pl.BlockSpec((length, PAIR), lambda p: (0, first + p)),
            pl.BlockSpec((length, PAIR), lambda p: (0, first + p)),
            pl.BlockSpec((1, 8, length), lambda p: (first + p, 0, 0)),
            pl.BlockSpec(normed_t.shape, lambda p: (0, 0)),
        ]
        + [ANY_SPEC] * len(after),
        out_specs=[
            pl.BlockSpec((length, 3 * PAIR), lambda p: (0, p)),
            pl.BlockSpec((width, 3 * PAIR), lambda p: (0, p)),
            TICK_SPEC,
        ],
        out_shape=[
            jax.ShapeDtypeStruct((length, count * 3 * PAIR), BF16),
            jax.ShapeDtypeStruct((width, count * 3 * PAIR), BF16),
            TICK,
        ],
        scratch_shapes=[
            pltpu.VMEM((2, length, PAIR), BF16),
            pltpu.VMEM((2, length, PAIR), BF16),
            pltpu.VMEM((2, length, PAIR), BF16),
            pltpu.VMEM((2, length, PAIR), BF16),
            pltpu.VMEM((PAIR, length), BF16),
            pltpu.VMEM((8, length), F32),
            pltpu.VMEM((PAIR, length), F32),
            pltpu.VMEM((BLK, PAIR), F32),
            pltpu.VMEM((BLK, PAIR), F32),
        ],
        compiler_params=pltpu.CompilerParams(vmem_limit_bytes=VMEM_LIMIT),
        cost_estimate=SMALL_COST,
    )(qkv, query_code, key_code, attended, grad_attended, log_total, normed_t, *after)


def norm_forward(source):
    average = jnp.mean(source, axis=-1, keepdims=True)
    centred = source - average
    spread = jnp.mean(centred * centred, axis=-1, keepdims=True)
    scale = lax.rsqrt(spread + EPSILON)
    return centred * scale, scale


def norm_backward(normal, scale, grad):
    return scale * (
        grad
        - jnp.mean(grad, axis=-1, keepdims=True)
        - normal * jnp.mean(grad * normal, axis=-1, keepdims=True)
    )


GELU_A = 0.7978845608028654
GELU_B = 0.044715


def gelu_parts(source):
    square = source * source
    inner = jnp.tanh(GELU_A * (source + GELU_B * source * square))
    value = 0.5 * source * (1.0 + inner)
    slope = 0.5 * (1.0 + inner) + 0.5 * source * (1.0 - inner * inner) * (
        GELU_A * (1.0 + 3.0 * GELU_B * square)
    )
    return value, slope


def swap(value, axis):
    return lax.ppermute(value, axis, [(0, 1), (1, 0)])


def pick(flag, first, second):
    return jnp.where(flag == 0, first, second), jnp.where(flag == 0, second, first)


class Links:
    def __init__(self):
        self.size = lax.axis_size("dp")
        at = lax.axis_index("dp")
        self.groups = {}
        shift, name = 0, "y"
        while (1 << shift) < self.size:
            bits = 1 if shift == 0 else min(2, self.size.bit_length() - 1 - shift)
            self.groups[name] = (shift, bits, (at >> shift) & ((1 << bits) - 1))
            shift += bits
            name = "z" + str(shift)
        self.rest = [name for name in reversed(self.groups) if name != "y"]
        self.dims = self.rest + ["y", "x"]
        self.side = lax.axis_index("xx")

    def counts(self, dims):
        return [{"x": 2, "yx": 4}.get(d) or 1 << self.groups[d][1] for d in dims]

    def send(self, value, d, mask):
        if d == "x":
            return swap(value, "xx")
        if d == "yx":
            return lax.ppermute(
                value, ("dp", "xx"), [(i, i ^ mask) for i in range(2 * self.size)]
            )
        move = mask << self.groups[d][0]
        return lax.ppermute(value, "dp", [(i, i ^ move) for i in range(self.size)])

    def place(self, d):
        if d == "yx":
            return self.groups["y"][2] * 2 + self.side
        return self.side if d == "x" else self.groups[d][2]

    def scatter(self, pieces, dims, d, after=()):
        axis = dims.index(d)
        shares = fold(pieces, self.counts(dims), axis, self.place(d), list(after))
        come = [self.send(share, d, mask) for mask, share in enumerate(shares) if mask > 0]
        return [[shares[0], *come]], [other for other in dims if other != d]

    def scatter_rest(self, state, start=0):
        for d in self.rest[start:]:
            state = self.scatter(*state, d)
        total = 0.0
        for array in state[0][0]:
            total = total + array.astype(F32)
        return total[0]

    def begin_gather(self, state, d):
        array, dims = state
        come = [self.send(array, d, mask) for mask in range(1, self.counts([d])[0])]
        return array, come, dims, d

    def end_gather(self, begun, tick=None):
        array, come, dims, d = begun
        parts = [array] + come
        for bit in range(len(parts).bit_length() - 1):
            flag = (self.place(d) >> bit) & 1
            for low in range(len(parts)):
                if not low & (1 << bit):
                    high = low | (1 << bit)
                    parts[low], parts[high] = pick(flag, parts[low], parts[high])
        dims = [other for other in self.dims if other in dims or other == d]
        joined = jnp.stack(parts, axis=dims.index(d))
        if tick is not None:
            joined = joined + tick[0, 0].astype(joined.dtype)
        return joined, dims

    def gather(self, state, d, tick=None):
        return self.end_gather(self.begin_gather(state, d), tick)

def body(
    tokens,
    segments,
    ln1_gain,
    ln1_bias,
    qkv_weight,
    q_bias,
    v_bias,
    out_weight,
    out_bias,
    ln2_gain,
    ln2_bias,
    up_weight,
    up_bias,
    down_weight,
    down_bias,
    cotangent,
):
    side = lax.axis_index("xx")
    core = lax.axis_index("core")
    chips = lax.axis_size("dp") * lax.axis_size("xx")
    seq_count, quarter, width = tokens.shape
    length = segments.shape[1]
    own = qkv_weight.shape[0]
    pair_row = 2 * own
    hidden_own = up_bias.shape[0]
    half = width // 2
    cols = 3 * half
    pairs = half // PAIR
    splits = hidden_own // pair_row
    hidden = splits * width

    def at_index(array, index):
        return lax.dynamic_index_in_dim(array, index, 0, keepdims=False)

    def to_sequence(array, tick=None):
        kept = at_index(array, side)
        sent = at_index(array, 1 - side)
        if tick is not None:
            sent = sent + tick[0, 0].astype(sent.dtype)
        come = swap(sent, "xx")
        low, high = pick(side, kept, come)
        mine = jnp.stack([low, high])
        other = swap(mine, "core")
        even, odd = pick(core, mine, other)
        return jnp.stack([even, odd], axis=1).reshape(length, width), come, other

    def own_rows(array):
        return lax.dynamic_index_in_dim(
            array.reshape(2, 2, quarter, array.shape[-1]), core, 1, keepdims=False
        )

    def other_rows(array):
        return lax.dynamic_index_in_dim(
            array.reshape(2, 2, quarter, array.shape[-1]), 1 - core, 1, keepdims=False
        )

    def from_sequence(mine):
        come = swap(at_index(mine, 1 - side), "xx")
        return merged(at_index(mine, side), come), come

    def merged(kept, come, tick=None):
        if tick is not None:
            kept = kept + tick[0, 0].astype(kept.dtype)
        first, second = pick(side, kept, come)
        return jnp.stack([first, second])

    qkv_cols = qkv_weight.reshape(own, 3, 2, pairs, PAIR).transpose(2, 0, 3, 1, 4).reshape(2, own, cols)
    up_cols = (
        up_weight.reshape(own, chips, 2, splits, pair_row)
        .transpose(2, 0, 3, 1, 4)
        .reshape(2, own, hidden)
    )
    vectors = jnp.stack(
        [ln1_gain, ln1_bias, q_bias, v_bias, out_bias, ln2_gain, ln2_bias, down_bias], axis=1
    )
    vectors = jnp.pad(vectors, ((0, 0), (0, PAIR - vectors.shape[1])))

    def with_partner(two):
        mine, theirs = at_index(two, core), at_index(two, 1 - core)
        first, second = pick(core, mine, swap(theirs, "core"))
        return jnp.concatenate([first, second], axis=0)

    early = with_partner(
        jnp.concatenate([qkv_cols, jnp.broadcast_to(vectors, (2, own, PAIR))], axis=2)
    )
    early = jnp.concatenate(
        [
            early[:, : cols + 8],
            up_bias.reshape(splits, pair_row).T,
            early[:, cols + 8 + splits :],
        ],
        axis=1,
    )
    links = Links()

    def gather_rest(array, tick=None):
        state = (array, [])
        for d in links.rest:
            state = links.gather(state, d, tick if d == links.rest[-1] else None)
        return state

    def halves_of(state):
        middle = state[0].shape[-1] // 2
        return [(state[0][..., :middle], state[1]), (state[0][..., middle:], state[1])]

    def joined(halves):
        return [half_state[0].reshape(width, -1) for half_state in halves]

    inputs_low, come, other = to_sequence(tokens)
    grad_out_low, grad_come, _ = to_sequence(cotangent, gate([come]))
    state = (early, [])
    for d in links.rest[:-1]:
        state = links.gather(state, d)
    first_stage = links.begin_gather(state, links.rest[-1])
    begun = [
        links.begin_gather(piece, d)
        for piece, d in zip(halves_of(links.end_gather(first_stage)), "yx")
    ]
    early_halves = [links.end_gather(piece) for piece in begun]
    early_a, early_b = joined(
        [links.gather(piece, d) for piece, d in zip(early_halves, "xy")]
    )
    split = early_a.shape[1]
    late = with_partner(
        jnp.concatenate([up_cols, jnp.broadcast_to(out_weight, (2, own, width))], axis=2)
    )
    down_own = down_weight.reshape(splits, pair_row, width)
    late = pack(
        [late, *(down_own[i] for i in range(splits))], [block for block in first_stage[1]] + [come]
    )
    late = lax.all_gather(late, ("dp", "xx"), axis=0, tiled=True)
    small = early_b[:, cols - split :].astype(F32).T
    gain_one, shift_one, query_shift, value_shift, out_shift, gain_two, shift_two, down_shift = (
        small[i] for i in range(8)
    )
    up_shift = small[8 : 8 + splits].reshape(hidden)

    inputs = inputs_low.astype(F32)
    seg = at_index(segments, side)
    numbers = jnp.arange(PAIR, dtype=jnp.int32) % HEAD_DIM
    same = seg[:, None] == numbers[None, :]
    coded = numbers[None, :] < 4
    query_code = jnp.where(same & coded, 1.0, 0.0).astype(BF16)
    key_code = jnp.where(same | ~coded, 0.0, NEG).astype(BF16)

    def head_cols(vector):
        return lax.dynamic_slice_in_dim(vector, core * half, half, 0).reshape(pairs, 1, PAIR)

    zeros = jnp.zeros((pairs, 1, PAIR), F32)
    qkv_shift = jnp.concatenate(
        [head_cols(query_shift), zeros, head_cols(value_shift)], axis=1
    ).reshape(1, cols)
    qkv_scale = jnp.tile(jnp.repeat(jnp.array([0.125, 1.0, 1.0], F32), PAIR), pairs)[None]
    normed_t, qkv, tick = qkv_projection(
        inputs_low,
        early_a,
        early_b,
        jnp.pad(jnp.stack([gain_one, shift_one]), ((0, 6), (0, 0))),
        jnp.pad(jnp.concatenate([qkv_shift, qkv_scale]), ((0, 6), (0, 0))),
        [],
    )
    attended, log_total, _ = attention_forward(qkv, query_code, key_code, [grad_come])
    core_at = core.reshape(1).astype(jnp.int32)
    branch = out_projection(core_at, attended, late, splits, [])
    branch_come = swap(branch, "core")
    mid_vectors = jnp.pad(
        jnp.stack([out_shift, gain_two, shift_two, down_shift]), ((0, 4), (0, 0))
    )
    normed_two_low, hidden_low, grad_pre_low, mixed_part, ffn_other, partial_two, up_sums = feed_forward(
        core_at,
        inputs_low,
        branch,
        branch_come,
        grad_out_low,
        late,
        splits,
        mid_vectors,
        jnp.pad(up_shift[None], ((0, 7), (0, 0))),
    )
    partial_come = swap(partial_two, "core")
    def blocks(array):
        return array.reshape(chips, pair_row, array.shape[1])

    grad_proj_down = [
        mm(hidden_low[:, i * width : (i + 1) * width], grad_out_low, TN).astype(BF16)
        for i in range(splits)
    ]
    grad_proj_up = mm(normed_two_low, grad_pre_low, TN).astype(BF16)
    late_grads = jnp.concatenate([grad_proj_up, *grad_proj_down], axis=1)
    late_own = lax.psum_scatter(late_grads, "dp", scatter_dimension=0, tiled=True)
    grad_middle, branch_low, grad_attended, mid_sums = norm_two(
        core_at,
        inputs_low,
        branch,
        branch_come,
        grad_out_low,
        partial_two,
        partial_come,
        late,
        splits,
        mid_vectors,
        [late_grads],
    )
    grad_proj_out = mm(attended, branch_low, TN)

    def as_column(vectors):
        table = jnp.stack(vectors, axis=1)
        return jnp.pad(table, ((0, 0), (0, PAIR - table.shape[1])))

    def only_mine(flag, array):
        return jnp.where(flag, array, jnp.zeros_like(array))

    small_two = [mid_sums[i] for i in range(4)] + [
        up_sums[0, i * width : (i + 1) * width] for i in range(splits)
    ]
    out_low = grad_proj_out.astype(BF16)
    grad_out_rows = jnp.concatenate(
        [only_mine(core == 0, out_low), only_mine(core == 1, out_low)], axis=0
    )

    def pairs_backward(first, count, after):
        return attention_backward(
            first, count, qkv, query_code, key_code, attended, grad_attended, log_total, normed_t, after
        )

    out_piece = links.scatter([[blocks(grad_out_rows)]], links.dims, "y")
    ffn_come = swap(ffn_other + mid_sums[7, 0].astype(BF16), "core")
    mixed_own = (mixed_part + ffn_come.astype(F32)).astype(BF16).reshape(2, quarter, width)
    mixed_come = swap(at_index(mixed_own, 1 - side), "xx")
    grad_a, weight_grad_a, tick = pairs_backward(0, pairs - 1, [out_piece[0][0][0]])
    first_piece = links.scatter([[blocks(weight_grad_a)]], links.dims, "y", [tick])
    mixed = merge(at_index(mixed_own, side), mixed_come, side, [tick])
    grad_b, weight_grad_b, tick = pairs_backward(
        pairs - 1, 1, [first_piece[0][0][0], tick, mixed]
    )
    grads = [grad_a, grad_b]
    first_piece = links.scatter(out_piece[0] + first_piece[0], first_piece[1], "x", [tick])
    last_piece = links.scatter([[blocks(weight_grad_b)]], links.rest + ["yx"], "yx", [tick])
    norm_vectors = jnp.pad(jnp.stack([gain_one, shift_one]), ((0, 6), (0, 0)))
    partial_one, norm_sums, bias_sums, tick = norm_one(
        False, core_at, grads, early_a, early_b, cols, inputs_low, [], [first_piece[0][0][0], last_piece[0][0][0]]
    )
    come = swap(partial_one, "core")
    token_own, norm_sums_own, bias_sums_own, tick = norm_one(
        True,
        core_at,
        grads,
        early_a,
        early_b,
        cols,
        inputs_low,
        [come, grad_middle, norm_vectors],
        [late_own],
    )
    norm_sums = norm_sums + norm_sums_own
    bias_sums = bias_sums + bias_sums_own
    token_grad, come = from_sequence(token_own.reshape(2, quarter, width))
    grad_by_pair = bias_sums[0].reshape(pairs, 3, PAIR)

    def padded(vector):
        vector = vector.reshape(half)
        return jnp.concatenate([only_mine(core == 0, vector), only_mine(core == 1, vector)])

    small = as_column(
        [
            norm_sums[0],
            norm_sums[1],
            padded(grad_by_pair[:, 0]),
            padded(grad_by_pair[:, 2]),
        ]
        + small_two
    )
    late_piece = links.scatter([[late_own.reshape(2, pair_row, -1)]], ["x"], "x", [tick])
    small_piece = links.scatter([[blocks(small.astype(BF16))]], links.rest + ["yx"], "yx", [tick])
    first_piece = links.scatter(
        first_piece[0] + last_piece[0] + small_piece[0],
        first_piece[1],
        links.rest[0],
        late_piece[0][0][1:],
    )
    first_ready = first_piece[0][0][0]
    first_own = links.scatter_rest(first_piece, 1)

    def rows_of(array, index):
        return lax.dynamic_slice_in_dim(array, index * own, own, 0)

    def by_core(mine, come):
        return jnp.stack(pick(core, mine, come))

    def shared(array):
        return rows_of(array, core), swap(rows_of(array, 1 - core), "core")

    up_own, down_grad = widen(*(array[0] for array in late_piece[0][0]), width, [first_ready])
    late_mine, late_come = shared(up_own)
    first_mine, first_come = shared(first_own)
    out_grad = first_mine[:, :width] + first_come[:, :width]
    up_grad = (
        by_core(late_mine, late_come)
        .reshape(2, own, splits, chips, pair_row)
        .transpose(1, 3, 0, 2, 4)
        .reshape(own, 2 * hidden)
        .astype(F32)
    )
    down_grad = down_grad.reshape(hidden_own, width)
    tail = width + cols + 8
    qkv_grad = (
        by_core(first_mine[:, width : width + cols], first_come[:, width : width + cols])
        .reshape(2, own, pairs, 3, PAIR)
        .transpose(1, 3, 0, 2, 4)
        .reshape(own, 2 * cols)
    )
    small_mine = first_mine[:, tail - 8 : tail]
    one = small_mine[:, :4] + first_come[:, tail - 8 : tail - 4]
    up_shift_grad = first_own[:, tail : tail + splits].T.reshape(hidden_own)
    two = small_mine[:, 4:]
    return (
        mixed,
        token_grad,
        one[:, 0],
        one[:, 1],
        qkv_grad,
        one[:, 2],
        one[:, 3],
        out_grad,
        two[:, 0],
        two[:, 1],
        two[:, 2],
        up_grad,
        up_shift_grad,
        down_grad,
        two[:, 3],
    )


def solution(mesh):
    parts = (mesh.shape["dp"], mesh.shape["ctx"] // 2, 2)
    split_mesh = Mesh(mesh.devices.reshape(parts), ("dp", "xx", "core"))
    rows = ("dp", "xx", "core")
    acts = P("dp", ("xx", "core"), None)
    vec, mat = P(rows), P(rows, None)
    return jax.shard_map(
        body,
        mesh=split_mesh,
        in_specs=(
            acts, P("dp", None), vec, vec, mat, vec, vec, mat, vec, vec, vec, mat, vec, mat, vec, acts,
        ),
        out_specs=(
            acts, acts, vec, vec, mat, vec, vec, mat, vec, vec, vec, mat, vec, mat, vec,
        ),
        check_vma=False,
    )
```

```python
import functools

import jax
import jax.numpy as jnp
from jax import lax
from jax.experimental import pallas as pl
from jax.experimental.pallas import tpu as pltpu
from jax.sharding import Mesh, PartitionSpec as P

HEAD_DIM = 64
PAIR = 2 * HEAD_DIM
EPSILON = 1e-05
NEG = -1e30
BLK = 512
F32 = jnp.float32
BF16 = jnp.bfloat16

NN = (((1,), (0,)), ((), ()))
NT = (((1,), (1,)), ((), ()))
TN = (((0,), (0,)), ((), ()))


def mm(left, right, dims=NN):
    return lax.dot_general(left, right, dims, preferred_element_type=F32)


def build_scores_operands(qkv_ref, qs_ref, ks_ref, rows, qx, kx):
    lane = lax.broadcasted_iota(jnp.int32, (BLK, PAIR), 1)
    first = lane < HEAD_DIM
    q = qkv_ref[rows, 0:PAIR].astype(F32)
    k = qkv_ref[rows, PAIR : 2 * PAIR].astype(F32)
    qs = qs_ref[rows, :].astype(F32)
    ks = ks_ref[rows, :].astype(F32)
    qx[0, rows, :] = jnp.where(first, q, qs).astype(BF16)
    qx[1, rows, :] = jnp.where(first, qs, q).astype(BF16)
    kx[0, rows, :] = jnp.where(first, k, ks).astype(BF16)
    kx[1, rows, :] = jnp.where(first, ks, k).astype(BF16)
    return first, q, k


def causal_block(scores):
    key_at = lax.broadcasted_iota(jnp.int32, scores.shape, 0)
    query_at = lax.broadcasted_iota(jnp.int32, scores.shape, 1)
    return jnp.where(key_at <= query_at, scores, NEG)


def attention_forward_kernel(qkv_ref, qs_ref, ks_ref, *rest):
    o_ref, lse_ref, tick_ref, qx, kx, vt, acc = rest[-7:]
    tick_ref[...] = jnp.zeros_like(tick_ref)
    length = qkv_ref.shape[0]
    blocks = length // BLK

    @pl.loop(0, blocks)
    def _(i):
        rows = pl.ds(pl.multiple_of(i * BLK, BLK), BLK)
        build_scores_operands(qkv_ref, qs_ref, ks_ref, rows, qx, kx)
        v_t = qkv_ref[rows, 2 * PAIR : 3 * PAIR].astype(F32).T
        ones = jnp.ones((16, BLK), BF16)
        for h in range(2):
            vt[h, 0:HEAD_DIM, rows] = v_t[h * HEAD_DIM : (h + 1) * HEAD_DIM].astype(BF16)
            vt[h, HEAD_DIM : HEAD_DIM + 16, rows] = ones

    @pl.loop(0, blocks)
    def _(i):
        rows = pl.ds(pl.multiple_of(i * BLK, BLK), BLK)
        queries = [qx[h, rows, :] for h in range(2)]
        tops = []
        for h in range(2):
            s = causal_block(mm(kx[h, rows, :], queries[h], NT))
            top = jnp.max(s, axis=0, keepdims=True)
            p = jnp.exp(s - top).astype(BF16)
            acc[h] = mm(vt[h, :, rows], p)
            tops.append(top)

        def step(j, carry):
            keys = pl.ds(pl.multiple_of(j * BLK, BLK), BLK)
            out = []
            for h in range(2):
                s = mm(kx[h, keys, :], qx[h, rows, :], NT)
                top = jnp.maximum(carry[h], jnp.max(s, axis=0, keepdims=True))
                p = jnp.exp(s - top).astype(BF16)
                acc[h] = acc[h] * jnp.exp(carry[h] - top) + mm(vt[h, :, keys], p)
                out.append(top)
            return tuple(out)

        tops = lax.fori_loop(0, i, step, tuple(tops))
        parts = []
        for h in range(2):
            total = acc[h, HEAD_DIM : HEAD_DIM + 1, :]
            parts.append(acc[h, 0:HEAD_DIM, :] / total)
            lse_ref[0, h : h + 1, rows] = tops[h] + jnp.log(total)
        o_ref[rows, :] = jnp.concatenate(parts, axis=0).T.astype(BF16)


def attention_backward_kernel(qkv_ref, qs_ref, ks_ref, o_ref, do_ref, lse_ref, at_ref, *rest):
    d_ref, dw_ref, tick_ref, qx, kx, qm, dm, kt, delta, dqt, dk, dv = rest[-12:]
    tick_ref[...] = jnp.zeros_like(tick_ref)
    length = qkv_ref.shape[0]
    blocks = length // BLK

    @pl.loop(0, blocks)
    def _(i):
        rows = pl.ds(pl.multiple_of(i * BLK, BLK), BLK)
        first, q, k = build_scores_operands(qkv_ref, qs_ref, ks_ref, rows, qx, kx)
        do = do_ref[rows, :].astype(F32)
        zero = jnp.zeros_like(q)
        qm[0, rows, :] = jnp.where(first, q, zero).astype(BF16)
        qm[1, rows, :] = jnp.where(first, zero, q).astype(BF16)
        dm[0, rows, :] = jnp.where(first, do, zero).astype(BF16)
        dm[1, rows, :] = jnp.where(first, zero, do).astype(BF16)
        kt[:, rows] = k.T.astype(BF16)
        inner = (do * o_ref[rows, :].astype(F32)).T
        for h in range(2):
            delta[h : h + 1, rows] = jnp.sum(
                inner[h * HEAD_DIM : (h + 1) * HEAD_DIM], axis=0, keepdims=True
            )
        dqt[:, rows] = jnp.zeros((PAIR, BLK), F32)

    def tile(keys, rows, masked):
        values = qkv_ref[keys, 2 * PAIR : 3 * PAIR]
        dv_part, dk_part = None, None
        for h in range(2):
            s = mm(kx[h, keys, :], qx[h, rows, :], NT)
            if masked:
                s = causal_block(s)
            p = jnp.exp(s - lse_ref[0, h : h + 1, rows])
            dp = mm(values, dm[h, rows, :], NT)
            ds = (p * (dp - delta[h : h + 1, rows])).astype(BF16)
            dv_h = mm(p.astype(BF16), dm[h, rows, :])
            dk_h = mm(ds, qm[h, rows, :])
            dv_part = dv_h if h == 0 else dv_part + dv_h
            dk_part = dk_h if h == 0 else dk_part + dk_h
            part = slice(h * HEAD_DIM, (h + 1) * HEAD_DIM)
            dqt[part, rows] += mm(kt[part, keys], ds)
        return dk_part, dv_part

    @pl.loop(0, blocks)
    def _(j):
        keys = pl.ds(pl.multiple_of(j * BLK, BLK), BLK)
        dk[...], dv[...] = tile(keys, keys, True)

        @pl.loop(j + 1, blocks)
        def _(i):
            dk_part, dv_part = tile(keys, pl.ds(pl.multiple_of(i * BLK, BLK), BLK), False)
            dk[...] += dk_part
            dv[...] += dv_part

        d_ref[keys, PAIR : 2 * PAIR] = dk[...].astype(BF16)
        d_ref[keys, 2 * PAIR : 3 * PAIR] = dv[...].astype(BF16)

    @pl.loop(0, blocks)
    def _(i):
        rows = pl.ds(pl.multiple_of(i * BLK, BLK), BLK)
        d_ref[rows, 0:PAIR] = (dqt[:, rows].T.astype(BF16).astype(F32) * 0.125).astype(BF16)

    @pl.loop(0, dw_ref.shape[0] // ROWS)
    def _(i):
        rows = pl.ds(pl.multiple_of(i * ROWS, ROWS), ROWS)
        dw_ref[rows, :] = mm(at_ref[rows, :], d_ref[...]).astype(BF16)


VMEM_LIMIT = 48 * 1024 * 1024


SMALL_COST = pl.CostEstimate(flops=1000, bytes_accessed=1000, transcendentals=0)


TICK = jax.ShapeDtypeStruct((8, 128), F32)
TICK_SPEC = pl.BlockSpec((8, 128), lambda i: (0, 0))
ANY_SPEC = pl.BlockSpec(memory_space=pl.ANY)


def pack_kernel(count, refs):
    refs[-1][...] = jnp.concatenate([ref[...] for ref in refs[:count]], axis=-1)


def pack(parts, after):
    rows = parts[0].shape[0]
    width = sum(part.shape[1] for part in parts)
    return pl.pallas_call(
        lambda *refs: pack_kernel(len(parts), refs),
        grid=(1,),
        in_specs=[pl.BlockSpec(part.shape, lambda i: (0, 0)) for part in parts]
        + [ANY_SPEC] * len(after),
        out_specs=pl.BlockSpec((rows, width), lambda i: (0, 0)),
        out_shape=jax.ShapeDtypeStruct((rows, width), BF16),
        compiler_params=pltpu.CompilerParams(vmem_limit_bytes=VMEM_LIMIT),
        cost_estimate=SMALL_COST,
    )(*parts, *after)


def widen(source, width, after):
    rows, cols = source.shape
    count = cols // width - 2

    def kernel(source_ref, *refs):
        up_ref, down_ref = refs[-2:]
        up_ref[...] = source_ref[:, : 2 * width].astype(F32)
        for i in range(count):
            down_ref[i] = source_ref[:, (2 + i) * width : (3 + i) * width].astype(F32)

    return pl.pallas_call(
        kernel,
        grid=(1,),
        in_specs=[pl.BlockSpec((rows, cols), lambda i: (0, 0))] + [ANY_SPEC] * len(after),
        out_specs=[
            pl.BlockSpec((rows, 2 * width), lambda i: (0, 0)),
            pl.BlockSpec((count, rows, width), lambda i: (0, 0, 0)),
        ],
        out_shape=[
            jax.ShapeDtypeStruct((rows, 2 * width), F32),
            jax.ShapeDtypeStruct((count, rows, width), F32),
        ],
        compiler_params=pltpu.CompilerParams(vmem_limit_bytes=VMEM_LIMIT),
        cost_estimate=SMALL_COST,
    )(source, *after)


def merge(kept, come, side, after):
    def kernel(side_ref, kept_ref, come_ref, *rest):
        mine = pl.program_id(0) == side_ref[0]

        @pl.when(mine)
        def _():
            rest[-1][0] = kept_ref[...]

        @pl.when(jnp.logical_not(mine))
        def _():
            rest[-1][0] = come_ref[...]

    whole = pl.BlockSpec(kept.shape, lambda i, side_ref: (0, 0))
    return pl.pallas_call(
        kernel,
        grid_spec=pltpu.PrefetchScalarGridSpec(
            num_scalar_prefetch=1,
            grid=(2,),
            in_specs=[whole, whole] + [ANY_SPEC] * len(after),
            out_specs=pl.BlockSpec((1, *kept.shape), lambda i, side_ref: (i, 0, 0)),
        ),
        out_shape=jax.ShapeDtypeStruct((2, *kept.shape), kept.dtype),
        compiler_params=pltpu.CompilerParams(vmem_limit_bytes=VMEM_LIMIT),
        cost_estimate=SMALL_COST,
    )(side.reshape(1).astype(jnp.int32), kept, come, *after)


def gate_kernel(*refs):
    refs[-1][...] = jnp.zeros_like(refs[-1])


def gate(after):
    return pl.pallas_call(
        gate_kernel,
        grid=(1,),
        in_specs=[ANY_SPEC] * len(after),
        out_specs=TICK_SPEC,
        out_shape=TICK,
        cost_estimate=SMALL_COST,
    )(*after)


def fold_kernel(parts, comes, outs, refs):
    for m in range(outs):
        value = None
        for term in range(1 + comes):
            at = 1 + (term * outs + m) * parts
            side = jnp.concatenate([ref[0] for ref in refs[at : at + parts]], axis=-1)
            if comes:
                side = side.astype(F32)
            value = side if term == 0 else value + side
        refs[len(refs) - outs + m][0] = value.astype(BF16)


def fold(parts, comes, sizes, axis, at, after):
    blocks, rows = parts[0].shape[:2]
    width = sum(part.shape[2] for part in parts)
    outs = sizes[axis] if axis is not None else 1
    inner = 1
    if axis is not None:
        for size in sizes[axis + 1 :]:
            inner *= size

    def spec(array, m):
        def index(j, at_ref):
            if axis is None:
                return j, 0, 0
            return (j // inner) * (outs * inner) + (at_ref[0] ^ m) * inner + j % inner, 0, 0

        return pl.BlockSpec((1, rows, array.shape[2]), index)

    def kernel(*refs):
        ins = 1 + (1 + len(comes)) * len(parts) * outs
        fold_kernel(len(parts), len(comes), outs, refs[:ins] + refs[ins + len(after) :])

    out = pl.BlockSpec((1, rows, width), lambda j, at_ref: (j, 0, 0))
    return pl.pallas_call(
        kernel,
        grid_spec=pltpu.PrefetchScalarGridSpec(
            num_scalar_prefetch=1,
            grid=(blocks // outs,),
            in_specs=[spec(part, m) for m in range(outs) for part in parts]
            + [spec(part, m) for come in comes for m in range(outs) for part in come]
            + [ANY_SPEC] * len(after),
            out_specs=[out] * outs,
        ),
        out_shape=[jax.ShapeDtypeStruct((blocks // outs, rows, width), BF16)] * outs,
        compiler_params=pltpu.CompilerParams(vmem_limit_bytes=VMEM_LIMIT),
        cost_estimate=SMALL_COST,
    )(at.reshape(1).astype(jnp.int32), *(list(parts) * outs), *[part for come in comes for part in list(come) * outs], *after)


def qkv_kernel(x_ref, wa_ref, wb_ref, vec_ref, col_ref, *rest_refs):
    a_ref, qkv_ref, tick_ref = rest_refs[-3:]
    split = wa_ref.shape[1]
    rest = qkv_ref.shape[1] - split
    for part in range(2):
        rows = slice(part * ROWS, (part + 1) * ROWS)
        normal, _ = norm_forward(x_ref[rows, :].astype(F32))
        normed = (normal * vec_ref[0:1, :] + vec_ref[1:2, :]).astype(BF16)
        a_ref[:, rows] = normed.astype(F32).T.astype(BF16)
        for w, cols in ((wa_ref[...], slice(0, split)), (wb_ref[:, :rest], slice(split, None))):
            shift, scale = col_ref[0:1, cols], col_ref[1:2, cols]
            qkv_ref[rows, cols] = ((mm(normed, w) + shift) * scale).astype(BF16)
    tick_ref[...] = jnp.zeros_like(tick_ref)


def qkv_projection(inputs, weight_a, weight_b, vectors, columns, after):
    length, width = inputs.shape
    cols = columns.shape[1]
    return pl.pallas_call(
        qkv_kernel,
        grid=(length // (2 * ROWS),),
        in_specs=[
            pl.BlockSpec((2 * ROWS, width), lambda i: (i, 0)),
            pl.BlockSpec(weight_a.shape, lambda i: (0, 0)),
            pl.BlockSpec(weight_b.shape, lambda i: (0, 0)),
            pl.BlockSpec(vectors.shape, lambda i: (0, 0)),
            pl.BlockSpec(columns.shape, lambda i: (0, 0)),
        ]
        + [ANY_SPEC] * len(after),
        out_specs=[
            pl.BlockSpec((width, 2 * ROWS), lambda i: (0, i)),
            pl.BlockSpec((2 * ROWS, cols), lambda i: (i, 0)),
            TICK_SPEC,
        ],
        out_shape=[
            jax.ShapeDtypeStruct((width, length), BF16),
            jax.ShapeDtypeStruct((length, cols), BF16),
            TICK,
        ],
        compiler_params=pltpu.CompilerParams(vmem_limit_bytes=VMEM_LIMIT),
        cost_estimate=SMALL_COST,
    )(inputs, weight_a, weight_b, vectors, columns, *after)


def out_projection(core, attended, late, block, after):
    length, cols = attended.shape
    width = late.shape[0]
    rows = length // 4

    def kernel(core_ref, a_ref, w_ref, *rest):
        rest[-1][...] = mm(a_ref[...], w_ref[...]).astype(BF16)

    return pl.pallas_call(
        kernel,
        grid_spec=pltpu.PrefetchScalarGridSpec(
            num_scalar_prefetch=1,
            grid=(4,),
            in_specs=[
                pl.BlockSpec((rows, cols), lambda i, core_ref: (i, 0)),
                pl.BlockSpec((cols, width), lambda i, core_ref: (core_ref[0], block)),
            ]
            + [ANY_SPEC] * len(after),
            out_specs=pl.BlockSpec((rows, width), lambda i, core_ref: (i, 0)),
        ),
        out_shape=jax.ShapeDtypeStruct((length, width), BF16),
        compiler_params=pltpu.CompilerParams(vmem_limit_bytes=VMEM_LIMIT),
        cost_estimate=SMALL_COST,
    )(core, attended, late, *after)


def middle_of(x_ref, b0_ref, b1_ref, vec_ref):
    both = b0_ref[...].astype(F32) + b1_ref[...].astype(F32)
    return x_ref[...].astype(F32) + both + vec_ref[0:1, :]


def feed_forward_kernel(splits, core_ref, x_ref, b0_ref, b1_ref, dy_ref, up_ref, *rest):
    down_refs, (vec_ref, shift_ref) = rest[:splits], rest[splits : splits + 2]
    a_ref, g_ref, du_ref, own_ref, other_ref, dh_ref, sums_ref = rest[splits + 2 :]
    at = pl.program_id(0)

    @pl.when(at == 0)
    def _():
        sums_ref[...] = jnp.zeros_like(sums_ref)

    middle = middle_of(x_ref, b0_ref, b1_ref, vec_ref)
    normal, _ = norm_forward(middle)
    normed = (normal * vec_ref[1:2, :] + vec_ref[2:3, :]).astype(BF16)
    a_ref[...] = normed
    dy = dy_ref[...]
    ffn, dh = None, None
    width = dy.shape[1]
    for i, down_ref in enumerate(down_refs):
        cols = slice(i * width, (i + 1) * width)
        up, down = up_ref[:, cols], down_ref[...]
        value, slope = gelu_parts(mm(normed, up) + shift_ref[0:1, cols])
        du = slope * mm(dy, down, NT)
        value, du = value.astype(BF16), du.astype(BF16)
        g_ref[:, cols] = value
        du_ref[:, cols] = du
        sums_ref[0:1, cols] += jnp.sum(du.astype(F32), axis=0, keepdims=True)
        ffn_part, dh_part = mm(value, down), mm(du, up, NT)
        ffn = ffn_part if i == 0 else ffn + ffn_part
        dh = dh_part if i == 0 else dh + dh_part
    dh_ref[...] = dh.astype(BF16)
    mine = at % 2 == core_ref[0]

    @pl.when(mine)
    def _():
        own_ref[...] = middle_of(x_ref, b0_ref, b1_ref, vec_ref) + ffn + vec_ref[3:4, :]

    @pl.when(jnp.logical_not(mine))
    def _():
        other_ref[...] = ffn.astype(BF16)


def feed_forward(core, inputs, branch, branch_come, grad_out, late, splits, vectors, up_shift):
    length, width = inputs.shape
    rows = length // 4
    hidden = splits * width
    narrow = pl.BlockSpec((rows, width), lambda i, core_ref: (i, 0))
    wide = pl.BlockSpec((rows, hidden), lambda i, core_ref: (i, 0))
    shared = pl.BlockSpec((rows, width), lambda i, core_ref: (i // 2, 0))

    def whole(array):
        return pl.BlockSpec(array.shape, lambda i, core_ref: (0, 0))

    def down(i):
        return pl.BlockSpec((width, width), lambda _, core_ref: (0, splits + 1 + i))

    return pl.pallas_call(
        functools.partial(feed_forward_kernel, splits),
        grid_spec=pltpu.PrefetchScalarGridSpec(
            num_scalar_prefetch=1,
            grid=(4,),
            in_specs=[narrow] * 4
            + [pl.BlockSpec((width, hidden), lambda i, core_ref: (0, 0))]
            + [down(i) for i in range(splits)]
            + [whole(vectors), whole(up_shift)],
            out_specs=[
                narrow, wide, wide, shared, shared, narrow,
                pl.BlockSpec((8, hidden), lambda i, core_ref: (0, 0)),
            ],
        ),
        out_shape=[
            jax.ShapeDtypeStruct((length, width), BF16),
            jax.ShapeDtypeStruct((length, hidden), BF16),
            jax.ShapeDtypeStruct((length, hidden), BF16),
            jax.ShapeDtypeStruct((length // 2, width), F32),
            jax.ShapeDtypeStruct((length // 2, width), BF16),
            jax.ShapeDtypeStruct((length, width), BF16),
            jax.ShapeDtypeStruct((8, hidden), F32),
        ],
        compiler_params=pltpu.CompilerParams(vmem_limit_bytes=VMEM_LIMIT),
        cost_estimate=SMALL_COST,
    )(core, inputs, branch, branch_come, grad_out, late, *([late] * splits), vectors, up_shift)


def norm_two_kernel(core_ref, x_ref, b0_ref, b1_ref, dy_ref, p0_ref, p1_ref, w_ref, vec_ref, *rest):
    mid_ref, low_ref, do_ref, sums_ref = rest[-4:]

    @pl.when(pl.program_id(0) == 0)
    def _():
        sums_ref[...] = jnp.zeros_like(sums_ref)

    normal, scale = norm_forward(middle_of(x_ref, b0_ref, b1_ref, vec_ref))
    grad = p0_ref[...].astype(F32) + p1_ref[...].astype(F32)
    dy = dy_ref[...].astype(F32)
    mid = dy + norm_backward(normal, scale, grad * vec_ref[1:2, :])
    low = mid.astype(BF16)
    low_ref[...] = low
    do_ref[...] = mm(low, w_ref[...], NT).astype(BF16)
    for i, value in enumerate((low.astype(F32), grad * normal, grad, dy)):
        sums_ref[i : i + 1, :] += jnp.sum(value, axis=0, keepdims=True)

    @pl.when(pl.program_id(0) % 2 == core_ref[0])
    def _():
        mid_ref[...] = mid


def norm_two(core, inputs, branch, branch_come, grad_out, partial, partial_come, late, block, vectors, after):
    length, width = inputs.shape
    rows = length // 4
    cols = width // 2
    narrow = pl.BlockSpec((rows, width), lambda i, core_ref: (i, 0))
    return pl.pallas_call(
        norm_two_kernel,
        grid_spec=pltpu.PrefetchScalarGridSpec(
            num_scalar_prefetch=1,
            grid=(4,),
            in_specs=[narrow] * 6
            + [
                pl.BlockSpec((cols, width), lambda i, core_ref: (core_ref[0], block)),
                pl.BlockSpec(vectors.shape, lambda i, core_ref: (0, 0)),
            ]
            + [ANY_SPEC] * len(after),
            out_specs=[
                pl.BlockSpec((rows, width), lambda i, core_ref: (i // 2, 0)),
                narrow,
                pl.BlockSpec((rows, cols), lambda i, core_ref: (i, 0)),
                pl.BlockSpec((8, width), lambda i, core_ref: (0, 0)),
            ],
        ),
        out_shape=[
            jax.ShapeDtypeStruct((length // 2, width), F32),
            jax.ShapeDtypeStruct((length, width), BF16),
            jax.ShapeDtypeStruct((length, cols), BF16),
            jax.ShapeDtypeStruct((8, width), F32),
        ],
        compiler_params=pltpu.CompilerParams(vmem_limit_bytes=VMEM_LIMIT),
        cost_estimate=SMALL_COST,
    )(core, inputs, branch, branch_come, grad_out, partial, partial_come, late, vectors, *after)


ROWS = 256


def attention_forward(qkv, query_code, key_code, after):
    length, width = qkv.shape
    pairs = width // (3 * PAIR)
    return pl.pallas_call(
        attention_forward_kernel,
        grid=(pairs,),
        in_specs=[
            pl.BlockSpec((length, 3 * PAIR), lambda p: (0, p)),
            pl.BlockSpec((length, PAIR), lambda p: (0, 0)),
            pl.BlockSpec((length, PAIR), lambda p: (0, 0)),
        ]
        + [ANY_SPEC] * len(after),
        out_specs=[
            pl.BlockSpec((length, PAIR), lambda p: (0, p)),
            pl.BlockSpec((1, 8, length), lambda p: (p, 0, 0)),
            TICK_SPEC,
        ],
        out_shape=[
            jax.ShapeDtypeStruct((length, pairs * PAIR), BF16),
            jax.ShapeDtypeStruct((pairs, 8, length), F32),
            TICK,
        ],
        scratch_shapes=[
            pltpu.VMEM((2, length, PAIR), BF16),
            pltpu.VMEM((2, length, PAIR), BF16),
            pltpu.VMEM((2, HEAD_DIM + 16, length), BF16),
            pltpu.VMEM((2, HEAD_DIM + 16, BLK), F32),
        ],
        compiler_params=pltpu.CompilerParams(vmem_limit_bytes=VMEM_LIMIT),
        cost_estimate=SMALL_COST,
    )(qkv, query_code, key_code, *after)


def norm_one_kernel(own, core_ref, d0_ref, d1_ref, wa_ref, wb_ref, x_ref, *rest):
    if own:
        come_ref, mid_ref, vec_ref, out_ref, sums_ref, bias_ref, tick_ref, w = rest
    else:
        out_ref, sums_ref, bias_ref, tick_ref, w = rest
    split = wa_ref.shape[1]

    @pl.when(pl.program_id(0) == 0)
    def _():
        sums_ref[...] = jnp.zeros_like(sums_ref)
        bias_ref[...] = jnp.zeros_like(bias_ref)
        w[:, :split] = wa_ref[...]
        w[:, split:] = wb_ref[:, : w.shape[1] - split]
        tick_ref[...] = jnp.zeros_like(tick_ref)

    total = None
    for i, ref in enumerate((d0_ref, d1_ref)):
        cols = slice(0, ref.shape[1]) if i == 0 else slice(d0_ref.shape[1], None)
        grad = ref[...]
        part = mm(grad, w[:, cols], NT)
        total = part if i == 0 else total + part
        bias_ref[0:1, cols] += jnp.sum(grad.astype(F32), axis=0, keepdims=True)
    normal, scale = norm_forward(x_ref[...].astype(F32))
    sums_ref[0:1, :] += jnp.sum(total * normal, axis=0, keepdims=True)
    sums_ref[1:2, :] += jnp.sum(total, axis=0, keepdims=True)
    if own:
        grad = (total + come_ref[...].astype(F32)) * vec_ref[0:1, :]
        out_ref[...] = (mid_ref[...] + norm_backward(normal, scale, grad)).astype(BF16)
    else:
        out_ref[...] = total.astype(BF16)


def norm_one(own, core, grads, weight_a, weight_b, cols, inputs, extra, after):
    length, width = inputs.shape
    count = length // (2 * ROWS)
    per = count // 2

    def block(i, core_ref):
        which = core_ref[0] if own else 1 - core_ref[0]
        return ((i // per) * 2 + which) * per + i % per, 0

    def at_zero(i, core_ref):
        return 0, 0

    plain = pl.BlockSpec((ROWS, width), lambda i, core_ref: (i, 0))
    rows = pl.BlockSpec((ROWS, width), block)
    in_specs = [pl.BlockSpec((ROWS, grad.shape[1]), block) for grad in grads] + [
        pl.BlockSpec(weight_a.shape, at_zero),
        pl.BlockSpec(weight_b.shape, at_zero),
        rows,
    ]
    out_specs = [
        plain,
        pl.BlockSpec((8, width), at_zero),
        pl.BlockSpec((8, cols), at_zero),
        pl.BlockSpec((8, 128), at_zero),
    ]
    out_shape = [
        jax.ShapeDtypeStruct((count * ROWS, width), BF16),
        jax.ShapeDtypeStruct((8, width), F32),
        jax.ShapeDtypeStruct((8, cols), F32),
        TICK,
    ]
    if own:
        in_specs += [plain, plain, pl.BlockSpec(extra[2].shape, at_zero)]

    def kernel(*refs):
        inner = refs[: 1 + len(in_specs)] + refs[1 + len(in_specs) + len(after) :]
        norm_one_kernel(own, *inner)

    return pl.pallas_call(
        kernel,
        grid_spec=pltpu.PrefetchScalarGridSpec(
            num_scalar_prefetch=1,
            grid=(count,),
            in_specs=in_specs + [ANY_SPEC] * len(after),
            out_specs=out_specs,
            scratch_shapes=[pltpu.VMEM((width, cols), BF16)],
        ),
        out_shape=out_shape,
        compiler_params=pltpu.CompilerParams(vmem_limit_bytes=VMEM_LIMIT),
        cost_estimate=SMALL_COST,
    )(core, *grads, weight_a, weight_b, inputs, *extra, *after)


def attention_backward(
    first, count, qkv, query_code, key_code, attended, grad_attended, log_total, normed_t, after
):
    length = qkv.shape[0]
    width = normed_t.shape[0]
    return pl.pallas_call(
        attention_backward_kernel,
        grid=(count,),
        in_specs=[
            pl.BlockSpec((length, 3 * PAIR), lambda p: (0, first + p)),
            pl.BlockSpec((length, PAIR), lambda p: (0, 0)),
            pl.BlockSpec((length, PAIR), lambda p: (0, 0)),
            pl.BlockSpec((length, PAIR), lambda p: (0, first + p)),
            pl.BlockSpec((length, PAIR), lambda p: (0, first + p)),
            pl.BlockSpec((1, 8, length), lambda p: (first + p, 0, 0)),
            pl.BlockSpec(normed_t.shape, lambda p: (0, 0)),
        ]
        + [ANY_SPEC] * len(after),
        out_specs=[
            pl.BlockSpec((length, 3 * PAIR), lambda p: (0, p)),
            pl.BlockSpec((width, 3 * PAIR), lambda p: (0, p)),
            TICK_SPEC,
        ],
        out_shape=[
            jax.ShapeDtypeStruct((length, count * 3 * PAIR), BF16),
            jax.ShapeDtypeStruct((width, count * 3 * PAIR), BF16),
            TICK,
        ],
        scratch_shapes=[
            pltpu.VMEM((2, length, PAIR), BF16),
            pltpu.VMEM((2, length, PAIR), BF16),
            pltpu.VMEM((2, length, PAIR), BF16),
            pltpu.VMEM((2, length, PAIR), BF16),
            pltpu.VMEM((PAIR, length), BF16),
            pltpu.VMEM((8, length), F32),
            pltpu.VMEM((PAIR, length), F32),
            pltpu.VMEM((BLK, PAIR), F32),
            pltpu.VMEM((BLK, PAIR), F32),
        ],
        compiler_params=pltpu.CompilerParams(vmem_limit_bytes=VMEM_LIMIT),
        cost_estimate=SMALL_COST,
    )(qkv, query_code, key_code, attended, grad_attended, log_total, normed_t, *after)


def norm_forward(source):
    average = jnp.mean(source, axis=-1, keepdims=True)
    centred = source - average
    spread = jnp.mean(centred * centred, axis=-1, keepdims=True)
    scale = lax.rsqrt(spread + EPSILON)
    return centred * scale, scale


def norm_backward(normal, scale, grad):
    return scale * (
        grad
        - jnp.mean(grad, axis=-1, keepdims=True)
        - normal * jnp.mean(grad * normal, axis=-1, keepdims=True)
    )


GELU_A = 0.7978845608028654
GELU_B = 0.044715


def gelu_parts(source):
    square = source * source
    inner = jnp.tanh(GELU_A * (source + GELU_B * source * square))
    value = 0.5 * source * (1.0 + inner)
    slope = 0.5 * (1.0 + inner) + 0.5 * source * (1.0 - inner * inner) * (
        GELU_A * (1.0 + 3.0 * GELU_B * square)
    )
    return value, slope


def swap(value, axis):
    return lax.ppermute(value, axis, [(0, 1), (1, 0)])


def pick(flag, first, second):
    return jnp.where(flag == 0, first, second), jnp.where(flag == 0, second, first)


class Links:
    def __init__(self):
        self.size = lax.axis_size("dp")
        at = lax.axis_index("dp")
        self.groups = {}
        shift, name = 0, "y"
        while (1 << shift) < self.size:
            bits = 1 if shift == 0 else min(2, self.size.bit_length() - 1 - shift)
            self.groups[name] = (shift, bits, (at >> shift) & ((1 << bits) - 1))
            shift += bits
            name = "z" + str(shift)
        self.rest = [name for name in reversed(self.groups) if name != "y"]
        self.dims = self.rest + ["y", "x"]
        self.side = lax.axis_index("xx")

    def counts(self, dims):
        return [2 if d == "x" else 1 << self.groups[d][1] for d in dims]

    def send(self, value, d, mask):
        if d == "x":
            return swap(value, "xx")
        move = mask << self.groups[d][0]
        return lax.ppermute(value, "dp", [(i, i ^ move) for i in range(self.size)])

    def place(self, d):
        return self.side if d == "x" else self.groups[d][2]

    def scatter(self, parts, comes, dims, d, after=()):
        axis = dims.index(d)
        shares = fold(parts, comes, self.counts(dims), axis, self.place(d), list(after))
        come = [[self.send(share, d, mask)] for mask, share in enumerate(shares) if mask > 0]
        return [shares[0]], come, [other for other in dims if other != d]

    def scatter_rest(self, state, after):
        for d in self.rest:
            state = self.scatter(*state, d, after)
        return self.total(state)

    def total(self, state):
        parts, comes, dims = state
        total = parts[0].astype(F32)
        for (come,) in comes:
            total = total + come.astype(F32)
        return total[0]

    def begin_gather(self, state, d):
        array, dims = state
        come = [self.send(array, d, mask) for mask in range(1, self.counts([d])[0])]
        return array, come, dims, d

    def end_gather(self, begun, tick=None):
        array, come, dims, d = begun
        parts = [array] + come
        for bit in range(len(parts).bit_length() - 1):
            flag = (self.place(d) >> bit) & 1
            for low in range(len(parts)):
                if not low & (1 << bit):
                    high = low | (1 << bit)
                    parts[low], parts[high] = pick(flag, parts[low], parts[high])
        dims = [other for other in self.dims if other in dims or other == d]
        joined = jnp.stack(parts, axis=dims.index(d))
        if tick is not None:
            joined = joined + tick[0, 0].astype(joined.dtype)
        return joined, dims

    def gather(self, state, d, tick=None):
        return self.end_gather(self.begin_gather(state, d), tick)

def body(
    tokens,
    segments,
    ln1_gain,
    ln1_bias,
    qkv_weight,
    q_bias,
    v_bias,
    out_weight,
    out_bias,
    ln2_gain,
    ln2_bias,
    up_weight,
    up_bias,
    down_weight,
    down_bias,
    cotangent,
):
    side = lax.axis_index("xx")
    core = lax.axis_index("core")
    chips = lax.axis_size("dp") * lax.axis_size("xx")
    seq_count, quarter, width = tokens.shape
    length = segments.shape[1]
    own = qkv_weight.shape[0]
    pair_row = 2 * own
    hidden_own = up_bias.shape[0]
    half = width // 2
    cols = 3 * half
    pairs = half // PAIR
    splits = hidden_own // pair_row
    hidden = splits * width

    def at_index(array, index):
        return lax.dynamic_index_in_dim(array, index, 0, keepdims=False)

    def to_sequence(array, tick=None):
        kept = at_index(array, side)
        sent = at_index(array, 1 - side)
        if tick is not None:
            sent = sent + tick[0, 0].astype(sent.dtype)
        come = swap(sent, "xx")
        low, high = pick(side, kept, come)
        mine = jnp.stack([low, high])
        other = swap(mine, "core")
        even, odd = pick(core, mine, other)
        return jnp.stack([even, odd], axis=1).reshape(length, width), come, other

    def own_rows(array):
        return lax.dynamic_index_in_dim(
            array.reshape(2, 2, quarter, array.shape[-1]), core, 1, keepdims=False
        )

    def other_rows(array):
        return lax.dynamic_index_in_dim(
            array.reshape(2, 2, quarter, array.shape[-1]), 1 - core, 1, keepdims=False
        )

    def from_sequence(mine):
        come = swap(at_index(mine, 1 - side), "xx")
        return merged(at_index(mine, side), come), come

    def merged(kept, come, tick=None):
        if tick is not None:
            kept = kept + tick[0, 0].astype(kept.dtype)
        first, second = pick(side, kept, come)
        return jnp.stack([first, second])

    qkv_cols = qkv_weight.reshape(own, 3, 2, pairs, PAIR).transpose(2, 0, 3, 1, 4).reshape(2, own, cols)
    up_cols = (
        up_weight.reshape(own, chips, 2, splits, pair_row)
        .transpose(2, 0, 3, 1, 4)
        .reshape(2, own, hidden)
    )
    vectors = jnp.stack(
        [ln1_gain, ln1_bias, q_bias, v_bias, out_bias, ln2_gain, ln2_bias, down_bias], axis=1
    )
    vectors = jnp.pad(vectors, ((0, 0), (0, PAIR - vectors.shape[1])))

    def with_partner(two):
        mine, theirs = at_index(two, core), at_index(two, 1 - core)
        first, second = pick(core, mine, swap(theirs, "core"))
        return jnp.concatenate([first, second], axis=0)

    early = with_partner(
        jnp.concatenate([qkv_cols, jnp.broadcast_to(vectors, (2, own, PAIR))], axis=2)
    )
    early = jnp.concatenate(
        [
            early[:, : cols + 8],
            up_bias.reshape(splits, pair_row).T,
            early[:, cols + 8 + splits :],
        ],
        axis=1,
    )
    links = Links()

    def gather_rest(array, tick=None):
        state = (array, [])
        for d in links.rest:
            state = links.gather(state, d, tick if d == links.rest[-1] else None)
        return state

    def halves_of(state):
        middle = state[0].shape[-1] // 2
        return [(state[0][..., :middle], state[1]), (state[0][..., middle:], state[1])]

    def joined(halves):
        return [half_state[0].reshape(width, -1) for half_state in halves]

    inputs_low, come, other = to_sequence(tokens)
    grad_out_low, grad_come, _ = to_sequence(cotangent, gate([come]))
    state = (early, [])
    for d in links.rest[:-1]:
        state = links.gather(state, d)
    first_stage = links.begin_gather(state, links.rest[-1])
    begun = [
        links.begin_gather(piece, d)
        for piece, d in zip(halves_of(links.end_gather(first_stage)), "yx")
    ]
    early_halves = [links.end_gather(piece) for piece in begun]
    early_a, early_b = joined(
        [links.gather(piece, d) for piece, d in zip(early_halves, "xy")]
    )
    split = early_a.shape[1]
    late = with_partner(
        jnp.concatenate([up_cols, jnp.broadcast_to(out_weight, (2, own, width))], axis=2)
    )
    down_own = down_weight.reshape(splits, pair_row, width)
    late = lax.all_gather(
        pack([late, *(down_own[i] for i in range(splits))], [*first_stage[1], come]),
        ("dp", "xx"),
        axis=0,
        tiled=True,
    )
    small = early_b[:, cols - split :].astype(F32).T
    gain_one, shift_one, query_shift, value_shift, out_shift, gain_two, shift_two, down_shift = (
        small[i] for i in range(8)
    )
    up_shift = small[8 : 8 + splits].reshape(hidden)

    inputs = inputs_low.astype(F32)
    seg = at_index(segments, side)
    numbers = jnp.arange(PAIR, dtype=jnp.int32) % HEAD_DIM
    same = seg[:, None] == numbers[None, :]
    coded = numbers[None, :] < 4
    query_code = jnp.where(same & coded, 1.0, 0.0).astype(BF16)
    key_code = jnp.where(same | ~coded, 0.0, NEG).astype(BF16)

    def head_cols(vector):
        return lax.dynamic_slice_in_dim(vector, core * half, half, 0).reshape(pairs, 1, PAIR)

    zeros = jnp.zeros((pairs, 1, PAIR), F32)
    qkv_shift = jnp.concatenate(
        [head_cols(query_shift), zeros, head_cols(value_shift)], axis=1
    ).reshape(1, cols)
    qkv_scale = jnp.tile(jnp.repeat(jnp.array([0.125, 1.0, 1.0], F32), PAIR), pairs)[None]
    normed_t, qkv, tick = qkv_projection(
        inputs_low,
        early_a,
        early_b,
        jnp.pad(jnp.stack([gain_one, shift_one]), ((0, 6), (0, 0))),
        jnp.pad(jnp.concatenate([qkv_shift, qkv_scale]), ((0, 6), (0, 0))),
        [],
    )
    attended, log_total, _ = attention_forward(qkv, query_code, key_code, [grad_come])
    core_at = core.reshape(1).astype(jnp.int32)
    branch = out_projection(core_at, attended, late, splits, [])
    branch_come = swap(branch, "core")
    mid_vectors = jnp.pad(
        jnp.stack([out_shift, gain_two, shift_two, down_shift]), ((0, 4), (0, 0))
    )
    normed_two_low, hidden_low, grad_pre_low, mixed_part, ffn_other, partial_two, up_sums = feed_forward(
        core_at,
        inputs_low,
        branch,
        branch_come,
        grad_out_low,
        late,
        splits,
        mid_vectors,
        jnp.pad(up_shift[None], ((0, 7), (0, 0))),
    )
    partial_come = swap(partial_two, "core")
    mixed_own = (mixed_part + swap(ffn_other, "core").astype(F32)).astype(BF16)
    mixed_own = mixed_own.reshape(2, quarter, width)
    mixed_come = swap(at_index(mixed_own, 1 - side), "xx")

    grad_proj_down = [
        mm(hidden_low[:, i * width : (i + 1) * width], grad_out_low, TN).astype(BF16)
        for i in range(splits)
    ]
    grad_proj_up = mm(normed_two_low, grad_pre_low, TN).astype(BF16)
    late_grads = jnp.concatenate([grad_proj_up, *grad_proj_down], axis=1)
    late_own = lax.psum_scatter(late_grads, ("dp", "xx"), scatter_dimension=0, tiled=True)
    grad_middle, branch_low, grad_attended, mid_sums = norm_two(
        core_at,
        inputs_low,
        branch,
        branch_come,
        grad_out_low,
        partial_two,
        partial_come,
        late,
        splits,
        mid_vectors,
        [late_grads],
    )
    grad_proj_out = mm(attended, branch_low, TN)

    def as_column(vectors):
        table = jnp.stack(vectors, axis=1)
        return jnp.pad(table, ((0, 0), (0, PAIR - table.shape[1])))

    def only_mine(flag, array):
        return jnp.where(flag, array, jnp.zeros_like(array))

    small_two = [mid_sums[i] for i in range(4)] + [
        up_sums[0, i * width : (i + 1) * width] for i in range(splits)
    ]
    out_low = grad_proj_out.astype(BF16)
    grad_out_rows = jnp.concatenate(
        [only_mine(core == 0, out_low), only_mine(core == 1, out_low)], axis=0
    )

    def blocks(array):
        return array.reshape(chips, pair_row, array.shape[1])

    def pairs_backward(first, count, after):
        return attention_backward(
            first, count, qkv, query_code, key_code, attended, grad_attended, log_total, normed_t, after
        )

    out_piece = links.scatter([blocks(grad_out_rows)], [], links.dims, "y")
    grad_a, weight_grad_a, tick = pairs_backward(0, pairs - 1, [out_piece[0][0]])
    out_piece = links.scatter(*out_piece, "x", [tick])
    first_piece = links.scatter([blocks(weight_grad_a)], [], links.dims, "y", [tick])
    mixed = merge(at_index(mixed_own, side), mixed_come, side, [tick])
    grad_b, weight_grad_b, tick = pairs_backward(
        pairs - 1, 1, [out_piece[0][0], first_piece[0][0], tick, mixed]
    )
    grads = [grad_a, grad_b]
    first_piece = links.scatter(*first_piece, "x", [tick])
    norm_vectors = jnp.pad(jnp.stack([gain_one, shift_one]), ((0, 6), (0, 0)))
    partial_one, norm_sums, bias_sums, tick = norm_one(
        False, core_at, grads, early_a, early_b, cols, inputs_low, [], [first_piece[0][0]]
    )
    come = swap(partial_one, "core")
    token_own, norm_sums_own, bias_sums_own, tick = norm_one(
        True,
        core_at,
        grads,
        early_a,
        early_b,
        cols,
        inputs_low,
        [come, grad_middle, norm_vectors],
        [],
    )
    norm_sums = norm_sums + norm_sums_own
    bias_sums = bias_sums + bias_sums_own
    token_grad, come = from_sequence(token_own.reshape(2, quarter, width))
    grad_by_pair = bias_sums[0].reshape(pairs, 3, PAIR)

    def padded(vector):
        vector = vector.reshape(half)
        return jnp.concatenate([only_mine(core == 0, vector), only_mine(core == 1, vector)])

    small = as_column(
        [
            norm_sums[0],
            norm_sums[1],
            padded(grad_by_pair[:, 0]),
            padded(grad_by_pair[:, 2]),
        ]
        + small_two
    )
    last_piece = links.scatter(
        [blocks(weight_grad_b), blocks(small.astype(BF16))], [], links.dims, "y", [tick]
    )
    first_piece = (
        out_piece[0] + first_piece[0],
        [out_piece[1][0] + first_piece[1][0]],
        first_piece[2],
    )
    first_own = links.scatter_rest(first_piece, [tick])
    last_piece = links.scatter(*last_piece, "x")
    last_ready = last_piece[0][0]
    last_own = links.scatter_rest(last_piece, [come])

    def rows_of(array, index):
        return lax.dynamic_slice_in_dim(array, index * own, own, 0)

    def by_core(mine, come):
        return jnp.stack(pick(core, mine, come))

    def shared(array):
        return rows_of(array, core), swap(rows_of(array, 1 - core), "core")

    up_own, down_grad = widen(late_own, width, [last_ready])
    late_mine, late_come = shared(up_own)
    early_mine, early_come = shared(jnp.concatenate([first_own, last_own], axis=1).astype(BF16))
    out_grad = early_mine[:, :width].astype(F32) + early_come[:, :width].astype(F32)
    up_grad = (
        by_core(late_mine, late_come)
        .reshape(2, own, splits, chips, pair_row)
        .transpose(1, 3, 0, 2, 4)
        .reshape(own, 2 * hidden)
        .astype(F32)
    )
    down_grad = down_grad.reshape(hidden_own, width)
    qkv_grad = (
        by_core(early_mine[:, width : width + cols], early_come[:, width : width + cols])
        .reshape(2, own, pairs, 3, PAIR)
        .transpose(1, 3, 0, 2, 4)
        .reshape(own, 2 * cols)
        .astype(F32)
    )
    tail, first = width + cols + 8, first_own.shape[1]
    small_mine = early_mine[:, tail - 8 : tail].astype(F32)
    one = small_mine[:, :4] + early_come[:, tail - 8 : tail - 4].astype(F32)
    up_shift_grad = (
        last_own[:, tail - first : tail - first + splits].T.reshape(hidden_own).astype(F32)
    )
    two = small_mine[:, 4:]
    return (
        mixed,
        token_grad,
        one[:, 0],
        one[:, 1],
        qkv_grad,
        one[:, 2],
        one[:, 3],
        out_grad,
        two[:, 0],
        two[:, 1],
        two[:, 2],
        up_grad,
        up_shift_grad,
        down_grad,
        two[:, 3],
    )


def solution(mesh):
    parts = (mesh.shape["dp"], mesh.shape["ctx"] // 2, 2)
    split_mesh = Mesh(mesh.devices.reshape(parts), ("dp", "xx", "core"))
    rows = ("dp", "xx", "core")
    acts = P("dp", ("xx", "core"), None)
    vec, mat = P(rows), P(rows, None)
    return jax.shard_map(
        body,
        mesh=split_mesh,
        in_specs=(
            acts, P("dp", None), vec, vec, mat, vec, vec, mat, vec, vec, vec, mat, vec, mat, vec, acts,
        ),
        out_specs=(
            acts, acts, vec, vec, mat, vec, vec, mat, vec, vec, vec, mat, vec, mat, vec,
        ),
        check_vma=False,
    )
```

```python
import functools

import jax
import jax.numpy as jnp
from jax import lax
from jax.experimental import pallas as pl
from jax.experimental.pallas import tpu as pltpu
from jax.sharding import Mesh, PartitionSpec as P

HEAD_DIM = 64
PAIR = 2 * HEAD_DIM
EPSILON = 1e-05
NEG = -1e30
BLK = 512
F32 = jnp.float32
BF16 = jnp.bfloat16

NN = (((1,), (0,)), ((), ()))
NT = (((1,), (1,)), ((), ()))
TN = (((0,), (0,)), ((), ()))


def mm(left, right, dims=NN):
    return lax.dot_general(left, right, dims, preferred_element_type=F32)


def build_scores_operands(qkv_ref, qs_ref, ks_ref, rows, qx, kx):
    lane = lax.broadcasted_iota(jnp.int32, (BLK, PAIR), 1)
    first = lane < HEAD_DIM
    q = qkv_ref[rows, 0:PAIR].astype(F32)
    k = qkv_ref[rows, PAIR : 2 * PAIR].astype(F32)
    qs = qs_ref[rows, :].astype(F32)
    ks = ks_ref[rows, :].astype(F32)
    qx[0, rows, :] = jnp.where(first, q, qs).astype(BF16)
    qx[1, rows, :] = jnp.where(first, qs, q).astype(BF16)
    kx[0, rows, :] = jnp.where(first, k, ks).astype(BF16)
    kx[1, rows, :] = jnp.where(first, ks, k).astype(BF16)
    return first, q, k


def causal_block(scores):
    key_at = lax.broadcasted_iota(jnp.int32, scores.shape, 0)
    query_at = lax.broadcasted_iota(jnp.int32, scores.shape, 1)
    return jnp.where(key_at <= query_at, scores, NEG)


def attention_forward_kernel(qkv_ref, qs_ref, ks_ref, *rest):
    o_ref, lse_ref, tick_ref, qx, kx, vt, acc = rest[-7:]
    tick_ref[...] = jnp.zeros_like(tick_ref)
    length = qkv_ref.shape[0]
    blocks = length // BLK

    @pl.loop(0, blocks)
    def _(i):
        rows = pl.ds(pl.multiple_of(i * BLK, BLK), BLK)
        build_scores_operands(qkv_ref, qs_ref, ks_ref, rows, qx, kx)
        v_t = qkv_ref[rows, 2 * PAIR : 3 * PAIR].astype(F32).T
        ones = jnp.ones((16, BLK), BF16)
        for h in range(2):
            vt[h, 0:HEAD_DIM, rows] = v_t[h * HEAD_DIM : (h + 1) * HEAD_DIM].astype(BF16)
            vt[h, HEAD_DIM : HEAD_DIM + 16, rows] = ones

    @pl.loop(0, blocks)
    def _(i):
        rows = pl.ds(pl.multiple_of(i * BLK, BLK), BLK)
        queries = [qx[h, rows, :] for h in range(2)]
        tops = []
        for h in range(2):
            s = causal_block(mm(kx[h, rows, :], queries[h], NT))
            top = jnp.max(s, axis=0, keepdims=True)
            p = jnp.exp(s - top).astype(BF16)
            acc[h] = mm(vt[h, :, rows], p)
            tops.append(top)

        def step(j, carry):
            keys = pl.ds(pl.multiple_of(j * BLK, BLK), BLK)
            out = []
            for h in range(2):
                s = mm(kx[h, keys, :], qx[h, rows, :], NT)
                top = jnp.maximum(carry[h], jnp.max(s, axis=0, keepdims=True))
                p = jnp.exp(s - top).astype(BF16)
                acc[h] = acc[h] * jnp.exp(carry[h] - top) + mm(vt[h, :, keys], p)
                out.append(top)
            return tuple(out)

        tops = lax.fori_loop(0, i, step, tuple(tops))
        parts = []
        for h in range(2):
            total = acc[h, HEAD_DIM : HEAD_DIM + 1, :]
            parts.append(acc[h, 0:HEAD_DIM, :] / total)
            lse_ref[0, h : h + 1, rows] = tops[h] + jnp.log(total)
        o_ref[rows, :] = jnp.concatenate(parts, axis=0).T.astype(BF16)


def attention_backward_kernel(qkv_ref, qs_ref, ks_ref, o_ref, do_ref, lse_ref, at_ref, *rest):
    d_ref, dw_ref, tick_ref, qx, kx, qm, dm, kt, delta, dqt, dk, dv = rest[-12:]
    tick_ref[...] = jnp.zeros_like(tick_ref)
    length = qkv_ref.shape[0]
    blocks = length // BLK

    @pl.loop(0, blocks)
    def _(i):
        rows = pl.ds(pl.multiple_of(i * BLK, BLK), BLK)
        first, q, k = build_scores_operands(qkv_ref, qs_ref, ks_ref, rows, qx, kx)
        do = do_ref[rows, :].astype(F32)
        zero = jnp.zeros_like(q)
        qm[0, rows, :] = jnp.where(first, q, zero).astype(BF16)
        qm[1, rows, :] = jnp.where(first, zero, q).astype(BF16)
        dm[0, rows, :] = jnp.where(first, do, zero).astype(BF16)
        dm[1, rows, :] = jnp.where(first, zero, do).astype(BF16)
        kt[:, rows] = k.T.astype(BF16)
        inner = (do * o_ref[rows, :].astype(F32)).T
        for h in range(2):
            delta[h : h + 1, rows] = jnp.sum(
                inner[h * HEAD_DIM : (h + 1) * HEAD_DIM], axis=0, keepdims=True
            )
        dqt[:, rows] = jnp.zeros((PAIR, BLK), F32)

    def tile(keys, rows, masked):
        values = qkv_ref[keys, 2 * PAIR : 3 * PAIR]
        dv_part, dk_part = None, None
        for h in range(2):
            s = mm(kx[h, keys, :], qx[h, rows, :], NT)
            if masked:
                s = causal_block(s)
            p = jnp.exp(s - lse_ref[0, h : h + 1, rows])
            dp = mm(values, dm[h, rows, :], NT)
            ds = (p * (dp - delta[h : h + 1, rows])).astype(BF16)
            dv_h = mm(p.astype(BF16), dm[h, rows, :])
            dk_h = mm(ds, qm[h, rows, :])
            dv_part = dv_h if h == 0 else dv_part + dv_h
            dk_part = dk_h if h == 0 else dk_part + dk_h
            part = slice(h * HEAD_DIM, (h + 1) * HEAD_DIM)
            dqt[part, rows] += mm(kt[part, keys], ds)
        return dk_part, dv_part

    @pl.loop(0, blocks)
    def _(j):
        keys = pl.ds(pl.multiple_of(j * BLK, BLK), BLK)
        dk[...], dv[...] = tile(keys, keys, True)

        @pl.loop(j + 1, blocks)
        def _(i):
            dk_part, dv_part = tile(keys, pl.ds(pl.multiple_of(i * BLK, BLK), BLK), False)
            dk[...] += dk_part
            dv[...] += dv_part

        d_ref[keys, PAIR : 2 * PAIR] = dk[...].astype(BF16)
        d_ref[keys, 2 * PAIR : 3 * PAIR] = dv[...].astype(BF16)

    @pl.loop(0, blocks)
    def _(i):
        rows = pl.ds(pl.multiple_of(i * BLK, BLK), BLK)
        d_ref[rows, 0:PAIR] = (dqt[:, rows].T.astype(BF16).astype(F32) * 0.125).astype(BF16)

    @pl.loop(0, dw_ref.shape[0] // ROWS)
    def _(i):
        rows = pl.ds(pl.multiple_of(i * ROWS, ROWS), ROWS)
        dw_ref[rows, :] = mm(at_ref[rows, :], d_ref[...]).astype(BF16)


VMEM_LIMIT = 48 * 1024 * 1024


SMALL_COST = pl.CostEstimate(flops=1000, bytes_accessed=1000, transcendentals=0)


TICK = jax.ShapeDtypeStruct((8, 128), F32)
TICK_SPEC = pl.BlockSpec((8, 128), lambda i: (0, 0))
ANY_SPEC = pl.BlockSpec(memory_space=pl.ANY)


def pack_kernel(count, refs):
    refs[-1][...] = jnp.concatenate([ref[...] for ref in refs[:count]], axis=-1)


def pack(parts, after):
    rows = parts[0].shape[0]
    width = sum(part.shape[1] for part in parts)
    return pl.pallas_call(
        lambda *refs: pack_kernel(len(parts), refs),
        grid=(1,),
        in_specs=[pl.BlockSpec(part.shape, lambda i: (0, 0)) for part in parts]
        + [ANY_SPEC] * len(after),
        out_specs=pl.BlockSpec((rows, width), lambda i: (0, 0)),
        out_shape=jax.ShapeDtypeStruct((rows, width), BF16),
        compiler_params=pltpu.CompilerParams(vmem_limit_bytes=VMEM_LIMIT),
        cost_estimate=SMALL_COST,
    )(*parts, *after)


def widen(source, width, after):
    rows, cols = source.shape
    count = cols // width - 2

    def kernel(source_ref, *refs):
        up_ref, down_ref = refs[-2:]
        up_ref[...] = source_ref[:, : 2 * width].astype(F32)
        for i in range(count):
            down_ref[i] = source_ref[:, (2 + i) * width : (3 + i) * width].astype(F32)

    return pl.pallas_call(
        kernel,
        grid=(1,),
        in_specs=[pl.BlockSpec((rows, cols), lambda i: (0, 0))] + [ANY_SPEC] * len(after),
        out_specs=[
            pl.BlockSpec((rows, 2 * width), lambda i: (0, 0)),
            pl.BlockSpec((count, rows, width), lambda i: (0, 0, 0)),
        ],
        out_shape=[
            jax.ShapeDtypeStruct((rows, 2 * width), F32),
            jax.ShapeDtypeStruct((count, rows, width), F32),
        ],
        compiler_params=pltpu.CompilerParams(vmem_limit_bytes=VMEM_LIMIT),
        cost_estimate=SMALL_COST,
    )(source, *after)


def merge(kept, come, side, after):
    def kernel(side_ref, kept_ref, come_ref, *rest):
        mine = pl.program_id(0) == side_ref[0]

        @pl.when(mine)
        def _():
            rest[-1][0] = kept_ref[...]

        @pl.when(jnp.logical_not(mine))
        def _():
            rest[-1][0] = come_ref[...]

    whole = pl.BlockSpec(kept.shape, lambda i, side_ref: (0, 0))
    return pl.pallas_call(
        kernel,
        grid_spec=pltpu.PrefetchScalarGridSpec(
            num_scalar_prefetch=1,
            grid=(2,),
            in_specs=[whole, whole] + [ANY_SPEC] * len(after),
            out_specs=pl.BlockSpec((1, *kept.shape), lambda i, side_ref: (i, 0, 0)),
        ),
        out_shape=jax.ShapeDtypeStruct((2, *kept.shape), kept.dtype),
        compiler_params=pltpu.CompilerParams(vmem_limit_bytes=VMEM_LIMIT),
        cost_estimate=SMALL_COST,
    )(side.reshape(1).astype(jnp.int32), kept, come, *after)


def gate_kernel(*refs):
    refs[-1][...] = jnp.zeros_like(refs[-1])


def gate(after):
    return pl.pallas_call(
        gate_kernel,
        grid=(1,),
        in_specs=[ANY_SPEC] * len(after),
        out_specs=TICK_SPEC,
        out_shape=TICK,
        cost_estimate=SMALL_COST,
    )(*after)


def fold_kernel(parts, comes, outs, refs):
    for m in range(outs):
        value = None
        for term in range(1 + comes):
            at = 1 + (term * outs + m) * parts
            side = jnp.concatenate([ref[0] for ref in refs[at : at + parts]], axis=-1)
            if comes:
                side = side.astype(F32)
            value = side if term == 0 else value + side
        refs[len(refs) - outs + m][0] = value.astype(BF16)


def fold(parts, comes, sizes, axis, at, after):
    blocks, rows = parts[0].shape[:2]
    width = sum(part.shape[2] for part in parts)
    outs = sizes[axis] if axis is not None else 1
    inner = 1
    if axis is not None:
        for size in sizes[axis + 1 :]:
            inner *= size

    def spec(array, m):
        def index(j, at_ref):
            if axis is None:
                return j, 0, 0
            return (j // inner) * (outs * inner) + (at_ref[0] ^ m) * inner + j % inner, 0, 0

        return pl.BlockSpec((1, rows, array.shape[2]), index)

    def kernel(*refs):
        ins = 1 + (1 + len(comes)) * len(parts) * outs
        fold_kernel(len(parts), len(comes), outs, refs[:ins] + refs[ins + len(after) :])

    out = pl.BlockSpec((1, rows, width), lambda j, at_ref: (j, 0, 0))
    return pl.pallas_call(
        kernel,
        grid_spec=pltpu.PrefetchScalarGridSpec(
            num_scalar_prefetch=1,
            grid=(blocks // outs,),
            in_specs=[spec(part, m) for m in range(outs) for part in parts]
            + [spec(part, m) for come in comes for m in range(outs) for part in come]
            + [ANY_SPEC] * len(after),
            out_specs=[out] * outs,
        ),
        out_shape=[jax.ShapeDtypeStruct((blocks // outs, rows, width), BF16)] * outs,
        compiler_params=pltpu.CompilerParams(vmem_limit_bytes=VMEM_LIMIT),
        cost_estimate=SMALL_COST,
    )(at.reshape(1).astype(jnp.int32), *(list(parts) * outs), *[part for come in comes for part in list(come) * outs], *after)


def qkv_kernel(x_ref, wa_ref, wb_ref, vec_ref, col_ref, *rest_refs):
    a_ref, qkv_ref, tick_ref = rest_refs[-3:]
    split = wa_ref.shape[1]
    rest = qkv_ref.shape[1] - split
    for part in range(2):
        rows = slice(part * ROWS, (part + 1) * ROWS)
        normal, _ = norm_forward(x_ref[rows, :].astype(F32))
        normed = (normal * vec_ref[0:1, :] + vec_ref[1:2, :]).astype(BF16)
        a_ref[:, rows] = normed.astype(F32).T.astype(BF16)
        for w, cols in ((wa_ref[...], slice(0, split)), (wb_ref[:, :rest], slice(split, None))):
            shift, scale = col_ref[0:1, cols], col_ref[1:2, cols]
            qkv_ref[rows, cols] = ((mm(normed, w) + shift) * scale).astype(BF16)
    tick_ref[...] = jnp.zeros_like(tick_ref)


def qkv_projection(inputs, weight_a, weight_b, vectors, columns, after):
    length, width = inputs.shape
    cols = columns.shape[1]
    return pl.pallas_call(
        qkv_kernel,
        grid=(length // (2 * ROWS),),
        in_specs=[
            pl.BlockSpec((2 * ROWS, width), lambda i: (i, 0)),
            pl.BlockSpec(weight_a.shape, lambda i: (0, 0)),
            pl.BlockSpec(weight_b.shape, lambda i: (0, 0)),
            pl.BlockSpec(vectors.shape, lambda i: (0, 0)),
            pl.BlockSpec(columns.shape, lambda i: (0, 0)),
        ]
        + [ANY_SPEC] * len(after),
        out_specs=[
            pl.BlockSpec((width, 2 * ROWS), lambda i: (0, i)),
            pl.BlockSpec((2 * ROWS, cols), lambda i: (i, 0)),
            TICK_SPEC,
        ],
        out_shape=[
            jax.ShapeDtypeStruct((width, length), BF16),
            jax.ShapeDtypeStruct((length, cols), BF16),
            TICK,
        ],
        compiler_params=pltpu.CompilerParams(vmem_limit_bytes=VMEM_LIMIT),
        cost_estimate=SMALL_COST,
    )(inputs, weight_a, weight_b, vectors, columns, *after)


def out_projection(core, attended, late, block, after):
    length, cols = attended.shape
    width = late.shape[0]
    rows = length // 4

    def kernel(core_ref, a_ref, w_ref, *rest):
        rest[-1][...] = mm(a_ref[...], w_ref[...]).astype(BF16)

    return pl.pallas_call(
        kernel,
        grid_spec=pltpu.PrefetchScalarGridSpec(
            num_scalar_prefetch=1,
            grid=(4,),
            in_specs=[
                pl.BlockSpec((rows, cols), lambda i, core_ref: (i, 0)),
                pl.BlockSpec((cols, width), lambda i, core_ref: (core_ref[0], block)),
            ]
            + [ANY_SPEC] * len(after),
            out_specs=pl.BlockSpec((rows, width), lambda i, core_ref: (i, 0)),
        ),
        out_shape=jax.ShapeDtypeStruct((length, width), BF16),
        compiler_params=pltpu.CompilerParams(vmem_limit_bytes=VMEM_LIMIT),
        cost_estimate=SMALL_COST,
    )(core, attended, late, *after)


def middle_of(x_ref, b0_ref, b1_ref, vec_ref):
    both = b0_ref[...].astype(F32) + b1_ref[...].astype(F32)
    return x_ref[...].astype(F32) + both + vec_ref[0:1, :]


HIDDEN = 256


def feed_forward_kernel(splits, core_ref, x_ref, b0_ref, b1_ref, dy_ref, up_ref, *rest):
    down_refs, (vec_ref, shift_ref) = rest[:splits], rest[splits : splits + 2]
    a_ref, g_ref, du_ref, own_ref, other_ref, dh_ref, sums_ref = rest[splits + 2 :]
    at = pl.program_id(0)

    @pl.when(at == 0)
    def _():
        sums_ref[...] = jnp.zeros_like(sums_ref)

    middle = middle_of(x_ref, b0_ref, b1_ref, vec_ref)
    normal, _ = norm_forward(middle)
    normed = (normal * vec_ref[1:2, :] + vec_ref[2:3, :]).astype(BF16)
    a_ref[...] = normed
    dy = dy_ref[...]
    ffn, dh = None, None
    width = dy.shape[1]
    per = width // HIDDEN

    def weights(chunk):
        cols = slice(chunk * HIDDEN, (chunk + 1) * HIDDEN)
        at_row = (chunk % per) * HIDDEN
        return cols, up_ref[:, cols], down_refs[chunk // per][at_row : at_row + HIDDEN, :]

    def products(chunk):
        cols, up, down = weights(chunk)
        return mm(normed, up), mm(dy, down, NT)

    ahead = products(0)
    for chunk in range(splits * per):
        before, grad = ahead
        if chunk + 1 < splits * per:
            ahead = products(chunk + 1)
        cols, up, down = weights(chunk)
        value, slope = gelu_parts(before + shift_ref[0:1, cols])
        du = slope * grad
        value, du = value.astype(BF16), du.astype(BF16)
        g_ref[:, cols] = value
        du_ref[:, cols] = du
        sums_ref[0:1, cols] += jnp.sum(du.astype(F32), axis=0, keepdims=True)
        ffn_part, dh_part = mm(value, down), mm(du, up, NT)
        ffn = ffn_part if chunk == 0 else ffn + ffn_part
        dh = dh_part if chunk == 0 else dh + dh_part
    dh_ref[...] = dh.astype(BF16)
    mine = at % 2 == core_ref[0]

    @pl.when(mine)
    def _():
        own_ref[...] = middle_of(x_ref, b0_ref, b1_ref, vec_ref) + ffn + vec_ref[3:4, :]

    @pl.when(jnp.logical_not(mine))
    def _():
        other_ref[...] = ffn.astype(BF16)


def feed_forward(core, inputs, branch, branch_come, grad_out, late, splits, vectors, up_shift):
    length, width = inputs.shape
    rows = length // 4
    hidden = splits * width
    narrow = pl.BlockSpec((rows, width), lambda i, core_ref: (i, 0))
    wide = pl.BlockSpec((rows, hidden), lambda i, core_ref: (i, 0))
    shared = pl.BlockSpec((rows, width), lambda i, core_ref: (i // 2, 0))

    def whole(array):
        return pl.BlockSpec(array.shape, lambda i, core_ref: (0, 0))

    def down(i):
        return pl.BlockSpec((width, width), lambda _, core_ref: (0, splits + 1 + i))

    return pl.pallas_call(
        functools.partial(feed_forward_kernel, splits),
        grid_spec=pltpu.PrefetchScalarGridSpec(
            num_scalar_prefetch=1,
            grid=(4,),
            in_specs=[narrow] * 4
            + [pl.BlockSpec((width, hidden), lambda i, core_ref: (0, 0))]
            + [down(i) for i in range(splits)]
            + [whole(vectors), whole(up_shift)],
            out_specs=[
                narrow, wide, wide, shared, shared, narrow,
                pl.BlockSpec((8, hidden), lambda i, core_ref: (0, 0)),
            ],
        ),
        out_shape=[
            jax.ShapeDtypeStruct((length, width), BF16),
            jax.ShapeDtypeStruct((length, hidden), BF16),
            jax.ShapeDtypeStruct((length, hidden), BF16),
            jax.ShapeDtypeStruct((length // 2, width), F32),
            jax.ShapeDtypeStruct((length // 2, width), BF16),
            jax.ShapeDtypeStruct((length, width), BF16),
            jax.ShapeDtypeStruct((8, hidden), F32),
        ],
        compiler_params=pltpu.CompilerParams(vmem_limit_bytes=VMEM_LIMIT),
        cost_estimate=SMALL_COST,
    )(core, inputs, branch, branch_come, grad_out, late, *([late] * splits), vectors, up_shift)


def norm_two_kernel(core_ref, x_ref, b0_ref, b1_ref, dy_ref, p0_ref, p1_ref, w_ref, vec_ref, *rest):
    mid_ref, low_ref, do_ref, sums_ref = rest[-4:]

    @pl.when(pl.program_id(0) == 0)
    def _():
        sums_ref[...] = jnp.zeros_like(sums_ref)

    normal, scale = norm_forward(middle_of(x_ref, b0_ref, b1_ref, vec_ref))
    grad = p0_ref[...].astype(F32) + p1_ref[...].astype(F32)
    dy = dy_ref[...].astype(F32)
    mid = dy + norm_backward(normal, scale, grad * vec_ref[1:2, :])
    low = mid.astype(BF16)
    low_ref[...] = low
    do_ref[...] = mm(low, w_ref[...], NT).astype(BF16)
    for i, value in enumerate((low.astype(F32), grad * normal, grad, dy)):
        sums_ref[i : i + 1, :] += jnp.sum(value, axis=0, keepdims=True)

    @pl.when(pl.program_id(0) % 2 == core_ref[0])
    def _():
        mid_ref[...] = mid


def norm_two(core, inputs, branch, branch_come, grad_out, partial, partial_come, late, block, vectors, after):
    length, width = inputs.shape
    rows = length // 4
    cols = width // 2
    narrow = pl.BlockSpec((rows, width), lambda i, core_ref: (i, 0))
    return pl.pallas_call(
        norm_two_kernel,
        grid_spec=pltpu.PrefetchScalarGridSpec(
            num_scalar_prefetch=1,
            grid=(4,),
            in_specs=[narrow] * 6
            + [
                pl.BlockSpec((cols, width), lambda i, core_ref: (core_ref[0], block)),
                pl.BlockSpec(vectors.shape, lambda i, core_ref: (0, 0)),
            ]
            + [ANY_SPEC] * len(after),
            out_specs=[
                pl.BlockSpec((rows, width), lambda i, core_ref: (i // 2, 0)),
                narrow,
                pl.BlockSpec((rows, cols), lambda i, core_ref: (i, 0)),
                pl.BlockSpec((8, width), lambda i, core_ref: (0, 0)),
            ],
        ),
        out_shape=[
            jax.ShapeDtypeStruct((length // 2, width), F32),
            jax.ShapeDtypeStruct((length, width), BF16),
            jax.ShapeDtypeStruct((length, cols), BF16),
            jax.ShapeDtypeStruct((8, width), F32),
        ],
        compiler_params=pltpu.CompilerParams(vmem_limit_bytes=VMEM_LIMIT),
        cost_estimate=SMALL_COST,
    )(core, inputs, branch, branch_come, grad_out, partial, partial_come, late, vectors, *after)


ROWS = 256


def attention_forward(qkv, query_code, key_code, after):
    length, width = qkv.shape
    pairs = width // (3 * PAIR)
    return pl.pallas_call(
        attention_forward_kernel,
        grid=(pairs,),
        in_specs=[
            pl.BlockSpec((length, 3 * PAIR), lambda p: (0, p)),
            pl.BlockSpec((length, PAIR), lambda p: (0, 0)),
            pl.BlockSpec((length, PAIR), lambda p: (0, 0)),
        ]
        + [ANY_SPEC] * len(after),
        out_specs=[
            pl.BlockSpec((length, PAIR), lambda p: (0, p)),
            pl.BlockSpec((1, 8, length), lambda p: (p, 0, 0)),
            TICK_SPEC,
        ],
        out_shape=[
            jax.ShapeDtypeStruct((length, pairs * PAIR), BF16),
            jax.ShapeDtypeStruct((pairs, 8, length), F32),
            TICK,
        ],
        scratch_shapes=[
            pltpu.VMEM((2, length, PAIR), BF16),
            pltpu.VMEM((2, length, PAIR), BF16),
            pltpu.VMEM((2, HEAD_DIM + 16, length), BF16),
            pltpu.VMEM((2, HEAD_DIM + 16, BLK), F32),
        ],
        compiler_params=pltpu.CompilerParams(vmem_limit_bytes=VMEM_LIMIT),
        cost_estimate=SMALL_COST,
    )(qkv, query_code, key_code, *after)


def norm_one_kernel(own, core_ref, d0_ref, d1_ref, wa_ref, wb_ref, x_ref, *rest):
    if own:
        come_ref, mid_ref, vec_ref, out_ref, sums_ref, bias_ref, tick_ref, w = rest
    else:
        out_ref, sums_ref, bias_ref, tick_ref, w = rest
    split = wa_ref.shape[1]

    @pl.when(pl.program_id(0) == 0)
    def _():
        sums_ref[...] = jnp.zeros_like(sums_ref)
        bias_ref[...] = jnp.zeros_like(bias_ref)
        w[:, :split] = wa_ref[...]
        w[:, split:] = wb_ref[:, : w.shape[1] - split]
        tick_ref[...] = jnp.zeros_like(tick_ref)

    total = None
    for i, ref in enumerate((d0_ref, d1_ref)):
        cols = slice(0, ref.shape[1]) if i == 0 else slice(d0_ref.shape[1], None)
        grad = ref[...]
        part = mm(grad, w[:, cols], NT)
        total = part if i == 0 else total + part
        bias_ref[0:1, cols] += jnp.sum(grad.astype(F32), axis=0, keepdims=True)
    normal, scale = norm_forward(x_ref[...].astype(F32))
    sums_ref[0:1, :] += jnp.sum(total * normal, axis=0, keepdims=True)
    sums_ref[1:2, :] += jnp.sum(total, axis=0, keepdims=True)
    if own:
        grad = (total + come_ref[...].astype(F32)) * vec_ref[0:1, :]
        out_ref[...] = (mid_ref[...] + norm_backward(normal, scale, grad)).astype(BF16)
    else:
        out_ref[...] = total.astype(BF16)


def norm_one(own, core, grads, weight_a, weight_b, cols, inputs, extra, after):
    length, width = inputs.shape
    count = length // (2 * ROWS)
    per = count // 2

    def block(i, core_ref):
        which = core_ref[0] if own else 1 - core_ref[0]
        return ((i // per) * 2 + which) * per + i % per, 0

    def at_zero(i, core_ref):
        return 0, 0

    plain = pl.BlockSpec((ROWS, width), lambda i, core_ref: (i, 0))
    rows = pl.BlockSpec((ROWS, width), block)
    in_specs = [pl.BlockSpec((ROWS, grad.shape[1]), block) for grad in grads] + [
        pl.BlockSpec(weight_a.shape, at_zero),
        pl.BlockSpec(weight_b.shape, at_zero),
        rows,
    ]
    out_specs = [
        plain,
        pl.BlockSpec((8, width), at_zero),
        pl.BlockSpec((8, cols), at_zero),
        pl.BlockSpec((8, 128), at_zero),
    ]
    out_shape = [
        jax.ShapeDtypeStruct((count * ROWS, width), BF16),
        jax.ShapeDtypeStruct((8, width), F32),
        jax.ShapeDtypeStruct((8, cols), F32),
        TICK,
    ]
    if own:
        in_specs += [plain, plain, pl.BlockSpec(extra[2].shape, at_zero)]

    def kernel(*refs):
        inner = refs[: 1 + len(in_specs)] + refs[1 + len(in_specs) + len(after) :]
        norm_one_kernel(own, *inner)

    return pl.pallas_call(
        kernel,
        grid_spec=pltpu.PrefetchScalarGridSpec(
            num_scalar_prefetch=1,
            grid=(count,),
            in_specs=in_specs + [ANY_SPEC] * len(after),
            out_specs=out_specs,
            scratch_shapes=[pltpu.VMEM((width, cols), BF16)],
        ),
        out_shape=out_shape,
        compiler_params=pltpu.CompilerParams(vmem_limit_bytes=VMEM_LIMIT),
        cost_estimate=SMALL_COST,
    )(core, *grads, weight_a, weight_b, inputs, *extra, *after)


def attention_backward(
    first, count, qkv, query_code, key_code, attended, grad_attended, log_total, normed_t, after
):
    length = qkv.shape[0]
    width = normed_t.shape[0]
    return pl.pallas_call(
        attention_backward_kernel,
        grid=(count,),
        in_specs=[
            pl.BlockSpec((length, 3 * PAIR), lambda p: (0, first + p)),
            pl.BlockSpec((length, PAIR), lambda p: (0, 0)),
            pl.BlockSpec((length, PAIR), lambda p: (0, 0)),
            pl.BlockSpec((length, PAIR), lambda p: (0, first + p)),
            pl.BlockSpec((length, PAIR), lambda p: (0, first + p)),
            pl.BlockSpec((1, 8, length), lambda p: (first + p, 0, 0)),
            pl.BlockSpec(normed_t.shape, lambda p: (0, 0)),
        ]
        + [ANY_SPEC] * len(after),
        out_specs=[
            pl.BlockSpec((length, 3 * PAIR), lambda p: (0, p)),
            pl.BlockSpec((width, 3 * PAIR), lambda p: (0, p)),
            TICK_SPEC,
        ],
        out_shape=[
            jax.ShapeDtypeStruct((length, count * 3 * PAIR), BF16),
            jax.ShapeDtypeStruct((width, count * 3 * PAIR), BF16),
            TICK,
        ],
        scratch_shapes=[
            pltpu.VMEM((2, length, PAIR), BF16),
            pltpu.VMEM((2, length, PAIR), BF16),
            pltpu.VMEM((2, length, PAIR), BF16),
            pltpu.VMEM((2, length, PAIR), BF16),
            pltpu.VMEM((PAIR, length), BF16),
            pltpu.VMEM((8, length), F32),
            pltpu.VMEM((PAIR, length), F32),
            pltpu.VMEM((BLK, PAIR), F32),
            pltpu.VMEM((BLK, PAIR), F32),
        ],
        compiler_params=pltpu.CompilerParams(vmem_limit_bytes=VMEM_LIMIT),
        cost_estimate=SMALL_COST,
    )(qkv, query_code, key_code, attended, grad_attended, log_total, normed_t, *after)


def norm_forward(source):
    average = jnp.mean(source, axis=-1, keepdims=True)
    centred = source - average
    spread = jnp.mean(centred * centred, axis=-1, keepdims=True)
    scale = lax.rsqrt(spread + EPSILON)
    return centred * scale, scale


def norm_backward(normal, scale, grad):
    return scale * (
        grad
        - jnp.mean(grad, axis=-1, keepdims=True)
        - normal * jnp.mean(grad * normal, axis=-1, keepdims=True)
    )


GELU_A = 0.7978845608028654
GELU_B = 0.044715


def gelu_parts(source):
    square = source * source
    inner = jnp.tanh(GELU_A * (source + GELU_B * source * square))
    value = 0.5 * source * (1.0 + inner)
    slope = 0.5 * (1.0 + inner) + 0.5 * source * (1.0 - inner * inner) * (
        GELU_A * (1.0 + 3.0 * GELU_B * square)
    )
    return value, slope


def swap(value, axis):
    return lax.ppermute(value, axis, [(0, 1), (1, 0)])


def pick(flag, first, second):
    return jnp.where(flag == 0, first, second), jnp.where(flag == 0, second, first)


class Links:
    def __init__(self):
        self.size = lax.axis_size("dp")
        at = lax.axis_index("dp")
        self.groups = {}
        shift, name = 0, "y"
        while (1 << shift) < self.size:
            bits = 1 if shift == 0 else min(2, self.size.bit_length() - 1 - shift)
            self.groups[name] = (shift, bits, (at >> shift) & ((1 << bits) - 1))
            shift += bits
            name = "z" + str(shift)
        self.rest = [name for name in reversed(self.groups) if name != "y"]
        self.dims = self.rest + ["y", "x"]
        self.side = lax.axis_index("xx")

    def counts(self, dims):
        return [2 if d == "x" else 1 << self.groups[d][1] for d in dims]

    def send(self, value, d, mask):
        if d == "x":
            return swap(value, "xx")
        move = mask << self.groups[d][0]
        return lax.ppermute(value, "dp", [(i, i ^ move) for i in range(self.size)])

    def place(self, d):
        return self.side if d == "x" else self.groups[d][2]

    def scatter(self, parts, comes, dims, d, after=()):
        axis = dims.index(d)
        shares = fold(parts, comes, self.counts(dims), axis, self.place(d), list(after))
        come = [[self.send(share, d, mask)] for mask, share in enumerate(shares) if mask > 0]
        return [shares[0]], come, [other for other in dims if other != d]

    def scatter_rest(self, state, after):
        for d in self.rest:
            state = self.scatter(*state, d, after)
        return self.total(state)

    def total(self, state):
        parts, comes, dims = state
        total = parts[0].astype(F32)
        for (come,) in comes:
            total = total + come.astype(F32)
        return total[0]

    def begin_gather(self, state, d):
        array, dims = state
        come = [self.send(array, d, mask) for mask in range(1, self.counts([d])[0])]
        return array, come, dims, d

    def end_gather(self, begun, tick=None):
        array, come, dims, d = begun
        parts = [array] + come
        for bit in range(len(parts).bit_length() - 1):
            flag = (self.place(d) >> bit) & 1
            for low in range(len(parts)):
                if not low & (1 << bit):
                    high = low | (1 << bit)
                    parts[low], parts[high] = pick(flag, parts[low], parts[high])
        dims = [other for other in self.dims if other in dims or other == d]
        joined = jnp.stack(parts, axis=dims.index(d))
        if tick is not None:
            joined = joined + tick[0, 0].astype(joined.dtype)
        return joined, dims

    def gather(self, state, d, tick=None):
        return self.end_gather(self.begin_gather(state, d), tick)

def body(
    tokens,
    segments,
    ln1_gain,
    ln1_bias,
    qkv_weight,
    q_bias,
    v_bias,
    out_weight,
    out_bias,
    ln2_gain,
    ln2_bias,
    up_weight,
    up_bias,
    down_weight,
    down_bias,
    cotangent,
):
    side = lax.axis_index("xx")
    core = lax.axis_index("core")
    chips = lax.axis_size("dp") * lax.axis_size("xx")
    seq_count, quarter, width = tokens.shape
    length = segments.shape[1]
    own = qkv_weight.shape[0]
    pair_row = 2 * own
    hidden_own = up_bias.shape[0]
    half = width // 2
    cols = 3 * half
    pairs = half // PAIR
    splits = hidden_own // pair_row
    hidden = splits * width

    def at_index(array, index):
        return lax.dynamic_index_in_dim(array, index, 0, keepdims=False)

    def to_sequence(array, tick=None):
        kept = at_index(array, side)
        sent = at_index(array, 1 - side)
        if tick is not None:
            sent = sent + tick[0, 0].astype(sent.dtype)
        come = swap(sent, "xx")
        low, high = pick(side, kept, come)
        mine = jnp.stack([low, high])
        other = swap(mine, "core")
        even, odd = pick(core, mine, other)
        return jnp.stack([even, odd], axis=1).reshape(length, width), come, other

    def own_rows(array):
        return lax.dynamic_index_in_dim(
            array.reshape(2, 2, quarter, array.shape[-1]), core, 1, keepdims=False
        )

    def other_rows(array):
        return lax.dynamic_index_in_dim(
            array.reshape(2, 2, quarter, array.shape[-1]), 1 - core, 1, keepdims=False
        )

    def from_sequence(mine):
        come = swap(at_index(mine, 1 - side), "xx")
        return merged(at_index(mine, side), come), come

    def merged(kept, come, tick=None):
        if tick is not None:
            kept = kept + tick[0, 0].astype(kept.dtype)
        first, second = pick(side, kept, come)
        return jnp.stack([first, second])

    qkv_cols = qkv_weight.reshape(own, 3, 2, pairs, PAIR).transpose(2, 0, 3, 1, 4).reshape(2, own, cols)
    up_cols = (
        up_weight.reshape(own, chips, 2, splits, pair_row)
        .transpose(2, 0, 3, 1, 4)
        .reshape(2, own, hidden)
    )
    vectors = jnp.stack(
        [ln1_gain, ln1_bias, q_bias, v_bias, out_bias, ln2_gain, ln2_bias, down_bias], axis=1
    )
    vectors = jnp.pad(vectors, ((0, 0), (0, PAIR - vectors.shape[1])))

    def with_partner(two):
        mine, theirs = at_index(two, core), at_index(two, 1 - core)
        first, second = pick(core, mine, swap(theirs, "core"))
        return jnp.concatenate([first, second], axis=0)

    early = with_partner(
        jnp.concatenate([qkv_cols, jnp.broadcast_to(vectors, (2, own, PAIR))], axis=2)
    )
    early = jnp.concatenate(
        [
            early[:, : cols + 8],
            up_bias.reshape(splits, pair_row).T,
            early[:, cols + 8 + splits :],
        ],
        axis=1,
    )
    links = Links()

    def gather_rest(array, tick=None):
        state = (array, [])
        for d in links.rest:
            state = links.gather(state, d, tick if d == links.rest[-1] else None)
        return state

    def halves_of(state):
        middle = state[0].shape[-1] // 2
        return [(state[0][..., :middle], state[1]), (state[0][..., middle:], state[1])]

    def joined(halves):
        return [half_state[0].reshape(width, -1) for half_state in halves]

    inputs_low, come, other = to_sequence(tokens)
    grad_out_low, grad_come, _ = to_sequence(cotangent, gate([come]))
    state = (early, [])
    for d in links.rest[:-1]:
        state = links.gather(state, d)
    first_stage = links.begin_gather(state, links.rest[-1])
    begun = [
        links.begin_gather(piece, d)
        for piece, d in zip(halves_of(links.end_gather(first_stage)), "yx")
    ]
    early_halves = [links.end_gather(piece) for piece in begun]
    early_a, early_b = joined(
        [links.gather(piece, d) for piece, d in zip(early_halves, "xy")]
    )
    split = early_a.shape[1]
    late = with_partner(
        jnp.concatenate([up_cols, jnp.broadcast_to(out_weight, (2, own, width))], axis=2)
    )
    down_own = down_weight.reshape(splits, pair_row, width)
    late = lax.all_gather(
        pack([late, *(down_own[i] for i in range(splits))], [*first_stage[1], come]),
        ("dp", "xx"),
        axis=0,
        tiled=True,
    )
    small = early_b[:, cols - split :].astype(F32).T
    gain_one, shift_one, query_shift, value_shift, out_shift, gain_two, shift_two, down_shift = (
        small[i] for i in range(8)
    )
    up_shift = small[8 : 8 + splits].reshape(hidden)

    inputs = inputs_low.astype(F32)
    seg = at_index(segments, side)
    numbers = jnp.arange(PAIR, dtype=jnp.int32) % HEAD_DIM
    same = seg[:, None] == numbers[None, :]
    coded = numbers[None, :] < 4
    query_code = jnp.where(same & coded, 1.0, 0.0).astype(BF16)
    key_code = jnp.where(same | ~coded, 0.0, NEG).astype(BF16)

    def head_cols(vector):
        return lax.dynamic_slice_in_dim(vector, core * half, half, 0).reshape(pairs, 1, PAIR)

    zeros = jnp.zeros((pairs, 1, PAIR), F32)
    qkv_shift = jnp.concatenate(
        [head_cols(query_shift), zeros, head_cols(value_shift)], axis=1
    ).reshape(1, cols)
    qkv_scale = jnp.tile(jnp.repeat(jnp.array([0.125, 1.0, 1.0], F32), PAIR), pairs)[None]
    normed_t, qkv, tick = qkv_projection(
        inputs_low,
        early_a,
        early_b,
        jnp.pad(jnp.stack([gain_one, shift_one]), ((0, 6), (0, 0))),
        jnp.pad(jnp.concatenate([qkv_shift, qkv_scale]), ((0, 6), (0, 0))),
        [],
    )
    attended, log_total, _ = attention_forward(qkv, query_code, key_code, [grad_come])
    core_at = core.reshape(1).astype(jnp.int32)
    branch = out_projection(core_at, attended, late, splits, [])
    branch_come = swap(branch, "core")
    mid_vectors = jnp.pad(
        jnp.stack([out_shift, gain_two, shift_two, down_shift]), ((0, 4), (0, 0))
    )
    normed_two_low, hidden_low, grad_pre_low, mixed_part, ffn_other, partial_two, up_sums = feed_forward(
        core_at,
        inputs_low,
        branch,
        branch_come,
        grad_out_low,
        late,
        splits,
        mid_vectors,
        jnp.pad(up_shift[None], ((0, 7), (0, 0))),
    )
    partial_come = swap(partial_two, "core")
    mixed_own = (mixed_part + swap(ffn_other, "core").astype(F32)).astype(BF16)
    mixed_own = mixed_own.reshape(2, quarter, width)
    mixed_come = swap(at_index(mixed_own, 1 - side), "xx")

    grad_proj_down = [
        mm(hidden_low[:, i * width : (i + 1) * width], grad_out_low, TN).astype(BF16)
        for i in range(splits)
    ]
    grad_proj_up = mm(normed_two_low, grad_pre_low, TN).astype(BF16)
    late_grads = jnp.concatenate([grad_proj_up, *grad_proj_down], axis=1)
    late_own = lax.psum_scatter(late_grads, ("dp", "xx"), scatter_dimension=0, tiled=True)
    grad_middle, branch_low, grad_attended, mid_sums = norm_two(
        core_at,
        inputs_low,
        branch,
        branch_come,
        grad_out_low,
        partial_two,
        partial_come,
        late,
        splits,
        mid_vectors,
        [late_grads],
    )
    grad_proj_out = mm(attended, branch_low, TN)

    def as_column(vectors):
        table = jnp.stack(vectors, axis=1)
        return jnp.pad(table, ((0, 0), (0, PAIR - table.shape[1])))

    def only_mine(flag, array):
        return jnp.where(flag, array, jnp.zeros_like(array))

    small_two = [mid_sums[i] for i in range(4)] + [
        up_sums[0, i * width : (i + 1) * width] for i in range(splits)
    ]
    out_low = grad_proj_out.astype(BF16)
    grad_out_rows = jnp.concatenate(
        [only_mine(core == 0, out_low), only_mine(core == 1, out_low)], axis=0
    )

    def blocks(array):
        return array.reshape(chips, pair_row, array.shape[1])

    def pairs_backward(first, count, after):
        return attention_backward(
            first, count, qkv, query_code, key_code, attended, grad_attended, log_total, normed_t, after
        )

    out_piece = links.scatter([blocks(grad_out_rows)], [], links.dims, "y")
    grad_a, weight_grad_a, tick = pairs_backward(0, pairs - 1, [out_piece[0][0]])
    out_piece = links.scatter(*out_piece, "x", [tick])
    first_piece = links.scatter([blocks(weight_grad_a)], [], links.dims, "y", [tick])
    mixed = merge(at_index(mixed_own, side), mixed_come, side, [tick])
    grad_b, weight_grad_b, tick = pairs_backward(
        pairs - 1, 1, [out_piece[0][0], first_piece[0][0], tick, mixed]
    )
    grads = [grad_a, grad_b]
    first_piece = links.scatter(*first_piece, "x", [tick])
    norm_vectors = jnp.pad(jnp.stack([gain_one, shift_one]), ((0, 6), (0, 0)))
    partial_one, norm_sums, bias_sums, tick = norm_one(
        False, core_at, grads, early_a, early_b, cols, inputs_low, [], [first_piece[0][0]]
    )
    come = swap(partial_one, "core")
    token_own, norm_sums_own, bias_sums_own, tick = norm_one(
        True,
        core_at,
        grads,
        early_a,
        early_b,
        cols,
        inputs_low,
        [come, grad_middle, norm_vectors],
        [],
    )
    norm_sums = norm_sums + norm_sums_own
    bias_sums = bias_sums + bias_sums_own
    token_grad, come = from_sequence(token_own.reshape(2, quarter, width))
    grad_by_pair = bias_sums[0].reshape(pairs, 3, PAIR)

    def padded(vector):
        vector = vector.reshape(half)
        return jnp.concatenate([only_mine(core == 0, vector), only_mine(core == 1, vector)])

    small = as_column(
        [
            norm_sums[0],
            norm_sums[1],
            padded(grad_by_pair[:, 0]),
            padded(grad_by_pair[:, 2]),
        ]
        + small_two
    )
    last_piece = links.scatter(
        [blocks(weight_grad_b), blocks(small.astype(BF16))], [], links.dims, "y", [tick]
    )
    first_piece = (
        out_piece[0] + first_piece[0],
        [out_piece[1][0] + first_piece[1][0]],
        first_piece[2],
    )
    first_own = links.scatter_rest(first_piece, [tick])
    last_piece = links.scatter(*last_piece, "x")
    last_ready = last_piece[0][0]
    last_own = links.scatter_rest(last_piece, [come])

    def rows_of(array, index):
        return lax.dynamic_slice_in_dim(array, index * own, own, 0)

    def by_core(mine, come):
        return jnp.stack(pick(core, mine, come))

    def shared(array):
        return rows_of(array, core), swap(rows_of(array, 1 - core), "core")

    up_own, down_grad = widen(late_own, width, [last_ready])
    late_mine, late_come = shared(up_own)
    early_mine, early_come = shared(jnp.concatenate([first_own, last_own], axis=1).astype(BF16))
    out_grad = early_mine[:, :width].astype(F32) + early_come[:, :width].astype(F32)
    up_grad = (
        by_core(late_mine, late_come)
        .reshape(2, own, splits, chips, pair_row)
        .transpose(1, 3, 0, 2, 4)
        .reshape(own, 2 * hidden)
        .astype(F32)
    )
    down_grad = down_grad.reshape(hidden_own, width)
    qkv_grad = (
        by_core(early_mine[:, width : width + cols], early_come[:, width : width + cols])
        .reshape(2, own, pairs, 3, PAIR)
        .transpose(1, 3, 0, 2, 4)
        .reshape(own, 2 * cols)
        .astype(F32)
    )
    tail, first = width + cols + 8, first_own.shape[1]
    small_mine = early_mine[:, tail - 8 : tail].astype(F32)
    one = small_mine[:, :4] + early_come[:, tail - 8 : tail - 4].astype(F32)
    up_shift_grad = (
        last_own[:, tail - first : tail - first + splits].T.reshape(hidden_own).astype(F32)
    )
    two = small_mine[:, 4:]
    return (
        mixed,
        token_grad,
        one[:, 0],
        one[:, 1],
        qkv_grad,
        one[:, 2],
        one[:, 3],
        out_grad,
        two[:, 0],
        two[:, 1],
        two[:, 2],
        up_grad,
        up_shift_grad,
        down_grad,
        two[:, 3],
    )


def solution(mesh):
    parts = (mesh.shape["dp"], mesh.shape["ctx"] // 2, 2)
    split_mesh = Mesh(mesh.devices.reshape(parts), ("dp", "xx", "core"))
    rows = ("dp", "xx", "core")
    acts = P("dp", ("xx", "core"), None)
    vec, mat = P(rows), P(rows, None)
    return jax.shard_map(
        body,
        mesh=split_mesh,
        in_specs=(
            acts, P("dp", None), vec, vec, mat, vec, vec, mat, vec, vec, vec, mat, vec, mat, vec, acts,
        ),
        out_specs=(
            acts, acts, vec, vec, mat, vec, vec, mat, vec, vec, vec, mat, vec, mat, vec,
        ),
        check_vma=False,
    )
```

```python
import functools

import jax
import jax.numpy as jnp
from jax import lax
from jax.experimental import pallas as pl
from jax.experimental.pallas import tpu as pltpu
from jax.sharding import Mesh, PartitionSpec as P

HEAD_DIM = 64
PAIR = 2 * HEAD_DIM
EPSILON = 1e-05
NEG = -1e30
BLK = 512
F32 = jnp.float32
BF16 = jnp.bfloat16

NN = (((1,), (0,)), ((), ()))
NT = (((1,), (1,)), ((), ()))
TN = (((0,), (0,)), ((), ()))


def mm(left, right, dims=NN):
    return lax.dot_general(left, right, dims, preferred_element_type=F32)


def build_scores_operands(qkv_ref, qs_ref, ks_ref, rows, qx, kx):
    lane = lax.broadcasted_iota(jnp.int32, (BLK, PAIR), 1)
    first = lane < HEAD_DIM
    q = qkv_ref[rows, 0:PAIR].astype(F32)
    k = qkv_ref[rows, PAIR : 2 * PAIR].astype(F32)
    qs = qs_ref[rows, :].astype(F32)
    ks = ks_ref[rows, :].astype(F32)
    qx[0, rows, :] = jnp.where(first, q, qs).astype(BF16)
    qx[1, rows, :] = jnp.where(first, qs, q).astype(BF16)
    kx[0, rows, :] = jnp.where(first, k, ks).astype(BF16)
    kx[1, rows, :] = jnp.where(first, ks, k).astype(BF16)
    return first, q, k


def causal_block(scores):
    key_at = lax.broadcasted_iota(jnp.int32, scores.shape, 0)
    query_at = lax.broadcasted_iota(jnp.int32, scores.shape, 1)
    return jnp.where(key_at <= query_at, scores, NEG)


def attention_forward_kernel(qkv_ref, qs_ref, ks_ref, *rest):
    o_ref, lse_ref, tick_ref, qx, kx, vt, acc = rest[-7:]
    tick_ref[...] = jnp.zeros_like(tick_ref)
    length = qkv_ref.shape[0]
    blocks = length // BLK

    @pl.loop(0, blocks)
    def _(i):
        rows = pl.ds(pl.multiple_of(i * BLK, BLK), BLK)
        build_scores_operands(qkv_ref, qs_ref, ks_ref, rows, qx, kx)
        v_t = qkv_ref[rows, 2 * PAIR : 3 * PAIR].astype(F32).T
        ones = jnp.ones((16, BLK), BF16)
        for h in range(2):
            vt[h, 0:HEAD_DIM, rows] = v_t[h * HEAD_DIM : (h + 1) * HEAD_DIM].astype(BF16)
            vt[h, HEAD_DIM : HEAD_DIM + 16, rows] = ones

    @pl.loop(0, blocks)
    def _(i):
        rows = pl.ds(pl.multiple_of(i * BLK, BLK), BLK)
        queries = [qx[h, rows, :] for h in range(2)]
        tops = []
        for h in range(2):
            s = causal_block(mm(kx[h, rows, :], queries[h], NT))
            top = jnp.max(s, axis=0, keepdims=True)
            p = jnp.exp(s - top).astype(BF16)
            acc[h] = mm(vt[h, :, rows], p)
            tops.append(top)

        def step(j, carry):
            keys = pl.ds(pl.multiple_of(j * BLK, BLK), BLK)
            out = []
            for h in range(2):
                s = mm(kx[h, keys, :], qx[h, rows, :], NT)
                top = jnp.maximum(carry[h], jnp.max(s, axis=0, keepdims=True))
                p = jnp.exp(s - top).astype(BF16)
                acc[h] = acc[h] * jnp.exp(carry[h] - top) + mm(vt[h, :, keys], p)
                out.append(top)
            return tuple(out)

        tops = lax.fori_loop(0, i, step, tuple(tops))
        parts = []
        for h in range(2):
            total = acc[h, HEAD_DIM : HEAD_DIM + 1, :]
            parts.append(acc[h, 0:HEAD_DIM, :] / total)
            lse_ref[0, h : h + 1, rows] = tops[h] + jnp.log(total)
        o_ref[rows, :] = jnp.concatenate(parts, axis=0).T.astype(BF16)


def attention_backward_kernel(qkv_ref, qs_ref, ks_ref, o_ref, do_ref, lse_ref, at_ref, *rest):
    d_ref, dw_ref, tick_ref, qx, kx, qm, dm, kt, delta, dqt, dk, dv = rest[-12:]
    tick_ref[...] = jnp.zeros_like(tick_ref)
    length = qkv_ref.shape[0]
    blocks = length // BLK

    @pl.loop(0, blocks)
    def _(i):
        rows = pl.ds(pl.multiple_of(i * BLK, BLK), BLK)
        first, q, k = build_scores_operands(qkv_ref, qs_ref, ks_ref, rows, qx, kx)
        do = do_ref[rows, :].astype(F32)
        zero = jnp.zeros_like(q)
        qm[0, rows, :] = jnp.where(first, q, zero).astype(BF16)
        qm[1, rows, :] = jnp.where(first, zero, q).astype(BF16)
        dm[0, rows, :] = jnp.where(first, do, zero).astype(BF16)
        dm[1, rows, :] = jnp.where(first, zero, do).astype(BF16)
        kt[:, rows] = k.T.astype(BF16)
        inner = (do * o_ref[rows, :].astype(F32)).T
        for h in range(2):
            delta[h : h + 1, rows] = jnp.sum(
                inner[h * HEAD_DIM : (h + 1) * HEAD_DIM], axis=0, keepdims=True
            )
        dqt[:, rows] = jnp.zeros((PAIR, BLK), F32)

    def tile(keys, rows, masked):
        values = qkv_ref[keys, 2 * PAIR : 3 * PAIR]
        lows, slopes = [], []
        for h in range(2):
            s = mm(kx[h, keys, :], qx[h, rows, :], NT)
            if masked:
                s = causal_block(s)
            p = jnp.exp(s - lse_ref[0, h : h + 1, rows])
            dp = mm(values, dm[h, rows, :], NT)
            ds = (p * (dp - delta[h : h + 1, rows])).astype(BF16)
            lows.append(p.astype(BF16))
            slopes.append(ds)
            part = slice(h * HEAD_DIM, (h + 1) * HEAD_DIM)
            dqt[part, rows] += mm(kt[part, keys], ds)
        dk_part, dv_part = (
            mm(
                jnp.concatenate(sides, axis=1),
                jnp.concatenate([ref[0, rows, :], ref[1, rows, :]], axis=0),
            )
            for sides, ref in ((slopes, qm), (lows, dm))
        )
        return dk_part, dv_part

    @pl.loop(0, blocks)
    def _(j):
        keys = pl.ds(pl.multiple_of(j * BLK, BLK), BLK)
        dk[...], dv[...] = tile(keys, keys, True)

        @pl.loop(j + 1, blocks)
        def _(i):
            dk_part, dv_part = tile(keys, pl.ds(pl.multiple_of(i * BLK, BLK), BLK), False)
            dk[...] += dk_part
            dv[...] += dv_part

        d_ref[keys, PAIR : 2 * PAIR] = dk[...].astype(BF16)
        d_ref[keys, 2 * PAIR : 3 * PAIR] = dv[...].astype(BF16)

    @pl.loop(0, blocks)
    def _(i):
        rows = pl.ds(pl.multiple_of(i * BLK, BLK), BLK)
        d_ref[rows, 0:PAIR] = (dqt[:, rows].T.astype(BF16).astype(F32) * 0.125).astype(BF16)

    @pl.loop(0, dw_ref.shape[0] // ROWS)
    def _(i):
        rows = pl.ds(pl.multiple_of(i * ROWS, ROWS), ROWS)
        dw_ref[rows, :] = mm(at_ref[rows, :], d_ref[...]).astype(BF16)


VMEM_LIMIT = 48 * 1024 * 1024


SMALL_COST = pl.CostEstimate(flops=1000, bytes_accessed=1000, transcendentals=0)


TICK = jax.ShapeDtypeStruct((8, 128), F32)
TICK_SPEC = pl.BlockSpec((8, 128), lambda i: (0, 0))
ANY_SPEC = pl.BlockSpec(memory_space=pl.ANY)


def pack_kernel(count, refs):
    refs[-1][...] = jnp.concatenate([ref[...] for ref in refs[:count]], axis=-1)


def pack(parts, after):
    rows = parts[0].shape[0]
    width = sum(part.shape[1] for part in parts)
    return pl.pallas_call(
        lambda *refs: pack_kernel(len(parts), refs),
        grid=(1,),
        in_specs=[pl.BlockSpec(part.shape, lambda i: (0, 0)) for part in parts]
        + [ANY_SPEC] * len(after),
        out_specs=pl.BlockSpec((rows, width), lambda i: (0, 0)),
        out_shape=jax.ShapeDtypeStruct((rows, width), BF16),
        compiler_params=pltpu.CompilerParams(vmem_limit_bytes=VMEM_LIMIT),
        cost_estimate=SMALL_COST,
    )(*parts, *after)


def widen(source, width, after):
    rows, cols = source.shape
    count = cols // width - 2

    def kernel(source_ref, *refs):
        up_ref, down_ref = refs[-2:]
        up_ref[...] = source_ref[:, : 2 * width].astype(F32)
        for i in range(count):
            down_ref[i] = source_ref[:, (2 + i) * width : (3 + i) * width].astype(F32)

    return pl.pallas_call(
        kernel,
        grid=(1,),
        in_specs=[pl.BlockSpec((rows, cols), lambda i: (0, 0))] + [ANY_SPEC] * len(after),
        out_specs=[
            pl.BlockSpec((rows, 2 * width), lambda i: (0, 0)),
            pl.BlockSpec((count, rows, width), lambda i: (0, 0, 0)),
        ],
        out_shape=[
            jax.ShapeDtypeStruct((rows, 2 * width), F32),
            jax.ShapeDtypeStruct((count, rows, width), F32),
        ],
        compiler_params=pltpu.CompilerParams(vmem_limit_bytes=VMEM_LIMIT),
        cost_estimate=SMALL_COST,
    )(source, *after)


def merge(kept, come, side, after):
    def kernel(side_ref, kept_ref, come_ref, *rest):
        mine = pl.program_id(0) == side_ref[0]

        @pl.when(mine)
        def _():
            rest[-1][0] = kept_ref[...]

        @pl.when(jnp.logical_not(mine))
        def _():
            rest[-1][0] = come_ref[...]

    whole = pl.BlockSpec(kept.shape, lambda i, side_ref: (0, 0))
    return pl.pallas_call(
        kernel,
        grid_spec=pltpu.PrefetchScalarGridSpec(
            num_scalar_prefetch=1,
            grid=(2,),
            in_specs=[whole, whole] + [ANY_SPEC] * len(after),
            out_specs=pl.BlockSpec((1, *kept.shape), lambda i, side_ref: (i, 0, 0)),
        ),
        out_shape=jax.ShapeDtypeStruct((2, *kept.shape), kept.dtype),
        compiler_params=pltpu.CompilerParams(vmem_limit_bytes=VMEM_LIMIT),
        cost_estimate=SMALL_COST,
    )(side.reshape(1).astype(jnp.int32), kept, come, *after)


def gate_kernel(*refs):
    refs[-1][...] = jnp.zeros_like(refs[-1])


def gate(after):
    return pl.pallas_call(
        gate_kernel,
        grid=(1,),
        in_specs=[ANY_SPEC] * len(after),
        out_specs=TICK_SPEC,
        out_shape=TICK,
        cost_estimate=SMALL_COST,
    )(*after)


def fold_kernel(parts, comes, outs, refs):
    for m in range(outs):
        value = None
        for term in range(1 + comes):
            at = 1 + (term * outs + m) * parts
            side = jnp.concatenate([ref[0] for ref in refs[at : at + parts]], axis=-1)
            if comes:
                side = side.astype(F32)
            value = side if term == 0 else value + side
        refs[len(refs) - outs + m][0] = value.astype(BF16)


def fold(parts, comes, sizes, axis, at, after):
    blocks, rows = parts[0].shape[:2]
    width = sum(part.shape[2] for part in parts)
    outs = sizes[axis] if axis is not None else 1
    inner = 1
    if axis is not None:
        for size in sizes[axis + 1 :]:
            inner *= size

    def spec(array, m):
        def index(j, at_ref):
            if axis is None:
                return j, 0, 0
            return (j // inner) * (outs * inner) + (at_ref[0] ^ m) * inner + j % inner, 0, 0

        return pl.BlockSpec((1, rows, array.shape[2]), index)

    def kernel(*refs):
        ins = 1 + (1 + len(comes)) * len(parts) * outs
        fold_kernel(len(parts), len(comes), outs, refs[:ins] + refs[ins + len(after) :])

    out = pl.BlockSpec((1, rows, width), lambda j, at_ref: (j, 0, 0))
    return pl.pallas_call(
        kernel,
        grid_spec=pltpu.PrefetchScalarGridSpec(
            num_scalar_prefetch=1,
            grid=(blocks // outs,),
            in_specs=[spec(part, m) for m in range(outs) for part in parts]
            + [spec(part, m) for come in comes for m in range(outs) for part in come]
            + [ANY_SPEC] * len(after),
            out_specs=[out] * outs,
        ),
        out_shape=[jax.ShapeDtypeStruct((blocks // outs, rows, width), BF16)] * outs,
        compiler_params=pltpu.CompilerParams(vmem_limit_bytes=VMEM_LIMIT),
        cost_estimate=SMALL_COST,
    )(at.reshape(1).astype(jnp.int32), *(list(parts) * outs), *[part for come in comes for part in list(come) * outs], *after)


def qkv_kernel(x_ref, wa_ref, wb_ref, vec_ref, col_ref, *rest_refs):
    a_ref, qkv_ref, tick_ref = rest_refs[-3:]
    split = wa_ref.shape[1]
    rest = qkv_ref.shape[1] - split
    for part in range(2):
        rows = slice(part * ROWS, (part + 1) * ROWS)
        normal, _ = norm_forward(x_ref[rows, :].astype(F32))
        normed = (normal * vec_ref[0:1, :] + vec_ref[1:2, :]).astype(BF16)
        a_ref[:, rows] = normed.astype(F32).T.astype(BF16)
        for w, cols in ((wa_ref[...], slice(0, split)), (wb_ref[:, :rest], slice(split, None))):
            shift, scale = col_ref[0:1, cols], col_ref[1:2, cols]
            qkv_ref[rows, cols] = ((mm(normed, w) + shift) * scale).astype(BF16)
    tick_ref[...] = jnp.zeros_like(tick_ref)


def qkv_projection(inputs, weight_a, weight_b, vectors, columns, after):
    length, width = inputs.shape
    cols = columns.shape[1]
    return pl.pallas_call(
        qkv_kernel,
        grid=(length // (2 * ROWS),),
        in_specs=[
            pl.BlockSpec((2 * ROWS, width), lambda i: (i, 0)),
            pl.BlockSpec(weight_a.shape, lambda i: (0, 0)),
            pl.BlockSpec(weight_b.shape, lambda i: (0, 0)),
            pl.BlockSpec(vectors.shape, lambda i: (0, 0)),
            pl.BlockSpec(columns.shape, lambda i: (0, 0)),
        ]
        + [ANY_SPEC] * len(after),
        out_specs=[
            pl.BlockSpec((width, 2 * ROWS), lambda i: (0, i)),
            pl.BlockSpec((2 * ROWS, cols), lambda i: (i, 0)),
            TICK_SPEC,
        ],
        out_shape=[
            jax.ShapeDtypeStruct((width, length), BF16),
            jax.ShapeDtypeStruct((length, cols), BF16),
            TICK,
        ],
        compiler_params=pltpu.CompilerParams(vmem_limit_bytes=VMEM_LIMIT),
        cost_estimate=SMALL_COST,
    )(inputs, weight_a, weight_b, vectors, columns, *after)


def out_projection(core, attended, late, block, after):
    length, cols = attended.shape
    width = late.shape[0]
    rows = length // 4

    def kernel(core_ref, a_ref, w_ref, *rest):
        rest[-1][...] = mm(a_ref[...], w_ref[...]).astype(BF16)

    return pl.pallas_call(
        kernel,
        grid_spec=pltpu.PrefetchScalarGridSpec(
            num_scalar_prefetch=1,
            grid=(4,),
            in_specs=[
                pl.BlockSpec((rows, cols), lambda i, core_ref: (i, 0)),
                pl.BlockSpec((cols, width), lambda i, core_ref: (core_ref[0], block)),
            ]
            + [ANY_SPEC] * len(after),
            out_specs=pl.BlockSpec((rows, width), lambda i, core_ref: (i, 0)),
        ),
        out_shape=jax.ShapeDtypeStruct((length, width), BF16),
        compiler_params=pltpu.CompilerParams(vmem_limit_bytes=VMEM_LIMIT),
        cost_estimate=SMALL_COST,
    )(core, attended, late, *after)


def middle_of(x_ref, b0_ref, b1_ref, vec_ref):
    both = b0_ref[...].astype(F32) + b1_ref[...].astype(F32)
    return x_ref[...].astype(F32) + both + vec_ref[0:1, :]


def feed_forward_kernel(splits, core_ref, x_ref, b0_ref, b1_ref, dy_ref, up_ref, *rest):
    down_refs, (vec_ref, shift_ref) = rest[:splits], rest[splits : splits + 2]
    a_ref, g_ref, du_ref, own_ref, other_ref, dh_ref, sums_ref = rest[splits + 2 :]
    at = pl.program_id(0)

    @pl.when(at == 0)
    def _():
        sums_ref[...] = jnp.zeros_like(sums_ref)

    middle = middle_of(x_ref, b0_ref, b1_ref, vec_ref)
    normal, _ = norm_forward(middle)
    normed = (normal * vec_ref[1:2, :] + vec_ref[2:3, :]).astype(BF16)
    a_ref[...] = normed
    dy = dy_ref[...]
    ffn, dh = None, None
    width = dy.shape[1]
    for i, down_ref in enumerate(down_refs):
        cols = slice(i * width, (i + 1) * width)
        up, down = up_ref[:, cols], down_ref[...]
        value, slope = gelu_parts(mm(normed, up) + shift_ref[0:1, cols])
        du = slope * mm(dy, down, NT)
        value, du = value.astype(BF16), du.astype(BF16)
        g_ref[:, cols] = value
        du_ref[:, cols] = du
        sums_ref[0:1, cols] += jnp.sum(du.astype(F32), axis=0, keepdims=True)
        ffn_part, dh_part = mm(value, down), mm(du, up, NT)
        ffn = ffn_part if i == 0 else ffn + ffn_part
        dh = dh_part if i == 0 else dh + dh_part
    dh_ref[...] = dh.astype(BF16)
    mine = at % 2 == core_ref[0]

    @pl.when(mine)
    def _():
        own_ref[...] = middle_of(x_ref, b0_ref, b1_ref, vec_ref) + ffn + vec_ref[3:4, :]

    @pl.when(jnp.logical_not(mine))
    def _():
        other_ref[...] = ffn.astype(BF16)


def feed_forward(core, inputs, branch, branch_come, grad_out, late, splits, vectors, up_shift):
    length, width = inputs.shape
    rows = length // 4
    hidden = splits * width
    narrow = pl.BlockSpec((rows, width), lambda i, core_ref: (i, 0))
    wide = pl.BlockSpec((rows, hidden), lambda i, core_ref: (i, 0))
    shared = pl.BlockSpec((rows, width), lambda i, core_ref: (i // 2, 0))

    def whole(array):
        return pl.BlockSpec(array.shape, lambda i, core_ref: (0, 0))

    def down(i):
        return pl.BlockSpec((width, width), lambda _, core_ref: (0, splits + 1 + i))

    return pl.pallas_call(
        functools.partial(feed_forward_kernel, splits),
        grid_spec=pltpu.PrefetchScalarGridSpec(
            num_scalar_prefetch=1,
            grid=(4,),
            in_specs=[narrow] * 4
            + [pl.BlockSpec((width, hidden), lambda i, core_ref: (0, 0))]
            + [down(i) for i in range(splits)]
            + [whole(vectors), whole(up_shift)],
            out_specs=[
                narrow, wide, wide, shared, shared, narrow,
                pl.BlockSpec((8, hidden), lambda i, core_ref: (0, 0)),
            ],
        ),
        out_shape=[
            jax.ShapeDtypeStruct((length, width), BF16),
            jax.ShapeDtypeStruct((length, hidden), BF16),
            jax.ShapeDtypeStruct((length, hidden), BF16),
            jax.ShapeDtypeStruct((length // 2, width), F32),
            jax.ShapeDtypeStruct((length // 2, width), BF16),
            jax.ShapeDtypeStruct((length, width), BF16),
            jax.ShapeDtypeStruct((8, hidden), F32),
        ],
        compiler_params=pltpu.CompilerParams(vmem_limit_bytes=VMEM_LIMIT),
        cost_estimate=SMALL_COST,
    )(core, inputs, branch, branch_come, grad_out, late, *([late] * splits), vectors, up_shift)


def norm_two_kernel(core_ref, x_ref, b0_ref, b1_ref, dy_ref, p0_ref, p1_ref, w_ref, vec_ref, *rest):
    mid_ref, low_ref, do_ref, sums_ref = rest[-4:]

    @pl.when(pl.program_id(0) == 0)
    def _():
        sums_ref[...] = jnp.zeros_like(sums_ref)

    normal, scale = norm_forward(middle_of(x_ref, b0_ref, b1_ref, vec_ref))
    grad = p0_ref[...].astype(F32) + p1_ref[...].astype(F32)
    dy = dy_ref[...].astype(F32)
    mid = dy + norm_backward(normal, scale, grad * vec_ref[1:2, :])
    low = mid.astype(BF16)
    low_ref[...] = low
    do_ref[...] = mm(low, w_ref[...], NT).astype(BF16)
    for i, value in enumerate((low.astype(F32), grad * normal, grad, dy)):
        sums_ref[i : i + 1, :] += jnp.sum(value, axis=0, keepdims=True)

    @pl.when(pl.program_id(0) % 2 == core_ref[0])
    def _():
        mid_ref[...] = mid


def norm_two(core, inputs, branch, branch_come, grad_out, partial, partial_come, late, block, vectors, after):
    length, width = inputs.shape
    rows = length // 4
    cols = width // 2
    narrow = pl.BlockSpec((rows, width), lambda i, core_ref: (i, 0))
    return pl.pallas_call(
        norm_two_kernel,
        grid_spec=pltpu.PrefetchScalarGridSpec(
            num_scalar_prefetch=1,
            grid=(4,),
            in_specs=[narrow] * 6
            + [
                pl.BlockSpec((cols, width), lambda i, core_ref: (core_ref[0], block)),
                pl.BlockSpec(vectors.shape, lambda i, core_ref: (0, 0)),
            ]
            + [ANY_SPEC] * len(after),
            out_specs=[
                pl.BlockSpec((rows, width), lambda i, core_ref: (i // 2, 0)),
                narrow,
                pl.BlockSpec((rows, cols), lambda i, core_ref: (i, 0)),
                pl.BlockSpec((8, width), lambda i, core_ref: (0, 0)),
            ],
        ),
        out_shape=[
            jax.ShapeDtypeStruct((length // 2, width), F32),
            jax.ShapeDtypeStruct((length, width), BF16),
            jax.ShapeDtypeStruct((length, cols), BF16),
            jax.ShapeDtypeStruct((8, width), F32),
        ],
        compiler_params=pltpu.CompilerParams(vmem_limit_bytes=VMEM_LIMIT),
        cost_estimate=SMALL_COST,
    )(core, inputs, branch, branch_come, grad_out, partial, partial_come, late, vectors, *after)


ROWS = 256


def attention_forward(qkv, query_code, key_code, after):
    length, width = qkv.shape
    pairs = width // (3 * PAIR)
    return pl.pallas_call(
        attention_forward_kernel,
        grid=(pairs,),
        in_specs=[
            pl.BlockSpec((length, 3 * PAIR), lambda p: (0, p)),
            pl.BlockSpec((length, PAIR), lambda p: (0, 0)),
            pl.BlockSpec((length, PAIR), lambda p: (0, 0)),
        ]
        + [ANY_SPEC] * len(after),
        out_specs=[
            pl.BlockSpec((length, PAIR), lambda p: (0, p)),
            pl.BlockSpec((1, 8, length), lambda p: (p, 0, 0)),
            TICK_SPEC,
        ],
        out_shape=[
            jax.ShapeDtypeStruct((length, pairs * PAIR), BF16),
            jax.ShapeDtypeStruct((pairs, 8, length), F32),
            TICK,
        ],
        scratch_shapes=[
            pltpu.VMEM((2, length, PAIR), BF16),
            pltpu.VMEM((2, length, PAIR), BF16),
            pltpu.VMEM((2, HEAD_DIM + 16, length), BF16),
            pltpu.VMEM((2, HEAD_DIM + 16, BLK), F32),
        ],
        compiler_params=pltpu.CompilerParams(vmem_limit_bytes=VMEM_LIMIT),
        cost_estimate=SMALL_COST,
    )(qkv, query_code, key_code, *after)


def norm_one_kernel(own, core_ref, d0_ref, d1_ref, wa_ref, wb_ref, x_ref, *rest):
    if own:
        come_ref, mid_ref, vec_ref, out_ref, sums_ref, bias_ref, tick_ref, w = rest
    else:
        out_ref, sums_ref, bias_ref, tick_ref, w = rest
    split = wa_ref.shape[1]

    @pl.when(pl.program_id(0) == 0)
    def _():
        sums_ref[...] = jnp.zeros_like(sums_ref)
        bias_ref[...] = jnp.zeros_like(bias_ref)
        w[:, :split] = wa_ref[...]
        w[:, split:] = wb_ref[:, : w.shape[1] - split]
        tick_ref[...] = jnp.zeros_like(tick_ref)

    total = None
    for i, ref in enumerate((d0_ref, d1_ref)):
        cols = slice(0, ref.shape[1]) if i == 0 else slice(d0_ref.shape[1], None)
        grad = ref[...]
        part = mm(grad, w[:, cols], NT)
        total = part if i == 0 else total + part
        bias_ref[0:1, cols] += jnp.sum(grad.astype(F32), axis=0, keepdims=True)
    normal, scale = norm_forward(x_ref[...].astype(F32))
    sums_ref[0:1, :] += jnp.sum(total * normal, axis=0, keepdims=True)
    sums_ref[1:2, :] += jnp.sum(total, axis=0, keepdims=True)
    if own:
        grad = (total + come_ref[...].astype(F32)) * vec_ref[0:1, :]
        out_ref[...] = (mid_ref[...] + norm_backward(normal, scale, grad)).astype(BF16)
    else:
        out_ref[...] = total.astype(BF16)


def norm_one(own, core, grads, weight_a, weight_b, cols, inputs, extra, after):
    length, width = inputs.shape
    count = length // (2 * ROWS)
    per = count // 2

    def block(i, core_ref):
        which = core_ref[0] if own else 1 - core_ref[0]
        return ((i // per) * 2 + which) * per + i % per, 0

    def at_zero(i, core_ref):
        return 0, 0

    plain = pl.BlockSpec((ROWS, width), lambda i, core_ref: (i, 0))
    rows = pl.BlockSpec((ROWS, width), block)
    in_specs = [pl.BlockSpec((ROWS, grad.shape[1]), block) for grad in grads] + [
        pl.BlockSpec(weight_a.shape, at_zero),
        pl.BlockSpec(weight_b.shape, at_zero),
        rows,
    ]
    out_specs = [
        plain,
        pl.BlockSpec((8, width), at_zero),
        pl.BlockSpec((8, cols), at_zero),
        pl.BlockSpec((8, 128), at_zero),
    ]
    out_shape = [
        jax.ShapeDtypeStruct((count * ROWS, width), BF16),
        jax.ShapeDtypeStruct((8, width), F32),
        jax.ShapeDtypeStruct((8, cols), F32),
        TICK,
    ]
    if own:
        in_specs += [plain, plain, pl.BlockSpec(extra[2].shape, at_zero)]

    def kernel(*refs):
        inner = refs[: 1 + len(in_specs)] + refs[1 + len(in_specs) + len(after) :]
        norm_one_kernel(own, *inner)

    return pl.pallas_call(
        kernel,
        grid_spec=pltpu.PrefetchScalarGridSpec(
            num_scalar_prefetch=1,
            grid=(count,),
            in_specs=in_specs + [ANY_SPEC] * len(after),
            out_specs=out_specs,
            scratch_shapes=[pltpu.VMEM((width, cols), BF16)],
        ),
        out_shape=out_shape,
        compiler_params=pltpu.CompilerParams(vmem_limit_bytes=VMEM_LIMIT),
        cost_estimate=SMALL_COST,
    )(core, *grads, weight_a, weight_b, inputs, *extra, *after)


def attention_backward(
    first, count, qkv, query_code, key_code, attended, grad_attended, log_total, normed_t, after
):
    length = qkv.shape[0]
    width = normed_t.shape[0]
    return pl.pallas_call(
        attention_backward_kernel,
        grid=(count,),
        in_specs=[
            pl.BlockSpec((length, 3 * PAIR), lambda p: (0, first + p)),
            pl.BlockSpec((length, PAIR), lambda p: (0, 0)),
            pl.BlockSpec((length, PAIR), lambda p: (0, 0)),
            pl.BlockSpec((length, PAIR), lambda p: (0, first + p)),
            pl.BlockSpec((length, PAIR), lambda p: (0, first + p)),
            pl.BlockSpec((1, 8, length), lambda p: (first + p, 0, 0)),
            pl.BlockSpec(normed_t.shape, lambda p: (0, 0)),
        ]
        + [ANY_SPEC] * len(after),
        out_specs=[
            pl.BlockSpec((length, 3 * PAIR), lambda p: (0, p)),
            pl.BlockSpec((width, 3 * PAIR), lambda p: (0, p)),
            TICK_SPEC,
        ],
        out_shape=[
            jax.ShapeDtypeStruct((length, count * 3 * PAIR), BF16),
            jax.ShapeDtypeStruct((width, count * 3 * PAIR), BF16),
            TICK,
        ],
        scratch_shapes=[
            pltpu.VMEM((2, length, PAIR), BF16),
            pltpu.VMEM((2, length, PAIR), BF16),
            pltpu.VMEM((2, length, PAIR), BF16),
            pltpu.VMEM((2, length, PAIR), BF16),
            pltpu.VMEM((PAIR, length), BF16),
            pltpu.VMEM((8, length), F32),
            pltpu.VMEM((PAIR, length), F32),
            pltpu.VMEM((BLK, PAIR), F32),
            pltpu.VMEM((BLK, PAIR), F32),
        ],
        compiler_params=pltpu.CompilerParams(vmem_limit_bytes=VMEM_LIMIT),
        cost_estimate=SMALL_COST,
    )(qkv, query_code, key_code, attended, grad_attended, log_total, normed_t, *after)


def norm_forward(source):
    average = jnp.mean(source, axis=-1, keepdims=True)
    centred = source - average
    spread = jnp.mean(centred * centred, axis=-1, keepdims=True)
    scale = lax.rsqrt(spread + EPSILON)
    return centred * scale, scale


def norm_backward(normal, scale, grad):
    return scale * (
        grad
        - jnp.mean(grad, axis=-1, keepdims=True)
        - normal * jnp.mean(grad * normal, axis=-1, keepdims=True)
    )


GELU_A = 0.7978845608028654
GELU_B = 0.044715


def gelu_parts(source):
    square = source * source
    inner = jnp.tanh(GELU_A * (source + GELU_B * source * square))
    value = 0.5 * source * (1.0 + inner)
    slope = 0.5 * (1.0 + inner) + 0.5 * source * (1.0 - inner * inner) * (
        GELU_A * (1.0 + 3.0 * GELU_B * square)
    )
    return value, slope


def swap(value, axis):
    return lax.ppermute(value, axis, [(0, 1), (1, 0)])


def pick(flag, first, second):
    return jnp.where(flag == 0, first, second), jnp.where(flag == 0, second, first)


class Links:
    def __init__(self):
        self.size = lax.axis_size("dp")
        at = lax.axis_index("dp")
        self.groups = {}
        shift, name = 0, "y"
        while (1 << shift) < self.size:
            bits = 1 if shift == 0 else min(2, self.size.bit_length() - 1 - shift)
            self.groups[name] = (shift, bits, (at >> shift) & ((1 << bits) - 1))
            shift += bits
            name = "z" + str(shift)
        self.rest = [name for name in reversed(self.groups) if name != "y"]
        self.dims = self.rest + ["y", "x"]
        self.side = lax.axis_index("xx")

    def counts(self, dims):
        return [2 if d == "x" else 1 << self.groups[d][1] for d in dims]

    def send(self, value, d, mask):
        if d == "x":
            return swap(value, "xx")
        move = mask << self.groups[d][0]
        return lax.ppermute(value, "dp", [(i, i ^ move) for i in range(self.size)])

    def place(self, d):
        return self.side if d == "x" else self.groups[d][2]

    def scatter(self, parts, comes, dims, d, after=()):
        axis = dims.index(d)
        shares = fold(parts, comes, self.counts(dims), axis, self.place(d), list(after))
        come = [[self.send(share, d, mask)] for mask, share in enumerate(shares) if mask > 0]
        return [shares[0]], come, [other for other in dims if other != d]

    def scatter_rest(self, state, after):
        for d in self.rest:
            state = self.scatter(*state, d, after)
        return self.total(state)

    def total(self, state):
        parts, comes, dims = state
        total = parts[0].astype(F32)
        for (come,) in comes:
            total = total + come.astype(F32)
        return total[0]

    def begin_gather(self, state, d):
        array, dims = state
        come = [self.send(array, d, mask) for mask in range(1, self.counts([d])[0])]
        return array, come, dims, d

    def end_gather(self, begun, tick=None):
        array, come, dims, d = begun
        parts = [array] + come
        for bit in range(len(parts).bit_length() - 1):
            flag = (self.place(d) >> bit) & 1
            for low in range(len(parts)):
                if not low & (1 << bit):
                    high = low | (1 << bit)
                    parts[low], parts[high] = pick(flag, parts[low], parts[high])
        dims = [other for other in self.dims if other in dims or other == d]
        joined = jnp.stack(parts, axis=dims.index(d))
        if tick is not None:
            joined = joined + tick[0, 0].astype(joined.dtype)
        return joined, dims

    def gather(self, state, d, tick=None):
        return self.end_gather(self.begin_gather(state, d), tick)

def body(
    tokens,
    segments,
    ln1_gain,
    ln1_bias,
    qkv_weight,
    q_bias,
    v_bias,
    out_weight,
    out_bias,
    ln2_gain,
    ln2_bias,
    up_weight,
    up_bias,
    down_weight,
    down_bias,
    cotangent,
):
    side = lax.axis_index("xx")
    core = lax.axis_index("core")
    chips = lax.axis_size("dp") * lax.axis_size("xx")
    seq_count, quarter, width = tokens.shape
    length = segments.shape[1]
    own = qkv_weight.shape[0]
    pair_row = 2 * own
    hidden_own = up_bias.shape[0]
    half = width // 2
    cols = 3 * half
    pairs = half // PAIR
    splits = hidden_own // pair_row
    hidden = splits * width

    def at_index(array, index):
        return lax.dynamic_index_in_dim(array, index, 0, keepdims=False)

    def to_sequence(array, tick=None):
        kept = at_index(array, side)
        sent = at_index(array, 1 - side)
        if tick is not None:
            sent = sent + tick[0, 0].astype(sent.dtype)
        come = swap(sent, "xx")
        low, high = pick(side, kept, come)
        mine = jnp.stack([low, high])
        other = swap(mine, "core")
        even, odd = pick(core, mine, other)
        return jnp.stack([even, odd], axis=1).reshape(length, width), come, other

    def own_rows(array):
        return lax.dynamic_index_in_dim(
            array.reshape(2, 2, quarter, array.shape[-1]), core, 1, keepdims=False
        )

    def other_rows(array):
        return lax.dynamic_index_in_dim(
            array.reshape(2, 2, quarter, array.shape[-1]), 1 - core, 1, keepdims=False
        )

    def from_sequence(mine):
        come = swap(at_index(mine, 1 - side), "xx")
        return merged(at_index(mine, side), come), come

    def merged(kept, come, tick=None):
        if tick is not None:
            kept = kept + tick[0, 0].astype(kept.dtype)
        first, second = pick(side, kept, come)
        return jnp.stack([first, second])

    qkv_cols = qkv_weight.reshape(own, 3, 2, pairs, PAIR).transpose(2, 0, 3, 1, 4).reshape(2, own, cols)
    up_cols = (
        up_weight.reshape(own, chips, 2, splits, pair_row)
        .transpose(2, 0, 3, 1, 4)
        .reshape(2, own, hidden)
    )
    vectors = jnp.stack(
        [ln1_gain, ln1_bias, q_bias, v_bias, out_bias, ln2_gain, ln2_bias, down_bias], axis=1
    )
    vectors = jnp.pad(vectors, ((0, 0), (0, PAIR - vectors.shape[1])))

    def with_partner(two):
        mine, theirs = at_index(two, core), at_index(two, 1 - core)
        first, second = pick(core, mine, swap(theirs, "core"))
        return jnp.concatenate([first, second], axis=0)

    early = with_partner(
        jnp.concatenate([qkv_cols, jnp.broadcast_to(vectors, (2, own, PAIR))], axis=2)
    )
    early = jnp.concatenate(
        [
            early[:, : cols + 8],
            up_bias.reshape(splits, pair_row).T,
            early[:, cols + 8 + splits :],
        ],
        axis=1,
    )
    links = Links()

    def gather_rest(array, tick=None):
        state = (array, [])
        for d in links.rest:
            state = links.gather(state, d, tick if d == links.rest[-1] else None)
        return state

    def halves_of(state):
        middle = state[0].shape[-1] // 2
        return [(state[0][..., :middle], state[1]), (state[0][..., middle:], state[1])]

    def joined(halves):
        return [half_state[0].reshape(width, -1) for half_state in halves]

    inputs_low, come, other = to_sequence(tokens)
    grad_out_low, grad_come, _ = to_sequence(cotangent, gate([come]))
    state = (early, [])
    for d in links.rest[:-1]:
        state = links.gather(state, d)
    first_stage = links.begin_gather(state, links.rest[-1])
    begun = [
        links.begin_gather(piece, d)
        for piece, d in zip(halves_of(links.end_gather(first_stage)), "yx")
    ]
    early_halves = [links.end_gather(piece) for piece in begun]
    early_a, early_b = joined(
        [links.gather(piece, d) for piece, d in zip(early_halves, "xy")]
    )
    split = early_a.shape[1]
    late = with_partner(
        jnp.concatenate([up_cols, jnp.broadcast_to(out_weight, (2, own, width))], axis=2)
    )
    down_own = down_weight.reshape(splits, pair_row, width)
    late = lax.all_gather(
        pack([late, *(down_own[i] for i in range(splits))], [*first_stage[1], come]),
        ("dp", "xx"),
        axis=0,
        tiled=True,
    )
    small = early_b[:, cols - split :].astype(F32).T
    gain_one, shift_one, query_shift, value_shift, out_shift, gain_two, shift_two, down_shift = (
        small[i] for i in range(8)
    )
    up_shift = small[8 : 8 + splits].reshape(hidden)

    inputs = inputs_low.astype(F32)
    seg = at_index(segments, side)
    numbers = jnp.arange(PAIR, dtype=jnp.int32) % HEAD_DIM
    same = seg[:, None] == numbers[None, :]
    coded = numbers[None, :] < 4
    query_code = jnp.where(same & coded, 1.0, 0.0).astype(BF16)
    key_code = jnp.where(same | ~coded, 0.0, NEG).astype(BF16)

    def head_cols(vector):
        return lax.dynamic_slice_in_dim(vector, core * half, half, 0).reshape(pairs, 1, PAIR)

    zeros = jnp.zeros((pairs, 1, PAIR), F32)
    qkv_shift = jnp.concatenate(
        [head_cols(query_shift), zeros, head_cols(value_shift)], axis=1
    ).reshape(1, cols)
    qkv_scale = jnp.tile(jnp.repeat(jnp.array([0.125, 1.0, 1.0], F32), PAIR), pairs)[None]
    normed_t, qkv, tick = qkv_projection(
        inputs_low,
        early_a,
        early_b,
        jnp.pad(jnp.stack([gain_one, shift_one]), ((0, 6), (0, 0))),
        jnp.pad(jnp.concatenate([qkv_shift, qkv_scale]), ((0, 6), (0, 0))),
        [],
    )
    attended, log_total, _ = attention_forward(qkv, query_code, key_code, [grad_come])
    core_at = core.reshape(1).astype(jnp.int32)
    branch = out_projection(core_at, attended, late, splits, [])
    branch_come = swap(branch, "core")
    mid_vectors = jnp.pad(
        jnp.stack([out_shift, gain_two, shift_two, down_shift]), ((0, 4), (0, 0))
    )
    normed_two_low, hidden_low, grad_pre_low, mixed_part, ffn_other, partial_two, up_sums = feed_forward(
        core_at,
        inputs_low,
        branch,
        branch_come,
        grad_out_low,
        late,
        splits,
        mid_vectors,
        jnp.pad(up_shift[None], ((0, 7), (0, 0))),
    )
    partial_come = swap(partial_two, "core")
    mixed_own = (mixed_part + swap(ffn_other, "core").astype(F32)).astype(BF16)
    mixed_own = mixed_own.reshape(2, quarter, width)
    mixed_come = swap(at_index(mixed_own, 1 - side), "xx")

    grad_proj_down = [
        mm(hidden_low[:, i * width : (i + 1) * width], grad_out_low, TN).astype(BF16)
        for i in range(splits)
    ]
    grad_proj_up = mm(normed_two_low, grad_pre_low, TN).astype(BF16)
    late_grads = jnp.concatenate([grad_proj_up, *grad_proj_down], axis=1)
    late_own = lax.psum_scatter(late_grads, ("dp", "xx"), scatter_dimension=0, tiled=True)
    grad_middle, branch_low, grad_attended, mid_sums = norm_two(
        core_at,
        inputs_low,
        branch,
        branch_come,
        grad_out_low,
        partial_two,
        partial_come,
        late,
        splits,
        mid_vectors,
        [late_grads],
    )
    grad_proj_out = mm(attended, branch_low, TN)

    def as_column(vectors):
        table = jnp.stack(vectors, axis=1)
        return jnp.pad(table, ((0, 0), (0, PAIR - table.shape[1])))

    def only_mine(flag, array):
        return jnp.where(flag, array, jnp.zeros_like(array))

    small_two = [mid_sums[i] for i in range(4)] + [
        up_sums[0, i * width : (i + 1) * width] for i in range(splits)
    ]
    out_low = grad_proj_out.astype(BF16)
    grad_out_rows = jnp.concatenate(
        [only_mine(core == 0, out_low), only_mine(core == 1, out_low)], axis=0
    )

    def blocks(array):
        return array.reshape(chips, pair_row, array.shape[1])

    def pairs_backward(first, count, after):
        return attention_backward(
            first, count, qkv, query_code, key_code, attended, grad_attended, log_total, normed_t, after
        )

    out_piece = links.scatter([blocks(grad_out_rows)], [], links.dims, "y")
    grad_a, weight_grad_a, tick = pairs_backward(0, pairs - 1, [out_piece[0][0]])
    out_piece = links.scatter(*out_piece, "x", [tick])
    first_piece = links.scatter([blocks(weight_grad_a)], [], links.dims, "y", [tick])
    mixed = merge(at_index(mixed_own, side), mixed_come, side, [tick])
    grad_b, weight_grad_b, tick = pairs_backward(
        pairs - 1, 1, [out_piece[0][0], first_piece[0][0], tick, mixed]
    )
    grads = [grad_a, grad_b]
    first_piece = links.scatter(*first_piece, "x", [tick])
    norm_vectors = jnp.pad(jnp.stack([gain_one, shift_one]), ((0, 6), (0, 0)))
    partial_one, norm_sums, bias_sums, tick = norm_one(
        False, core_at, grads, early_a, early_b, cols, inputs_low, [], [first_piece[0][0]]
    )
    come = swap(partial_one, "core")
    token_own, norm_sums_own, bias_sums_own, tick = norm_one(
        True,
        core_at,
        grads,
        early_a,
        early_b,
        cols,
        inputs_low,
        [come, grad_middle, norm_vectors],
        [],
    )
    norm_sums = norm_sums + norm_sums_own
    bias_sums = bias_sums + bias_sums_own
    token_grad, come = from_sequence(token_own.reshape(2, quarter, width))
    grad_by_pair = bias_sums[0].reshape(pairs, 3, PAIR)

    def padded(vector):
        vector = vector.reshape(half)
        return jnp.concatenate([only_mine(core == 0, vector), only_mine(core == 1, vector)])

    small = as_column(
        [
            norm_sums[0],
            norm_sums[1],
            padded(grad_by_pair[:, 0]),
            padded(grad_by_pair[:, 2]),
        ]
        + small_two
    )
    last_piece = links.scatter(
        [blocks(weight_grad_b), blocks(small.astype(BF16))], [], links.dims, "y", [tick]
    )
    first_piece = (
        out_piece[0] + first_piece[0],
        [out_piece[1][0] + first_piece[1][0]],
        first_piece[2],
    )
    first_own = links.scatter_rest(first_piece, [tick])
    last_piece = links.scatter(*last_piece, "x")
    last_ready = last_piece[0][0]
    last_own = links.scatter_rest(last_piece, [come])

    def rows_of(array, index):
        return lax.dynamic_slice_in_dim(array, index * own, own, 0)

    def by_core(mine, come):
        return jnp.stack(pick(core, mine, come))

    def shared(array):
        return rows_of(array, core), swap(rows_of(array, 1 - core), "core")

    up_own, down_grad = widen(late_own, width, [last_ready])
    late_mine, late_come = shared(up_own)
    early_mine, early_come = shared(jnp.concatenate([first_own, last_own], axis=1).astype(BF16))
    out_grad = early_mine[:, :width].astype(F32) + early_come[:, :width].astype(F32)
    up_grad = (
        by_core(late_mine, late_come)
        .reshape(2, own, splits, chips, pair_row)
        .transpose(1, 3, 0, 2, 4)
        .reshape(own, 2 * hidden)
        .astype(F32)
    )
    down_grad = down_grad.reshape(hidden_own, width)
    qkv_grad = (
        by_core(early_mine[:, width : width + cols], early_come[:, width : width + cols])
        .reshape(2, own, pairs, 3, PAIR)
        .transpose(1, 3, 0, 2, 4)
        .reshape(own, 2 * cols)
        .astype(F32)
    )
    tail, first = width + cols + 8, first_own.shape[1]
    small_mine = early_mine[:, tail - 8 : tail].astype(F32)
    one = small_mine[:, :4] + early_come[:, tail - 8 : tail - 4].astype(F32)
    up_shift_grad = (
        last_own[:, tail - first : tail - first + splits].T.reshape(hidden_own).astype(F32)
    )
    two = small_mine[:, 4:]
    return (
        mixed,
        token_grad,
        one[:, 0],
        one[:, 1],
        qkv_grad,
        one[:, 2],
        one[:, 3],
        out_grad,
        two[:, 0],
        two[:, 1],
        two[:, 2],
        up_grad,
        up_shift_grad,
        down_grad,
        two[:, 3],
    )


def solution(mesh):
    parts = (mesh.shape["dp"], mesh.shape["ctx"] // 2, 2)
    split_mesh = Mesh(mesh.devices.reshape(parts), ("dp", "xx", "core"))
    rows = ("dp", "xx", "core")
    acts = P("dp", ("xx", "core"), None)
    vec, mat = P(rows), P(rows, None)
    return jax.shard_map(
        body,
        mesh=split_mesh,
        in_specs=(
            acts, P("dp", None), vec, vec, mat, vec, vec, mat, vec, vec, vec, mat, vec, mat, vec, acts,
        ),
        out_specs=(
            acts, acts, vec, vec, mat, vec, vec, mat, vec, vec, vec, mat, vec, mat, vec,
        ),
        check_vma=False,
    )
```
